32 devices in a mesh: dp: 8 (over y, x, core), mp: 4 (over z).
Axes of the slice: x: 2, y: 2, z: 4, core: 2. Of those that a mesh axis runs over, the one named last changes fastest.
Arguments:
- tokens_in: bfloat16 [192, 196, 384], P(('dp', 'mp')), may hold values from -6 to 6
- image_counts: int32 [8], P('dp'), may hold values from 1 to 24, as said below
- norm1_gain: float32 [384], replicated, may hold values from 0.25 to 1.75
- norm1_bias: float32 [384], replicated, may hold values from -1.75 to 1.75
- qkv_weight: bfloat16 [384, 1152], replicated, may hold values from -0.3125 to 0.3125
- qkv_bias: float32 [1152], replicated, may hold values from -1.75 to 1.75
- mix_pre: float32 [8, 8], replicated, may hold values from -3 to 3
- mix_post: float32 [8, 8], replicated, may hold values from -2 to 2
- mix_post_bias: float32 [8], replicated, may hold values from -0.0625 to 0.0625
- proj_weight: bfloat16 [384, 384], replicated, may hold values from -2 to 2
- proj_bias: float32 [384], replicated, may hold values from -1.75 to 1.75
- gamma1: float32 [384], replicated, may hold values from 0.25 to 1.75
- norm2_gain: float32 [384], replicated, may hold values from 0.25 to 1.75
- norm2_bias: float32 [384], replicated, may hold values from -1.75 to 1.75
- fc1_weight: bfloat16 [384, 1536], P(None, 'mp'), may hold values from -0.3125 to 0.3125
- fc1_bias: float32 [1536], P('mp'), may hold values from -1.75 to 1.75
- fc2_weight: bfloat16 [1536, 384], P('mp'), may hold values from -0.15625 to 0.15625
- fc2_bias: float32 [384], replicated, may hold values from -1.75 to 1.75
- gamma2: float32 [384], replicated, may hold values from 0.25 to 1.75
- out_grad: bfloat16 [192, 196, 384], P(('dp', 'mp')), may hold values from -6 to 6
Outputs:
- layer_out: bfloat16 [192, 196, 384], P(('dp', 'mp'))
- in_grad: float32 [192, 196, 384], P(('dp', 'mp'))
- grad_norm1_gain: float32 [384], P('dp')
- grad_norm1_bias: float32 [384], P('dp')
- grad_qkv_weight: float32 [384, 1152], P(None, 'dp')
- grad_qkv_bias: float32 [1152], P('dp')
- grad_mix_pre: float32 [8, 8], replicated
- grad_mix_post: float32 [8, 8], replicated
- grad_mix_post_bias: float32 [8], replicated
- grad_proj_weight: float32 [384, 384], P(None, 'dp')
- grad_proj_bias: float32 [384], P('dp')
- grad_gamma1: float32 [384], P('dp')
- grad_norm2_gain: float32 [384], P('dp')
- grad_norm2_bias: float32 [384], P('dp')
- grad_fc1_weight: float32 [384, 1536], P(None, ('mp', 'dp'))
- grad_fc1_bias: float32 [1536], P(('mp', 'dp'))
- grad_fc2_weight: float32 [1536, 384], P('mp', 'dp')
- grad_fc2_bias: float32 [384], P('dp')
- grad_gamma2: float32 [384], P('dp')
The draws below stay inside these ranges and needn't reach their ends.
Inputs may be any that keep to these rules, and one draw needn't show every extreme that they name: image_counts[g] images of data group g are present, filling its first slots; some group holds all 24.
All inputs are finite; a program needn't handle non-finite values.
Results may differ from the reference program's by a relative error of at most 0.015.
The reference program's roundings to bfloat16 on the way count: a program that leaves them out, or rounds other values in their place, can miss the bound.
Values may be sent and summed in bfloat16 or wider, within the bound.
No kernel may reach another device: no remote copies, remote signals or barrier semaphores. Data moves between devices by JAX's collectives and lax.ppermute only.
A program may use at most 192 MiB of HBM per device.

```python
import jax
import jax.numpy as jnp
from jax import lax

D = 384
HEADS = 8
FF = 1536
PATCHES = 196
IMG_GROUP = 24
GROUPS = 8
IMAGES = 192


def draw_image_counts(key, part):
    key = jax.random.fold_in(key, 7)
    first_key, second_key, pick_key = jax.random.split(key, 3)
    first_draw = jax.random.randint(first_key, (GROUPS,), 1, IMG_GROUP + 1)
    second_draw = jax.random.randint(second_key, (GROUPS,), 1, IMG_GROUP + 1)
    chosen_group = jax.random.randint(pick_key, (), 0, GROUPS)
    smaller = jnp.minimum(first_draw, second_draw)
    return jnp.where(jnp.arange(GROUPS) == chosen_group, IMG_GROUP, smaller).astype(jnp.int32)


def strengthened(array, stream_key, source, target, shards_of, factor):
    def block_of(axis_at):
        return (jnp.arange(array.shape[axis_at]) // (array.shape[axis_at] // shards_of)).reshape((-1,) + (1,) * (array.ndim - 1 - axis_at))

    near = jax.random.permutation(stream_key, shards_of)[block_of(target)]
    far = (block_of(target) + shards_of // 2) % shards_of
    return jnp.where((block_of(source) == near) | (block_of(source) == far), factor * array, array)


def block_scale(own_key, extent, shards, low, high):
    level = 1.0
    for position, blocks in shards:
        steps = jax.random.uniform(jax.random.fold_in(jax.random.fold_in(own_key, 6), position), (blocks,), jnp.float32, low / len(shards), high / len(shards))
        level = level * jnp.repeat(jnp.exp(steps), extent[position] // blocks).reshape((-1,) + (1,) * (len(extent) - 1 - position))
    return level


def centred(stream_key, dims, spread, reach, cuts=(), kind=jnp.bfloat16):
    drawn = jax.random.normal(stream_key, dims, jnp.float32) * spread
    if len(cuts) > 0:
        drawn = block_scale(stream_key, dims, cuts, -0.22, 0.18) * drawn
    return jnp.clip(drawn, min=-reach, max=reach).astype(kind)


def bell_draw_with(own_key, extent, deviation, most, cuts, heavy, held_as=jnp.bfloat16):
    entries = deviation * jax.random.normal(own_key, extent, jnp.float32)
    if cuts:
        entries = entries * block_scale(own_key, extent, cuts, -0.22, 0.18)
    return jnp.clip(strengthened(entries, jax.random.fold_in(own_key, 3), *heavy), -most, most).astype(held_as)


def setup_inputs(seed: int = 0) -> dict:
    arg_keys = jax.random.split(jax.random.key(seed), 21)
    tokens_in = centred(arg_keys[0], (IMAGES, PATCHES, D), 1.0, 6.0, ((0, 32),))
    image_counts = draw_image_counts(jax.random.fold_in(arg_keys[20], 71), 0)
    norm1_gain = jnp.clip(1.0 + 0.15 * jax.random.normal(arg_keys[2], (D,), jnp.float32), 0.25, 1.75)
    norm1_bias = centred(arg_keys[3], (D,), 0.3, 1.75, (), jnp.float32)
    qkv_weight = centred(arg_keys[4], (D, 3 * D), D ** -0.5, 0.3125)
    qkv_bias = centred(arg_keys[5], (3 * D,), 0.3, 1.75, (), jnp.float32)
    mix_pre = centred(arg_keys[6], (HEADS, HEADS), 0.5, 3.0, (), jnp.float32)
    mix_post = centred(arg_keys[7], (HEADS, HEADS), 0.35, 2.0, (), jnp.float32)
    mix_post_bias = centred(arg_keys[8], (HEADS,), 0.01, 0.0625, (), jnp.float32)
    proj_weight = centred(arg_keys[9], (D, D), (D // 48) ** -0.5, 2.0)
    proj_bias = centred(arg_keys[10], (D,), 0.3, 1.75, (), jnp.float32)
    gamma1 = jnp.clip(1.0 + 0.15 * jax.random.normal(arg_keys[11], (D,), jnp.float32), 0.25, 1.75)
    norm2_gain = jnp.clip(1.0 + 0.15 * jax.random.normal(arg_keys[12], (D,), jnp.float32), 0.25, 1.75)
    norm2_bias = centred(arg_keys[13], (D,), 0.3, 1.75, (), jnp.float32)
    fc1_weight = centred(arg_keys[14], (D, FF), D ** -0.5, 0.3125, ((1, 4),))
    fc1_bias = centred(arg_keys[15], (FF,), 0.3, 1.75, ((0, 4),), jnp.float32)
    fc2_weight = centred(arg_keys[16], (FF, D), FF ** -0.5, 0.15625, ((0, 4),))
    fc2_bias = centred(arg_keys[17], (D,), 0.3, 1.75, (), jnp.float32)
    gamma2 = jnp.clip(1.0 + 0.15 * jax.random.normal(arg_keys[18], (D,), jnp.float32), 0.25, 1.75)
    out_grad = bell_draw_with(arg_keys[19], (IMAGES, PATCHES, D), 1.0, 6.0, ((0, 32),), (0, 2, 32, 2.75))
    return {"tokens_in": tokens_in, "image_counts": image_counts, "norm1_gain": norm1_gain, "norm1_bias": norm1_bias, "qkv_weight": qkv_weight, "qkv_bias": qkv_bias, "mix_pre": mix_pre, "mix_post": mix_post, "mix_post_bias": mix_post_bias, "proj_weight": proj_weight, "proj_bias": proj_bias, "gamma1": gamma1, "norm2_gain": norm2_gain, "norm2_bias": norm2_bias, "fc1_weight": fc1_weight, "fc1_bias": fc1_bias, "fc2_weight": fc2_weight, "fc2_bias": fc2_bias, "gamma2": gamma2, "out_grad": out_grad}


@jax.custom_vjp
def low(v):
    return lax.optimization_barrier(v.astype(jnp.bfloat16)).astype(jnp.float32)

@jax.custom_vjp
def low_back(v):
    return v

def low_keep(v):
    return (low(v), None)

def low_pass(kept, grad):
    return (grad,)

def back_keep(v):
    return (v, None)

def back_low(kept, grad):
    return (low(grad),)
low.defvjp(low_keep, low_pass)
low_back.defvjp(back_keep, back_low)
PRECISE = lax.Precision.HIGHEST

def layer_norm(values, gain, bias):
    average = lax.optimization_barrier(jnp.mean(values, axis=-1, keepdims=True))
    centered = values - average
    variance = lax.optimization_barrier(jnp.mean(centered * centered, axis=-1, keepdims=True))
    return centered * lax.rsqrt(variance + 1e-06) * gain + bias

def rounded_both(values):
    return low_back(low(values))

def block(tokens, live_mask, params):
    norm1_gain, norm1_bias, qkv_weight, qkv_bias, mix_pre, mix_post, mix_post_bias, proj_weight, proj_bias, gamma1, norm2_gain, norm2_bias, fc1_weight, fc1_bias, fc2_weight, fc2_bias, gamma2 = params
    image_count, patches, features = tokens.shape
    head_count = mix_pre.shape[0]
    head_dim = features // head_count
    first_norm = low(layer_norm(tokens, norm1_gain, norm1_bias))
    qkv_all = jnp.einsum('ipd,de->ipe', first_norm, qkv_weight, precision=PRECISE) + qkv_bias
    qkv_split = qkv_all.reshape(image_count, patches, 3, head_count, head_dim)
    queries = rounded_both(qkv_split[:, :, 0])
    key_rows = rounded_both(qkv_split[:, :, 1])
    value_rows = rounded_both(qkv_split[:, :, 2])
    scores = low_back(jnp.einsum('iphe,ishe->ihps', queries, key_rows, precision=PRECISE))
    logits = jnp.einsum('gh,ihps->igps', mix_pre, scores, precision=PRECISE) * head_dim ** (-0.5)
    shifted = logits - lax.optimization_barrier(jnp.max(logits, axis=-1, keepdims=True))
    expo = jnp.exp(shifted)
    probability = expo / lax.optimization_barrier(jnp.sum(expo, axis=-1, keepdims=True))
    mixed = low(jnp.einsum('gh,ihps->igps', mix_post, probability, precision=PRECISE) + mix_post_bias[None, :, None, None])
    attended = jnp.einsum('igps,isge->ipge', mixed, value_rows, precision=PRECISE)
    attended = rounded_both(attended.reshape(image_count, patches, features))
    branch = low_back(jnp.einsum('ipd,de->ipe', attended, proj_weight, precision=PRECISE) + proj_bias)
    middle = tokens + gamma1 * branch
    second_norm = low(layer_norm(middle, norm2_gain, norm2_bias))
    pre_act = low_back(jnp.einsum('ipd,df->ipf', second_norm, fc1_weight, precision=PRECISE) + fc1_bias)
    hidden = low(jax.nn.gelu(pre_act, approximate=False))
    mlp_out = low_back(jnp.einsum('ipf,fd->ipd', hidden, fc2_weight, precision=PRECISE) + fc2_bias)
    return live_mask[:, None, None] * (middle + gamma2 * mlp_out)

def reference(tokens_in, image_counts, norm1_gain, norm1_bias, qkv_weight, qkv_bias, mix_pre, mix_post, mix_post_bias, proj_weight, proj_bias, gamma1, norm2_gain, norm2_bias, fc1_weight, fc1_bias, fc2_weight, fc2_bias, gamma2, out_grad):
    params = tuple((w.astype(jnp.float32) for w in (norm1_gain, norm1_bias, qkv_weight, qkv_bias, mix_pre, mix_post, mix_post_bias, proj_weight, proj_bias, gamma1, norm2_gain, norm2_bias, fc1_weight, fc1_bias, fc2_weight, fc2_bias, gamma2)))
    slot_index = (jnp.arange(IMAGES) % IMG_GROUP).astype(jnp.int32)
    group_index = (jnp.arange(IMAGES) // IMG_GROUP).astype(jnp.int32)
    live_mask = (slot_index < image_counts[group_index]).astype(jnp.float32)
    scanned = (tokens_in.astype(jnp.float32).reshape(GROUPS, IMG_GROUP, PATCHES, D), live_mask.reshape(GROUPS, IMG_GROUP), out_grad.astype(jnp.float32).reshape(GROUPS, IMG_GROUP, PATCHES, D))

    def group_step(totals, group_item):
        group_tokens, group_live, group_cot = group_item
        result, pullback = jax.vjp(lambda inputs, weights: block(inputs, group_live, weights), group_tokens, params)
        grad_tokens, grad_weights = pullback(group_cot)
        return (jax.tree.map(jnp.add, totals, grad_weights), (result.astype(jnp.bfloat16), grad_tokens))
    zero_grads = jax.tree.map(jnp.zeros_like, params)
    totals, (outputs, input_grads) = lax.scan(group_step, zero_grads, scanned)
    return (outputs.reshape(IMAGES, PATCHES, D), input_grads.reshape(IMAGES, PATCHES, D), totals[0], totals[1], totals[2], totals[3], totals[4], totals[5], totals[6], totals[7], totals[8], totals[9], totals[10], totals[11], totals[12], totals[13], totals[14], totals[15], totals[16])
```

```python
import functools

import jax
import jax.numpy as jnp
from jax import lax
from jax.experimental import pallas as pl
from jax.experimental.pallas import tpu as pltpu
from jax.sharding import PartitionSpec as P

BF = jnp.bfloat16
F32 = jnp.float32
LOG2E = 1.4426950408889634
EPS = 1e-06
VMEM_LIMIT = 56 * 1024 * 1024

N1G, N1B, QKVB, PROJB, GAMMA1, N2G, N2B, FC2B, GAMMA2, MIXB = 0, 1, 2, 5, 6, 7, 8, 9, 10, 11


def nn(a, b):
    return lax.dot_general(a, b, (((1,), (0,)), ((), ())), preferred_element_type=F32)


def nt(a, b):
    return lax.dot_general(a, b, (((1,), (1,)), ((), ())), preferred_element_type=F32)


def tn(a, b):
    return lax.dot_general(a, b, (((0,), (0,)), ((), ())), preferred_element_type=F32)


def normalized(x):
    mean = jnp.mean(x, axis=-1, keepdims=True)
    c = x - mean
    r = lax.rsqrt(jnp.mean(c * c, axis=-1, keepdims=True) + EPS)
    return c * r, r


def norm_back(cot, n, r, gain):
    cg = cot * gain
    return r * (
        cg
        - jnp.mean(cg, axis=-1, keepdims=True)
        - n * jnp.mean(cg * n, axis=-1, keepdims=True)
    )


def colsum(x):
    return jnp.sum(x, axis=0, keepdims=True)


def split(x):
    hi = x.astype(BF)
    return jnp.concatenate([hi, (x - hi.astype(F32)).astype(BF)], axis=1)


def gelu_parts(z):
    e = jnp.exp2(z * z * (-0.5 * LOG2E))
    t = 1.0 / (1.0 + jnp.abs(z) * (0.3275911 * 0.7071067811865476))
    poly = t * (
        0.5 * 0.254829592
        + t
        * (
            0.5 * -0.284496736
            + t * (0.5 * 1.421413741 + t * (0.5 * -1.453152027 + t * (0.5 * 1.061405429)))
        )
    )
    tail = poly * e
    phi = jnp.where(z >= 0, 1.0 - tail, tail)
    return phi, phi + z * e * 0.3989422804014327


def attn_fwd_kernel(
    info, tok, og, vec, mpre, mpost, wqkv, wproj,
    a1_o, q_o, k_o, v_o, p_o, o_o, x1_o, u_o, a2_o, dy_o,
    pad,
):
    i = pl.program_id(0)
    patches, feats = tok.shape[1:]
    rows = pad.shape[0]
    heads = mpre.shape[0]
    slots = k_o.shape[1]
    row = lambda j: vec[j : j + 1, :]
    live_rows = lax.broadcasted_iota(jnp.int32, (rows, feats), 0) < patches

    pad[patches:, :] = jnp.zeros((rows - patches, feats), F32)
    live = (i < info[0]).astype(F32)
    pad[0:patches, :] = og[0].astype(F32) * live
    dy_o[0] = pad[...].astype(BF)
    pad[0:patches, :] = tok[0].astype(F32)
    x = pad[...]
    n, _ = normalized(x)
    a1 = (n * row(N1G) + row(N1B)).astype(BF)
    a1_o[0] = a1
    qkv = [
        nn(a1, wqkv[:, j * feats : (j + 1) * feats]) + row(QKVB + j) for j in range(3)
    ]
    q = qkv[0].astype(BF)
    k = qkv[1].astype(BF)
    v = jnp.where(live_rows, qkv[2], 0.0).astype(BF)
    q_o[0] = q
    k_o[0, 0:rows] = k
    k_o[0, rows:] = jnp.zeros((slots - rows, feats), BF)
    v_o[0, 0:rows] = v
    v_o[0, rows:] = jnp.zeros((slots - rows, feats), BF)
    k2 = jnp.concatenate([k_o[0], k_o[0]], axis=1)
    vs = v_o[0]
    qf = q.astype(F32)
    valid = lax.broadcasted_iota(jnp.int32, (rows, slots), 1) < patches

    def logits(g):
        return nt(split(qf * mpre[g : g + 1, :]), k2)

    def values(h, p):
        return nn(p, vs) * mpost[h : h + 1, :]

    attended = row(MIXB) * colsum(v.astype(F32))
    upcoming = logits(0)
    before = None
    for g in range(heads):
        current = upcoming
        if g + 1 < heads:
            upcoming = logits(g + 1)
        if before is not None:
            attended = attended + values(g - 1, before)
        current = jnp.where(valid, current, -1e30)
        e = jnp.exp2(current - jnp.max(current, axis=-1, keepdims=True))
        p = (e * (1.0 / jnp.sum(e, axis=-1, keepdims=True))).astype(BF)
        p_o[0, g] = p
        before = p
    attended = attended + values(heads - 1, before)
    o = attended.astype(BF)
    o_o[0] = o
    u = nn(o, wproj[...]) + row(PROJB)
    x1 = x + row(GAMMA1) * u
    u_o[0] = u
    x1_o[0] = x1
    n, _ = normalized(x1)
    a2_o[0] = (n * row(N2G) + row(N2B)).astype(BF)


def store_blocks(info, value, count, put):
    size = value.shape[0] // count
    for b in range(count):
        place = jnp.bitwise_xor(jnp.int32(b), info[1])
        block = value[b * size : (b + 1) * size]

        @pl.when(jnp.bitwise_and(place, 1) == 0)
        def _():
            put(0, jnp.right_shift(place, 1), block)

        @pl.when(jnp.bitwise_and(place, 1) == 1)
        def _():
            put(1, jnp.right_shift(place, 1), block)


def mlp_first_kernel(
    info, a2, dy, vec, w1, b1, w2,
    f_o, da2_o, keep, send, b1_o,
    hids, dzs, dfs,
):
    i = pl.program_id(0)
    rows = f_o.shape[1]
    mine = pl.ds(pl.multiple_of(i * rows, rows), rows)
    df = (dy[i].astype(F32) * vec[GAMMA2 : GAMMA2 + 1, :]).astype(BF)
    dfs[mine, :] = df
    z = nn(a2[i], w1[...]) + b1[...]
    phi, slope = gelu_parts(z)
    hid = (z * phi).astype(BF)
    dz = (nt(df, w2[...]) * slope).astype(BF)
    hids[mine, :] = hid
    dzs[mine, :] = dz
    f_o[0] = nn(hid, w2[...])
    da2_o[0] = nt(dz, w1[...])

    @pl.when(i == 0)
    def _():
        b1_o[...] = jnp.zeros_like(b1_o)

    b1_o[...] += colsum(dz.astype(F32))

    @pl.when(i == pl.num_programs(0) - 1)
    def _():
        count = 2 * keep.shape[0]
        size = keep.shape[1] // 2
        outs = (keep, send)
        a2_all = a2[...].reshape(dzs.shape[0], a2.shape[2])

        def put(part):
            def inner(which, place, block):
                outs[which][place, part * size : (part + 1) * size, :] = block.astype(BF)
            return inner

        store_blocks(info, tn(dzs[...], a2_all), count, put(0))
        store_blocks(info, tn(dfs[...], hids[...]), count, put(1))


def mlp_rest_kernel(
    info, a2, dy, x1, u, o, f0, da20, vec, near, far, b1, wproj,
    out_o, dx1_o, do_o, keep, send, b1_o, acc_o,
    w1, w2, hids, dzs, dfs, dus,
):
    i = pl.program_id(0)
    rows = f0.shape[1]
    patches = out_o.shape[1]
    feats = f0.shape[2]
    chunks = near.shape[0]
    row = lambda j: vec[j : j + 1, :]
    mine = pl.ds(pl.multiple_of(i * rows, rows), rows)

    @pl.when(i == 0)
    def _():
        b1_o[...] = jnp.zeros_like(b1_o)
        acc_o[...] = jnp.zeros_like(acc_o)

    for core in range(2):

        @pl.when(jnp.logical_and(i == 0, jnp.bitwise_and(info[1], 1) == core))
        def _(core=core):
            first, second = (near, far) if core == 0 else (far, near)
            for c in range(chunks):
                w1[:, c * feats : (c + 1) * feats] = first[c]
                w2[c * feats : (c + 1) * feats, :] = second[c]

    dyf = dy[i].astype(F32)
    df = (dyf * row(GAMMA2)).astype(BF)
    dfs[mine, :] = df
    f = f0[0]
    da2 = da20[0]
    for c in range(chunks):
        part = slice(c * feats, (c + 1) * feats)
        z = nn(a2[i], w1[:, part]) + b1[:, part]
        phi, slope = gelu_parts(z)
        hid = (z * phi).astype(BF)
        dz = (nt(df, w2[part, :]) * slope).astype(BF)
        hids[mine, part] = hid
        dzs[mine, part] = dz
        f = f + nn(hid, w2[part, :])
        da2 = da2 + nt(dz, w1[:, part])
        b1_o[:, part] += colsum(dz.astype(F32))
    f = f + row(FC2B)
    live = (i < info[0]).astype(F32)
    x1v = x1[0]
    out_o[0] = ((x1v + row(GAMMA2) * f) * live)[0:patches].astype(BF)
    n, r = normalized(x1v)
    dx1 = dyf + norm_back(da2, n, r, row(N2G))
    dx1_o[0] = dx1
    du = (dx1 * row(GAMMA1)).astype(BF)
    dus[mine, :] = du
    do_o[0] = nt(du, wproj[...]).astype(BF)
    acc_o[0:1, :] += colsum(du.astype(F32))
    acc_o[1:2, :] += colsum(u[0] * dx1)
    acc_o[2:3, :] += colsum(da2 * n)
    acc_o[3:4, :] += colsum(da2)
    acc_o[4:5, :] += colsum(f * dyf)
    acc_o[5:6, :] += colsum(df.astype(F32))

    @pl.when(i == pl.num_programs(0) - 1)
    def _():
        count = 2 * keep.shape[0]
        size = feats // count
        outs = (keep, send)
        total = dzs.shape[0]

        def put(at):
            def inner(which, place, block):
                outs[which][place, at : at + size, :] = block.astype(BF)
            return inner

        a2_all = a2[...].reshape(total, feats)
        for c in range(chunks):
            part = slice(c * feats, (c + 1) * feats)
            store_blocks(info, tn(dzs[:, part], a2_all), count, put(2 * c * size))
            store_blocks(info, tn(dfs[...], hids[:, part]), count, put((2 * c + 1) * size))
        o_all = o[...].reshape(total, feats)
        store_blocks(info, tn(dus[...], o_all), count, put(2 * chunks * size))


def attn_bwd_kernel(
    do_r, q_r, k_r, v_r, p_r, vec, mpre, mpost,
    dqkv_o, acc_o,
    dls, qgs,
):
    i = pl.program_id(0)
    rows, feats = do_r.shape[1:]
    heads = mpre.shape[0]
    slots = k_r.shape[1]

    @pl.when(i == 0)
    def _():
        acc_o[...] = jnp.zeros_like(acc_o)

    do = do_r[0]
    dof = do.astype(F32)
    qf = q_r[0].astype(F32)
    k = k_r[0]
    v = v_r[0]
    vf = v.astype(F32)
    v2 = jnp.concatenate([v, v], axis=1)
    real = lax.broadcasted_iota(jnp.int32, (rows, feats), 0) < PATCHES_OF[rows]

    def prob_grad(h):
        return nt(split(dof * mpost[h : h + 1, :]), v2)

    dq = jnp.zeros((rows, feats), F32)
    dv = jnp.zeros((slots, feats), F32)
    upcoming = prob_grad(0)
    for h in range(heads):
        dp = upcoming
        if h + 1 < heads:
            upcoming = prob_grad(h + 1)
        p = p_r[0, h]
        dvh = tn(p, do)
        pf = p.astype(F32)
        mean = jnp.sum(dp * pf, axis=-1, keepdims=True) / jnp.sum(pf, axis=-1, keepdims=True)
        dl = (pf * (dp - mean)).astype(BF)
        dls[h * rows : (h + 1) * rows, :] = dl
        scale = mpre[h : h + 1, :]
        qgs[h * rows : (h + 1) * rows, :] = (qf * scale).astype(BF)
        t = nn(dl, k)
        dq = dq + t * scale
        acc_o[heads + h : heads + h + 1, :] += colsum(qf * t)
        dv = dv + dvh * mpost[h : h + 1, :]
        acc_o[h : h + 1, :] += colsum(vf * dvh)
    dk = tn(dls[...], qgs[...])[0:rows] * (1.0 / LOG2E)
    dq = dq * (1.0 / LOG2E)
    do_sum = colsum(dof)
    dv = jnp.where(real, dv[0:rows] + vec[MIXB : MIXB + 1, :] * do_sum, 0.0)
    for j, part in enumerate((dq, dk, dv)):
        low = part.astype(BF)
        dqkv_o[0, :, j * feats : (j + 1) * feats] = low
        acc_o[2 * heads + j : 2 * heads + j + 1, :] += colsum(low.astype(F32))
    acc_o[2 * heads + 3 : 2 * heads + 4, :] += do_sum * colsum(vf)


PATCHES_OF = {208: 196}


def qkv_grad_kernel(info, *refs):
    parts, a1, keep, send = refs[:-3], refs[-3], refs[-2], refs[-1]
    outs = (keep, send)
    feats = a1.shape[2]
    count = 2 * keep.shape[0]
    total = tn(
        jnp.concatenate([p[...].reshape(-1, p.shape[2]) for p in parts], axis=0),
        a1[...].reshape(-1, feats),
    )

    def put(which, place, block):
        outs[which][place] = block.astype(BF)

    store_blocks(info, total, count, put)


def input_grad_kernel(tok, dx1, dqkv, vec, wqkv, in_o, acc_o, pad):
    i = pl.program_id(0)
    patches, feats = tok.shape[1:]
    rows = pad.shape[0]

    @pl.when(i == 0)
    def _():
        acc_o[...] = jnp.zeros_like(acc_o)

    pad[patches:, :] = jnp.zeros((rows - patches, feats), F32)
    pad[0:patches, :] = tok[0].astype(F32)
    n, r = normalized(pad[...])
    da1 = nt(dqkv[0], wqkv[...])
    grad = dx1[0] + norm_back(da1, n, r, vec[N1G : N1G + 1, :])
    in_o[0] = grad[0:patches]
    acc_o[0:1, :] += colsum(da1 * n)
    acc_o[1:2, :] += colsum(da1)


def whole(shape):
    return pl.BlockSpec(shape, lambda i: (0,) * len(shape))


def each(shape, first=0):
    return pl.BlockSpec((1,) + shape[1:], lambda i: (i + first,) + (0,) * (len(shape) - 1))


SCALARS = pl.BlockSpec(memory_space=pltpu.SMEM)


def sds(shape, dtype):
    return jax.ShapeDtypeStruct(shape, dtype)


def call(kernel, grid, ins, in_specs, outs, out_specs, scratch=(), flops=0, name=None):
    size = lambda a: a.size * a.dtype.itemsize
    return pl.pallas_call(
        kernel,
        grid=grid,
        in_specs=in_specs,
        out_specs=out_specs,
        out_shape=outs,
        scratch_shapes=scratch,
        compiler_params=pltpu.CompilerParams(vmem_limit_bytes=VMEM_LIMIT),
        cost_estimate=pl.CostEstimate(
            flops=flops,
            bytes_accessed=sum(size(a) for a in ins) + sum(size(a) for a in outs),
            transcendentals=0,
        ),
        name=name,
    )(*ins)


def xor_perm(count, mask):
    return [(j, j ^ mask) for j in range(count)]


def dp_hops(dp):
    bits = dp.bit_length() - 1
    groups = []
    at = 1
    while at < bits:
        groups.append((at, min(2, bits - at)))
        at += groups[-1][1]
    return groups


def dp_scatter(keep, received, dp):
    value = keep.astype(F32) + received.astype(F32)
    for at, many in dp_hops(dp):
        value = value.reshape((-1, 1 << many) + value.shape[1:])
        got = [
            lax.ppermute(value[:, j].astype(BF), "dp", xor_perm(dp, j << at))
            for j in range(1, 1 << many)
        ]
        value = value[:, 0] + sum(g.astype(F32) for g in got)
    return value.reshape(value.shape[-2:])


def per_device(
    dp, mp,
    tokens_in, image_counts, norm1_gain, norm1_bias, qkv_weight, qkv_bias,
    mix_pre, mix_post, mix_post_bias, proj_weight, proj_bias, gamma1,
    norm2_gain, norm2_bias, fc1_weight, fc1_bias, fc2_weight, fc2_bias, gamma2, out_grad,
):
    images, patches, feats = tokens_in.shape
    heads = mix_pre.shape[0]
    head_dim = feats // heads
    factor = head_dim ** (-0.5)
    rows = -(-patches // 16) * 16
    slots = -(-patches // 128) * 128
    PATCHES_OF[rows] = patches
    hidden = fc1_weight.shape[1]
    d_idx = lax.axis_index("dp")
    m_idx = lax.axis_index("mp")
    info = jnp.stack([image_counts[0] - m_idx * images, d_idx]).astype(jnp.int32)

    core = jnp.bitwise_and(d_idx, 1)
    half = jnp.where(core == 0, fc1_weight, fc2_weight)
    near = [lax.ppermute(half, "mp", xor_perm(mp, j)) for j in range(1, mp)]
    bias_near = [
        lax.ppermute(fc1_bias[None, :], "mp", xor_perm(mp, j)) for j in range(1, mp)
    ]

    vec = jnp.concatenate(
        [
            norm1_gain[None], norm1_bias[None], qkv_bias.reshape(3, feats), proj_bias[None],
            gamma1[None], norm2_gain[None], norm2_bias[None], fc2_bias[None], gamma2[None],
            jnp.repeat(mix_post_bias, head_dim)[None],
        ]
    )
    mpre = jnp.repeat(mix_pre * (factor * LOG2E), head_dim, axis=1)
    mpost = jnp.repeat(mix_post.T, head_dim, axis=1)

    tok_rows = (images, rows, feats)
    slot_rows = (images, slots, feats)
    prob_shape = (images, heads, rows, slots)
    ins = [info, tokens_in, out_grad, vec, mpre, mpost, qkv_weight, proj_weight]
    a1, q, k, v, prob, o, x1, u, a2, dy = call(
        attn_fwd_kernel,
        (images,),
        ins,
        [SCALARS, each(tokens_in.shape), each(out_grad.shape)] + [whole(a.shape) for a in ins[3:]],
        [
            sds(tok_rows, BF), sds(tok_rows, BF), sds(slot_rows, BF), sds(slot_rows, BF),
            sds(prob_shape, BF), sds(tok_rows, BF), sds(tok_rows, F32), sds(tok_rows, F32),
            sds(tok_rows, BF), sds(tok_rows, BF),
        ],
        [each(s) for s in (tok_rows, tok_rows, slot_rows, slot_rows, prob_shape)]
        + [each(tok_rows)] * 5,
        [pltpu.VMEM((rows, feats), F32)],
        flops=images * 15 * 10**8,
        name="attn_fwd",
    )

    near_all = jnp.stack(near)
    near_all, x1 = lax.optimization_barrier((near_all, x1))
    far_all = lax.ppermute(near_all, "dp", xor_perm(dp, 1))

    block = feats // dp
    total = images * rows
    ins = [info, a2, dy, vec, fc1_weight, fc1_bias[None, :], fc2_weight]
    f0, da20, keep0, send0, b1_0 = call(
        mlp_first_kernel,
        (images,),
        ins,
        [SCALARS] + [whole(a.shape) for a in ins[1:]],
        [
            sds(tok_rows, F32), sds(tok_rows, F32), sds((dp // 2, 2 * block, feats), BF),
            sds((dp // 2, 2 * block, feats), BF), sds((1, hidden), F32),
        ],
        [
            each(tok_rows), each(tok_rows), whole((dp // 2, 2 * block, feats)),
            whole((dp // 2, 2 * block, feats)), whole((1, hidden)),
        ],
        [pltpu.VMEM((total, hidden), BF), pltpu.VMEM((total, hidden), BF), pltpu.VMEM((total, feats), BF)],
        flops=images * 4 * 10**8,
        name="mlp_first",
    )
    got0 = lax.ppermute(send0, "dp", xor_perm(dp, 1))

    b1_rest = jnp.concatenate(bias_near, axis=1)
    rest = (mp - 1) * hidden
    grad_rows = (2 * (mp - 1) + 1) * block
    ins = [info, a2, dy, x1, u, o, f0, da20, vec, near_all, far_all, b1_rest, proj_weight]
    layer_out, dx1, do, keep1, send1, b1_1, acc_mlp = call(
        mlp_rest_kernel,
        (images,),
        ins,
        [SCALARS, whole(tok_rows), whole(tok_rows), each(tok_rows), each(tok_rows), whole(tok_rows),
         each(tok_rows), each(tok_rows)]
        + [whole(a.shape) for a in ins[8:]],
        [
            sds(tokens_in.shape, BF), sds(tok_rows, F32), sds(tok_rows, BF),
            sds((dp // 2, grad_rows, feats), BF), sds((dp // 2, grad_rows, feats), BF),
            sds((1, rest), F32), sds((8, feats), F32),
        ],
        [
            each(tokens_in.shape), each(tok_rows), each(tok_rows),
            whole((dp // 2, grad_rows, feats)), whole((dp // 2, grad_rows, feats)),
            whole((1, rest)), whole((8, feats)),
        ],
        [
            pltpu.VMEM((feats, rest), BF), pltpu.VMEM((rest, feats), BF),
            pltpu.VMEM((total, rest), BF), pltpu.VMEM((total, rest), BF),
            pltpu.VMEM((total, feats), BF), pltpu.VMEM((total, feats), BF),
        ],
        flops=images * 14 * 10**8,
        name="mlp_rest",
    )
    got1 = lax.ppermute(send1, "dp", xor_perm(dp, 1))

    steps = 3 if images % 3 == 0 else 1
    share = images // steps
    dqkvs = []
    accs = []
    for s in range(steps):
        ins = [do, q, k, v, prob, vec, mpre, mpost]
        dqkv, acc = call(
            attn_bwd_kernel,
            (share,),
            ins,
            [each(a.shape, s * share) for a in ins[:5]] + [whole(a.shape) for a in ins[5:]],
            [sds((share, rows, 3 * feats), BF), sds((24, feats), F32)],
            [each((share, rows, 3 * feats)), whole((24, feats))],
            [pltpu.VMEM((heads * rows, slots), BF), pltpu.VMEM((heads * rows, feats), BF)],
            flops=share * 20 * 10**8,
            name="attn_bwd",
        )
        dqkvs.append(dqkv)
        accs.append(acc)

    mine0 = dp_scatter(keep0, got0, dp)
    mine1 = dp_scatter(keep1, got1, dp)
    proj_part = mine1[2 * (mp - 1) * block :]
    fc_sum = mine0
    proj_sum = proj_part
    for j in range(1, mp):
        payload = jnp.concatenate([mine1[2 * (j - 1) * block : 2 * j * block], proj_part]).astype(BF)
        got = lax.ppermute(payload, "mp", xor_perm(mp, j)).astype(F32)
        fc_sum = fc_sum + got[: 2 * block]
        proj_sum = proj_sum + got[2 * block :]

    q_block = 3 * feats // dp
    half_shape = (dp // 2, q_block, feats)
    ins = [info] + dqkvs + [a1]
    keep2, send2 = call(
        qkv_grad_kernel,
        (1,),
        ins,
        [SCALARS] + [whole(a.shape) for a in ins[1:]],
        [sds(half_shape, BF), sds(half_shape, BF)],
        [whole(half_shape), whole(half_shape)],
        flops=11 * 10**8,
        name="qkv_grad",
    )
    got2 = lax.ppermute(send2, "dp", xor_perm(dp, 1))
    dqkv_all = jnp.concatenate(dqkvs) if steps > 1 else dqkvs[0]
    ins = [tokens_in, dx1, dqkv_all, vec, qkv_weight]
    in_grad, acc_in = call(
        input_grad_kernel,
        (images,),
        ins,
        [each(a.shape) for a in ins[:3]] + [whole(a.shape) for a in ins[3:]],
        [sds(tokens_in.shape, F32), sds((8, feats), F32)],
        [each(tokens_in.shape), whole((8, feats))],
        [pltpu.VMEM((rows, feats), F32)],
        flops=images * 2 * 10**8,
        name="input_grad",
    )
    qkv_mine = dp_scatter(keep2, got2, dp)
    qkv_low = qkv_mine.astype(BF)
    qkv_sum = qkv_mine
    for j in range(1, mp):
        qkv_sum = qkv_sum + lax.ppermute(qkv_low, "mp", xor_perm(mp, j)).astype(F32)

    acc = sum(accs)
    post_part = acc[0:heads].reshape(heads, heads, head_dim).sum(-1).T
    pre_part = acc[heads : 2 * heads].reshape(heads, heads, head_dim).sum(-1) * factor
    bias_part = acc[2 * heads + 3].reshape(heads, head_dim).sum(-1)
    mix_row = jnp.concatenate(
        [post_part.reshape(-1), pre_part.reshape(-1), bias_part,
         jnp.zeros((feats - 2 * heads * heads - heads,), F32)]
    )
    b1_rel = jnp.concatenate([b1_0, b1_1], axis=1).reshape(mp, hidden)
    b1_abs = b1_rel[jnp.bitwise_xor(jnp.arange(mp, dtype=jnp.int32), m_idx)]
    small = jnp.concatenate(
        [acc_in[0:2], acc_mlp[0:6], acc[2 * heads : 2 * heads + 3], mix_row[None],
         b1_abs.reshape(-1, feats)]
    )
    small = small + lax.ppermute(small, "dp", xor_perm(dp, 1))
    for at, many in dp_hops(dp):
        small = small + sum(
            lax.ppermute(small, "dp", xor_perm(dp, j << at)) for j in range(1, 1 << many)
        )
    small = small + sum(lax.ppermute(small, "mp", xor_perm(mp, j)) for j in range(1, mp))
    vecs = lax.dynamic_slice(small[0:8], (0, d_idx * block), (8, block))
    qkvb = lax.dynamic_slice(small[8:11].reshape(-1), (d_idx * q_block,), (q_block,))
    b1_size = hidden // dp
    b1_grad = lax.dynamic_slice(
        small[12:].reshape(-1), (m_idx * hidden + d_idx * b1_size,), (b1_size,)
    )
    mixes = small[11]
    hh = heads * heads
    return (
        layer_out,
        in_grad,
        vecs[0],
        vecs[1],
        qkv_sum.T,
        qkvb,
        mixes[hh : 2 * hh].reshape(heads, heads),
        mixes[0:hh].reshape(heads, heads),
        mixes[2 * hh : 2 * hh + heads],
        proj_sum.T,
        vecs[2],
        vecs[3],
        vecs[4],
        vecs[5],
        fc_sum[:block].T,
        b1_grad,
        fc_sum[block:].T,
        vecs[7],
        vecs[6],
    )


def solution(mesh):
    tokens = P(("dp", "mp"), None, None)
    placed = (
        (tokens, P("dp")) + (P(),) * 12 + (P(None, "mp"), P("mp"), P("mp", None), P(), P(), tokens)
    )
    return jax.shard_map(
        functools.partial(per_device, mesh.shape["dp"], mesh.shape["mp"]),
        mesh=mesh,
        in_specs=placed,
        out_specs=(
            tokens, tokens, P("dp"), P("dp"), P(None, "dp"), P("dp"), P(), P(), P(),
            P(None, "dp"), P("dp"), P("dp"), P("dp"), P("dp"), P(None, ("mp", "dp")),
            P(("mp", "dp")), P("mp", "dp"), P("dp"), P("dp"),
        ),
        check_vma=False,
    )
```

```python
import functools

import jax
import jax.numpy as jnp
from jax import lax
from jax.experimental import pallas as pl
from jax.experimental.pallas import tpu as pltpu
from jax.sharding import PartitionSpec as P

BF = jnp.bfloat16
F32 = jnp.float32
LOG2E = 1.4426950408889634
EPS = 1e-06
VMEM_LIMIT = 56 * 1024 * 1024


def nn(a, b):
    return lax.dot_general(a, b, (((1,), (0,)), ((), ())), preferred_element_type=F32)


def nt(a, b):
    return lax.dot_general(a, b, (((1,), (1,)), ((), ())), preferred_element_type=F32)


def tn(a, b):
    return lax.dot_general(a, b, (((0,), (0,)), ((), ())), preferred_element_type=F32)


def exact(a, b, dims):
    return lax.dot_general(
        a, b, (dims, ((), ())), precision=lax.Precision.HIGHEST, preferred_element_type=F32
    )


def normalized(x):
    mean = jnp.mean(x, axis=-1, keepdims=True)
    c = x - mean
    r = lax.rsqrt(jnp.mean(c * c, axis=-1, keepdims=True) + EPS)
    return c * r, r


def norm_back(cot, n, r, gain):
    cg = cot * gain
    return r * (
        cg
        - jnp.mean(cg, axis=-1, keepdims=True)
        - n * jnp.mean(cg * n, axis=-1, keepdims=True)
    )


def colsum(x):
    return jnp.sum(x, axis=0, keepdims=True)


def split(x):
    hi = x.astype(BF)
    return jnp.concatenate([hi, (x - hi.astype(F32)).astype(BF)], axis=1)


def row(ref):
    return ref[...].reshape(1, ref.shape[0])


def gelu_parts(z):
    e = jnp.exp2(z * z * (-0.5 * LOG2E))
    t = 1.0 / (1.0 + jnp.abs(z) * (0.3275911 * 0.7071067811865476))
    poly = t * (
        0.5 * 0.254829592
        + t
        * (
            0.5 * -0.284496736
            + t * (0.5 * 1.421413741 + t * (0.5 * -1.453152027 + t * (0.5 * 1.061405429)))
        )
    )
    tail = poly * e
    phi = jnp.where(z >= 0, 1.0 - tail, tail)
    return phi, phi + z * e * 0.3989422804014327


def head_of_lane(shape, axis, head_dim):
    return lax.broadcasted_iota(jnp.int32, shape, axis) // head_dim


def attn_fwd_kernel(
    counts, tok, og, n1g, n1b, qkvb, pre, post, postb, projb, gamma1, n2g, n2b, wqkv, wproj,
    a1_o, q_o, k_o, v_o, p_o, o_o, x1_o, u_o, a2_o, dy_o, mpre, mpost, mixb,
    pad, qq,
):
    i = pl.program_id(0)
    images = pl.num_programs(0)
    patches, feats = tok.shape[1:]
    rows = pad.shape[0]
    heads = mpre.shape[0]
    head_dim = feats // heads
    slots = k_o.shape[1]
    live_rows = lax.broadcasted_iota(jnp.int32, (rows, feats), 0) < patches

    @pl.when(i == 0)
    def _():
        spread = (
            head_of_lane((heads, feats), 1, head_dim)
            == lax.broadcasted_iota(jnp.int32, (heads, feats), 0)
        ).astype(F32)
        mpre[...] = exact(pre[...], spread, ((1,), (0,))) * (head_dim**-0.5 * LOG2E)
        mpost[...] = exact(post[...], spread, ((0,), (0,)))
        mixb[...] = exact(row(postb), spread, ((1,), (0,)))

    pad[patches:, :] = jnp.zeros((rows - patches, feats), F32)
    live = (lax.axis_index("mp") * images + i < counts[0]).astype(F32)
    pad[0:patches, :] = og[0].astype(F32) * live
    dy_o[0] = pad[...].astype(BF)
    pad[0:patches, :] = tok[0].astype(F32)
    x = pad[...]
    n, _ = normalized(x)
    a1 = (n * row(n1g) + row(n1b)).astype(BF)
    a1_o[0] = a1
    bias = row(qkvb)
    qkv = [
        nn(a1, wqkv[:, j * feats : (j + 1) * feats]) + bias[:, j * feats : (j + 1) * feats]
        for j in range(3)
    ]
    q = qkv[0].astype(BF)
    k = qkv[1].astype(BF)
    v = jnp.where(live_rows, qkv[2], 0.0).astype(BF)
    q_o[0] = q
    k_o[0, 0:rows] = k
    k_o[0, rows:] = jnp.zeros((slots - rows, feats), BF)
    v_o[0, 0:rows] = v
    v_o[0, rows:] = jnp.zeros((slots - rows, feats), BF)
    qf = q.astype(F32)
    for g in range(heads):
        qq[g * rows : (g + 1) * rows, :] = split(qf * mpre[g : g + 1, :])
    k2 = jnp.concatenate([k_o[0], k_o[0]], axis=1)
    vs = v_o[0]
    valid = lax.broadcasted_iota(jnp.int32, (rows, slots), 1) < patches
    half = heads // 2 * rows
    logits = [nt(qq[s * half : (s + 1) * half, :], k2) for s in range(2)]
    attended = mixb[...] * colsum(v.astype(F32))
    for s in range(2):
        for j in range(heads // 2):
            g = s * (heads // 2) + j
            part = jnp.where(valid, logits[s][j * rows : (j + 1) * rows], -1e30)
            e = jnp.exp2(part - jnp.max(part, axis=-1, keepdims=True))
            p_o[0, g] = (e * (1.0 / jnp.sum(e, axis=-1, keepdims=True))).astype(BF)
        each_head = p_o[0, s * (heads // 2) : (s + 1) * (heads // 2)].reshape(half, slots)
        mixed = nn(each_head, vs)
        for j in range(heads // 2):
            g = s * (heads // 2) + j
            attended = attended + mixed[j * rows : (j + 1) * rows] * mpost[g : g + 1, :]
    o = attended.astype(BF)
    o_o[0] = o
    u = nn(o, wproj[...]) + row(projb)
    x1 = x + row(gamma1) * u
    u_o[0] = u
    x1_o[0] = x1
    n, _ = normalized(x1)
    a2_o[0] = (n * row(n2g) + row(n2b)).astype(BF)


def store_blocks(value, count, put):
    size = value.shape[0] // count
    mine = lax.axis_index("dp")
    for b in range(count):
        place = jnp.bitwise_xor(jnp.int32(b), mine)
        block = value[b * size : (b + 1) * size].astype(BF)

        @pl.when(jnp.bitwise_and(place, 1) == 0)
        def _():
            put(0, jnp.right_shift(place, 1), block)

        @pl.when(jnp.bitwise_and(place, 1) == 1)
        def _():
            put(1, jnp.right_shift(place, 1), block)


def mlp_first_kernel(
    a2, dy, gamma2, w1, b1, w2,
    f_o, da2_o, keep, send, b1_o,
    hids, dzs, dfs,
):
    i = pl.program_id(0)
    rows = f_o.shape[0]
    mine = pl.ds(pl.multiple_of(i * rows, rows), rows)
    df = (dy[mine, :].astype(F32) * row(gamma2)).astype(BF)
    dfs[mine, :] = df
    z = nn(a2[mine, :], w1[...]) + row(b1)
    grad_hidden = nt(df, w2[...])
    phi, slope = gelu_parts(z)
    hid = (z * phi).astype(BF)
    dz = (grad_hidden * slope).astype(BF)
    hids[mine, :] = hid
    dzs[mine, :] = dz
    f_o[...] = nn(hid, w2[...])
    da2_o[...] = nt(dz, w1[...])

    @pl.when(i == 0)
    def _():
        b1_o[...] = jnp.zeros_like(b1_o)

    b1_o[...] += colsum(dz.astype(F32))

    @pl.when(i == pl.num_programs(0) - 1)
    def _():
        count = 2 * keep.shape[0]
        size = keep.shape[1] // 2
        outs = (keep, send)

        def put(part):
            def inner(which, place, block):
                outs[which][place, part * size : (part + 1) * size, :] = block
            return inner

        store_blocks(tn(a2[...], dzs[...]).T, count, put(0))
        store_blocks(tn(dfs[...], hids[...]), count, put(1))


def mlp_rest_kernel(
    counts, a2, dy, x1, u, o, f0, da20, near, far, b1_all, wproj, gamma1, n2g, fc2b, gamma2,
    out_o, dx1_o, do_o, keep, send, b1_o, acc_o,
    w1, w2, b1, hids, dzs, dfs, dus,
):
    i = pl.program_id(0)
    rows, feats = f0.shape
    group, patches = out_o.shape[:2]
    image_rows = rows // group
    chunks = near.shape[0] - 1
    mine = pl.ds(pl.multiple_of(i * rows, rows), rows)
    m_idx = lax.axis_index("mp")

    @pl.when(i == 0)
    def _():
        b1_o[...] = jnp.zeros_like(b1_o)
        acc_o[...] = jnp.zeros_like(acc_o)
        for c in range(chunks):
            at = jnp.bitwise_xor(m_idx, c + 1)
            b1[:, c * feats : (c + 1) * feats] = b1_all[pl.ds(at, 1), :]

    for core in range(2):

        @pl.when(jnp.logical_and(i == 0, jnp.bitwise_and(lax.axis_index("dp"), 1) == core))
        def _(core=core):
            first, second = (near, far) if core == 0 else (far, near)
            for c in range(chunks):
                at = jnp.bitwise_xor(m_idx, c + 1)
                w1[:, c * feats : (c + 1) * feats] = first[at]
                w2[c * feats : (c + 1) * feats, :] = second[at]

    dyf = dy[mine, :].astype(F32)
    df = (dyf * row(gamma2)).astype(BF)
    dfs[mine, :] = df
    f = f0[...]
    da2 = da20[...]
    act = a2[mine, :]
    for c in range(chunks):
        part = slice(c * feats, (c + 1) * feats)
        z = nn(act, w1[:, part]) + b1[:, part]
        grad_hidden = nt(df, w2[part, :])
        phi, slope = gelu_parts(z)
        hid = (z * phi).astype(BF)
        dz = (grad_hidden * slope).astype(BF)
        hids[mine, part] = hid
        dzs[mine, part] = dz
        f = f + nn(hid, w2[part, :])
        da2 = da2 + nt(dz, w1[:, part])
        b1_o[:, part] += colsum(dz.astype(F32))
    f = f + row(fc2b)
    x1v = x1[...]
    layer_out = x1v + row(gamma2) * f
    for j in range(group):
        live = (m_idx * (group * pl.num_programs(0)) + i * group + j < counts[0]).astype(F32)
        out_o[j] = (layer_out[j * image_rows : j * image_rows + patches] * live).astype(BF)
    n, r = normalized(x1v)
    dx1 = dyf + norm_back(da2, n, r, row(n2g))
    dx1_o[...] = dx1
    du = (dx1 * row(gamma1)).astype(BF)
    dus[mine, :] = du
    do_o[...] = nt(du, wproj[...]).astype(BF)
    acc_o[0:1, :] += colsum(du.astype(F32))
    acc_o[1:2, :] += colsum(u[...] * dx1)
    acc_o[2:3, :] += colsum(da2 * n)
    acc_o[3:4, :] += colsum(da2)
    acc_o[4:5, :] += colsum(df.astype(F32))
    acc_o[5:6, :] += colsum(f * dyf)

    @pl.when(i == pl.num_programs(0) - 1)
    def _():
        count = 2 * keep.shape[0]
        size = feats // count
        outs = (keep, send)

        def put(at):
            def inner(which, place, block):
                outs[which][place, at : at + size, :] = block
            return inner

        for c in range(chunks):
            part = slice(c * feats, (c + 1) * feats)
            store_blocks(tn(a2[...], dzs[:, part]).T, count, put(2 * c * size))
            store_blocks(tn(dfs[...], hids[:, part]), count, put((2 * c + 1) * size))
        store_blocks(tn(dus[...], o[...]), count, put(2 * chunks * size))


def attn_bwd_kernel(do_r, q_r, k_r, v_r, p_r, dx1, tok, mpre, mpost, mixb, wqkv, n1g, *refs):
    dqkv_o, in_o, acc_o, dogs, dls, qgs, pad = refs[-7:]
    i = pl.program_id(0)
    rows, feats = do_r.shape[1:]
    patches = tok.shape[1]
    heads = mpre.shape[0]
    slots = k_r.shape[1]

    @pl.when(i == 0)
    def _():
        acc_o[...] = jnp.zeros_like(acc_o)

    do = do_r[0]
    dof = do.astype(F32)
    qf = q_r[0].astype(F32)
    k = k_r[0]
    v = v_r[0]
    vf = v.astype(F32)
    real = lax.broadcasted_iota(jnp.int32, (rows, feats), 0) < patches
    for h in range(heads):
        dogs[h * rows : (h + 1) * rows, :] = (dof * mpost[h : h + 1, :]).astype(BF)
        qgs[h * rows : (h + 1) * rows, :] = (qf * mpre[h : h + 1, :]).astype(BF)
    many = heads // 2
    half = many * rows
    dps = [nt(dogs[s * half : (s + 1) * half, :], v) for s in range(2)]
    dq = jnp.zeros((rows, feats), F32)
    dv = jnp.zeros((slots, feats), F32)
    for s in range(2):
        probs = [p_r[0, s * many + j] for j in range(many)]
        dvh = tn(jnp.concatenate(probs, axis=1), do)
        for j in range(many):
            h = s * many + j
            dp = dps[s][j * rows : (j + 1) * rows]
            pf = probs[j].astype(F32)
            mean = jnp.sum(dp * pf, axis=-1, keepdims=True) / jnp.sum(pf, axis=-1, keepdims=True)
            dls[h * rows : (h + 1) * rows, :] = (pf * (dp - mean)).astype(BF)
        for j in range(many):
            h = s * many + j
            this = dvh[j * slots : (j + 1) * slots]
            dv = dv + this * mpost[h : h + 1, :]
            acc_o[h : h + 1, :] += colsum(vf * this)
        t = nn(dls[s * half : (s + 1) * half, :], k)
        for j in range(many):
            h = s * many + j
            this = t[j * rows : (j + 1) * rows]
            dq = dq + this * mpre[h : h + 1, :]
            acc_o[heads + h : heads + h + 1, :] += colsum(qf * this)
    dk = tn(dls[...], qgs[...])[0:rows] * (1.0 / LOG2E)
    dq = dq * (1.0 / LOG2E)
    do_sum = colsum(dof)
    dv = jnp.where(real, dv[0:rows] + mixb[...] * do_sum, 0.0)
    acc_o[2 * heads : 2 * heads + 1, :] += do_sum * colsum(vf)
    for j, part in enumerate((dq, dk, dv)):
        low = part.astype(BF)
        dqkv_o[0, :, j * feats : (j + 1) * feats] = low
        acc_o[2 * heads + 8 + j : 2 * heads + 9 + j, :] += colsum(low.astype(F32))
    pad[patches:, :] = jnp.zeros((rows - patches, feats), F32)
    pad[0:patches, :] = tok[0].astype(F32)
    n, r = normalized(pad[...])
    da1 = nt(dqkv_o[0], wqkv[...])
    grad = dx1[0] + norm_back(da1, n, r, row(n1g))
    in_o[0] = grad[0:patches]
    acc_o[2 * heads + 11 : 2 * heads + 12, :] += colsum(da1 * n)
    acc_o[2 * heads + 12 : 2 * heads + 13, :] += colsum(da1)


def qkv_grad_kernel(heads, dqkv, *refs):
    accs = refs[:-6]
    a1, acc_mlp, b1_first, b1_rest, out, small = refs[-6:]
    feats = a1.shape[1]
    count, block_rows = out.shape[:2]
    size = 3 * feats // count
    chunks = b1_rest.shape[1] // feats
    acc = accs[0][...]
    for other in accs[1:]:
        acc = acc + other[...]
    small[...] = jnp.zeros_like(small)
    small[0:2, :] = acc[2 * heads + 11 : 2 * heads + 13]
    small[2:8, :] = acc_mlp[0:6, :]
    small[8:11, :] = acc[2 * heads + 8 : 2 * heads + 11]
    head_dim = feats // heads
    lanes = 2 * heads * heads
    gather = (
        head_of_lane((feats, lanes), 0, head_dim)
        == lax.broadcasted_iota(jnp.int32, (feats, lanes), 1) % heads
    ).astype(F32)
    sums = exact(acc[0 : 2 * heads + 8], gather, ((1,), (0,)))
    place = head_of_lane((2 * heads, lanes), 1, heads) == lax.broadcasted_iota(
        jnp.int32, (2 * heads, lanes), 0
    )
    small[11:12, 0:lanes] = colsum(jnp.where(place, sums[0 : 2 * heads], 0.0))
    small[11:12, lanes : 2 * lanes] = sums[2 * heads : 2 * heads + 1]
    m_idx = lax.axis_index("mp")
    small[pl.ds(12 + m_idx, 1), :] = b1_first[...]
    for c in range(chunks):
        small[pl.ds(12 + jnp.bitwise_xor(m_idx, c + 1), 1), :] = b1_rest[
            :, c * feats : (c + 1) * feats
        ]
    low = small[...].astype(BF)
    total = tn(dqkv[...], a1[...])
    for b in range(count):
        out[b, 0:size, :] = total[b * size : (b + 1) * size].astype(BF)
        out[b, size:, :] = low


def final_kernel(heads, size, mine, got, qkv_o, qkvb_o, pre_o, post_o, postb_o, b1_o, *vecs_o):
    total = mine[...]
    for j in range(got.shape[0]):
        total = total + got[j].astype(F32)
    feats = total.shape[1]
    qkv_o[...] = total[0:size]
    small = total[size:]
    d_idx = lax.axis_index("dp")
    m_idx = lax.axis_index("mp")

    def own(value, width, first):
        lane = lax.broadcasted_iota(jnp.int32, (value.shape[1], width), 0)
        want = lax.broadcasted_iota(jnp.int32, (value.shape[1], width), 1) + first
        return exact(value, (lane == want).astype(F32), ((1,), (0,)))

    width = vecs_o[0].shape[1]
    vecs = own(small[0:8], width, d_idx * width)
    for j, ref in enumerate(vecs_o):
        ref[...] = vecs[j : j + 1]
    wide = qkvb_o.shape[1]
    flat = 0.0
    for j in range(3):
        flat = flat + own(small[8 + j : 9 + j], wide, d_idx * wide - j * feats)
    qkvb_o[...] = flat
    b1 = own(small[12:16], b1_o.shape[1], d_idx * b1_o.shape[1])
    pick = lax.broadcasted_iota(jnp.int32, b1.shape, 0) == m_idx
    b1_o[...] = colsum(jnp.where(pick, b1, 0.0))
    mix = small[11:12]
    hh = heads * heads
    line = lax.broadcasted_iota(jnp.int32, (heads, hh), 0)
    lane = lax.broadcasted_iota(jnp.int32, (heads, hh), 1)
    fold = (
        lax.broadcasted_iota(jnp.int32, (hh, heads), 0) % heads
        == lax.broadcasted_iota(jnp.int32, (hh, heads), 1)
    ).astype(F32)
    head_dim = feats // heads

    def square(values):
        return exact(jnp.where(lane // heads == line, values, 0.0), fold, ((1,), (0,)))

    post_o[...] = square(mix[:, 0:hh]).T
    pre_o[...] = square(mix[:, hh : 2 * hh]) * (head_dim**-0.5)
    postb_o[...] = mix[:, 2 * hh : 2 * hh + heads]


def whole(shape):
    return pl.BlockSpec(shape, lambda i: (0,) * len(shape))


def each(shape, first=0, many=1):
    return pl.BlockSpec((many,) + shape[1:], lambda i: (i + first,) + (0,) * (len(shape) - 1))


SCALARS = pl.BlockSpec(memory_space=pltpu.SMEM)


def sds(shape, dtype):
    return jax.ShapeDtypeStruct(shape, dtype)


def call(
    kernel, grid, ins, in_specs, outs, out_specs, scratch=(), flops=0, name=None, aliases=None
):
    size = lambda a: a.size * a.dtype.itemsize
    return pl.pallas_call(
        kernel,
        grid=grid,
        in_specs=in_specs,
        out_specs=out_specs,
        out_shape=outs,
        scratch_shapes=scratch,
        input_output_aliases=aliases or {},
        compiler_params=pltpu.CompilerParams(vmem_limit_bytes=VMEM_LIMIT),
        cost_estimate=pl.CostEstimate(
            flops=flops,
            bytes_accessed=sum(size(a) for a in ins) + sum(size(a) for a in outs),
            transcendentals=0,
        ),
        name=name,
    )(*ins)


def xor_perm(count, mask):
    return [(j, j ^ mask) for j in range(count)]


def dp_hops(dp):
    bits = dp.bit_length() - 1
    groups = []
    at = 1
    while at < bits:
        groups.append((at, min(2, bits - at)))
        at += groups[-1][1]
    return groups


def dp_scatter(value, dp):
    for at, many in dp_hops(dp):
        value = value.reshape((-1, 1 << many) + value.shape[1:])
        got = [
            lax.ppermute(value[:, j].astype(BF), "dp", xor_perm(dp, j << at))
            for j in range(1, 1 << many)
        ]
        value = value[:, 0] + sum(g.astype(F32) for g in got)
    return value.reshape(value.shape[-2:])


def per_device(
    dp, mp,
    tokens_in, image_counts, norm1_gain, norm1_bias, qkv_weight, qkv_bias,
    mix_pre, mix_post, mix_post_bias, proj_weight, proj_bias, gamma1,
    norm2_gain, norm2_bias, fc1_weight, fc1_bias, fc2_weight, fc2_bias, gamma2, out_grad,
):
    images, patches, feats = tokens_in.shape
    heads = mix_pre.shape[0]
    rows = -(-patches // 16) * 16
    slots = -(-patches // 128) * 128
    hidden = fc1_weight.shape[1]
    core = jnp.bitwise_and(lax.axis_index("dp"), 1)

    near = lax.all_gather(jnp.where(core == 0, fc1_weight, fc2_weight), "mp")
    b1_all = lax.all_gather(fc1_bias, "mp")

    tok_rows = (images, rows, feats)
    slot_rows = (images, slots, feats)
    prob_shape = (images, heads, rows, slots)
    mix_shape = (heads, feats)
    ins = [
        image_counts, tokens_in, out_grad, norm1_gain, norm1_bias, qkv_bias, mix_pre, mix_post,
        mix_post_bias, proj_bias, gamma1, norm2_gain, norm2_bias, qkv_weight, proj_weight,
    ]
    a1, q, k, v, prob, o, x1, u, a2, dy, mpre, mpost, mixb = call(
        attn_fwd_kernel,
        (images,),
        ins,
        [SCALARS, each(tokens_in.shape), each(out_grad.shape)] + [whole(a.shape) for a in ins[3:]],
        [
            sds(tok_rows, BF), sds(tok_rows, BF), sds(slot_rows, BF), sds(slot_rows, BF),
            sds(prob_shape, BF), sds(tok_rows, BF), sds(tok_rows, F32), sds(tok_rows, F32),
            sds(tok_rows, BF), sds(tok_rows, BF), sds(mix_shape, F32), sds(mix_shape, F32),
            sds((1, feats), F32),
        ],
        [each(s) for s in (tok_rows, tok_rows, slot_rows, slot_rows, prob_shape)]
        + [each(tok_rows)] * 5
        + [whole(mix_shape)] * 2
        + [whole((1, feats))],
        [pltpu.VMEM((rows, feats), F32), pltpu.VMEM((heads * rows, 2 * feats), BF)],
        flops=images * 15 * 10**8,
        name="attn_fwd",
    )

    block = feats // dp
    total = images * rows
    group = 2 if images % 2 == 0 else 1
    flat = (total, feats)
    step = (group * rows, feats)
    a2, dy, x1, u, o = (a.reshape(flat) for a in (a2, dy, x1, u, o))
    ins = [a2, dy, gamma2, fc1_weight, fc1_bias, fc2_weight]
    blocked = pl.BlockSpec(step, lambda i: (i, 0))
    f0, da20, keep0, send0, b1_0 = call(
        mlp_first_kernel,
        (images // group,),
        ins,
        [whole(a.shape) for a in ins],
        [
            sds(flat, F32), sds(flat, F32), sds((dp // 2, 2 * block, feats), BF),
            sds((dp // 2, 2 * block, feats), BF), sds((1, hidden), F32),
        ],
        [
            blocked, blocked, whole((dp // 2, 2 * block, feats)),
            whole((dp // 2, 2 * block, feats)), whole((1, hidden)),
        ],
        [pltpu.VMEM((total, hidden), BF), pltpu.VMEM((total, hidden), BF), pltpu.VMEM(flat, BF)],
        flops=images * 4 * 10**8,
        name="mlp_first",
    )
    near, f0 = lax.optimization_barrier((near, f0))
    far = lax.ppermute(near, "dp", xor_perm(dp, 1))
    got0 = lax.ppermute(send0, "dp", xor_perm(dp, 1))

    rest = (mp - 1) * hidden
    grad_rows = (2 * (mp - 1) + 1) * block
    ins = [
        image_counts, a2, dy, x1, u, o, f0, da20, near, far, b1_all, proj_weight, gamma1,
        norm2_gain, fc2_bias, gamma2,
    ]
    layer_out, dx1, do, keep1, send1, b1_1, acc_mlp = call(
        mlp_rest_kernel,
        (images // group,),
        ins,
        [SCALARS, whole(flat), whole(flat), blocked, blocked, whole(flat), blocked, blocked]
        + [whole(a.shape) for a in ins[8:]],
        [
            sds(tokens_in.shape, BF), sds(flat, F32), sds(flat, BF),
            sds((dp // 2, grad_rows, feats), BF), sds((dp // 2, grad_rows, feats), BF),
            sds((1, rest), F32), sds((8, feats), F32),
        ],
        [
            each(tokens_in.shape, 0, group), blocked, blocked,
            whole((dp // 2, grad_rows, feats)), whole((dp // 2, grad_rows, feats)),
            whole((1, rest)), whole((8, feats)),
        ],
        [
            pltpu.VMEM((feats, rest), BF), pltpu.VMEM((rest, feats), BF),
            pltpu.VMEM((1, rest), F32),
            pltpu.VMEM((total, rest), BF), pltpu.VMEM((total, rest), BF),
            pltpu.VMEM(flat, BF), pltpu.VMEM(flat, BF),
        ],
        flops=images * 14 * 10**8,
        name="mlp_rest",
    )
    got1 = lax.ppermute(send1, "dp", xor_perm(dp, 1))
    dx1 = dx1.reshape(tok_rows)
    do = do.reshape(tok_rows)

    steps = 3 if images % 3 == 0 else 1
    share = images // steps
    dqkv_shape = (images, rows, 3 * feats)
    carried, accs = [], []
    for s in range(steps):
        ins = [do, q, k, v, prob, dx1, tokens_in, mpre, mpost, mixb, qkv_weight, norm1_gain]
        *carried, acc = call(
            attn_bwd_kernel,
            (share,),
            ins + carried,
            [each(a.shape, s * share) for a in ins[:7]]
            + [whole(a.shape) for a in ins[7:]]
            + [pl.BlockSpec(memory_space=pl.ANY)] * len(carried),
            [sds(dqkv_shape, BF), sds(tokens_in.shape, F32), sds((2 * heads + 16, feats), F32)],
            [
                each(dqkv_shape, s * share), each(tokens_in.shape, s * share),
                whole((2 * heads + 16, feats)),
            ],
            [
                pltpu.VMEM((heads * rows, feats), BF), pltpu.VMEM((heads * rows, slots), BF),
                pltpu.VMEM((heads * rows, feats), BF), pltpu.VMEM((rows, feats), F32),
            ],
            flops=share * 20 * 10**8,
            name="attn_bwd",
            aliases={len(ins): 0, len(ins) + 1: 1} if carried else None,
        )
        accs.append(acc)
        if s == 0:
            (keep0, got0, keep1, got1), acc = lax.optimization_barrier(
                ((keep0, got0, keep1, got1), acc)
            )
            mine0 = dp_scatter(keep0.astype(F32) + got0.astype(F32), dp)
            mine1 = dp_scatter(keep1.astype(F32) + got1.astype(F32), dp)
            accs[0], do = lax.optimization_barrier((acc, do))
        if s == min(1, steps - 1):
            (mine0, mine1), acc = lax.optimization_barrier(((mine0, mine1), acc))
            proj_part = mine1[2 * (mp - 1) * block :]
            payloads = [
                jnp.concatenate([mine1[2 * (j - 1) * block : 2 * j * block], proj_part]).astype(BF)
                for j in range(1, mp)
            ]
            got_z = [
                lax.ppermute(payloads[j - 1], "mp", xor_perm(mp, j)) for j in range(1, mp)
            ]
            accs[s], do = lax.optimization_barrier((acc, do))
    dqkv, in_grad = carried
    got_z, dqkv = lax.optimization_barrier((got_z, dqkv))
    got_z = [g.astype(F32) for g in got_z]
    fc_sum = mine0 + sum(g[: 2 * block] for g in got_z)
    proj_sum = proj_part + sum(g[2 * block :] for g in got_z)

    q_block = 3 * feats // dp
    out_shape = (dp, q_block + 16, feats)
    ins = [dqkv.reshape(total, 3 * feats)] + accs + [a1.reshape(flat), acc_mlp, b1_0, b1_1]
    shares = call(
        functools.partial(qkv_grad_kernel, heads),
        (1,),
        ins,
        [whole(a.shape) for a in ins],
        [sds(out_shape, BF)],
        [whole(out_shape)],
        [pltpu.VMEM((16, feats), F32)],
        flops=11 * 10**8,
        name="qkv_grad",
    )[0]
    arrived = lax.all_to_all(shares, "dp", 0, 0, tiled=True)
    mine = jnp.sum(arrived.astype(F32), axis=0)
    low = mine.astype(BF)
    got = jnp.stack([lax.ppermute(low, "mp", xor_perm(mp, j)) for j in range(1, mp)])
    b1_size = hidden // dp
    ins = [mine, got]
    outs = [
        sds((q_block, feats), F32), sds((1, q_block), F32), sds((heads, heads), F32),
        sds((heads, heads), F32), sds((1, heads), F32), sds((1, b1_size), F32),
    ] + [sds((1, block), F32)] * 8
    qkvw, qkvb, pre, post, postb, b1g, *vecs = call(
        functools.partial(final_kernel, heads, q_block),
        (1,),
        ins,
        [whole(a.shape) for a in ins],
        outs,
        [whole(a.shape) for a in outs],
        name="final",
    )
    vecs = [a.reshape(-1) for a in vecs]
    return (
        layer_out,
        in_grad,
        vecs[0],
        vecs[1],
        qkvw.T,
        qkvb.reshape(-1),
        pre,
        post,
        postb.reshape(-1),
        proj_sum.T,
        vecs[2],
        vecs[3],
        vecs[4],
        vecs[5],
        fc_sum[:block].T,
        b1g.reshape(-1),
        fc_sum[block:].T,
        vecs[6],
        vecs[7],
    )


def solution(mesh):
    tokens = P(("dp", "mp"), None, None)
    placed = (
        (tokens, P("dp")) + (P(),) * 12 + (P(None, "mp"), P("mp"), P("mp", None), P(), P(), tokens)
    )
    return jax.shard_map(
        functools.partial(per_device, mesh.shape["dp"], mesh.shape["mp"]),
        mesh=mesh,
        in_specs=placed,
        out_specs=(
            tokens, tokens, P("dp"), P("dp"), P(None, "dp"), P("dp"), P(), P(), P(),
            P(None, "dp"), P("dp"), P("dp"), P("dp"), P("dp"), P(None, ("mp", "dp")),
            P(("mp", "dp")), P("mp", "dp"), P("dp"), P("dp"),
        ),
        check_vma=False,
    )
```

```python
import functools

import jax
import jax.numpy as jnp
from jax import lax
from jax.experimental import pallas as pl
from jax.experimental.pallas import tpu as pltpu
from jax.sharding import PartitionSpec as P

BF = jnp.bfloat16
F32 = jnp.float32
LOG2E = 1.4426950408889634
EPS = 1e-06
VMEM_LIMIT = 56 * 1024 * 1024


def nn(a, b):
    return lax.dot_general(a, b, (((1,), (0,)), ((), ())), preferred_element_type=F32)


def nt(a, b):
    return lax.dot_general(a, b, (((1,), (1,)), ((), ())), preferred_element_type=F32)


def tn(a, b):
    return lax.dot_general(a, b, (((0,), (0,)), ((), ())), preferred_element_type=F32)


def exact(a, b, dims):
    return lax.dot_general(
        a, b, (dims, ((), ())), precision=lax.Precision.HIGHEST, preferred_element_type=F32
    )


def normalized(x):
    mean = jnp.mean(x, axis=-1, keepdims=True)
    c = x - mean
    r = lax.rsqrt(jnp.mean(c * c, axis=-1, keepdims=True) + EPS)
    return c * r, r


def norm_back(cot, n, r, gain):
    cg = cot * gain
    return r * (
        cg
        - jnp.mean(cg, axis=-1, keepdims=True)
        - n * jnp.mean(cg * n, axis=-1, keepdims=True)
    )


def colsum(x):
    return jnp.sum(x, axis=0, keepdims=True)


def split(x):
    hi = x.astype(BF)
    return jnp.concatenate([hi, (x - hi.astype(F32)).astype(BF)], axis=1)


def row(ref):
    return ref[...].reshape(1, ref.shape[0])


def gelu_parts(z):
    e = jnp.exp2(z * z * (-0.5 * LOG2E))
    t = 1.0 / (1.0 + jnp.abs(z) * (0.3275911 * 0.7071067811865476))
    poly = t * (
        0.5 * 0.254829592
        + t
        * (
            0.5 * -0.284496736
            + t * (0.5 * 1.421413741 + t * (0.5 * -1.453152027 + t * (0.5 * 1.061405429)))
        )
    )
    tail = poly * e
    phi = jnp.where(z >= 0, 1.0 - tail, tail)
    return phi, phi + z * e * 0.3989422804014327


def head_of_lane(shape, axis, head_dim):
    return lax.broadcasted_iota(jnp.int32, shape, axis) // head_dim


def chunks(count, size=16):
    return [slice(at, at + size) for at in range(0, count, size)]


def fold(x):
    return sum(x[at : at + 8] for at in range(8, x.shape[0], 8)) + x[0:8]


def attn_fwd_kernel(
    counts, tok, og, n1g, n1b, qkvb, pre, post, postb, projb, gamma1, n2g, n2b, wqkv, wproj,
    a1_o, q_o, k_o, v_o, p_o, o_o, x1_o, u_o, a2_o, dy_o, mpre, mpost, mixb,
    pad, qq,
):
    i = pl.program_id(0)
    images = pl.num_programs(0)
    patches, feats = tok.shape[1:]
    rows = pad.shape[0]
    heads = mpre.shape[0]
    head_dim = feats // heads
    slots = k_o.shape[1]

    @pl.when(i == 0)
    def _():
        spread = (
            head_of_lane((heads, feats), 1, head_dim)
            == lax.broadcasted_iota(jnp.int32, (heads, feats), 0)
        ).astype(F32)
        mpre[...] = exact(pre[...], spread, ((1,), (0,))) * (head_dim**-0.5 * LOG2E)
        mpost[...] = exact(post[...], spread, ((0,), (0,)))
        mixb[...] = exact(row(postb), spread, ((1,), (0,)))

    pad[patches:, :] = jnp.zeros((rows - patches, feats), F32)
    live = (lax.axis_index("mp") * images + i < counts[0]).astype(F32)
    pad[0:patches, :] = og[0].astype(F32) * live
    dy_o[0] = pad[...].astype(BF)
    pad[0:patches, :] = tok[0].astype(F32)
    gain, shift = row(n1g), row(n1b)
    for c in chunks(rows):
        n, _ = normalized(pad[c, :])
        a1_o[0, c, :] = (n * gain + shift).astype(BF)
    qkv = nn(a1_o[0], wqkv[...])
    bias = row(qkvb)
    k_o[0, rows:] = jnp.zeros((slots - rows, feats), BF)
    v_o[0, rows:] = jnp.zeros((slots - rows, feats), BF)
    v_sum = jnp.zeros((8, feats), F32)
    for c in chunks(rows):
        q, k, v = (
            qkv[c, j * feats : (j + 1) * feats] + bias[:, j * feats : (j + 1) * feats]
            for j in range(3)
        )
        if c.stop > patches:
            inside = lax.broadcasted_iota(jnp.int32, v.shape, 0) < patches - c.start
            v = jnp.where(inside, v, 0.0)
        q = q.astype(BF)
        v = v.astype(BF)
        q_o[0, c, :] = q
        k_o[0, c, :] = k.astype(BF)
        v_o[0, c, :] = v
        v_sum = v_sum + fold(v.astype(F32))
        qf = q.astype(F32)
        for g in range(heads):
            at = slice(g * rows + c.start, g * rows + c.stop)
            scaled = qf * mpre[g : g + 1, :]
            hi = scaled.astype(BF)
            qq[at, 0:feats] = hi
            qq[at, feats:] = (scaled - hi.astype(F32)).astype(BF)
    k2 = jnp.concatenate([k_o[0], k_o[0]], axis=1)
    vs = v_o[0]
    many = heads // 2
    half = many * rows
    valid = lax.broadcasted_iota(jnp.int32, (16, slots // 2), 1) < patches - slots // 2
    logits = [nt(qq[s * half : (s + 1) * half, :], k2) for s in range(2)]
    mixed = []
    for s in range(2):
        for j in range(many):
            for c in chunks(rows):
                part = logits[s][j * rows + c.start : j * rows + c.stop]
                left = part[:, 0 : slots // 2]
                right = jnp.where(valid, part[:, slots // 2 :], -1e30)
                top = jnp.max(jnp.maximum(left, right), axis=-1, keepdims=True)
                left = jnp.exp2(left - top)
                right = jnp.exp2(right - top)
                inv = 1.0 / jnp.sum(left + right, axis=-1, keepdims=True)
                p_o[0, s * many + j, c, 0 : slots // 2] = (left * inv).astype(BF)
                p_o[0, s * many + j, c, slots // 2 :] = (right * inv).astype(BF)
        mixed.append(nn(p_o[0, s * many : (s + 1) * many].reshape(half, slots), vs))
    start = mixb[...] * colsum(v_sum)
    for c in chunks(rows):
        attended = start
        for g in range(heads):
            at = (g % many) * rows
            attended = attended + mixed[g // many][at + c.start : at + c.stop] * mpost[g : g + 1, :]
        o_o[0, c, :] = attended.astype(BF)
    product = nn(o_o[0], wproj[...])
    bias, scale, gain, shift = row(projb), row(gamma1), row(n2g), row(n2b)
    for c in chunks(rows):
        u = product[c] + bias
        x1 = pad[c, :] + scale * u
        u_o[0, c, :] = u
        x1_o[0, c, :] = x1
        n, _ = normalized(x1)
        a2_o[0, c, :] = (n * gain + shift).astype(BF)


def store_blocks(value, count, put):
    size = value.shape[0] // count
    mine = lax.axis_index("dp")
    for b in range(count):
        place = jnp.bitwise_xor(jnp.int32(b), mine)
        block = value[b * size : (b + 1) * size].astype(BF)

        @pl.when(jnp.bitwise_and(place, 1) == 0)
        def _():
            put(0, jnp.right_shift(place, 1), block)

        @pl.when(jnp.bitwise_and(place, 1) == 1)
        def _():
            put(1, jnp.right_shift(place, 1), block)


def mlp_step(act, df, w1, b1, w2, hids, dzs, at, b1_sum):
    z = nn(act, w1[...])
    grad_hidden = nt(df, w2[...])
    width = z.shape[1]
    rows = z.shape[0]
    lanes = 256
    for first in range(0, width, lanes):
        part = slice(first, first + lanes)
        bias = b1[:, part]
        sums = jnp.zeros((8, lanes), F32)
        for c in chunks(rows):
            zc = z[c, part] + bias
            phi, slope = gelu_parts(zc)
            dz = (grad_hidden[c, part] * slope).astype(BF)
            place = pl.ds(pl.multiple_of(at + c.start, 16), 16)
            hids[place, part] = (zc * phi).astype(BF)
            dzs[place, part] = dz
            sums = sums + fold(dz.astype(F32))
        b1_sum[:, part] += colsum(sums)
    here = pl.ds(pl.multiple_of(at, 16), rows)
    return nn(hids[here, :], w2[...]), nt(dzs[here, :], w1[...])


def mlp_first_kernel(
    a2, dy, gamma2, w1_own, b1_own, w2_own, near,
    f_o, da2_o, grads, b1_o,
    w1, w2, b1, hids, dzs, dfs,
):
    i = pl.program_id(0)
    rows, feats = f_o.shape
    at = i * rows
    here = pl.ds(pl.multiple_of(at, rows), rows)

    @pl.when(i == 0)
    def _():
        b1_o[...] = jnp.zeros_like(b1_o)
        w1[:, 0:feats] = w1_own[...]
        w1[:, feats:] = near[0:feats]
        w2[0:feats, :] = w2_own[...]
        w2[feats:, :] = near[feats : 2 * feats]
        b1[:, 0:feats] = row(b1_own)
        b1[:, feats:] = colsum(near[2 * feats : 2 * feats + 16].astype(F32))

    gain = row(gamma2)
    for c in chunks(rows):
        place = pl.ds(pl.multiple_of(at + c.start, 16), 16)
        dfs[place, :] = (dy[place, :].astype(F32) * gain).astype(BF)
    f, da2 = mlp_step(a2[here, :], dfs[here, :], w1, b1, w2, hids, dzs, at, b1_o)
    f_o[...] = f
    da2_o[...] = da2

    @pl.when(i == pl.num_programs(0) - 1)
    def _():
        grads[0] = tn(a2[...], dzs[...]).astype(BF).T
        down = tn(dfs[...], hids[...]).astype(BF)
        for c in range(2):
            grads[1, c * feats : (c + 1) * feats, :] = down[:, c * feats : (c + 1) * feats]


def mlp_rest_kernel(
    counts, a2, dy, x1, u, o, f0, da20, near, far, grads, wproj, gamma1, n2g, fc2b, gamma2,
    out_o, dx1_o, do_o, keep, send, b1_o, acc_o,
    w1, w2, b1, hids, dzs, dfs, dus,
):
    i = pl.program_id(0)
    rows, feats = f0.shape
    group, patches = out_o.shape[:2]
    image_rows = rows // group
    at = i * rows
    here = pl.ds(pl.multiple_of(at, rows), rows)
    m_idx = lax.axis_index("mp")

    @pl.when(i == 0)
    def _():
        b1_o[...] = jnp.zeros_like(b1_o)
        acc_o[...] = jnp.zeros_like(acc_o)
        for c in range(2):
            b1[:, c * feats : (c + 1) * feats] = colsum(near[c, feats : feats + 16].astype(F32))

    for core in range(2):

        @pl.when(jnp.logical_and(i == 0, jnp.bitwise_and(lax.axis_index("dp"), 1) == core))
        def _(core=core):
            first, second = (near, far) if core == 0 else (far, near)
            for c in range(2):
                w1[:, c * feats : (c + 1) * feats] = first[c, 0:feats]
                w2[c * feats : (c + 1) * feats, :] = second[c, 0:feats]

    gain2 = row(gamma2)
    for c in chunks(rows):
        place = pl.ds(pl.multiple_of(at + c.start, 16), 16)
        dfs[place, :] = (dy[place, :].astype(F32) * gain2).astype(BF)
    f, da2 = mlp_step(a2[here, :], dfs[here, :], w1, b1, w2, hids, dzs, at, b1_o)
    bias, gain, scale = row(fc2b), row(n2g), row(gamma1)
    sums = [jnp.zeros((8, feats), F32) for _ in range(6)]
    for c in chunks(rows):
        place = pl.ds(pl.multiple_of(at + c.start, 16), 16)
        fc = f[c] + f0[c, :] + bias
        dac = da2[c] + da20[c, :]
        x1c = x1[c, :]
        dyc = dy[place, :].astype(F32)
        n, r = normalized(x1c)
        dx1 = dyc + norm_back(dac, n, r, gain)
        dx1_o[c, :] = dx1
        du = (dx1 * scale).astype(BF)
        dus[place, :] = du
        image = c.start // image_rows
        first = c.start - image * image_rows
        live = (m_idx * (group * pl.num_programs(0)) + i * group + image < counts[0]).astype(F32)
        out = ((x1c + gain2 * fc) * live).astype(BF)
        if first + 16 <= patches:
            out_o[image, first : first + 16, :] = out
        else:
            out_o[image, first:patches, :] = out[0 : patches - first]
        terms = (
            du.astype(F32), u[c, :] * dx1, dac * n, dac, dfs[place, :].astype(F32), fc * dyc,
        )
        sums = [s + fold(t) for s, t in zip(sums, terms)]
    for j in range(6):
        acc_o[j : j + 1, :] += colsum(sums[j])
    do_o[...] = nt(dus[here, :], wproj[...]).astype(BF)

    @pl.when(i == pl.num_programs(0) - 1)
    def _():
        count = 2 * keep.shape[0]
        size = feats // count
        outs = (keep, send)

        def put(at):
            def inner(which, place, block):
                outs[which][place, at : at + size, :] = block
            return inner

        up = tn(a2[...], dzs[...]).astype(BF).T
        down = tn(dfs[...], hids[...]).astype(BF)
        for c in range(2):
            part = slice(c * feats, (c + 1) * feats)
            store_blocks(up[part], count, put((4 + 2 * c) * size))
            store_blocks(down[:, part], count, put((5 + 2 * c) * size))
            store_blocks(grads[0, part, :], count, put(2 * c * size))
            store_blocks(grads[1, part, :], count, put((2 * c + 1) * size))
        store_blocks(tn(dus[...], o[...]), count, put(8 * size))


def attn_bwd_kernel(do_r, q_r, k_r, v_r, p_r, dx1, tok, mpre, mpost, mixb, wqkv, n1g, *refs):
    dqkv_o, in_o, acc_o, dogs, dls, qgs, pad = refs[-7:]
    i = pl.program_id(0)
    rows, feats = do_r.shape[1:]
    patches = tok.shape[1]
    heads = mpre.shape[0]
    slots = k_r.shape[1]
    many = heads // 2
    half = many * rows

    @pl.when(i == 0)
    def _():
        acc_o[...] = jnp.zeros_like(acc_o)

    do_sum = jnp.zeros((8, feats), F32)
    for c in chunks(rows):
        dof = do_r[0, c, :].astype(F32)
        qf = q_r[0, c, :].astype(F32)
        do_sum = do_sum + fold(dof)
        for h in range(heads):
            place = slice(h * rows + c.start, h * rows + c.stop)
            dogs[place, :] = (dof * mpost[h : h + 1, :]).astype(BF)
            qgs[place, :] = (qf * mpre[h : h + 1, :]).astype(BF)
    do_sum = colsum(do_sum)
    k = k_r[0]
    v = v_r[0]
    do = do_r[0]
    dps = [nt(dogs[s * half : (s + 1) * half, :], v) for s in range(2)]
    ts, dvs = [], []
    for s in range(2):
        dvs.append(tn(jnp.concatenate([p_r[0, s * many + j] for j in range(many)], axis=1), do))
        for j in range(many):
            h = s * many + j
            for c in chunks(rows):
                dp = dps[s][j * rows + c.start : j * rows + c.stop]
                pf = p_r[0, h, c, :].astype(F32)
                mean = jnp.sum(dp * pf, axis=-1, keepdims=True) * (
                    1.0 / jnp.sum(pf, axis=-1, keepdims=True)
                )
                dls[h * rows + c.start : h * rows + c.stop, :] = (pf * (dp - mean)).astype(BF)
        ts.append(nn(dls[s * half : (s + 1) * half, :], k))
    dk_all = tn(dls[...], qgs[...])

    bias_row = mixb[...] * do_sum
    v_sum = jnp.zeros((8, feats), F32)
    dv_sum = jnp.zeros((8, feats), F32)
    sums = [jnp.zeros((8, feats), F32) for _ in range(heads)]
    for c in chunks(rows):
        vf = v_r[0, c, :].astype(F32)
        dv = bias_row
        for h in range(heads):
            at = (h % many) * slots
            this = dvs[h // many][at + c.start : at + c.stop]
            dv = dv + this * mpost[h : h + 1, :]
            sums[h] = sums[h] + fold(vf * this)
        if c.stop > patches:
            inside = lax.broadcasted_iota(jnp.int32, dv.shape, 0) < patches - c.start
            dv = jnp.where(inside, dv, 0.0)
        low = dv.astype(BF)
        dqkv_o[0, c, 2 * feats :] = low
        dv_sum = dv_sum + fold(low.astype(F32))
        v_sum = v_sum + fold(vf)
    for h in range(heads):
        acc_o[h : h + 1, :] += colsum(sums[h])
    acc_o[2 * heads : 2 * heads + 1, :] += do_sum * colsum(v_sum)
    acc_o[2 * heads + 10 : 2 * heads + 11, :] += colsum(dv_sum)

    dq_sum = jnp.zeros((8, feats), F32)
    dk_sum = jnp.zeros((8, feats), F32)
    sums = [jnp.zeros((8, feats), F32) for _ in range(heads)]
    for c in chunks(rows):
        qf = q_r[0, c, :].astype(F32)
        dq = 0.0
        for h in range(heads):
            at = (h % many) * rows
            this = ts[h // many][at + c.start : at + c.stop]
            dq = dq + this * mpre[h : h + 1, :]
            sums[h] = sums[h] + fold(qf * this)
        low = (dq * (1.0 / LOG2E)).astype(BF)
        dqkv_o[0, c, 0:feats] = low
        dq_sum = dq_sum + fold(low.astype(F32))
        low = (dk_all[c] * (1.0 / LOG2E)).astype(BF)
        dqkv_o[0, c, feats : 2 * feats] = low
        dk_sum = dk_sum + fold(low.astype(F32))
    for h in range(heads):
        acc_o[heads + h : heads + h + 1, :] += colsum(sums[h])
    acc_o[2 * heads + 8 : 2 * heads + 9, :] += colsum(dq_sum)
    acc_o[2 * heads + 9 : 2 * heads + 10, :] += colsum(dk_sum)

    pad[patches:, :] = jnp.zeros((rows - patches, feats), F32)
    pad[0:patches, :] = tok[0].astype(F32)
    da1 = nt(dqkv_o[0], wqkv[...])
    gain = row(n1g)
    sums = [jnp.zeros((8, feats), F32) for _ in range(2)]
    for c in chunks(rows):
        n, r = normalized(pad[c, :])
        cot = da1[c]
        grad = dx1[0, c, :] + norm_back(cot, n, r, gain)
        sums = [sums[0] + fold(cot * n), sums[1] + fold(cot)]
        if c.stop <= patches:
            in_o[0, c, :] = grad
        else:
            in_o[0, c.start : patches, :] = grad[0 : patches - c.start]
    for j in range(2):
        acc_o[2 * heads + 11 + j : 2 * heads + 12 + j, :] += colsum(sums[j])


def qkv_grad_kernel(heads, dqkv, *refs):
    accs = refs[:-7]
    a1, acc_mlp, b1_first, b1_rest, keep, send, small = refs[-7:]
    feats = a1.shape[1]
    count = 2 * keep.shape[0]
    size = 3 * feats // count
    acc = accs[0][...]
    for other in accs[1:]:
        acc = acc + other[...]
    small[...] = jnp.zeros_like(small)
    small[0:2, :] = acc[2 * heads + 11 : 2 * heads + 13]
    small[2:8, :] = acc_mlp[0:6, :]
    small[8:11, :] = acc[2 * heads + 8 : 2 * heads + 11]
    head_dim = feats // heads
    lanes = 2 * heads * heads
    gather = (
        head_of_lane((feats, lanes), 0, head_dim)
        == lax.broadcasted_iota(jnp.int32, (feats, lanes), 1) % heads
    ).astype(F32)
    sums = exact(acc[0 : 2 * heads + 8], gather, ((1,), (0,)))
    place = head_of_lane((2 * heads, lanes), 1, heads) == lax.broadcasted_iota(
        jnp.int32, (2 * heads, lanes), 0
    )
    small[11:12, 0:lanes] = colsum(jnp.where(place, sums[0 : 2 * heads], 0.0))
    small[11:12, lanes : 2 * lanes] = sums[2 * heads : 2 * heads + 1]
    m_idx = lax.axis_index("mp")
    for c, ref in enumerate((b1_first, b1_first, b1_rest, b1_rest)):
        place = 12 + jnp.bitwise_xor(m_idx, c)
        small[pl.ds(place, 1), :] = ref[:, (c % 2) * feats : (c % 2 + 1) * feats]
    low = small[...].astype(BF)
    outs = (keep, send)

    def put(which, place, block):
        outs[which][place, 0:size, :] = block
        outs[which][place, size:, :] = low

    store_blocks(tn(dqkv[...], a1[...]), count, put)


def final_kernel(heads, size, *refs):
    mine, got = refs[0], refs[1:-14]
    qkv_o, qkvb_o, pre_o, post_o, postb_o, b1_o, *vecs_o = refs[-14:]
    total = mine[...]
    for part in got:
        total = total + part[...].astype(F32)
    feats = total.shape[1]
    qkv_o[...] = total[0:size]
    small = total[size:]
    d_idx = lax.axis_index("dp")
    m_idx = lax.axis_index("mp")

    def own(value, width, first):
        lane = lax.broadcasted_iota(jnp.int32, (value.shape[1], width), 0)
        want = lax.broadcasted_iota(jnp.int32, (value.shape[1], width), 1) + first
        return exact(value, (lane == want).astype(F32), ((1,), (0,)))

    width = vecs_o[0].shape[1]
    vecs = own(small[0:8], width, d_idx * width)
    for j, ref in enumerate(vecs_o):
        ref[...] = vecs[j : j + 1]
    wide = qkvb_o.shape[1]
    flat = 0.0
    for j in range(3):
        flat = flat + own(small[8 + j : 9 + j], wide, d_idx * wide - j * feats)
    qkvb_o[...] = flat
    b1 = own(small[12:16], b1_o.shape[1], d_idx * b1_o.shape[1])
    pick = lax.broadcasted_iota(jnp.int32, b1.shape, 0) == m_idx
    b1_o[...] = colsum(jnp.where(pick, b1, 0.0))
    mix = small[11:12]
    hh = heads * heads
    line = lax.broadcasted_iota(jnp.int32, (heads, hh), 0)
    lane = lax.broadcasted_iota(jnp.int32, (heads, hh), 1)
    fold = (
        lax.broadcasted_iota(jnp.int32, (hh, heads), 0) % heads
        == lax.broadcasted_iota(jnp.int32, (hh, heads), 1)
    ).astype(F32)
    head_dim = feats // heads

    def square(values):
        return exact(jnp.where(lane // heads == line, values, 0.0), fold, ((1,), (0,)))

    post_o[...] = square(mix[:, 0:hh]).T
    pre_o[...] = square(mix[:, hh : 2 * hh]) * (head_dim**-0.5)
    postb_o[...] = mix[:, 2 * hh : 2 * hh + heads]


def whole(shape):
    return pl.BlockSpec(shape, lambda i: (0,) * len(shape))


def each(shape, first=0, many=1):
    return pl.BlockSpec((many,) + shape[1:], lambda i: (i + first,) + (0,) * (len(shape) - 1))


SCALARS = pl.BlockSpec(memory_space=pltpu.SMEM)


def sds(shape, dtype):
    return jax.ShapeDtypeStruct(shape, dtype)


def call(
    kernel, grid, ins, in_specs, outs, out_specs, scratch=(), flops=0, name=None, aliases=None
):
    size = lambda a: a.size * a.dtype.itemsize
    return pl.pallas_call(
        kernel,
        grid=grid,
        in_specs=in_specs,
        out_specs=out_specs,
        out_shape=outs,
        scratch_shapes=scratch,
        input_output_aliases=aliases or {},
        compiler_params=pltpu.CompilerParams(vmem_limit_bytes=VMEM_LIMIT),
        cost_estimate=pl.CostEstimate(
            flops=flops,
            bytes_accessed=sum(size(a) for a in ins) + sum(size(a) for a in outs),
            transcendentals=0,
        ),
        name=name,
    )(*ins)


def xor_perm(count, mask):
    return [(j, j ^ mask) for j in range(count)]


def dp_hops(dp):
    bits = dp.bit_length() - 1
    groups = []
    at = 1
    while at < bits:
        groups.append((at, min(2, bits - at)))
        at += groups[-1][1]
    return groups


def dp_scatter(value, dp):
    for at, many in dp_hops(dp):
        value = value.reshape((-1, 1 << many) + value.shape[1:])
        got = [
            lax.ppermute(value[:, j].astype(BF), "dp", xor_perm(dp, j << at))
            for j in range(1, 1 << many)
        ]
        value = value[:, 0] + sum(g.astype(F32) for g in got)
    return value.reshape(value.shape[-2:])


def per_device(
    dp, mp,
    tokens_in, image_counts, norm1_gain, norm1_bias, qkv_weight, qkv_bias,
    mix_pre, mix_post, mix_post_bias, proj_weight, proj_bias, gamma1,
    norm2_gain, norm2_bias, fc1_weight, fc1_bias, fc2_weight, fc2_bias, gamma2, out_grad,
):
    images, patches, feats = tokens_in.shape
    heads = mix_pre.shape[0]
    rows = -(-patches // 16) * 16
    slots = -(-patches // 128) * 128
    hidden = fc1_weight.shape[1]
    core = jnp.bitwise_and(lax.axis_index("dp"), 1)

    bias_parts = []
    left = fc1_bias
    for _ in range(3):
        bias_parts.append(left.astype(BF))
        left = left - bias_parts[-1].astype(F32)
    bias_rows = jnp.concatenate([jnp.stack(bias_parts), jnp.zeros((13, hidden), BF)])
    one = jnp.concatenate([fc1_weight, fc2_weight, bias_rows])
    other = jnp.concatenate([jnp.where(core == 0, fc1_weight, fc2_weight), bias_rows])
    near_one = lax.ppermute(one, "mp", xor_perm(mp, 1))
    near = [lax.ppermute(other, "mp", xor_perm(mp, j)) for j in range(2, mp)]

    tok_rows = (images, rows, feats)
    slot_rows = (images, slots, feats)
    prob_shape = (images, heads, rows, slots)
    mix_shape = (heads, feats)
    ins = [
        image_counts, tokens_in, out_grad, norm1_gain, norm1_bias, qkv_bias, mix_pre, mix_post,
        mix_post_bias, proj_bias, gamma1, norm2_gain, norm2_bias, qkv_weight, proj_weight,
    ]
    a1, q, k, v, prob, o, x1, u, a2, dy, mpre, mpost, mixb = call(
        attn_fwd_kernel,
        (images,),
        ins,
        [SCALARS, each(tokens_in.shape), each(out_grad.shape)] + [whole(a.shape) for a in ins[3:]],
        [
            sds(tok_rows, BF), sds(tok_rows, BF), sds(slot_rows, BF), sds(slot_rows, BF),
            sds(prob_shape, BF), sds(tok_rows, BF), sds(tok_rows, F32), sds(tok_rows, F32),
            sds(tok_rows, BF), sds(tok_rows, BF), sds(mix_shape, F32), sds(mix_shape, F32),
            sds((1, feats), F32),
        ],
        [each(s) for s in (tok_rows, tok_rows, slot_rows, slot_rows, prob_shape)]
        + [each(tok_rows)] * 5
        + [whole(mix_shape)] * 2
        + [whole((1, feats))],
        [pltpu.VMEM((rows, feats), F32), pltpu.VMEM((heads * rows, 2 * feats), BF)],
        flops=images * 15 * 10**8,
        name="attn_fwd",
    )

    block = feats // dp
    total = images * rows
    group = 2 if images % 2 == 0 else 1
    flat = (total, feats)
    step = (group * rows, feats)
    a2, dy, x1, u, o = (a.reshape(flat) for a in (a2, dy, x1, u, o))
    near_one, near, a2 = lax.optimization_barrier((near_one, near, a2))
    near = jnp.stack(near)
    far = lax.ppermute(near, "dp", xor_perm(dp, 1))
    ins = [a2, dy, gamma2, fc1_weight, fc1_bias, fc2_weight, near_one]
    blocked = pl.BlockSpec(step, lambda i: (i, 0))
    wide = 2 * hidden
    grad_shape = (2, wide, feats)
    f0, da20, grads0, b1_0 = call(
        mlp_first_kernel,
        (images // group,),
        ins,
        [whole(a.shape) for a in ins],
        [sds(flat, F32), sds(flat, F32), sds(grad_shape, BF), sds((1, wide), F32)],
        [blocked, blocked, whole(grad_shape), whole((1, wide))],
        [
            pltpu.VMEM((feats, wide), BF), pltpu.VMEM((wide, feats), BF),
            pltpu.VMEM((1, wide), F32), pltpu.VMEM((total, wide), BF),
            pltpu.VMEM((total, wide), BF), pltpu.VMEM(flat, BF),
        ],
        flops=images * 8 * 10**8,
        name="mlp_first",
    )

    grad_rows = 9 * block
    half_shape = (dp // 2, grad_rows, feats)
    ins = [
        image_counts, a2, dy, x1, u, o, f0, da20, near, far, grads0, proj_weight, gamma1,
        norm2_gain, fc2_bias, gamma2,
    ]
    layer_out, dx1, do, keep, send, b1_1, acc_mlp = call(
        mlp_rest_kernel,
        (images // group,),
        ins,
        [SCALARS, whole(flat), whole(flat), blocked, blocked, whole(flat), blocked, blocked]
        + [whole(a.shape) for a in ins[8:]],
        [
            sds(tokens_in.shape, BF), sds(flat, F32), sds(flat, BF), sds(half_shape, BF),
            sds(half_shape, BF), sds((1, wide), F32), sds((8, feats), F32),
        ],
        [
            each(tokens_in.shape, 0, group), blocked, blocked, whole(half_shape),
            whole(half_shape), whole((1, wide)), whole((8, feats)),
        ],
        [
            pltpu.VMEM((feats, wide), BF), pltpu.VMEM((wide, feats), BF),
            pltpu.VMEM((1, wide), F32), pltpu.VMEM((total, wide), BF),
            pltpu.VMEM((total, wide), BF), pltpu.VMEM(flat, BF), pltpu.VMEM(flat, BF),
        ],
        flops=images * 9 * 10**8,
        name="mlp_rest",
    )
    got = lax.ppermute(send, "dp", xor_perm(dp, 1))
    dx1 = dx1.reshape(tok_rows)
    do = do.reshape(tok_rows)

    steps = 3 if images % 3 == 0 else 1
    share = images // steps
    dqkv_shape = (images, rows, 3 * feats)
    carried, accs = [], []
    for s in range(steps):
        ins = [do, q, k, v, prob, dx1, tokens_in, mpre, mpost, mixb, qkv_weight, norm1_gain]
        *carried, acc = call(
            attn_bwd_kernel,
            (share,),
            ins + carried,
            [each(a.shape, s * share) for a in ins[:7]]
            + [whole(a.shape) for a in ins[7:]]
            + [pl.BlockSpec(memory_space=pl.ANY)] * len(carried),
            [sds(dqkv_shape, BF), sds(tokens_in.shape, F32), sds((2 * heads + 16, feats), F32)],
            [
                each(dqkv_shape, s * share), each(tokens_in.shape, s * share),
                whole((2 * heads + 16, feats)),
            ],
            [
                pltpu.VMEM((heads * rows, feats), BF), pltpu.VMEM((heads * rows, slots), BF),
                pltpu.VMEM((heads * rows, feats), BF), pltpu.VMEM((rows, feats), F32),
            ],
            flops=share * 20 * 10**8,
            name="attn_bwd",
            aliases={len(ins): 0, len(ins) + 1: 1} if carried else None,
        )
        accs.append(acc)
        if s == 0:
            (keep, got), acc = lax.optimization_barrier(((keep, got), acc))
            mine = dp_scatter(keep.astype(F32) + got.astype(F32), dp)
            accs[0], do = lax.optimization_barrier((acc, do))
        if s == min(1, steps - 1):
            mine, acc = lax.optimization_barrier((mine, acc))
            low = mine.astype(BF)
            proj = low[8 * block :]
            got_z = [
                lax.ppermute(
                    jnp.concatenate([low[2 * j * block : 2 * (j + 1) * block], proj]),
                    "mp",
                    xor_perm(mp, j),
                )
                for j in range(1, mp)
            ]
            accs[s], do = lax.optimization_barrier((acc, do))
    dqkv, in_grad = carried
    got_z, dqkv = lax.optimization_barrier((got_z, dqkv))
    sums = jnp.concatenate([mine[: 2 * block], mine[8 * block :]]) + sum(
        g.astype(F32) for g in got_z
    )
    fc1g, fc2g, projg = (sums[j * block : (j + 1) * block] for j in range(3))

    q_block = 3 * feats // dp
    half_shape = (dp // 2, q_block + 16, feats)
    ins = [dqkv.reshape(total, 3 * feats)] + accs + [a1.reshape(flat), acc_mlp, b1_0, b1_1]
    keep, send = call(
        functools.partial(qkv_grad_kernel, heads),
        (1,),
        ins,
        [whole(a.shape) for a in ins],
        [sds(half_shape, BF), sds(half_shape, BF)],
        [whole(half_shape), whole(half_shape)],
        [pltpu.VMEM((16, feats), F32)],
        flops=11 * 10**8,
        name="qkv_grad",
    )
    got = lax.ppermute(send, "dp", xor_perm(dp, 1))
    mine = dp_scatter(keep.astype(F32) + got.astype(F32), dp)
    low = mine.astype(BF)
    got = [lax.ppermute(low, "mp", xor_perm(mp, j)) for j in range(1, mp)]
    b1_size = hidden // dp
    ins = [mine] + got
    outs = [
        sds((q_block, feats), F32), sds((1, q_block), F32), sds((heads, heads), F32),
        sds((heads, heads), F32), sds((1, heads), F32), sds((1, b1_size), F32),
    ] + [sds((1, block), F32)] * 8
    qkvw, qkvb, pre, post, postb, b1g, *vecs = call(
        functools.partial(final_kernel, heads, q_block),
        (1,),
        ins,
        [whole(a.shape) for a in ins],
        outs,
        [whole(a.shape) for a in outs],
        name="final",
    )
    vecs = [a.reshape(-1) for a in vecs]
    return (
        layer_out,
        in_grad,
        vecs[0],
        vecs[1],
        qkvw.T,
        qkvb.reshape(-1),
        pre,
        post,
        postb.reshape(-1),
        projg.T,
        vecs[2],
        vecs[3],
        vecs[4],
        vecs[5],
        fc1g.T,
        b1g.reshape(-1),
        fc2g.T,
        vecs[6],
        vecs[7],
    )


def solution(mesh):
    tokens = P(("dp", "mp"), None, None)
    placed = (
        (tokens, P("dp")) + (P(),) * 12 + (P(None, "mp"), P("mp"), P("mp", None), P(), P(), tokens)
    )
    return jax.shard_map(
        functools.partial(per_device, mesh.shape["dp"], mesh.shape["mp"]),
        mesh=mesh,
        in_specs=placed,
        out_specs=(
            tokens, tokens, P("dp"), P("dp"), P(None, "dp"), P("dp"), P(), P(), P(),
            P(None, "dp"), P("dp"), P("dp"), P("dp"), P("dp"), P(None, ("mp", "dp")),
            P(("mp", "dp")), P("mp", "dp"), P("dp"), P("dp"),
        ),
        check_vma=False,
    )
```

```python
import functools

import jax
import jax.numpy as jnp
from jax import lax
from jax.experimental import pallas as pl
from jax.experimental.pallas import tpu as pltpu
from jax.sharding import PartitionSpec as P

BF = jnp.bfloat16
F32 = jnp.float32
LOG2E = 1.4426950408889634
EPS = 1e-06
VMEM_LIMIT = 56 * 1024 * 1024


def nn(a, b):
    return lax.dot_general(a, b, (((1,), (0,)), ((), ())), preferred_element_type=F32)


def nt(a, b):
    return lax.dot_general(a, b, (((1,), (1,)), ((), ())), preferred_element_type=F32)


def tn(a, b):
    return lax.dot_general(a, b, (((0,), (0,)), ((), ())), preferred_element_type=F32)


def exact(a, b, dims):
    return lax.dot_general(
        a, b, (dims, ((), ())), precision=lax.Precision.HIGHEST, preferred_element_type=F32
    )


def normalized(x):
    mean = jnp.mean(x, axis=-1, keepdims=True)
    c = x - mean
    r = lax.rsqrt(jnp.mean(c * c, axis=-1, keepdims=True) + EPS)
    return c * r, r


def norm_back(cot, n, r, gain):
    cg = cot * gain
    return r * (
        cg
        - jnp.mean(cg, axis=-1, keepdims=True)
        - n * jnp.mean(cg * n, axis=-1, keepdims=True)
    )


def colsum(x):
    return jnp.sum(x, axis=0, keepdims=True)


def split(x):
    hi = x.astype(BF)
    return jnp.concatenate([hi, (x - hi.astype(F32)).astype(BF)], axis=1)


def row(ref):
    return ref[...].reshape(1, ref.shape[0])


def gelu_parts(z):
    e = jnp.exp2(z * z * (-0.5 * LOG2E))
    t = 1.0 / (1.0 + jnp.abs(z) * (0.3275911 * 0.7071067811865476))
    poly = t * (
        0.5 * 0.254829592
        + t
        * (
            0.5 * -0.284496736
            + t * (0.5 * 1.421413741 + t * (0.5 * -1.453152027 + t * (0.5 * 1.061405429)))
        )
    )
    tail = poly * e
    phi = jnp.where(z >= 0, 1.0 - tail, tail)
    return phi, phi + z * e * 0.3989422804014327


def head_of_lane(shape, axis, head_dim):
    return lax.broadcasted_iota(jnp.int32, shape, axis) // head_dim


def chunks(count, size=16):
    return [slice(at, at + size) for at in range(0, count, size)]


def fold(x):
    return sum(x[at : at + 8] for at in range(8, x.shape[0], 8)) + x[0:8]


def pack_kernel(w1, w2, b1, one, other):
    feats = w1.shape[0]
    rest = row(b1)
    place = lax.broadcasted_iota(jnp.int32, (16, feats), 0)
    bias = jnp.zeros((16, feats), F32)
    for j in range(3):
        term = rest.astype(BF).astype(F32)
        bias = jnp.where(place == j, term, bias)
        rest = rest - term
    bias = bias.astype(BF)
    one[0:feats, :] = w1[...]
    one[feats : 2 * feats, :] = w2[...]
    one[2 * feats :, :] = bias
    other[feats:, :] = bias
    for core in range(2):

        @pl.when(jnp.bitwise_and(lax.axis_index("dp"), 1) == core)
        def _(core=core):
            other[0:feats, :] = (w1, w2)[core][...]


def attn_fwd_kernel(
    counts, tok, og, n1g, n1b, qkvb, pre, post, postb, projb, gamma1, n2g, n2b, wqkv, wproj,
    a1_o, q_o, k_o, v_o, p_o, o_o, x1_o, u_o, a2_o, dy_o, mpre, mpost, mixb, mpre_b,
    pad, kk, attended_t, mpost_b, mix_b,
):
    i = pl.program_id(0)
    images = pl.num_programs(0)
    patches, feats = tok.shape[1:]
    rows = pad.shape[0]
    heads = mpre.shape[0]
    head_dim = feats // heads
    slots = q_o.shape[1]

    @pl.when(i == 0)
    def _():
        spread = (
            head_of_lane((heads, feats), 1, head_dim)
            == lax.broadcasted_iota(jnp.int32, (heads, feats), 0)
        ).astype(F32)
        scale = head_dim**-0.5 * LOG2E
        mpre[...] = exact(pre[...], spread, ((1,), (0,))) * scale
        mpost[...] = exact(post[...], spread, ((0,), (0,)))
        mixb[...] = exact(row(postb), spread, ((1,), (0,)))
        ones = jnp.ones((1, 128), F32)
        for h in range(heads):
            column = exact(pre[h : h + 1, :], ones, ((0,), (0,))) * scale
            mpre_b[h] = exact(spread, column, ((0,), (0,)))
            mpost_b[h] = exact(spread, post[:, h : h + 1] * ones, ((0,), (0,)))
        mix_b[...] = exact(spread, exact(row(postb), ones, ((0,), (0,))), ((0,), (0,)))
        q_o[0, rows:] = jnp.zeros((slots - rows, feats), BF)

    pad[patches:, :] = jnp.zeros((rows - patches, feats), F32)
    live = (lax.axis_index("mp") * images + i < counts[0]).astype(F32)
    pad[0:patches, :] = og[0].astype(F32) * live
    dy_o[0] = pad[...].astype(BF)
    pad[0:patches, :] = tok[0].astype(F32)
    gain, shift = row(n1g), row(n1b)
    for c in chunks(rows):
        n, _ = normalized(pad[c, :])
        a1_o[0, c, :] = (n * gain + shift).astype(BF)
    qkv = nn(a1_o[0], wqkv[...])
    bias = row(qkvb)
    q_o[0, rows:] = jnp.zeros((slots - rows, feats), BF)
    for c in chunks(rows):
        q, k, v = (
            qkv[c, j * feats : (j + 1) * feats] + bias[:, j * feats : (j + 1) * feats]
            for j in range(3)
        )
        q_o[0, c, :] = q.astype(BF)
        v_o[0, c, :] = v.astype(BF)
        k = k.astype(BF)
        k_o[0, c, :] = k
        kf = k.astype(F32)
        for g in range(heads):
            at = slice(g * rows + c.start, g * rows + c.stop)
            scaled = kf * mpre[g : g + 1, :]
            hi = scaled.astype(BF)
            kk[at, 0:feats] = hi
            kk[at, feats:] = (scaled - hi.astype(F32)).astype(BF)
    q2 = jnp.concatenate([q_o[0], q_o[0]], axis=1)
    vt = v_o[0].T
    many = heads // 2
    half = many * rows
    tail = patches // 8 * 8
    inside = lax.broadcasted_iota(jnp.int32, (rows - tail, 128), 0) < patches - tail
    logits = [nt(kk[s * half : (s + 1) * half, :], q2) for s in range(2)]
    mixed = []
    for g in range(heads):
        for lane in range(0, slots, 128):
            x = logits[g // many][g % many * rows : (g % many + 1) * rows, lane : lane + 128]
            x = jnp.concatenate([x[0:tail], jnp.where(inside, x[tail:], -1e30)], axis=0)
            e = jnp.exp2(x - jnp.max(x, axis=0, keepdims=True))
            inv = 1.0 / jnp.sum(e, axis=0, keepdims=True)
            p_o[0, g, :, lane : lane + 128] = (e * inv).astype(BF)
        mixed.append(nn(vt, p_o[0, g]))
    real = (lax.broadcasted_iota(jnp.int32, (rows, 128), 0) < patches).astype(BF)
    start = nn(vt, real) * mix_b[...]
    for c in chunks(feats):
        for lane in range(0, slots, 128):
            total = start[c]
            for h in range(heads):
                total = total + mixed[h][c, lane : lane + 128] * mpost_b[h, c, :]
            attended_t[c, lane : lane + 128] = total.astype(BF)
    o_o[0] = attended_t[...].T[0:rows]
    product = nn(o_o[0], wproj[...])
    bias, scale, gain, shift = row(projb), row(gamma1), row(n2g), row(n2b)
    for c in chunks(rows):
        u = product[c] + bias
        x1 = pad[c, :] + scale * u
        u_o[0, c, :] = u
        x1_o[0, c, :] = x1
        n, _ = normalized(x1)
        a2_o[0, c, :] = (n * gain + shift).astype(BF)


def store_blocks(count, put):
    mine = lax.axis_index("dp")
    for core in range(2):

        @pl.when(jnp.bitwise_and(mine, 1) == core)
        def _(core=core):
            for b in range(count):
                place = jnp.bitwise_xor(jnp.int32(b >> 1), jnp.right_shift(mine, 1))
                put((b ^ core) & 1, place, b)


def mlp_step(act, df, w1, b1, w2, hids, dzs, at, b1_sum):
    z = nn(act, w1[...])
    grad_hidden = nt(df, w2[...])
    width = z.shape[1]
    rows = z.shape[0]
    lanes = 256
    for first in range(0, width, lanes):
        part = slice(first, first + lanes)
        bias = b1[:, part]
        sums = jnp.zeros((8, lanes), F32)
        for c in chunks(rows):
            zc = z[c, part] + bias
            phi, slope = gelu_parts(zc)
            dz = (grad_hidden[c, part] * slope).astype(BF)
            place = pl.ds(pl.multiple_of(at + c.start, 16), 16)
            hids[place, part] = (zc * phi).astype(BF)
            dzs[place, part] = dz
            sums = sums + fold(dz.astype(F32))
        b1_sum[:, part] += colsum(sums)
    here = pl.ds(pl.multiple_of(at, 16), rows)
    return nn(hids[here, :], w2[...]), nt(dzs[here, :], w1[...])


def mlp_first_kernel(
    a2, dy, gamma2, w1_own, b1_own, w2_own, near,
    f_o, da2_o, grads, b1_o, a2t, dft,
    w1, w2, b1, hids, dzs, dfs,
):
    i = pl.program_id(0)
    rows, feats = f_o.shape
    at = i * rows
    here = pl.ds(pl.multiple_of(at, rows), rows)

    @pl.when(i == 0)
    def _():
        b1_o[...] = jnp.zeros_like(b1_o)
        w1[:, 0:feats] = w1_own[...]
        w1[:, feats:] = near[0:feats]
        w2[0:feats, :] = w2_own[...]
        w2[feats:, :] = near[feats : 2 * feats]
        b1[:, 0:feats] = row(b1_own)
        b1[:, feats:] = colsum(near[2 * feats : 2 * feats + 16].astype(F32))

    gain = row(gamma2)
    for c in chunks(rows):
        place = pl.ds(pl.multiple_of(at + c.start, 16), 16)
        dfs[place, :] = (dy[place, :].astype(F32) * gain).astype(BF)
    f, da2 = mlp_step(a2[here, :], dfs[here, :], w1, b1, w2, hids, dzs, at, b1_o)
    f_o[...] = f
    da2_o[...] = da2

    @pl.when(i == pl.num_programs(0) - 1)
    def _():
        a2t[...] = a2[...].T
        dft[...] = dfs[...].T
        grads[0] = nn(a2t[...], dzs[...]).astype(BF).T
        down = nn(dft[...], hids[...]).astype(BF)
        for c in range(2):
            grads[1, c * feats : (c + 1) * feats, :] = down[:, c * feats : (c + 1) * feats]


def mlp_rest_kernel(
    counts, a2, dy, x1, u, o, f0, da20, near, far, grads, a2t, dft, wproj, gamma1, n2g, fc2b, gamma2,
    out_o, dx1_o, do_o, keep, send, b1_o, acc_o,
    w1, w2, b1, hids, dzs, dfs, dus, ups, downs, projs,
):
    i = pl.program_id(0)
    rows, feats = f0.shape
    group, patches = out_o.shape[:2]
    image_rows = rows // group
    at = i * rows
    here = pl.ds(pl.multiple_of(at, rows), rows)
    m_idx = lax.axis_index("mp")

    @pl.when(i == 0)
    def _():
        b1_o[...] = jnp.zeros_like(b1_o)
        acc_o[...] = jnp.zeros_like(acc_o)
        for c in range(2):
            b1[:, c * feats : (c + 1) * feats] = colsum(near[c, feats : feats + 16].astype(F32))

    for core in range(2):

        @pl.when(jnp.logical_and(i == 0, jnp.bitwise_and(lax.axis_index("dp"), 1) == core))
        def _(core=core):
            first, second = (near, far) if core == 0 else (far, near)
            for c in range(2):
                w1[:, c * feats : (c + 1) * feats] = first[c, 0:feats]
                w2[c * feats : (c + 1) * feats, :] = second[c, 0:feats]

    gain2 = row(gamma2)
    for c in chunks(rows):
        place = pl.ds(pl.multiple_of(at + c.start, 16), 16)
        dfs[place, :] = (dy[place, :].astype(F32) * gain2).astype(BF)
    f, da2 = mlp_step(a2[here, :], dfs[here, :], w1, b1, w2, hids, dzs, at, b1_o)
    bias, gain, scale = row(fc2b), row(n2g), row(gamma1)
    sums = [jnp.zeros((8, feats), F32) for _ in range(6)]
    for c in chunks(rows):
        place = pl.ds(pl.multiple_of(at + c.start, 16), 16)
        fc = f[c] + f0[c, :] + bias
        dac = da2[c] + da20[c, :]
        x1c = x1[c, :]
        dyc = dy[place, :].astype(F32)
        n, r = normalized(x1c)
        dx1 = dyc + norm_back(dac, n, r, gain)
        dx1_o[c, :] = dx1
        du = (dx1 * scale).astype(BF)
        dus[place, :] = du
        image = c.start // image_rows
        first = c.start - image * image_rows
        live = (m_idx * (group * pl.num_programs(0)) + i * group + image < counts[0]).astype(F32)
        out = ((x1c + gain2 * fc) * live).astype(BF)
        if first + 16 <= patches:
            out_o[image, first : first + 16, :] = out
        else:
            out_o[image, first:patches, :] = out[0 : patches - first]
        terms = (
            du.astype(F32), u[c, :] * dx1, dac * n, dac, dfs[place, :].astype(F32), fc * dyc,
        )
        sums = [s + fold(t) for s, t in zip(sums, terms)]
    for j in range(6):
        acc_o[j : j + 1, :] += colsum(sums[j])
    do = nt(dus[here, :], wproj[...]).astype(BF)
    for j in range(group):
        do_o[j, 0:image_rows] = do[j * image_rows : (j + 1) * image_rows]
        do_o[j, image_rows:] = jnp.zeros((do_o.shape[1] - image_rows, feats), BF)

    @pl.when(i == pl.num_programs(0) - 1)
    def _():
        count = 2 * keep.shape[0]
        size = feats // count
        outs = (keep, send)

        ups[...] = nn(a2t[...], dzs[...]).astype(BF).T
        downs[...] = nn(dft[...], hids[...]).astype(BF)
        projs[...] = tn(dus[...], o[...]).astype(BF)

        def put(which, place, b):
            out = outs[which]
            for c in range(2):
                part = slice(c * feats, (c + 1) * feats)
                up = slice(c * feats + b * size, c * feats + (b + 1) * size)
                down = slice(b * size, (b + 1) * size)
                pieces = (grads[0, up, :], grads[1, c * feats + b * size : c * feats + (b + 1) * size, :])
                for j, piece in enumerate(pieces):
                    out[place, (2 * c + j) * size : (2 * c + j + 1) * size, :] = piece
                pieces = (ups[up, :], downs[down, part])
                for j, piece in enumerate(pieces):
                    out[place, (4 + 2 * c + j) * size : (5 + 2 * c + j) * size, :] = piece
            out[place, 8 * size : 9 * size, :] = projs[b * size : (b + 1) * size, :]

        store_blocks(count, put)


def attn_bwd_kernel(
    do_r, q_r, k_r, v_r, p_r, dx1, tok, mpre, mpost, mixb, mpre_b, wqkv, n1g, *refs
):
    dqkv_o, in_o, acc_o, vgs, dls, dq_t, pad = refs[-7:]
    i = pl.program_id(0)
    slots, feats = do_r.shape[1:]
    patches = tok.shape[1]
    rows = k_r.shape[1]
    heads = mpre.shape[0]
    many = heads // 2
    half = many * rows

    @pl.when(i == 0)
    def _():
        acc_o[...] = jnp.zeros_like(acc_o)

    do_sum = jnp.zeros((8, feats), F32)
    for c in chunks(rows):
        vf = v_r[0, c, :].astype(F32)
        do_sum = do_sum + fold(do_r[0, c, :].astype(F32))
        for h in range(heads):
            vgs[h * rows + c.start : h * rows + c.stop, :] = (vf * mpost[h : h + 1, :]).astype(BF)
    do_sum = colsum(do_sum)
    q = q_r[0]
    do = do_r[0]
    kt = k_r[0].T
    dps = [nt(vgs[s * half : (s + 1) * half, :], do) for s in range(2)]
    dvs = [nn(p_r[0, s * many : (s + 1) * many].reshape(half, slots), do) for s in range(2)]
    dks, dqs = [], []
    for h in range(heads):
        for lane in range(0, slots, 128):
            dp = dps[h // many][h % many * rows : (h % many + 1) * rows, lane : lane + 128]
            pf = p_r[0, h, :, lane : lane + 128].astype(F32)
            mean = jnp.sum(dp * pf, axis=0, keepdims=True) / jnp.sum(pf, axis=0, keepdims=True)
            dls[h * rows : (h + 1) * rows, lane : lane + 128] = (pf * (dp - mean)).astype(BF)
        dqs.append(nn(kt, dls[h * rows : (h + 1) * rows, :]))
        if h % many == many - 1:
            s = h // many
            dks.append(nn(dls[s * half : (s + 1) * half, :], q))

    bias_row = mixb[...] * do_sum
    v_sum = jnp.zeros((8, feats), F32)
    dv_sum = jnp.zeros((8, feats), F32)
    sums = [jnp.zeros((8, feats), F32) for _ in range(heads)]
    for c in chunks(rows):
        vf = v_r[0, c, :].astype(F32)
        dv = bias_row
        for h in range(heads):
            at = (h % many) * rows
            this = dvs[h // many][at + c.start : at + c.stop]
            dv = dv + this * mpost[h : h + 1, :]
            sums[h] = sums[h] + fold(vf * this)
        if c.stop > patches:
            inside = lax.broadcasted_iota(jnp.int32, dv.shape, 0) < patches - c.start
            dv = jnp.where(inside, dv, 0.0)
            vf = jnp.where(inside, vf, 0.0)
        low = dv.astype(BF)
        dqkv_o[0, c, 2 * feats :] = low
        dv_sum = dv_sum + fold(low.astype(F32))
        v_sum = v_sum + fold(vf)
    for h in range(heads):
        acc_o[h : h + 1, :] += colsum(sums[h])
    acc_o[2 * heads : 2 * heads + 1, :] += do_sum * colsum(v_sum)
    acc_o[2 * heads + 10 : 2 * heads + 11, :] += colsum(dv_sum)

    for c in chunks(feats):
        for lane in range(0, slots, 128):
            total = 0.0
            for h in range(heads):
                total = total + dqs[h][c, lane : lane + 128] * mpre_b[h, c, :]
            dq_t[c, lane : lane + 128] = (total * (1.0 / LOG2E)).astype(BF)
    dq = dq_t[...].T[0:rows]
    dqkv_o[0, :, 0:feats] = dq
    dk_sum = jnp.zeros((8, feats), F32)
    sums = [jnp.zeros((8, feats), F32) for _ in range(heads)]
    for c in chunks(rows):
        kf = k_r[0, c, :].astype(F32)
        dk = 0.0
        for h in range(heads):
            at = (h % many) * rows
            this = dks[h // many][at + c.start : at + c.stop]
            dk = dk + this * mpre[h : h + 1, :]
            sums[h] = sums[h] + fold(kf * this)
        low = (dk * (1.0 / LOG2E)).astype(BF)
        dqkv_o[0, c, feats : 2 * feats] = low
        dk_sum = dk_sum + fold(low.astype(F32))
    for h in range(heads):
        acc_o[heads + h : heads + h + 1, :] += colsum(sums[h])
    acc_o[2 * heads + 8 : 2 * heads + 9, :] += colsum(dq.astype(F32))
    acc_o[2 * heads + 9 : 2 * heads + 10, :] += colsum(dk_sum)

    pad[patches:, :] = jnp.zeros((rows - patches, feats), F32)
    pad[0:patches, :] = tok[0].astype(F32)
    da1 = nt(dqkv_o[0], wqkv[...])
    gain = row(n1g)
    sums = [jnp.zeros((8, feats), F32) for _ in range(2)]
    for c in chunks(rows):
        n, r = normalized(pad[c, :])
        cot = da1[c]
        grad = dx1[0, c, :] + norm_back(cot, n, r, gain)
        sums = [sums[0] + fold(cot * n), sums[1] + fold(cot)]
        if c.stop <= patches:
            in_o[0, c, :] = grad
        else:
            in_o[0, c.start : patches, :] = grad[0 : patches - c.start]
    for j in range(2):
        acc_o[2 * heads + 11 + j : 2 * heads + 12 + j, :] += colsum(sums[j])


def qkv_grad_kernel(heads, dqkv, *refs):
    accs = refs[:-8]
    a1, acc_mlp, b1_first, b1_rest, keep, send, small, grads = refs[-8:]
    feats = a1.shape[1]
    count = 2 * keep.shape[0]
    size = 3 * feats // count
    acc = accs[0][...]
    for other in accs[1:]:
        acc = acc + other[...]
    small[...] = jnp.zeros_like(small)
    small[0:2, :] = acc[2 * heads + 11 : 2 * heads + 13]
    small[2:8, :] = acc_mlp[0:6, :]
    small[8:11, :] = acc[2 * heads + 8 : 2 * heads + 11]
    head_dim = feats // heads
    lanes = 2 * heads * heads
    gather = (
        head_of_lane((feats, lanes), 0, head_dim)
        == lax.broadcasted_iota(jnp.int32, (feats, lanes), 1) % heads
    ).astype(F32)
    sums = exact(acc[0 : 2 * heads + 8], gather, ((1,), (0,)))
    place = head_of_lane((2 * heads, lanes), 1, heads) == lax.broadcasted_iota(
        jnp.int32, (2 * heads, lanes), 0
    )
    small[11:12, 0:lanes] = colsum(jnp.where(place, sums[0 : 2 * heads], 0.0))
    small[11:12, lanes : 2 * lanes] = sums[2 * heads : 2 * heads + 1]
    m_idx = lax.axis_index("mp")
    for c, ref in enumerate((b1_first, b1_first, b1_rest, b1_rest)):
        place = 12 + jnp.bitwise_xor(m_idx, c)
        small[pl.ds(place, 1), :] = ref[:, (c % 2) * feats : (c % 2 + 1) * feats]
    low = small[...].astype(BF)
    outs = (keep, send)

    grads[...] = tn(a1[...], dqkv[...]).astype(BF).T

    def put(which, place, b):
        outs[which][place, 0:size, :] = grads[b * size : (b + 1) * size, :]
        outs[which][place, size:, :] = low

    store_blocks(count, put)


def final_kernel(heads, size, *refs):
    mine, got = refs[0], refs[1:-14]
    qkv_o, qkvb_o, pre_o, post_o, postb_o, b1_o, *vecs_o = refs[-14:]
    total = mine[...]
    for part in got:
        total = total + part[...].astype(F32)
    feats = total.shape[1]
    qkv_o[...] = total[0:size]
    small = total[size:]
    d_idx = lax.axis_index("dp")
    m_idx = lax.axis_index("mp")

    def own(value, width, index):
        lanes = value.shape[1]
        return pltpu.roll(value, lax.rem(lanes - index * width, lanes), axis=1)[:, 0:width]

    width = vecs_o[0].shape[1]
    vecs = own(small[0:8], width, d_idx)
    for j, ref in enumerate(vecs_o):
        ref[...] = vecs[j : j + 1]
    flat = jnp.concatenate([small[8 + j : 9 + j] for j in range(3)], axis=1)
    qkvb_o[...] = own(jnp.broadcast_to(flat, (8, 3 * feats)), qkvb_o.shape[1], d_idx)[0:1]
    b1 = own(small[8:16], b1_o.shape[1], d_idx)[4:8]
    pick = lax.broadcasted_iota(jnp.int32, b1.shape, 0) == m_idx
    b1_o[...] = colsum(jnp.where(pick, b1, 0.0))
    mix = small[11:12]
    hh = heads * heads
    line = lax.broadcasted_iota(jnp.int32, (heads, hh), 0)
    lane = lax.broadcasted_iota(jnp.int32, (heads, hh), 1)
    fold = (
        lax.broadcasted_iota(jnp.int32, (hh, heads), 0) % heads
        == lax.broadcasted_iota(jnp.int32, (hh, heads), 1)
    ).astype(F32)
    head_dim = feats // heads

    def square(values):
        return exact(jnp.where(lane // heads == line, values, 0.0), fold, ((1,), (0,)))

    post_o[...] = square(mix[:, 0:hh]).T
    pre_o[...] = square(mix[:, hh : 2 * hh]) * (head_dim**-0.5)
    postb_o[...] = mix[:, 2 * hh : 2 * hh + heads]


def whole(shape):
    return pl.BlockSpec(shape, lambda i: (0,) * len(shape))


def each(shape, first=0, many=1):
    return pl.BlockSpec((many,) + shape[1:], lambda i: (i + first,) + (0,) * (len(shape) - 1))


SCALARS = pl.BlockSpec(memory_space=pltpu.SMEM)


def sds(shape, dtype):
    return jax.ShapeDtypeStruct(shape, dtype)


def call(
    kernel, grid, ins, in_specs, outs, out_specs, scratch=(), flops=0, name=None, aliases=None
):
    size = lambda a: a.size * a.dtype.itemsize
    return pl.pallas_call(
        kernel,
        grid=grid,
        in_specs=in_specs,
        out_specs=out_specs,
        out_shape=outs,
        scratch_shapes=scratch,
        input_output_aliases=aliases or {},
        compiler_params=pltpu.CompilerParams(vmem_limit_bytes=VMEM_LIMIT),
        cost_estimate=pl.CostEstimate(
            flops=flops,
            bytes_accessed=sum(size(a) for a in ins) + sum(size(a) for a in outs),
            transcendentals=0,
        ),
        name=name,
    )(*ins)


def xor_perm(count, mask):
    return [(j, j ^ mask) for j in range(count)]


def dp_hops(dp):
    bits = dp.bit_length() - 1
    groups = []
    at = 1
    while at < bits:
        groups.append((at, min(2, bits - at)))
        at += groups[-1][1]
    return groups


def dp_scatter(value, dp):
    for at, many in dp_hops(dp):
        value = value.reshape((-1, 1 << many) + value.shape[1:])
        got = [
            lax.ppermute(value[:, j].astype(BF), "dp", xor_perm(dp, j << at))
            for j in range(1, 1 << many)
        ]
        value = value[:, 0] + sum(g.astype(F32) for g in got)
    return value.reshape(value.shape[-2:])


def per_device(
    dp, mp,
    tokens_in, image_counts, norm1_gain, norm1_bias, qkv_weight, qkv_bias,
    mix_pre, mix_post, mix_post_bias, proj_weight, proj_bias, gamma1,
    norm2_gain, norm2_bias, fc1_weight, fc1_bias, fc2_weight, fc2_bias, gamma2, out_grad,
):
    images, patches, feats = tokens_in.shape
    heads = mix_pre.shape[0]
    rows = -(-patches // 16) * 16
    slots = -(-patches // 128) * 128
    hidden = fc1_weight.shape[1]
    ins = [fc1_weight, fc2_weight, fc1_bias]
    outs = [sds((2 * feats + 16, hidden), BF), sds((feats + 16, hidden), BF)]
    one, other = call(
        pack_kernel,
        (1,),
        ins,
        [whole(a.shape) for a in ins],
        outs,
        [whole(a.shape) for a in outs],
        name="pack",
    )
    near_one = lax.ppermute(one, "mp", xor_perm(mp, 1))
    near = [lax.ppermute(other, "mp", xor_perm(mp, j)) for j in range(2, mp)]

    tok_rows = (images, rows, feats)
    slot_rows = (images, slots, feats)
    prob_shape = (images, heads, rows, slots)
    mix_shape = (heads, feats)
    mix_lanes = (heads, feats, 128)
    ins = [
        image_counts, tokens_in, out_grad, norm1_gain, norm1_bias, qkv_bias, mix_pre, mix_post,
        mix_post_bias, proj_bias, gamma1, norm2_gain, norm2_bias, qkv_weight, proj_weight,
    ]
    a1, q, k, v, prob, o, x1, u, a2, dy, mpre, mpost, mixb, mpre_b = call(
        attn_fwd_kernel,
        (images,),
        ins,
        [SCALARS, each(tokens_in.shape), each(out_grad.shape)] + [whole(a.shape) for a in ins[3:]],
        [
            sds(tok_rows, BF), sds(slot_rows, BF), sds(tok_rows, BF), sds(tok_rows, BF),
            sds(prob_shape, BF), sds(tok_rows, BF), sds(tok_rows, F32), sds(tok_rows, F32),
            sds(tok_rows, BF), sds(tok_rows, BF), sds(mix_shape, F32), sds(mix_shape, F32),
            sds((1, feats), F32), sds(mix_lanes, F32),
        ],
        [each(s) for s in (tok_rows, slot_rows, tok_rows, tok_rows, prob_shape)]
        + [each(tok_rows)] * 5
        + [whole(mix_shape)] * 2
        + [whole((1, feats)), whole(mix_lanes)],
        [
            pltpu.VMEM((rows, feats), F32), pltpu.VMEM((heads * rows, 2 * feats), BF),
            pltpu.VMEM((feats, slots), BF), pltpu.VMEM(mix_lanes, F32),
            pltpu.VMEM((feats, 128), F32),
        ],
        flops=images * 15 * 10**8,
        name="attn_fwd",
    )

    block = feats // dp
    total = images * rows
    group = 2 if images % 2 == 0 else 1
    flat = (total, feats)
    step = (group * rows, feats)
    a2, dy, x1, u, o = (a.reshape(flat) for a in (a2, dy, x1, u, o))
    near_one, near, a2 = lax.optimization_barrier((near_one, near, a2))
    near = jnp.stack(near)
    far = lax.ppermute(near, "dp", xor_perm(dp, 1))
    ins = [a2, dy, gamma2, fc1_weight, fc1_bias, fc2_weight, near_one]
    blocked = pl.BlockSpec(step, lambda i: (i, 0))
    wide = 2 * hidden
    grad_shape = (2, wide, feats)
    f0, da20, grads0, b1_0, a2t, dft = call(
        mlp_first_kernel,
        (images // group,),
        ins,
        [whole(a.shape) for a in ins],
        [
            sds(flat, F32), sds(flat, F32), sds(grad_shape, BF), sds((1, wide), F32),
            sds((feats, total), BF), sds((feats, total), BF),
        ],
        [blocked, blocked, whole(grad_shape), whole((1, wide))] + [whole((feats, total))] * 2,
        [
            pltpu.VMEM((feats, wide), BF), pltpu.VMEM((wide, feats), BF),
            pltpu.VMEM((1, wide), F32), pltpu.VMEM((total, wide), BF),
            pltpu.VMEM((total, wide), BF), pltpu.VMEM(flat, BF),
        ],
        flops=images * 8 * 10**8,
        name="mlp_first",
    )

    grad_rows = 9 * block
    half_shape = (dp // 2, grad_rows, feats)
    ins = [
        image_counts, a2, dy, x1, u, o, f0, da20, near, far, grads0, a2t, dft, proj_weight, gamma1,
        norm2_gain, fc2_bias, gamma2,
    ]
    layer_out, dx1, do, keep, send, b1_1, acc_mlp = call(
        mlp_rest_kernel,
        (images // group,),
        ins,
        [SCALARS, whole(flat), whole(flat), blocked, blocked, whole(flat), blocked, blocked]
        + [whole(a.shape) for a in ins[8:]],
        [
            sds(tokens_in.shape, BF), sds(flat, F32), sds(slot_rows, BF), sds(half_shape, BF),
            sds(half_shape, BF), sds((1, wide), F32), sds((8, feats), F32),
        ],
        [
            each(tokens_in.shape, 0, group), blocked, each(slot_rows, 0, group), whole(half_shape),
            whole(half_shape), whole((1, wide)), whole((8, feats)),
        ],
        [
            pltpu.VMEM((feats, wide), BF), pltpu.VMEM((wide, feats), BF),
            pltpu.VMEM((1, wide), F32), pltpu.VMEM((total, wide), BF),
            pltpu.VMEM((total, wide), BF), pltpu.VMEM(flat, BF), pltpu.VMEM(flat, BF),
            pltpu.VMEM((wide, feats), BF), pltpu.VMEM((feats, wide), BF),
            pltpu.VMEM((feats, feats), BF),
        ],
        flops=images * 9 * 10**8,
        name="mlp_rest",
    )
    got = lax.ppermute(send, "dp", xor_perm(dp, 1))
    dx1 = dx1.reshape(tok_rows)

    shares = [1, 3, 2] if images == 6 else [images]
    steps = len(shares)
    dqkv_shape = (images, rows, 3 * feats)
    carried, accs = [], []
    for s, share in enumerate(shares):
        first = sum(shares[:s])
        ins = [do, q, k, v, prob, dx1, tokens_in, mpre, mpost, mixb, mpre_b, qkv_weight, norm1_gain]
        *carried, acc = call(
            attn_bwd_kernel,
            (share,),
            ins + carried,
            [each(a.shape, first) for a in ins[:7]]
            + [whole(a.shape) for a in ins[7:]]
            + [pl.BlockSpec(memory_space=pl.ANY)] * len(carried),
            [sds(dqkv_shape, BF), sds(tokens_in.shape, F32), sds((2 * heads + 16, feats), F32)],
            [
                each(dqkv_shape, first), each(tokens_in.shape, first),
                whole((2 * heads + 16, feats)),
            ],
            [
                pltpu.VMEM((heads * rows, feats), BF), pltpu.VMEM((heads * rows, slots), BF),
                pltpu.VMEM((feats, slots), BF), pltpu.VMEM((rows, feats), F32),
            ],
            flops=share * 20 * 10**8,
            name="attn_bwd",
            aliases={len(ins): 0, len(ins) + 1: 1} if carried else None,
        )
        accs.append(acc)
        if s == 0:
            (keep, got), acc = lax.optimization_barrier(((keep, got), acc))
            mine = dp_scatter(keep.astype(F32) + got.astype(F32), dp)
            accs[0], do = lax.optimization_barrier((acc, do))
        if s == min(1, steps - 1):
            mine, acc = lax.optimization_barrier((mine, acc))
            low = mine.astype(BF)
            proj = low[8 * block :]
            got_z = [
                lax.ppermute(
                    jnp.concatenate([low[2 * j * block : 2 * (j + 1) * block], proj]),
                    "mp",
                    xor_perm(mp, j),
                )
                for j in range(1, mp)
            ]
            accs[s], do = lax.optimization_barrier((acc, do))
    dqkv, in_grad = carried
    got_z, dqkv = lax.optimization_barrier((got_z, dqkv))
    sums = jnp.concatenate([mine[: 2 * block], mine[8 * block :]]) + sum(
        g.astype(F32) for g in got_z
    )
    fc1g, fc2g, projg = (sums[j * block : (j + 1) * block] for j in range(3))

    q_block = 3 * feats // dp
    half_shape = (dp // 2, q_block + 16, feats)
    ins = [dqkv.reshape(total, 3 * feats)] + accs + [a1.reshape(flat), acc_mlp, b1_0, b1_1]
    keep, send = call(
        functools.partial(qkv_grad_kernel, heads),
        (1,),
        ins,
        [whole(a.shape) for a in ins],
        [sds(half_shape, BF), sds(half_shape, BF)],
        [whole(half_shape), whole(half_shape)],
        [pltpu.VMEM((16, feats), F32), pltpu.VMEM((3 * feats, feats), BF)],
        flops=11 * 10**8,
        name="qkv_grad",
    )
    got = lax.ppermute(send, "dp", xor_perm(dp, 1))
    mine = dp_scatter(keep.astype(F32) + got.astype(F32), dp)
    low = mine.astype(BF)
    got = [lax.ppermute(low, "mp", xor_perm(mp, j)) for j in range(1, mp)]
    b1_size = hidden // dp
    ins = [mine] + got
    outs = [
        sds((q_block, feats), F32), sds((1, q_block), F32), sds((heads, heads), F32),
        sds((heads, heads), F32), sds((1, heads), F32), sds((1, b1_size), F32),
    ] + [sds((1, block), F32)] * 8
    qkvw, qkvb, pre, post, postb, b1g, *vecs = call(
        functools.partial(final_kernel, heads, q_block),
        (1,),
        ins,
        [whole(a.shape) for a in ins],
        outs,
        [whole(a.shape) for a in outs],
        name="final",
    )
    vecs = [a.reshape(-1) for a in vecs]
    return (
        layer_out,
        in_grad,
        vecs[0],
        vecs[1],
        qkvw.T,
        qkvb.reshape(-1),
        pre,
        post,
        postb.reshape(-1),
        projg.T,
        vecs[2],
        vecs[3],
        vecs[4],
        vecs[5],
        fc1g.T,
        b1g.reshape(-1),
        fc2g.T,
        vecs[6],
        vecs[7],
    )


def solution(mesh):
    tokens = P(("dp", "mp"), None, None)
    placed = (
        (tokens, P("dp")) + (P(),) * 12 + (P(None, "mp"), P("mp"), P("mp", None), P(), P(), tokens)
    )
    return jax.shard_map(
        functools.partial(per_device, mesh.shape["dp"], mesh.shape["mp"]),
        mesh=mesh,
        in_specs=placed,
        out_specs=(
            tokens, tokens, P("dp"), P("dp"), P(None, "dp"), P("dp"), P(), P(), P(),
            P(None, "dp"), P("dp"), P("dp"), P("dp"), P("dp"), P(None, ("mp", "dp")),
            P(("mp", "dp")), P("mp", "dp"), P("dp"), P("dp"),
        ),
        check_vma=False,
    )
```

```python
import functools

import jax
import jax.numpy as jnp
from jax import lax
from jax.experimental import pallas as pl
from jax.experimental.pallas import tpu as pltpu
from jax.sharding import PartitionSpec as P

BF = jnp.bfloat16
F32 = jnp.float32
LOG2E = 1.4426950408889634
EPS = 1e-06
VMEM_LIMIT = 20 * 1024 * 1024


def nn(a, b):
    return lax.dot_general(a, b, (((1,), (0,)), ((), ())), preferred_element_type=F32)


def nt(a, b):
    return lax.dot_general(a, b, (((1,), (1,)), ((), ())), preferred_element_type=F32)


def tn(a, b):
    return lax.dot_general(a, b, (((0,), (0,)), ((), ())), preferred_element_type=F32)


def exact(a, b, dims):
    return lax.dot_general(
        a, b, (dims, ((), ())), precision=lax.Precision.HIGHEST, preferred_element_type=F32
    )


def normalized(x):
    mean = jnp.mean(x, axis=-1, keepdims=True)
    c = x - mean
    r = lax.rsqrt(jnp.mean(c * c, axis=-1, keepdims=True) + EPS)
    return c * r, r


def norm_back(cot, n, r, gain):
    cg = cot * gain
    return r * (
        cg
        - jnp.mean(cg, axis=-1, keepdims=True)
        - n * jnp.mean(cg * n, axis=-1, keepdims=True)
    )


def colsum(x):
    return jnp.sum(x, axis=0, keepdims=True)


def split(x):
    hi = x.astype(BF)
    return jnp.concatenate([hi, (x - hi.astype(F32)).astype(BF)], axis=1)


def row(ref):
    return ref[...].reshape(1, ref.shape[0])


def gelu_parts(z):
    e = jnp.exp2(z * z * (-0.5 * LOG2E))
    t = 1.0 / (1.0 + jnp.abs(z) * (0.3275911 * 0.7071067811865476))
    poly = t * (
        0.5 * 0.254829592
        + t
        * (
            0.5 * -0.284496736
            + t * (0.5 * 1.421413741 + t * (0.5 * -1.453152027 + t * (0.5 * 1.061405429)))
        )
    )
    tail = poly * e
    phi = jnp.where(z >= 0, 1.0 - tail, tail)
    return phi, phi + z * e * 0.3989422804014327


def head_of_lane(shape, axis, head_dim):
    return lax.broadcasted_iota(jnp.int32, shape, axis) // head_dim


def chunks(count, size=16):
    return [slice(at, at + size) for at in range(0, count, size)]


def fold(x):
    return sum(x[at : at + 8] for at in range(8, x.shape[0], 8)) + x[0:8]


def pack_kernel(w1, w2, b1, one, other):
    feats = w1.shape[0]
    rest = row(b1)
    place = lax.broadcasted_iota(jnp.int32, (16, feats), 0)
    bias = jnp.zeros((16, feats), F32)
    for j in range(3):
        term = rest.astype(BF).astype(F32)
        bias = jnp.where(place == j, term, bias)
        rest = rest - term
    bias = bias.astype(BF)
    one[0:feats, :] = w1[...]
    one[feats : 2 * feats, :] = w2[...]
    one[2 * feats :, :] = bias
    other[feats:, :] = bias
    for core in range(2):

        @pl.when(jnp.bitwise_and(lax.axis_index("dp"), 1) == core)
        def _(core=core):
            other[0:feats, :] = (w1, w2)[core][...]


def attn_fwd_kernel(
    counts, post_s, postb_s, tok, og, n1g, n1b, qkvb, pre, post, postb, projb, gamma1, n2g, n2b,
    wqkv, wproj,
    a1_o, q_o, k_o, v_o, p_o, o_o, x1_o, u_o, a2_o, dy_o, mpre, mpost, mixb,
    pad, kk, attended_t,
):
    i = pl.program_id(0)
    images = pl.num_programs(0)
    patches, feats = tok.shape[1:]
    rows = pad.shape[0]
    heads = mpre.shape[0]
    head_dim = feats // heads
    slots = q_o.shape[1]

    @pl.when(i == 0)
    def _():
        spread = (
            head_of_lane((heads, feats), 1, head_dim)
            == lax.broadcasted_iota(jnp.int32, (heads, feats), 0)
        ).astype(F32)
        mpre[...] = exact(pre[...], spread, ((1,), (0,))) * (head_dim**-0.5 * LOG2E)
        mpost[...] = exact(post[...], spread, ((0,), (0,)))
        mixb[...] = exact(row(postb), spread, ((1,), (0,)))

    pad[patches:, :] = jnp.zeros((rows - patches, feats), F32)
    live = (lax.axis_index("mp") * images + i < counts[0]).astype(F32)
    pad[0:patches, :] = og[0].astype(F32) * live
    dy_o[0] = pad[...].astype(BF)
    pad[0:patches, :] = tok[0].astype(F32)
    gain, shift = row(n1g), row(n1b)
    for c in chunks(rows):
        n, _ = normalized(pad[c, :])
        a1_o[0, c, :] = (n * gain + shift).astype(BF)
    qkv = nn(a1_o[0], wqkv[...])
    bias = row(qkvb)
    q_o[0, rows:] = jnp.zeros((slots - rows, feats), BF)
    for c in chunks(rows):
        q, k, v = (
            qkv[c, j * feats : (j + 1) * feats] + bias[:, j * feats : (j + 1) * feats]
            for j in range(3)
        )
        q_o[0, c, :] = q.astype(BF)
        v_o[0, c, :] = v.astype(BF)
        k = k.astype(BF)
        k_o[0, c, :] = k
        kf = k.astype(F32)
        for g in range(heads):
            at = slice(g * rows + c.start, g * rows + c.stop)
            scaled = kf * mpre[g : g + 1, :]
            hi = scaled.astype(BF)
            kk[at, 0:feats] = hi
            kk[at, feats:] = (scaled - hi.astype(F32)).astype(BF)
    q2 = jnp.concatenate([q_o[0], q_o[0]], axis=1)
    vt = v_o[0].T
    many = heads // 2
    half = many * rows
    tail = patches // 8 * 8
    inside = lax.broadcasted_iota(jnp.int32, (rows - tail, 128), 0) < patches - tail
    logits = [nt(kk[s * half : (s + 1) * half, :], q2) for s in range(2)]
    mixed = []
    for g in range(heads):
        for lane in range(0, slots, 128):
            x = logits[g // many][g % many * rows : (g % many + 1) * rows, lane : lane + 128]
            x = jnp.concatenate([x[0:tail], jnp.where(inside, x[tail:], -1e30)], axis=0)
            e = jnp.exp2(x - jnp.max(x, axis=0, keepdims=True))
            inv = 1.0 / jnp.sum(e, axis=0, keepdims=True)
            p_o[0, g, :, lane : lane + 128] = (e * inv).astype(BF)
        mixed.append(nn(vt, p_o[0, g]))
    real = (lax.broadcasted_iota(jnp.int32, (rows, 128), 0) < patches).astype(BF)
    start = nn(vt, real)
    for c in chunks(feats):
        g = c.start // head_dim
        first = start[c] * postb_s[g]
        for lane in range(0, slots, 128):
            total = first
            for h in range(heads):
                total = total + mixed[h][c, lane : lane + 128] * post_s[g, h]
            attended_t[c, lane : lane + 128] = total.astype(BF)
    o_o[0] = attended_t[...].T[0:rows]
    product = nn(o_o[0], wproj[...])
    bias, scale, gain, shift = row(projb), row(gamma1), row(n2g), row(n2b)
    for c in chunks(rows):
        u = product[c] + bias
        x1 = pad[c, :] + scale * u
        u_o[0, c, :] = u
        x1_o[0, c, :] = x1
        n, _ = normalized(x1)
        a2_o[0, c, :] = (n * gain + shift).astype(BF)


def store_blocks(count, put):
    mine = lax.axis_index("dp")
    for core in range(2):

        @pl.when(jnp.bitwise_and(mine, 1) == core)
        def _(core=core):
            for b in range(count):
                place = jnp.bitwise_xor(jnp.int32(b >> 1), jnp.right_shift(mine, 1))
                put((b ^ core) & 1, place, b)


def mlp_step(act, df, w1, b1, w2, hids, dzs, at, b1_sum):
    z = nn(act, w1[...])
    grad_hidden = nt(df, w2[...])
    width = z.shape[1]
    rows = z.shape[0]
    lanes = 256
    for first in range(0, width, lanes):
        part = slice(first, first + lanes)
        bias = b1[:, part]
        sums = jnp.zeros((8, lanes), F32)
        for c in chunks(rows):
            zc = z[c, part] + bias
            phi, slope = gelu_parts(zc)
            dz = (grad_hidden[c, part] * slope).astype(BF)
            place = pl.ds(pl.multiple_of(at + c.start, 16), 16)
            hids[place, part] = (zc * phi).astype(BF)
            dzs[place, part] = dz
            sums = sums + fold(dz.astype(F32))
        b1_sum[:, part] += colsum(sums)
    here = pl.ds(pl.multiple_of(at, 16), rows)
    return nn(hids[here, :], w2[...]), nt(dzs[here, :], w1[...])


def mlp_first_kernel(
    a2, dy, gamma2, w1_own, b1_own, w2_own, near,
    f_o, da2_o, grads, b1_o, a2t, dft,
    w1, w2, b1, hids, dzs, dfs,
):
    i = pl.program_id(0)
    rows, feats = f_o.shape
    at = i * rows
    here = pl.ds(pl.multiple_of(at, rows), rows)

    @pl.when(i == 0)
    def _():
        b1_o[...] = jnp.zeros_like(b1_o)
        w1[:, 0:feats] = w1_own[...]
        w1[:, feats:] = near[0:feats]
        w2[0:feats, :] = w2_own[...]
        w2[feats:, :] = near[feats : 2 * feats]
        b1[:, 0:feats] = row(b1_own)
        b1[:, feats:] = colsum(near[2 * feats : 2 * feats + 16].astype(F32))

    gain = row(gamma2)
    for c in chunks(rows):
        place = pl.ds(pl.multiple_of(at + c.start, 16), 16)
        dfs[place, :] = (dy[place, :].astype(F32) * gain).astype(BF)
    f, da2 = mlp_step(a2[here, :], dfs[here, :], w1, b1, w2, hids, dzs, at, b1_o)
    f_o[...] = f
    da2_o[...] = da2

    @pl.when(i == pl.num_programs(0) - 1)
    def _():
        a2t[...] = a2[...].T
        dft[...] = dfs[...].T
        grads[0] = nn(a2t[...], dzs[...]).astype(BF).T
        down = nn(dft[...], hids[...]).astype(BF)
        for c in range(2):
            grads[1, c * feats : (c + 1) * feats, :] = down[:, c * feats : (c + 1) * feats]


def mlp_rest_kernel(
    counts, a2, dy, x1, u, o, f0, da20, near, far, grads, a2t, dft, wproj, gamma1, n2g, fc2b, gamma2,
    out_o, dx1_o, do_o, keep, send, b1_o, acc_o,
    w1, w2, b1, hids, dzs, dfs, dus, ups, downs, projs,
):
    i = pl.program_id(0)
    rows, feats = f0.shape
    group, patches = out_o.shape[:2]
    image_rows = rows // group
    at = i * rows
    here = pl.ds(pl.multiple_of(at, rows), rows)
    m_idx = lax.axis_index("mp")

    @pl.when(i == 0)
    def _():
        b1_o[...] = jnp.zeros_like(b1_o)
        acc_o[...] = jnp.zeros_like(acc_o)
        for c in range(2):
            b1[:, c * feats : (c + 1) * feats] = colsum(near[c, feats : feats + 16].astype(F32))

    for core in range(2):

        @pl.when(jnp.logical_and(i == 0, jnp.bitwise_and(lax.axis_index("dp"), 1) == core))
        def _(core=core):
            first, second = (near, far) if core == 0 else (far, near)
            for c in range(2):
                w1[:, c * feats : (c + 1) * feats] = first[c, 0:feats]
                w2[c * feats : (c + 1) * feats, :] = second[c, 0:feats]

    gain2 = row(gamma2)
    for c in chunks(rows):
        place = pl.ds(pl.multiple_of(at + c.start, 16), 16)
        dfs[place, :] = (dy[place, :].astype(F32) * gain2).astype(BF)
    f, da2 = mlp_step(a2[here, :], dfs[here, :], w1, b1, w2, hids, dzs, at, b1_o)
    bias, gain, scale = row(fc2b), row(n2g), row(gamma1)
    sums = [jnp.zeros((8, feats), F32) for _ in range(6)]
    for c in chunks(rows):
        place = pl.ds(pl.multiple_of(at + c.start, 16), 16)
        fc = f[c] + f0[c, :] + bias
        dac = da2[c] + da20[c, :]
        x1c = x1[c, :]
        dyc = dy[place, :].astype(F32)
        n, r = normalized(x1c)
        dx1 = dyc + norm_back(dac, n, r, gain)
        dx1_o[c, :] = dx1
        du = (dx1 * scale).astype(BF)
        dus[place, :] = du
        image = c.start // image_rows
        first = c.start - image * image_rows
        live = (m_idx * (group * pl.num_programs(0)) + i * group + image < counts[0]).astype(F32)
        out = ((x1c + gain2 * fc) * live).astype(BF)
        if first + 16 <= patches:
            out_o[image, first : first + 16, :] = out
        else:
            out_o[image, first:patches, :] = out[0 : patches - first]
        terms = (
            du.astype(F32), u[c, :] * dx1, dac * n, dac, dfs[place, :].astype(F32), fc * dyc,
        )
        sums = [s + fold(t) for s, t in zip(sums, terms)]
    for j in range(6):
        acc_o[j : j + 1, :] += colsum(sums[j])
    do = nt(dus[here, :], wproj[...]).astype(BF)
    for j in range(group):
        do_o[j, 0:image_rows] = do[j * image_rows : (j + 1) * image_rows]
        do_o[j, image_rows:] = jnp.zeros((do_o.shape[1] - image_rows, feats), BF)

    @pl.when(i == pl.num_programs(0) - 1)
    def _():
        count = 2 * keep.shape[0]
        size = feats // count
        outs = (keep, send)

        ups[...] = nn(a2t[...], dzs[...]).astype(BF).T
        downs[...] = nn(dft[...], hids[...]).astype(BF)
        projs[...] = tn(dus[...], o[...]).astype(BF)

        def put(which, place, b):
            out = outs[which]
            for c in range(2):
                part = slice(c * feats, (c + 1) * feats)
                up = slice(c * feats + b * size, c * feats + (b + 1) * size)
                down = slice(b * size, (b + 1) * size)
                pieces = (grads[0, up, :], grads[1, c * feats + b * size : c * feats + (b + 1) * size, :])
                for j, piece in enumerate(pieces):
                    out[place, (2 * c + j) * size : (2 * c + j + 1) * size, :] = piece
                pieces = (ups[up, :], downs[down, part])
                for j, piece in enumerate(pieces):
                    out[place, (4 + 2 * c + j) * size : (5 + 2 * c + j) * size, :] = piece
            out[place, 8 * size : 9 * size, :] = projs[b * size : (b + 1) * size, :]

        store_blocks(count, put)


def attn_bwd_kernel(
    pre_s, do_r, q_r, k_r, v_r, p_r, dx1, tok, mpre, mpost, mixb, wqkv, n1g, *refs
):
    dqkv_o, in_o, acc_o, vgs, dls, dq_t, pad = refs[-7:]
    i = pl.program_id(0)
    slots, feats = do_r.shape[1:]
    patches = tok.shape[1]
    rows = k_r.shape[1]
    heads = mpre.shape[0]
    many = heads // 2
    half = many * rows

    @pl.when(i == 0)
    def _():
        acc_o[...] = jnp.zeros_like(acc_o)

    do_sum = jnp.zeros((8, feats), F32)
    for c in chunks(rows):
        vf = v_r[0, c, :].astype(F32)
        do_sum = do_sum + fold(do_r[0, c, :].astype(F32))
        for h in range(heads):
            vgs[h * rows + c.start : h * rows + c.stop, :] = (vf * mpost[h : h + 1, :]).astype(BF)
    do_sum = colsum(do_sum)
    q = q_r[0]
    do = do_r[0]
    kt = k_r[0].T
    dps = [nt(vgs[s * half : (s + 1) * half, :], do) for s in range(2)]
    dvs = [nn(p_r[0, s * many : (s + 1) * many].reshape(half, slots), do) for s in range(2)]
    dks, dqs = [], []
    for h in range(heads):
        for lane in range(0, slots, 128):
            dp = dps[h // many][h % many * rows : (h % many + 1) * rows, lane : lane + 128]
            pf = p_r[0, h, :, lane : lane + 128].astype(F32)
            mean = jnp.sum(dp * pf, axis=0, keepdims=True) / jnp.sum(pf, axis=0, keepdims=True)
            dls[h * rows : (h + 1) * rows, lane : lane + 128] = (pf * (dp - mean)).astype(BF)
        dqs.append(nn(kt, dls[h * rows : (h + 1) * rows, :]))
        if h % many == many - 1:
            s = h // many
            dks.append(nn(dls[s * half : (s + 1) * half, :], q))

    bias_row = mixb[...] * do_sum
    v_sum = jnp.zeros((8, feats), F32)
    dv_sum = jnp.zeros((8, feats), F32)
    sums = [jnp.zeros((8, feats), F32) for _ in range(heads)]
    for c in chunks(rows):
        vf = v_r[0, c, :].astype(F32)
        dv = bias_row
        for h in range(heads):
            at = (h % many) * rows
            this = dvs[h // many][at + c.start : at + c.stop]
            dv = dv + this * mpost[h : h + 1, :]
            sums[h] = sums[h] + fold(vf * this)
        if c.stop > patches:
            inside = lax.broadcasted_iota(jnp.int32, dv.shape, 0) < patches - c.start
            dv = jnp.where(inside, dv, 0.0)
            vf = jnp.where(inside, vf, 0.0)
        low = dv.astype(BF)
        dqkv_o[0, c, 2 * feats :] = low
        dv_sum = dv_sum + fold(low.astype(F32))
        v_sum = v_sum + fold(vf)
    for h in range(heads):
        acc_o[h : h + 1, :] += colsum(sums[h])
    acc_o[2 * heads : 2 * heads + 1, :] += do_sum * colsum(v_sum)
    acc_o[2 * heads + 10 : 2 * heads + 11, :] += colsum(dv_sum)

    head_dim = feats // heads
    for c in chunks(feats):
        g = c.start // head_dim
        for lane in range(0, slots, 128):
            total = 0.0
            for h in range(heads):
                total = total + dqs[h][c, lane : lane + 128] * pre_s[h, g]
            dq_t[c, lane : lane + 128] = (total * head_dim**-0.5).astype(BF)
    dq = dq_t[...].T[0:rows]
    dqkv_o[0, :, 0:feats] = dq
    dk_sum = jnp.zeros((8, feats), F32)
    sums = [jnp.zeros((8, feats), F32) for _ in range(heads)]
    for c in chunks(rows):
        kf = k_r[0, c, :].astype(F32)
        dk = 0.0
        for h in range(heads):
            at = (h % many) * rows
            this = dks[h // many][at + c.start : at + c.stop]
            dk = dk + this * mpre[h : h + 1, :]
            sums[h] = sums[h] + fold(kf * this)
        low = (dk * (1.0 / LOG2E)).astype(BF)
        dqkv_o[0, c, feats : 2 * feats] = low
        dk_sum = dk_sum + fold(low.astype(F32))
    for h in range(heads):
        acc_o[heads + h : heads + h + 1, :] += colsum(sums[h])
    acc_o[2 * heads + 8 : 2 * heads + 9, :] += colsum(dq.astype(F32))
    acc_o[2 * heads + 9 : 2 * heads + 10, :] += colsum(dk_sum)

    pad[patches:, :] = jnp.zeros((rows - patches, feats), F32)
    pad[0:patches, :] = tok[0].astype(F32)
    da1 = nt(dqkv_o[0], wqkv[...])
    gain = row(n1g)
    sums = [jnp.zeros((8, feats), F32) for _ in range(2)]
    for c in chunks(rows):
        n, r = normalized(pad[c, :])
        cot = da1[c]
        grad = dx1[0, c, :] + norm_back(cot, n, r, gain)
        sums = [sums[0] + fold(cot * n), sums[1] + fold(cot)]
        if c.stop <= patches:
            in_o[0, c, :] = grad
        else:
            in_o[0, c.start : patches, :] = grad[0 : patches - c.start]
    for j in range(2):
        acc_o[2 * heads + 11 + j : 2 * heads + 12 + j, :] += colsum(sums[j])


def qkv_grad_kernel(heads, dqkv, *refs):
    accs = refs[:-8]
    a1, acc_mlp, b1_first, b1_rest, keep, send, small, grads = refs[-8:]
    feats = a1.shape[1]
    count = 2 * keep.shape[0]
    size = 3 * feats // count
    acc = accs[0][...]
    for other in accs[1:]:
        acc = acc + other[...]
    small[...] = jnp.zeros_like(small)
    small[0:2, :] = acc[2 * heads + 11 : 2 * heads + 13]
    small[2:8, :] = acc_mlp[0:6, :]
    small[8:11, :] = acc[2 * heads + 8 : 2 * heads + 11]
    head_dim = feats // heads
    lanes = 2 * heads * heads
    gather = (
        head_of_lane((feats, lanes), 0, head_dim)
        == lax.broadcasted_iota(jnp.int32, (feats, lanes), 1) % heads
    ).astype(F32)
    sums = exact(acc[0 : 2 * heads + 8], gather, ((1,), (0,)))
    place = head_of_lane((2 * heads, lanes), 1, heads) == lax.broadcasted_iota(
        jnp.int32, (2 * heads, lanes), 0
    )
    small[11:12, 0:lanes] = colsum(jnp.where(place, sums[0 : 2 * heads], 0.0))
    small[11:12, lanes : 2 * lanes] = sums[2 * heads : 2 * heads + 1]
    m_idx = lax.axis_index("mp")
    for c, ref in enumerate((b1_first, b1_first, b1_rest, b1_rest)):
        place = 12 + jnp.bitwise_xor(m_idx, c)
        small[pl.ds(place, 1), :] = ref[:, (c % 2) * feats : (c % 2 + 1) * feats]
    low = small[...].astype(BF)
    outs = (keep, send)

    grads[...] = tn(a1[...], dqkv[...]).astype(BF).T

    def put(which, place, b):
        outs[which][place, 0:size, :] = grads[b * size : (b + 1) * size, :]
        outs[which][place, size:, :] = low

    store_blocks(count, put)


def final_kernel(heads, size, *refs):
    mine, got = refs[0], refs[1:-14]
    qkv_o, qkvb_o, pre_o, post_o, postb_o, b1_o, *vecs_o = refs[-14:]
    total = mine[...]
    for part in got:
        total = total + part[...].astype(F32)
    feats = total.shape[1]
    qkv_o[...] = total[0:size]
    small = total[size:]
    d_idx = lax.axis_index("dp")
    m_idx = lax.axis_index("mp")

    def own(value, width, index):
        lanes = value.shape[1]
        return pltpu.roll(value, lax.rem(lanes - index * width, lanes), axis=1)[:, 0:width]

    width = vecs_o[0].shape[1]
    vecs = own(small[0:8], width, d_idx)
    for j, ref in enumerate(vecs_o):
        ref[...] = vecs[j : j + 1]
    flat = jnp.concatenate([small[8 + j : 9 + j] for j in range(3)], axis=1)
    qkvb_o[...] = own(jnp.broadcast_to(flat, (8, 3 * feats)), qkvb_o.shape[1], d_idx)[0:1]
    b1 = own(small[8:16], b1_o.shape[1], d_idx)[4:8]
    pick = lax.broadcasted_iota(jnp.int32, b1.shape, 0) == m_idx
    b1_o[...] = colsum(jnp.where(pick, b1, 0.0))
    mix = small[11:12]
    hh = heads * heads
    line = lax.broadcasted_iota(jnp.int32, (heads, hh), 0)
    lane = lax.broadcasted_iota(jnp.int32, (heads, hh), 1)
    fold = (
        lax.broadcasted_iota(jnp.int32, (hh, heads), 0) % heads
        == lax.broadcasted_iota(jnp.int32, (hh, heads), 1)
    ).astype(F32)
    head_dim = feats // heads

    def square(values):
        return exact(jnp.where(lane // heads == line, values, 0.0), fold, ((1,), (0,)))

    post_o[...] = square(mix[:, 0:hh]).T
    pre_o[...] = square(mix[:, hh : 2 * hh]) * (head_dim**-0.5)
    postb_o[...] = mix[:, 2 * hh : 2 * hh + heads]


def whole(shape):
    return pl.BlockSpec(shape, lambda i: (0,) * len(shape))


def each(shape, first=0, many=1):
    return pl.BlockSpec((many,) + shape[1:], lambda i: (i + first,) + (0,) * (len(shape) - 1))


SCALARS = pl.BlockSpec(memory_space=pltpu.SMEM)


def sds(shape, dtype):
    return jax.ShapeDtypeStruct(shape, dtype)


def call(
    kernel, grid, ins, in_specs, outs, out_specs, scratch=(), flops=0, name=None, aliases=None
):
    size = lambda a: a.size * a.dtype.itemsize
    return pl.pallas_call(
        kernel,
        grid=grid,
        in_specs=in_specs,
        out_specs=out_specs,
        out_shape=outs,
        scratch_shapes=scratch,
        input_output_aliases=aliases or {},
        compiler_params=pltpu.CompilerParams(vmem_limit_bytes=VMEM_LIMIT),
        cost_estimate=pl.CostEstimate(
            flops=flops,
            bytes_accessed=sum(size(a) for a in ins) + sum(size(a) for a in outs),
            transcendentals=0,
        ),
        name=name,
    )(*ins)


def xor_perm(count, mask):
    return [(j, j ^ mask) for j in range(count)]


def dp_hops(dp):
    bits = dp.bit_length() - 1
    groups = []
    at = 1
    while at < bits:
        groups.append((at, min(2, bits - at)))
        at += groups[-1][1]
    return groups


def dp_scatter(value, dp):
    for at, many in dp_hops(dp):
        value = value.reshape((-1, 1 << many) + value.shape[1:])
        got = [
            lax.ppermute(value[:, j].astype(BF), "dp", xor_perm(dp, j << at))
            for j in range(1, 1 << many)
        ]
        value = value[:, 0] + sum(g.astype(F32) for g in got)
    return value.reshape(value.shape[-2:])


def per_device(
    dp, mp,
    tokens_in, image_counts, norm1_gain, norm1_bias, qkv_weight, qkv_bias,
    mix_pre, mix_post, mix_post_bias, proj_weight, proj_bias, gamma1,
    norm2_gain, norm2_bias, fc1_weight, fc1_bias, fc2_weight, fc2_bias, gamma2, out_grad,
):
    images, patches, feats = tokens_in.shape
    heads = mix_pre.shape[0]
    rows = -(-patches // 16) * 16
    slots = -(-patches // 128) * 128
    hidden = fc1_weight.shape[1]
    ins = [fc1_weight, fc2_weight, fc1_bias]
    outs = [sds((2 * feats + 16, hidden), BF), sds((feats + 16, hidden), BF)]
    one, other = call(
        pack_kernel,
        (1,),
        ins,
        [whole(a.shape) for a in ins],
        outs,
        [whole(a.shape) for a in outs],
        name="pack",
    )
    near_one = lax.ppermute(one, "mp", xor_perm(mp, 1))
    near = [lax.ppermute(other, "mp", xor_perm(mp, j)) for j in range(2, mp)]

    tok_rows = (images, rows, feats)
    slot_rows = (images, slots, feats)
    prob_shape = (images, heads, rows, slots)
    mix_shape = (heads, feats)
    ins = [
        image_counts, mix_post, mix_post_bias, tokens_in, out_grad, norm1_gain, norm1_bias, qkv_bias, mix_pre, mix_post,
        mix_post_bias, proj_bias, gamma1, norm2_gain, norm2_bias, qkv_weight, proj_weight,
    ]
    a1, q, k, v, prob, o, x1, u, a2, dy, mpre, mpost, mixb = call(
        attn_fwd_kernel,
        (images,),
        ins,
        [SCALARS] * 3
        + [each(tokens_in.shape), each(out_grad.shape)]
        + [whole(a.shape) for a in ins[5:]],
        [
            sds(tok_rows, BF), sds(slot_rows, BF), sds(tok_rows, BF), sds(tok_rows, BF),
            sds(prob_shape, BF), sds(tok_rows, BF), sds(tok_rows, F32), sds(tok_rows, F32),
            sds(tok_rows, BF), sds(tok_rows, BF), sds(mix_shape, F32), sds(mix_shape, F32),
            sds((1, feats), F32),
        ],
        [each(s) for s in (tok_rows, slot_rows, tok_rows, tok_rows, prob_shape)]
        + [each(tok_rows)] * 5
        + [whole(mix_shape)] * 2
        + [whole((1, feats))],
        [
            pltpu.VMEM((rows, feats), F32), pltpu.VMEM((heads * rows, 2 * feats), BF),
            pltpu.VMEM((feats, slots), BF),
        ],
        flops=images * 15 * 10**8,
        name="attn_fwd",
    )

    block = feats // dp
    total = images * rows
    group = 2 if images % 2 == 0 else 1
    flat = (total, feats)
    step = (group * rows, feats)
    a2, dy, x1, u, o = (a.reshape(flat) for a in (a2, dy, x1, u, o))
    near_one, near, a2 = lax.optimization_barrier((near_one, near, a2))
    near = jnp.stack(near)
    far = lax.ppermute(near, "dp", xor_perm(dp, 1))
    ins = [a2, dy, gamma2, fc1_weight, fc1_bias, fc2_weight, near_one]
    blocked = pl.BlockSpec(step, lambda i: (i, 0))
    wide = 2 * hidden
    grad_shape = (2, wide, feats)
    f0, da20, grads0, b1_0, a2t, dft = call(
        mlp_first_kernel,
        (images // group,),
        ins,
        [whole(a.shape) for a in ins],
        [
            sds(flat, F32), sds(flat, F32), sds(grad_shape, BF), sds((1, wide), F32),
            sds((feats, total), BF), sds((feats, total), BF),
        ],
        [blocked, blocked, whole(grad_shape), whole((1, wide))] + [whole((feats, total))] * 2,
        [
            pltpu.VMEM((feats, wide), BF), pltpu.VMEM((wide, feats), BF),
            pltpu.VMEM((1, wide), F32), pltpu.VMEM((total, wide), BF),
            pltpu.VMEM((total, wide), BF), pltpu.VMEM(flat, BF),
        ],
        flops=images * 8 * 10**8,
        name="mlp_first",
    )

    grad_rows = 9 * block
    half_shape = (dp // 2, grad_rows, feats)
    ins = [
        image_counts, a2, dy, x1, u, o, f0, da20, near, far, grads0, a2t, dft, proj_weight, gamma1,
        norm2_gain, fc2_bias, gamma2,
    ]
    layer_out, dx1, do, keep, send, b1_1, acc_mlp = call(
        mlp_rest_kernel,
        (images // group,),
        ins,
        [SCALARS, whole(flat), whole(flat), blocked, blocked, whole(flat), blocked, blocked]
        + [whole(a.shape) for a in ins[8:]],
        [
            sds(tokens_in.shape, BF), sds(flat, F32), sds(slot_rows, BF), sds(half_shape, BF),
            sds(half_shape, BF), sds((1, wide), F32), sds((8, feats), F32),
        ],
        [
            each(tokens_in.shape, 0, group), blocked, each(slot_rows, 0, group), whole(half_shape),
            whole(half_shape), whole((1, wide)), whole((8, feats)),
        ],
        [
            pltpu.VMEM((feats, wide), BF), pltpu.VMEM((wide, feats), BF),
            pltpu.VMEM((1, wide), F32), pltpu.VMEM((total, wide), BF),
            pltpu.VMEM((total, wide), BF), pltpu.VMEM(flat, BF), pltpu.VMEM(flat, BF),
            pltpu.VMEM((wide, feats), BF), pltpu.VMEM((feats, wide), BF),
            pltpu.VMEM((feats, feats), BF),
        ],
        flops=images * 9 * 10**8,
        name="mlp_rest",
    )
    got = lax.ppermute(send, "dp", xor_perm(dp, 1))
    dx1 = dx1.reshape(tok_rows)

    shares = [1, 3, 2] if images == 6 else [images]
    steps = len(shares)
    dqkv_shape = (images, rows, 3 * feats)
    carried, accs = [], []
    for s, share in enumerate(shares):
        first = sum(shares[:s])
        ins = [mix_pre, do, q, k, v, prob, dx1, tokens_in, mpre, mpost, mixb, qkv_weight, norm1_gain]
        *carried, acc = call(
            attn_bwd_kernel,
            (share,),
            ins + carried,
            [SCALARS]
            + [each(a.shape, first) for a in ins[1:8]]
            + [whole(a.shape) for a in ins[8:]]
            + [pl.BlockSpec(memory_space=pl.ANY)] * len(carried),
            [sds(dqkv_shape, BF), sds(tokens_in.shape, F32), sds((2 * heads + 16, feats), F32)],
            [
                each(dqkv_shape, first), each(tokens_in.shape, first),
                whole((2 * heads + 16, feats)),
            ],
            [
                pltpu.VMEM((heads * rows, feats), BF), pltpu.VMEM((heads * rows, slots), BF),
                pltpu.VMEM((feats, slots), BF), pltpu.VMEM((rows, feats), F32),
            ],
            flops=share * 20 * 10**8,
            name="attn_bwd",
            aliases={len(ins): 0, len(ins) + 1: 1} if carried else None,
        )
        accs.append(acc)
        if s == 0:
            (keep, got), acc = lax.optimization_barrier(((keep, got), acc))
            mine = dp_scatter(keep.astype(F32) + got.astype(F32), dp)
            accs[0], do = lax.optimization_barrier((acc, do))
        if s == min(1, steps - 1):
            mine, acc = lax.optimization_barrier((mine, acc))
            low = mine.astype(BF)
            proj = low[8 * block :]
            got_z = [
                lax.ppermute(
                    jnp.concatenate([low[2 * j * block : 2 * (j + 1) * block], proj]),
                    "mp",
                    xor_perm(mp, j),
                )
                for j in range(1, mp)
            ]
            accs[s], do = lax.optimization_barrier((acc, do))
    dqkv, in_grad = carried
    got_z, dqkv = lax.optimization_barrier((got_z, dqkv))
    sums = jnp.concatenate([mine[: 2 * block], mine[8 * block :]]) + sum(
        g.astype(F32) for g in got_z
    )
    fc1g, fc2g, projg = (sums[j * block : (j + 1) * block] for j in range(3))

    q_block = 3 * feats // dp
    half_shape = (dp // 2, q_block + 16, feats)
    ins = [dqkv.reshape(total, 3 * feats)] + accs + [a1.reshape(flat), acc_mlp, b1_0, b1_1]
    keep, send = call(
        functools.partial(qkv_grad_kernel, heads),
        (1,),
        ins,
        [whole(a.shape) for a in ins],
        [sds(half_shape, BF), sds(half_shape, BF)],
        [whole(half_shape), whole(half_shape)],
        [pltpu.VMEM((16, feats), F32), pltpu.VMEM((3 * feats, feats), BF)],
        flops=11 * 10**8,
        name="qkv_grad",
    )
    got = lax.ppermute(send, "dp", xor_perm(dp, 1))
    mine = dp_scatter(keep.astype(F32) + got.astype(F32), dp)
    low = mine.astype(BF)
    got = [lax.ppermute(low, "mp", xor_perm(mp, j)) for j in range(1, mp)]
    b1_size = hidden // dp
    ins = [mine] + got
    outs = [
        sds((q_block, feats), F32), sds((1, q_block), F32), sds((heads, heads), F32),
        sds((heads, heads), F32), sds((1, heads), F32), sds((1, b1_size), F32),
    ] + [sds((1, block), F32)] * 8
    qkvw, qkvb, pre, post, postb, b1g, *vecs = call(
        functools.partial(final_kernel, heads, q_block),
        (1,),
        ins,
        [whole(a.shape) for a in ins],
        outs,
        [whole(a.shape) for a in outs],
        name="final",
    )
    vecs = [a.reshape(-1) for a in vecs]
    return (
        layer_out,
        in_grad,
        vecs[0],
        vecs[1],
        qkvw.T,
        qkvb.reshape(-1),
        pre,
        post,
        postb.reshape(-1),
        projg.T,
        vecs[2],
        vecs[3],
        vecs[4],
        vecs[5],
        fc1g.T,
        b1g.reshape(-1),
        fc2g.T,
        vecs[6],
        vecs[7],
    )


def solution(mesh):
    tokens = P(("dp", "mp"), None, None)
    placed = (
        (tokens, P("dp")) + (P(),) * 12 + (P(None, "mp"), P("mp"), P("mp", None), P(), P(), tokens)
    )
    return jax.shard_map(
        functools.partial(per_device, mesh.shape["dp"], mesh.shape["mp"]),
        mesh=mesh,
        in_specs=placed,
        out_specs=(
            tokens, tokens, P("dp"), P("dp"), P(None, "dp"), P("dp"), P(), P(), P(),
            P(None, "dp"), P("dp"), P("dp"), P("dp"), P("dp"), P(None, ("mp", "dp")),
            P(("mp", "dp")), P("mp", "dp"), P("dp"), P("dp"),
        ),
        check_vma=False,
    )
```

```python
import functools

import jax
import jax.numpy as jnp
from jax import lax
from jax.experimental import pallas as pl
from jax.experimental.pallas import tpu as pltpu
from jax.sharding import PartitionSpec as P

BF = jnp.bfloat16
F32 = jnp.float32
LOG2E = 1.4426950408889634
EPS = 1e-06
VMEM_LIMIT = 20 * 1024 * 1024


def nn(a, b):
    return lax.dot_general(a, b, (((1,), (0,)), ((), ())), preferred_element_type=F32)


def nt(a, b):
    return lax.dot_general(a, b, (((1,), (1,)), ((), ())), preferred_element_type=F32)


def tn(a, b):
    return lax.dot_general(a, b, (((0,), (0,)), ((), ())), preferred_element_type=F32)


def exact(a, b, dims):
    return lax.dot_general(
        a, b, (dims, ((), ())), precision=lax.Precision.HIGHEST, preferred_element_type=F32
    )


def normalized(x):
    mean = jnp.mean(x, axis=-1, keepdims=True)
    c = x - mean
    r = lax.rsqrt(jnp.mean(c * c, axis=-1, keepdims=True) + EPS)
    return c * r, r


def norm_back(cot, n, r, gain):
    cg = cot * gain
    return r * (
        cg
        - jnp.mean(cg, axis=-1, keepdims=True)
        - n * jnp.mean(cg * n, axis=-1, keepdims=True)
    )


def colsum(x):
    return jnp.sum(x, axis=0, keepdims=True)


def split(x):
    hi = x.astype(BF)
    return jnp.concatenate([hi, (x - hi.astype(F32)).astype(BF)], axis=1)


def row(ref):
    return ref[...].reshape(1, ref.shape[0])


def gelu_parts(z):
    e = jnp.exp2(z * z * (-0.5 * LOG2E))
    t = 1.0 / (1.0 + jnp.abs(z) * (0.3275911 * 0.7071067811865476))
    poly = t * (
        0.5 * 0.254829592
        + t
        * (
            0.5 * -0.284496736
            + t * (0.5 * 1.421413741 + t * (0.5 * -1.453152027 + t * (0.5 * 1.061405429)))
        )
    )
    tail = poly * e
    phi = jnp.where(z >= 0, 1.0 - tail, tail)
    return phi, phi + z * e * 0.3989422804014327


def head_of_lane(shape, axis, head_dim):
    return lax.broadcasted_iota(jnp.int32, shape, axis) // head_dim


def chunks(count, size=16):
    return [slice(at, at + size) for at in range(0, count, size)]


def fold(x):
    return sum(x[at : at + 8] for at in range(8, x.shape[0], 8)) + x[0:8]


def pack_kernel(w1, w2, b1, one, other, b1_v, sems):
    feats = w1.shape[0]
    core = jnp.bitwise_and(lax.axis_index("dp"), 1)
    copies = [
        pltpu.make_async_copy(b1, b1_v, sems.at[0]),
        pltpu.make_async_copy(w1, one.at[0:feats], sems.at[1]),
        pltpu.make_async_copy(w2, one.at[feats : 2 * feats], sems.at[2]),
    ]
    own = [pltpu.make_async_copy(w, other.at[0:feats], sems.at[3]) for w in (w1, w2)]
    for copy in copies:
        copy.start()
    for j in range(2):
        pl.when(core == j)(own[j].start)
    copies[0].wait()
    rest = row(b1_v)
    place = lax.broadcasted_iota(jnp.int32, (16, feats), 0)
    bias = jnp.zeros((16, feats), F32)
    for j in range(3):
        term = rest.astype(BF).astype(F32)
        bias = jnp.where(place == j, term, bias)
        rest = rest - term
    bias = bias.astype(BF)
    one[2 * feats :, :] = bias
    other[feats:, :] = bias
    for copy in copies[1:]:
        copy.wait()
    for j in range(2):
        pl.when(core == j)(own[j].wait)


def attn_fwd_kernel(
    counts, post_s, postb_s, *refs
):
    sources, refs = refs[:14], refs[14:]
    a1_o, q_o, k_o, v_o, p_o, o_o, x1_o, u_o, a2_o, dy_o, mpre, mpost, mixb = refs[:13]
    held, (pad, kk, attended_t, sems) = refs[13:27], refs[27:]
    tok, og, n1g, n1b, qkvb, pre, post, postb, projb, gamma1, n2g, n2b, wqkv, wproj = held
    i = pl.program_id(0)
    images, patches, feats = tok.shape

    def image_copy(which, at):
        return pltpu.make_async_copy(
            sources[which].at[at], held[which].at[at], sems.at[which * images + at]
        )

    @pl.when(i == 0)
    def _():
        shared = [
            pltpu.make_async_copy(sources[j], held[j], sems.at[2 * images + j])
            for j in range(2, 14)
        ]
        image_copy(0, 0).start()
        image_copy(1, 0).start()
        for copy in shared:
            copy.start()
        for at in range(1, images):
            image_copy(0, at).start()
            image_copy(1, at).start()
        for copy in shared:
            copy.wait()

    image_copy(0, i).wait()
    image_copy(1, i).wait()
    rows = pad.shape[0]
    heads = mpre.shape[0]
    head_dim = feats // heads
    slots = q_o.shape[1]

    @pl.when(i == 0)
    def _():
        spread = (
            head_of_lane((heads, feats), 1, head_dim)
            == lax.broadcasted_iota(jnp.int32, (heads, feats), 0)
        ).astype(F32)
        mpre[...] = exact(pre[...], spread, ((1,), (0,))) * (head_dim**-0.5 * LOG2E)
        mpost[...] = exact(post[...], spread, ((0,), (0,)))
        mixb[...] = exact(row(postb), spread, ((1,), (0,)))

    pad[patches:, :] = jnp.zeros((rows - patches, feats), F32)
    live = (lax.axis_index("mp") * images + i < counts[0]).astype(F32)
    pad[0:patches, :] = og[i].astype(F32) * live
    dy_o[0] = pad[...].astype(BF)
    pad[0:patches, :] = tok[i].astype(F32)
    gain, shift = row(n1g), row(n1b)
    for c in chunks(rows):
        n, _ = normalized(pad[c, :])
        a1_o[0, c, :] = (n * gain + shift).astype(BF)
    qkv = nn(a1_o[0], wqkv[...])
    bias = row(qkvb)
    q_o[0, rows:] = jnp.zeros((slots - rows, feats), BF)
    for c in chunks(rows):
        q, k, v = (
            qkv[c, j * feats : (j + 1) * feats] + bias[:, j * feats : (j + 1) * feats]
            for j in range(3)
        )
        q_o[0, c, :] = q.astype(BF)
        v_o[0, c, :] = v.astype(BF)
        k = k.astype(BF)
        k_o[0, c, :] = k
        kf = k.astype(F32)
        for g in range(heads):
            at = slice(g * rows + c.start, g * rows + c.stop)
            scaled = kf * mpre[g : g + 1, :]
            hi = scaled.astype(BF)
            kk[at, 0:feats] = hi
            kk[at, feats:] = (scaled - hi.astype(F32)).astype(BF)
    q2 = jnp.concatenate([q_o[0], q_o[0]], axis=1)
    vt = v_o[0].T
    many = heads // 2
    half = many * rows
    tail = patches // 8 * 8
    inside = lax.broadcasted_iota(jnp.int32, (rows - tail, 128), 0) < patches - tail
    logits = [nt(kk[s * half : (s + 1) * half, :], q2) for s in range(2)]
    mixed = []
    for g in range(heads):
        for lane in range(0, slots, 128):
            x = logits[g // many][g % many * rows : (g % many + 1) * rows, lane : lane + 128]
            x = jnp.concatenate([x[0:tail], jnp.where(inside, x[tail:], -1e30)], axis=0)
            e = jnp.exp2(x - jnp.max(x, axis=0, keepdims=True))
            inv = 1.0 / jnp.sum(e, axis=0, keepdims=True)
            p_o[0, g, :, lane : lane + 128] = (e * inv).astype(BF)
        mixed.append(nn(vt, p_o[0, g]))
    real = (lax.broadcasted_iota(jnp.int32, (rows, 128), 0) < patches).astype(BF)
    start = nn(vt, real)
    for c in chunks(feats):
        g = c.start // head_dim
        first = start[c] * postb_s[g]
        for lane in range(0, slots, 128):
            total = first
            for h in range(heads):
                total = total + mixed[h][c, lane : lane + 128] * post_s[g, h]
            attended_t[c, lane : lane + 128] = total.astype(BF)
    o_o[0] = attended_t[...].T[0:rows]
    product = nn(o_o[0], wproj[...])
    bias, scale, gain, shift = row(projb), row(gamma1), row(n2g), row(n2b)
    for c in chunks(rows):
        u = product[c] + bias
        x1 = pad[c, :] + scale * u
        u_o[0, c, :] = u
        x1_o[0, c, :] = x1
        n, _ = normalized(x1)
        a2_o[0, c, :] = (n * gain + shift).astype(BF)


def store_blocks(count, put):
    mine = lax.axis_index("dp")
    for core in range(2):

        @pl.when(jnp.bitwise_and(mine, 1) == core)
        def _(core=core):
            for b in range(count):
                place = jnp.bitwise_xor(jnp.int32(b >> 1), jnp.right_shift(mine, 1))
                put((b ^ core) & 1, place, b)


def mlp_step(act, df, w1, b1, w2, hids, dzs, at, b1_sum):
    z = nn(act, w1[...])
    grad_hidden = nt(df, w2[...])
    width = z.shape[1]
    rows = z.shape[0]
    lanes = 256
    for first in range(0, width, lanes):
        part = slice(first, first + lanes)
        bias = b1[:, part]
        sums = jnp.zeros((8, lanes), F32)
        for c in chunks(rows):
            zc = z[c, part] + bias
            phi, slope = gelu_parts(zc)
            dz = (grad_hidden[c, part] * slope).astype(BF)
            place = pl.ds(pl.multiple_of(at + c.start, 16), 16)
            hids[place, part] = (zc * phi).astype(BF)
            dzs[place, part] = dz
            sums = sums + fold(dz.astype(F32))
        b1_sum[:, part] += colsum(sums)
    here = pl.ds(pl.multiple_of(at, 16), rows)
    return nn(hids[here, :], w2[...]), nt(dzs[here, :], w1[...])


def mlp_first_kernel(
    a2, dy, gamma2, w1_own, b1_own, w2_own, near,
    f_o, da2_o, grads, b1_o, a2t, dft,
    w1, w2, b1, hids, dzs, dfs,
):
    i = pl.program_id(0)
    rows, feats = f_o.shape
    at = i * rows
    here = pl.ds(pl.multiple_of(at, rows), rows)

    @pl.when(i == 0)
    def _():
        b1_o[...] = jnp.zeros_like(b1_o)
        w1[:, 0:feats] = w1_own[...]
        w1[:, feats:] = near[0:feats]
        w2[0:feats, :] = w2_own[...]
        w2[feats:, :] = near[feats : 2 * feats]
        b1[:, 0:feats] = row(b1_own)
        b1[:, feats:] = colsum(near[2 * feats : 2 * feats + 16].astype(F32))

    gain = row(gamma2)
    for c in chunks(rows):
        place = pl.ds(pl.multiple_of(at + c.start, 16), 16)
        dfs[place, :] = (dy[place, :].astype(F32) * gain).astype(BF)
    f, da2 = mlp_step(a2[here, :], dfs[here, :], w1, b1, w2, hids, dzs, at, b1_o)
    f_o[...] = f
    da2_o[...] = da2

    @pl.when(i == pl.num_programs(0) - 1)
    def _():
        a2t[...] = a2[...].T
        dft[...] = dfs[...].T
        grads[0] = nn(a2t[...], dzs[...]).astype(BF).T
        down = nn(dft[...], hids[...]).astype(BF)
        for c in range(2):
            grads[1, c * feats : (c + 1) * feats, :] = down[:, c * feats : (c + 1) * feats]


def mlp_rest_kernel(
    counts, a2, dy, x1, u, o, f0, da20, near, far, grads, a2t, dft, wproj, gamma1, n2g, fc2b, gamma2,
    out_o, dx1_o, do_o, keep, send, b1_o, acc_o,
    w1, w2, b1, hids, dzs, dfs, dus, ups, downs, projs,
):
    i = pl.program_id(0)
    rows, feats = f0.shape
    group, patches = out_o.shape[:2]
    image_rows = rows // group
    at = i * rows
    here = pl.ds(pl.multiple_of(at, rows), rows)
    m_idx = lax.axis_index("mp")

    @pl.when(i == 0)
    def _():
        b1_o[...] = jnp.zeros_like(b1_o)
        acc_o[...] = jnp.zeros_like(acc_o)
        for c in range(2):
            b1[:, c * feats : (c + 1) * feats] = colsum(near[c, feats : feats + 16].astype(F32))

    for core in range(2):

        @pl.when(jnp.logical_and(i == 0, jnp.bitwise_and(lax.axis_index("dp"), 1) == core))
        def _(core=core):
            first, second = (near, far) if core == 0 else (far, near)
            for c in range(2):
                w1[:, c * feats : (c + 1) * feats] = first[c, 0:feats]
                w2[c * feats : (c + 1) * feats, :] = second[c, 0:feats]

    gain2 = row(gamma2)
    for c in chunks(rows):
        place = pl.ds(pl.multiple_of(at + c.start, 16), 16)
        dfs[place, :] = (dy[place, :].astype(F32) * gain2).astype(BF)
    f, da2 = mlp_step(a2[here, :], dfs[here, :], w1, b1, w2, hids, dzs, at, b1_o)
    bias, gain, scale = row(fc2b), row(n2g), row(gamma1)
    sums = [jnp.zeros((8, feats), F32) for _ in range(6)]
    for c in chunks(rows):
        place = pl.ds(pl.multiple_of(at + c.start, 16), 16)
        fc = f[c] + f0[c, :] + bias
        dac = da2[c] + da20[c, :]
        x1c = x1[c, :]
        dyc = dy[place, :].astype(F32)
        n, r = normalized(x1c)
        dx1 = dyc + norm_back(dac, n, r, gain)
        dx1_o[c, :] = dx1
        du = (dx1 * scale).astype(BF)
        dus[place, :] = du
        image = c.start // image_rows
        first = c.start - image * image_rows
        live = (m_idx * (group * pl.num_programs(0)) + i * group + image < counts[0]).astype(F32)
        out = ((x1c + gain2 * fc) * live).astype(BF)
        if first + 16 <= patches:
            out_o[image, first : first + 16, :] = out
        else:
            out_o[image, first:patches, :] = out[0 : patches - first]
        terms = (
            du.astype(F32), u[c, :] * dx1, dac * n, dac, dfs[place, :].astype(F32), fc * dyc,
        )
        sums = [s + fold(t) for s, t in zip(sums, terms)]
    for j in range(6):
        acc_o[j : j + 1, :] += colsum(sums[j])
    do = nt(dus[here, :], wproj[...]).astype(BF)
    for j in range(group):
        do_o[j, 0:image_rows] = do[j * image_rows : (j + 1) * image_rows]
        do_o[j, image_rows:] = jnp.zeros((do_o.shape[1] - image_rows, feats), BF)

    @pl.when(i == pl.num_programs(0) - 1)
    def _():
        count = 2 * keep.shape[0]
        size = feats // count
        outs = (keep, send)

        ups[...] = nn(a2t[...], dzs[...]).astype(BF).T
        downs[...] = nn(dft[...], hids[...]).astype(BF)
        projs[...] = tn(dus[...], o[...]).astype(BF)

        def put(which, place, b):
            out = outs[which]
            for c in range(2):
                part = slice(c * feats, (c + 1) * feats)
                up = slice(c * feats + b * size, c * feats + (b + 1) * size)
                down = slice(b * size, (b + 1) * size)
                pieces = (grads[0, up, :], grads[1, c * feats + b * size : c * feats + (b + 1) * size, :])
                for j, piece in enumerate(pieces):
                    out[place, (2 * c + j) * size : (2 * c + j + 1) * size, :] = piece
                pieces = (ups[up, :], downs[down, part])
                for j, piece in enumerate(pieces):
                    out[place, (4 + 2 * c + j) * size : (5 + 2 * c + j) * size, :] = piece
            out[place, 8 * size : 9 * size, :] = projs[b * size : (b + 1) * size, :]

        store_blocks(count, put)


def attn_bwd_kernel(
    pre_s, do_r, q_r, k_r, v_r, p_r, dx1, tok, mpre, mpost, mixb, wqkv, n1g, *refs
):
    dqkv_o, in_o, acc_o, vgs, dls, dq_t, pad = refs[-7:]
    i = pl.program_id(0)
    slots, feats = do_r.shape[1:]
    patches = tok.shape[1]
    rows = k_r.shape[1]
    heads = mpre.shape[0]
    many = heads // 2
    half = many * rows

    @pl.when(i == 0)
    def _():
        acc_o[...] = jnp.zeros_like(acc_o)

    do_sum = jnp.zeros((8, feats), F32)
    for c in chunks(rows):
        vf = v_r[0, c, :].astype(F32)
        do_sum = do_sum + fold(do_r[0, c, :].astype(F32))
        for h in range(heads):
            vgs[h * rows + c.start : h * rows + c.stop, :] = (vf * mpost[h : h + 1, :]).astype(BF)
    do_sum = colsum(do_sum)
    q = q_r[0]
    do = do_r[0]
    kt = k_r[0].T
    dps = [nt(vgs[s * half : (s + 1) * half, :], do) for s in range(2)]
    dvs = [nn(p_r[0, s * many : (s + 1) * many].reshape(half, slots), do) for s in range(2)]
    dks, dqs = [], []
    for h in range(heads):
        for lane in range(0, slots, 128):
            dp = dps[h // many][h % many * rows : (h % many + 1) * rows, lane : lane + 128]
            pf = p_r[0, h, :, lane : lane + 128].astype(F32)
            mean = jnp.sum(dp * pf, axis=0, keepdims=True) / jnp.sum(pf, axis=0, keepdims=True)
            dls[h * rows : (h + 1) * rows, lane : lane + 128] = (pf * (dp - mean)).astype(BF)
        dqs.append(nn(kt, dls[h * rows : (h + 1) * rows, :]))
        if h % many == many - 1:
            s = h // many
            dks.append(nn(dls[s * half : (s + 1) * half, :], q))

    bias_row = mixb[...] * do_sum
    v_sum = jnp.zeros((8, feats), F32)
    dv_sum = jnp.zeros((8, feats), F32)
    sums = [jnp.zeros((8, feats), F32) for _ in range(heads)]
    for c in chunks(rows):
        vf = v_r[0, c, :].astype(F32)
        dv = bias_row
        for h in range(heads):
            at = (h % many) * rows
            this = dvs[h // many][at + c.start : at + c.stop]
            dv = dv + this * mpost[h : h + 1, :]
            sums[h] = sums[h] + fold(vf * this)
        if c.stop > patches:
            inside = lax.broadcasted_iota(jnp.int32, dv.shape, 0) < patches - c.start
            dv = jnp.where(inside, dv, 0.0)
            vf = jnp.where(inside, vf, 0.0)
        low = dv.astype(BF)
        dqkv_o[0, c, 2 * feats :] = low
        dv_sum = dv_sum + fold(low.astype(F32))
        v_sum = v_sum + fold(vf)
    for h in range(heads):
        acc_o[h : h + 1, :] += colsum(sums[h])
    acc_o[2 * heads : 2 * heads + 1, :] += do_sum * colsum(v_sum)
    acc_o[2 * heads + 10 : 2 * heads + 11, :] += colsum(dv_sum)

    head_dim = feats // heads
    for c in chunks(feats):
        g = c.start // head_dim
        for lane in range(0, slots, 128):
            total = 0.0
            for h in range(heads):
                total = total + dqs[h][c, lane : lane + 128] * pre_s[h, g]
            dq_t[c, lane : lane + 128] = (total * head_dim**-0.5).astype(BF)
    dq = dq_t[...].T[0:rows]
    dqkv_o[0, :, 0:feats] = dq
    dk_sum = jnp.zeros((8, feats), F32)
    sums = [jnp.zeros((8, feats), F32) for _ in range(heads)]
    for c in chunks(rows):
        kf = k_r[0, c, :].astype(F32)
        dk = 0.0
        for h in range(heads):
            at = (h % many) * rows
            this = dks[h // many][at + c.start : at + c.stop]
            dk = dk + this * mpre[h : h + 1, :]
            sums[h] = sums[h] + fold(kf * this)
        low = (dk * (1.0 / LOG2E)).astype(BF)
        dqkv_o[0, c, feats : 2 * feats] = low
        dk_sum = dk_sum + fold(low.astype(F32))
    for h in range(heads):
        acc_o[heads + h : heads + h + 1, :] += colsum(sums[h])
    acc_o[2 * heads + 8 : 2 * heads + 9, :] += colsum(dq.astype(F32))
    acc_o[2 * heads + 9 : 2 * heads + 10, :] += colsum(dk_sum)

    pad[patches:, :] = jnp.zeros((rows - patches, feats), F32)
    pad[0:patches, :] = tok[0].astype(F32)
    da1 = nt(dqkv_o[0], wqkv[...])
    gain = row(n1g)
    sums = [jnp.zeros((8, feats), F32) for _ in range(2)]
    for c in chunks(rows):
        n, r = normalized(pad[c, :])
        cot = da1[c]
        grad = dx1[0, c, :] + norm_back(cot, n, r, gain)
        sums = [sums[0] + fold(cot * n), sums[1] + fold(cot)]
        if c.stop <= patches:
            in_o[0, c, :] = grad
        else:
            in_o[0, c.start : patches, :] = grad[0 : patches - c.start]
    for j in range(2):
        acc_o[2 * heads + 11 + j : 2 * heads + 12 + j, :] += colsum(sums[j])


def qkv_grad_kernel(heads, dqkv, *refs):
    accs = refs[:-8]
    a1, acc_mlp, b1_first, b1_rest, keep, send, small, grads = refs[-8:]
    feats = a1.shape[1]
    count = 2 * keep.shape[0]
    size = 3 * feats // count
    acc = accs[0][...]
    for other in accs[1:]:
        acc = acc + other[...]
    small[...] = jnp.zeros_like(small)
    small[0:2, :] = acc[2 * heads + 11 : 2 * heads + 13]
    small[2:8, :] = acc_mlp[0:6, :]
    small[8:11, :] = acc[2 * heads + 8 : 2 * heads + 11]
    head_dim = feats // heads
    lanes = 2 * heads * heads
    gather = (
        head_of_lane((feats, lanes), 0, head_dim)
        == lax.broadcasted_iota(jnp.int32, (feats, lanes), 1) % heads
    ).astype(F32)
    sums = exact(acc[0 : 2 * heads + 8], gather, ((1,), (0,)))
    place = head_of_lane((2 * heads, lanes), 1, heads) == lax.broadcasted_iota(
        jnp.int32, (2 * heads, lanes), 0
    )
    small[11:12, 0:lanes] = colsum(jnp.where(place, sums[0 : 2 * heads], 0.0))
    small[11:12, lanes : 2 * lanes] = sums[2 * heads : 2 * heads + 1]
    m_idx = lax.axis_index("mp")
    for c, ref in enumerate((b1_first, b1_first, b1_rest, b1_rest)):
        place = 12 + jnp.bitwise_xor(m_idx, c)
        small[pl.ds(place, 1), :] = ref[:, (c % 2) * feats : (c % 2 + 1) * feats]
    low = small[...].astype(BF)
    outs = (keep, send)

    grads[...] = tn(a1[...], dqkv[...]).astype(BF).T

    def put(which, place, b):
        outs[which][place, 0:size, :] = grads[b * size : (b + 1) * size, :]
        outs[which][place, size:, :] = low

    store_blocks(count, put)


def final_kernel(heads, size, *refs):
    mine, got = refs[0], refs[1:-14]
    qkv_o, qkvb_o, pre_o, post_o, postb_o, b1_o, *vecs_o = refs[-14:]
    total = mine[...]
    for part in got:
        total = total + part[...].astype(F32)
    feats = total.shape[1]
    qkv_o[...] = total[0:size]
    small = total[size:]
    d_idx = lax.axis_index("dp")
    m_idx = lax.axis_index("mp")

    def own(value, width, index):
        lanes = value.shape[1]
        return pltpu.roll(value, lax.rem(lanes - index * width, lanes), axis=1)[:, 0:width]

    width = vecs_o[0].shape[1]
    vecs = own(small[0:8], width, d_idx)
    for j, ref in enumerate(vecs_o):
        ref[...] = vecs[j : j + 1]
    flat = jnp.concatenate([small[8 + j : 9 + j] for j in range(3)], axis=1)
    qkvb_o[...] = own(jnp.broadcast_to(flat, (8, 3 * feats)), qkvb_o.shape[1], d_idx)[0:1]
    b1 = own(small[8:16], b1_o.shape[1], d_idx)[4:8]
    pick = lax.broadcasted_iota(jnp.int32, b1.shape, 0) == m_idx
    b1_o[...] = colsum(jnp.where(pick, b1, 0.0))
    mix = small[11:12]
    hh = heads * heads
    line = lax.broadcasted_iota(jnp.int32, (heads, hh), 0)
    lane = lax.broadcasted_iota(jnp.int32, (heads, hh), 1)
    fold = (
        lax.broadcasted_iota(jnp.int32, (hh, heads), 0) % heads
        == lax.broadcasted_iota(jnp.int32, (hh, heads), 1)
    ).astype(F32)
    head_dim = feats // heads

    def square(values):
        return exact(jnp.where(lane // heads == line, values, 0.0), fold, ((1,), (0,)))

    post_o[...] = square(mix[:, 0:hh]).T
    pre_o[...] = square(mix[:, hh : 2 * hh]) * (head_dim**-0.5)
    postb_o[...] = mix[:, 2 * hh : 2 * hh + heads]


def whole(shape):
    return pl.BlockSpec(shape, lambda i: (0,) * len(shape))


def each(shape, first=0, many=1):
    return pl.BlockSpec((many,) + shape[1:], lambda i: (i + first,) + (0,) * (len(shape) - 1))


SCALARS = pl.BlockSpec(memory_space=pltpu.SMEM)
IN_HBM = pl.BlockSpec(memory_space=pltpu.HBM)


def kept(a):
    return pltpu.with_memory_space_constraint(a, pltpu.HBM)


def sds(shape, dtype):
    return jax.ShapeDtypeStruct(shape, dtype)


def call(
    kernel, grid, ins, in_specs, outs, out_specs, scratch=(), flops=0, name=None, aliases=None
):
    size = lambda a: a.size * a.dtype.itemsize
    return pl.pallas_call(
        kernel,
        grid=grid,
        in_specs=in_specs,
        out_specs=out_specs,
        out_shape=outs,
        scratch_shapes=scratch,
        input_output_aliases=aliases or {},
        compiler_params=pltpu.CompilerParams(vmem_limit_bytes=VMEM_LIMIT),
        cost_estimate=pl.CostEstimate(
            flops=flops,
            bytes_accessed=sum(size(a) for a in ins) + sum(size(a) for a in outs),
            transcendentals=0,
        ),
        name=name,
    )(*ins)


def xor_perm(count, mask):
    return [(j, j ^ mask) for j in range(count)]


def dp_hops(dp):
    bits = dp.bit_length() - 1
    groups = []
    at = 1
    while at < bits:
        groups.append((at, min(2, bits - at)))
        at += groups[-1][1]
    return groups


def dp_scatter(value, dp):
    for at, many in dp_hops(dp):
        value = value.reshape((-1, 1 << many) + value.shape[1:])
        got = [
            lax.ppermute(value[:, j].astype(BF), "dp", xor_perm(dp, j << at))
            for j in range(1, 1 << many)
        ]
        value = value[:, 0] + sum(g.astype(F32) for g in got)
    return value.reshape(value.shape[-2:])


def per_device(
    dp, mp,
    tokens_in, image_counts, norm1_gain, norm1_bias, qkv_weight, qkv_bias,
    mix_pre, mix_post, mix_post_bias, proj_weight, proj_bias, gamma1,
    norm2_gain, norm2_bias, fc1_weight, fc1_bias, fc2_weight, fc2_bias, gamma2, out_grad,
):
    images, patches, feats = tokens_in.shape
    heads = mix_pre.shape[0]
    rows = -(-patches // 16) * 16
    slots = -(-patches // 128) * 128
    hidden = fc1_weight.shape[1]
    ins = [kept(a) for a in (fc1_weight, fc2_weight, fc1_bias)]
    outs = [sds((2 * feats + 16, hidden), BF), sds((feats + 16, hidden), BF)]
    one, other = call(
        pack_kernel,
        (1,),
        ins,
        [IN_HBM] * 3,
        outs,
        [whole(a.shape) for a in outs],
        [pltpu.VMEM(fc1_bias.shape, F32), pltpu.SemaphoreType.DMA((4,))],
        name="pack",
    )
    near_one = lax.ppermute(one, "mp", xor_perm(mp, 1))
    near = [lax.ppermute(other, "mp", xor_perm(mp, j)) for j in range(2, mp)]

    tok_rows = (images, rows, feats)
    slot_rows = (images, slots, feats)
    prob_shape = (images, heads, rows, slots)
    mix_shape = (heads, feats)
    ins = [
        image_counts, mix_post, mix_post_bias, tokens_in, out_grad, norm1_gain, norm1_bias, qkv_bias, mix_pre, mix_post,
        mix_post_bias, proj_bias, gamma1, norm2_gain, norm2_bias, qkv_weight, proj_weight,
    ]
    ins[3:] = [kept(a) for a in ins[3:]]
    a1, q, k, v, prob, o, x1, u, a2, dy, mpre, mpost, mixb = call(
        attn_fwd_kernel,
        (images,),
        ins,
        [SCALARS] * 3 + [IN_HBM] * 14,
        [
            sds(tok_rows, BF), sds(slot_rows, BF), sds(tok_rows, BF), sds(tok_rows, BF),
            sds(prob_shape, BF), sds(tok_rows, BF), sds(tok_rows, F32), sds(tok_rows, F32),
            sds(tok_rows, BF), sds(tok_rows, BF), sds(mix_shape, F32), sds(mix_shape, F32),
            sds((1, feats), F32),
        ],
        [each(s) for s in (tok_rows, slot_rows, tok_rows, tok_rows, prob_shape)]
        + [each(tok_rows)] * 5
        + [whole(mix_shape)] * 2
        + [whole((1, feats))],
        [pltpu.VMEM(a.shape, a.dtype) for a in ins[3:]]
        + [
            pltpu.VMEM((rows, feats), F32), pltpu.VMEM((heads * rows, 2 * feats), BF),
            pltpu.VMEM((feats, slots), BF), pltpu.SemaphoreType.DMA((2 * images + 14,)),
        ],
        flops=images * 15 * 10**8,
        name="attn_fwd",
    )

    block = feats // dp
    total = images * rows
    group = 2 if images % 2 == 0 else 1
    flat = (total, feats)
    step = (group * rows, feats)
    a2, dy, x1, u, o = (a.reshape(flat) for a in (a2, dy, x1, u, o))
    near_one, near, a2 = lax.optimization_barrier((near_one, near, a2))
    near = jnp.stack(near)
    far = lax.ppermute(near, "dp", xor_perm(dp, 1))
    ins = [a2, dy, gamma2, fc1_weight, fc1_bias, fc2_weight, near_one]
    blocked = pl.BlockSpec(step, lambda i: (i, 0))
    wide = 2 * hidden
    grad_shape = (2, wide, feats)
    f0, da20, grads0, b1_0, a2t, dft = call(
        mlp_first_kernel,
        (images // group,),
        ins,
        [whole(a.shape) for a in ins],
        [
            sds(flat, F32), sds(flat, F32), sds(grad_shape, BF), sds((1, wide), F32),
            sds((feats, total), BF), sds((feats, total), BF),
        ],
        [blocked, blocked, whole(grad_shape), whole((1, wide))] + [whole((feats, total))] * 2,
        [
            pltpu.VMEM((feats, wide), BF), pltpu.VMEM((wide, feats), BF),
            pltpu.VMEM((1, wide), F32), pltpu.VMEM((total, wide), BF),
            pltpu.VMEM((total, wide), BF), pltpu.VMEM(flat, BF),
        ],
        flops=images * 8 * 10**8,
        name="mlp_first",
    )

    grad_rows = 9 * block
    half_shape = (dp // 2, grad_rows, feats)
    ins = [
        image_counts, a2, dy, x1, u, o, f0, da20, near, far, grads0, a2t, dft, proj_weight, gamma1,
        norm2_gain, fc2_bias, gamma2,
    ]
    layer_out, dx1, do, keep, send, b1_1, acc_mlp = call(
        mlp_rest_kernel,
        (images // group,),
        ins,
        [SCALARS, whole(flat), whole(flat), blocked, blocked, whole(flat), blocked, blocked]
        + [whole(a.shape) for a in ins[8:]],
        [
            sds(tokens_in.shape, BF), sds(flat, F32), sds(slot_rows, BF), sds(half_shape, BF),
            sds(half_shape, BF), sds((1, wide), F32), sds((8, feats), F32),
        ],
        [
            each(tokens_in.shape, 0, group), blocked, each(slot_rows, 0, group), whole(half_shape),
            whole(half_shape), whole((1, wide)), whole((8, feats)),
        ],
        [
            pltpu.VMEM((feats, wide), BF), pltpu.VMEM((wide, feats), BF),
            pltpu.VMEM((1, wide), F32), pltpu.VMEM((total, wide), BF),
            pltpu.VMEM((total, wide), BF), pltpu.VMEM(flat, BF), pltpu.VMEM(flat, BF),
            pltpu.VMEM((wide, feats), BF), pltpu.VMEM((feats, wide), BF),
            pltpu.VMEM((feats, feats), BF),
        ],
        flops=images * 9 * 10**8,
        name="mlp_rest",
    )
    got = lax.ppermute(send, "dp", xor_perm(dp, 1))
    dx1 = dx1.reshape(tok_rows)

    shares = [1, images - 1] if images > 1 else [1]
    dqkv_shape = (images, rows, 3 * feats)
    carried, accs = [], []
    for s, share in enumerate(shares):
        first = sum(shares[:s])
        ins = [mix_pre, do, q, k, v, prob, dx1, tokens_in, mpre, mpost, mixb, qkv_weight, norm1_gain]
        *carried, acc = call(
            attn_bwd_kernel,
            (share,),
            ins + carried,
            [SCALARS]
            + [each(a.shape, first) for a in ins[1:8]]
            + [whole(a.shape) for a in ins[8:]]
            + [pl.BlockSpec(memory_space=pl.ANY)] * len(carried),
            [sds(dqkv_shape, BF), sds(tokens_in.shape, F32), sds((2 * heads + 16, feats), F32)],
            [
                each(dqkv_shape, first), each(tokens_in.shape, first),
                whole((2 * heads + 16, feats)),
            ],
            [
                pltpu.VMEM((heads * rows, feats), BF), pltpu.VMEM((heads * rows, slots), BF),
                pltpu.VMEM((feats, slots), BF), pltpu.VMEM((rows, feats), F32),
            ],
            flops=share * 20 * 10**8,
            name="attn_bwd",
            aliases={len(ins): 0, len(ins) + 1: 1} if carried else None,
        )
        accs.append(acc)
        if s == 0:
            (keep, got), acc = lax.optimization_barrier(((keep, got), acc))
            mine = dp_scatter(keep.astype(F32) + got.astype(F32), dp)
            accs[0], do = lax.optimization_barrier((acc, do))
    dqkv, in_grad = carried
    mine, dqkv = lax.optimization_barrier((mine, dqkv))
    mlp_mine = mine
    low = mine.astype(BF)
    proj = low[8 * block :]
    got_z = [
        lax.ppermute(
            jnp.concatenate([low[2 * j * block : 2 * (j + 1) * block], proj]), "mp", xor_perm(mp, j)
        )
        for j in range(1, mp)
    ]

    q_block = 3 * feats // dp
    half_shape = (dp // 2, q_block + 16, feats)
    ins = [dqkv.reshape(total, 3 * feats)] + accs + [a1.reshape(flat), acc_mlp, b1_0, b1_1]
    keep, send = call(
        functools.partial(qkv_grad_kernel, heads),
        (1,),
        ins,
        [whole(a.shape) for a in ins],
        [sds(half_shape, BF), sds(half_shape, BF)],
        [whole(half_shape), whole(half_shape)],
        [pltpu.VMEM((16, feats), F32), pltpu.VMEM((3 * feats, feats), BF)],
        flops=11 * 10**8,
        name="qkv_grad",
    )
    got = lax.ppermute(send, "dp", xor_perm(dp, 1))
    mine = dp_scatter(keep.astype(F32) + got.astype(F32), dp)
    low = mine.astype(BF)
    low, got_z = lax.optimization_barrier((low, got_z))
    got = [lax.ppermute(low, "mp", xor_perm(mp, j)) for j in range(1, mp)]
    sums = jnp.concatenate([mlp_mine[: 2 * block], mlp_mine[8 * block :]]) + sum(
        g.astype(F32) for g in got_z
    )
    fc1g, fc2g, projg = (sums[j * block : (j + 1) * block] for j in range(3))
    b1_size = hidden // dp
    ins = [mine] + got
    outs = [
        sds((q_block, feats), F32), sds((1, q_block), F32), sds((heads, heads), F32),
        sds((heads, heads), F32), sds((1, heads), F32), sds((1, b1_size), F32),
    ] + [sds((1, block), F32)] * 8
    qkvw, qkvb, pre, post, postb, b1g, *vecs = call(
        functools.partial(final_kernel, heads, q_block),
        (1,),
        ins,
        [whole(a.shape) for a in ins],
        outs,
        [whole(a.shape) for a in outs],
        name="final",
    )
    vecs = [a.reshape(-1) for a in vecs]
    return (
        layer_out,
        in_grad,
        vecs[0],
        vecs[1],
        qkvw.T,
        qkvb.reshape(-1),
        pre,
        post,
        postb.reshape(-1),
        projg.T,
        vecs[2],
        vecs[3],
        vecs[4],
        vecs[5],
        fc1g.T,
        b1g.reshape(-1),
        fc2g.T,
        vecs[6],
        vecs[7],
    )


def solution(mesh):
    tokens = P(("dp", "mp"), None, None)
    placed = (
        (tokens, P("dp")) + (P(),) * 12 + (P(None, "mp"), P("mp"), P("mp", None), P(), P(), tokens)
    )
    return jax.shard_map(
        functools.partial(per_device, mesh.shape["dp"], mesh.shape["mp"]),
        mesh=mesh,
        in_specs=placed,
        out_specs=(
            tokens, tokens, P("dp"), P("dp"), P(None, "dp"), P("dp"), P(), P(), P(),
            P(None, "dp"), P("dp"), P("dp"), P("dp"), P("dp"), P(None, ("mp", "dp")),
            P(("mp", "dp")), P("mp", "dp"), P("dp"), P("dp"),
        ),
        check_vma=False,
    )
```

```python
import functools

import jax
import jax.numpy as jnp
from jax import lax
from jax.experimental import pallas as pl
from jax.experimental.pallas import tpu as pltpu
from jax.sharding import PartitionSpec as P

BF = jnp.bfloat16
F32 = jnp.float32
LOG2E = 1.4426950408889634
EPS = 1e-06
VMEM_LIMIT = 20 * 1024 * 1024


def nn(a, b):
    return lax.dot_general(a, b, (((1,), (0,)), ((), ())), preferred_element_type=F32)


def nt(a, b):
    return lax.dot_general(a, b, (((1,), (1,)), ((), ())), preferred_element_type=F32)


def tn(a, b):
    return lax.dot_general(a, b, (((0,), (0,)), ((), ())), preferred_element_type=F32)


def exact(a, b, dims):
    return lax.dot_general(
        a, b, (dims, ((), ())), precision=lax.Precision.HIGHEST, preferred_element_type=F32
    )


def normalized(x):
    mean = jnp.mean(x, axis=-1, keepdims=True)
    c = x - mean
    r = lax.rsqrt(jnp.mean(c * c, axis=-1, keepdims=True) + EPS)
    return c * r, r


def norm_back(cot, n, r, gain):
    cg = cot * gain
    return r * (
        cg
        - jnp.mean(cg, axis=-1, keepdims=True)
        - n * jnp.mean(cg * n, axis=-1, keepdims=True)
    )


def colsum(x):
    return jnp.sum(x, axis=0, keepdims=True)


def split(x):
    hi = x.astype(BF)
    return jnp.concatenate([hi, (x - hi.astype(F32)).astype(BF)], axis=1)


def row(ref):
    return ref[...].reshape(1, ref.shape[0])


def inverse(x):
    near = pl.reciprocal(x, approx=True)
    return near * (2.0 - x * near)


def gelu_parts(z):
    e = jnp.exp2(z * z * (-0.5 * LOG2E))
    t = inverse(1.0 + jnp.abs(z) * (0.3275911 * 0.7071067811865476))
    poly = t * (
        0.5 * 0.254829592
        + t
        * (
            0.5 * -0.284496736
            + t * (0.5 * 1.421413741 + t * (0.5 * -1.453152027 + t * (0.5 * 1.061405429)))
        )
    )
    tail = poly * e
    phi = jnp.where(z >= 0, 1.0 - tail, tail)
    return phi, phi + z * e * 0.3989422804014327


def head_of_lane(shape, axis, head_dim):
    return lax.broadcasted_iota(jnp.int32, shape, axis) // head_dim


def chunks(count, size=16):
    return [slice(at, at + size) for at in range(0, count, size)]


def fold(x):
    return sum(x[at : at + 8] for at in range(8, x.shape[0], 8)) + x[0:8]


def pack_kernel(w1, w2, b1, one, other, b1_v, sems):
    feats = w1.shape[0]
    core = jnp.bitwise_and(lax.axis_index("dp"), 1)
    copies = [
        pltpu.make_async_copy(b1, b1_v, sems.at[0]),
        pltpu.make_async_copy(w1, one.at[0:feats], sems.at[1]),
        pltpu.make_async_copy(w2, one.at[feats : 2 * feats], sems.at[2]),
    ]
    own = [pltpu.make_async_copy(w, other.at[0:feats], sems.at[3]) for w in (w1, w2)]
    for copy in copies:
        copy.start()
    for j in range(2):
        pl.when(core == j)(own[j].start)
    copies[0].wait()
    rest = row(b1_v)
    place = lax.broadcasted_iota(jnp.int32, (16, feats), 0)
    bias = jnp.zeros((16, feats), F32)
    for j in range(3):
        term = rest.astype(BF).astype(F32)
        bias = jnp.where(place == j, term, bias)
        rest = rest - term
    bias = bias.astype(BF)
    one[2 * feats :, :] = bias
    other[feats:, :] = bias
    for copy in copies[1:]:
        copy.wait()
    for j in range(2):
        pl.when(core == j)(own[j].wait)


def attn_fwd_kernel(
    counts, post_s, postb_s, *refs
):
    sources, refs = refs[:14], refs[14:]
    a1_o, q_o, k_o, v_o, p_o, o_o, x1_o, u_o, a2_o, dy_o, mpre, mpost, mixb = refs[:13]
    held, (pad, attended_t, sems) = refs[13:27], refs[27:]
    tok, og, n1g, n1b, qkvb, pre, post, postb, projb, gamma1, n2g, n2b, wqkv, wproj = held
    i = pl.program_id(0)
    images, patches, feats = tok.shape

    def image_copy(which, at):
        return pltpu.make_async_copy(
            sources[which].at[at], held[which].at[at], sems.at[which * images + at]
        )

    @pl.when(i == 0)
    def _():
        shared = [
            pltpu.make_async_copy(sources[j], held[j], sems.at[2 * images + j])
            for j in range(2, 14)
        ]
        image_copy(0, 0).start()
        image_copy(1, 0).start()
        for copy in shared:
            copy.start()
        for at in range(1, images):
            image_copy(0, at).start()
            image_copy(1, at).start()
        for copy in shared:
            copy.wait()

    image_copy(0, i).wait()
    image_copy(1, i).wait()
    rows = pad.shape[0]
    heads = mpre.shape[0]
    head_dim = feats // heads
    slots = q_o.shape[1]

    @pl.when(i == 0)
    def _():
        spread = (
            head_of_lane((heads, feats), 1, head_dim)
            == lax.broadcasted_iota(jnp.int32, (heads, feats), 0)
        ).astype(F32)
        mpre[...] = exact(pre[...], spread, ((1,), (0,))) * (head_dim**-0.5 * LOG2E)
        mpost[...] = exact(post[...], spread, ((0,), (0,)))
        mixb[...] = exact(row(postb), spread, ((1,), (0,)))

    pad[patches:, :] = jnp.zeros((rows - patches, feats), F32)
    live = (lax.axis_index("mp") * images + i < counts[0]).astype(F32)
    pad[0:patches, :] = og[i].astype(F32) * live
    dy_o[0] = pad[...].astype(BF)
    pad[0:patches, :] = tok[i].astype(F32)
    gain, shift = row(n1g), row(n1b)
    for c in chunks(rows):
        n, _ = normalized(pad[c, :])
        a1_o[0, c, :] = (n * gain + shift).astype(BF)
    qkv = nn(a1_o[0], wqkv[...])
    bias = row(qkvb)
    q_o[0, rows:] = jnp.zeros((slots - rows, feats), BF)
    for c in chunks(rows):
        q, k, v = (
            qkv[c, j * feats : (j + 1) * feats] + bias[:, j * feats : (j + 1) * feats]
            for j in range(3)
        )
        q_o[0, c, :] = q.astype(BF)
        v_o[0, c, :] = v.astype(BF)
        k_o[0, c, :] = k.astype(BF)
    q2 = jnp.concatenate([q_o[0], q_o[0]], axis=1)
    vt = v_o[0].T
    tail = patches // 8 * 8
    inside = lax.broadcasted_iota(jnp.int32, (rows - tail, 128), 0) < patches - tail
    lanes = range(0, slots, 128)
    real = (lax.broadcasted_iota(jnp.int32, (rows, 128), 0) < patches).astype(BF)
    start = nn(vt, real)

    def logits(pair):
        parts = []
        for g in pair:
            for c in chunks(rows):
                scaled = k_o[0, c, :].astype(F32) * mpre[g : g + 1, :]
                hi = scaled.astype(BF)
                parts.append(jnp.concatenate([hi, (scaled - hi.astype(F32)).astype(BF)], axis=1))
        return nt(jnp.concatenate(parts, axis=0), q2)

    totals = {}

    def add(pair, mixed):
        for h, product in zip(pair, mixed):
            for c in chunks(feats):
                g = c.start // head_dim
                for lane in lanes:
                    before = totals.get((c.start, lane))
                    if before is None:
                        before = start[c] * postb_s[g]
                    totals[c.start, lane] = before + product[c, lane : lane + 128] * post_s[g, h]

    pairs = [(g, g + 1) for g in range(0, heads, 2)]
    upcoming = logits(pairs[0])
    pending = None
    for s, pair in enumerate(pairs):
        current = upcoming
        if s + 1 < len(pairs):
            upcoming = logits(pairs[s + 1])
        mixed = []
        for j, g in enumerate(pair):
            columns = []
            for lane in lanes:
                x = current[j * rows : (j + 1) * rows, lane : lane + 128]
                x = jnp.concatenate([x[0:tail], jnp.where(inside, x[tail:], -1e30)], axis=0)
                e = jnp.exp2(x - jnp.max(x, axis=0, keepdims=True))
                inv = 1.0 / jnp.sum(e, axis=0, keepdims=True)
                columns.append((e * inv).astype(BF))
            p = jnp.concatenate(columns, axis=1)
            p_o[0, g] = p
            mixed.append(nn(vt, p))
        if pending is not None:
            add(*pending)
        pending = (pair, mixed)
    add(*pending)
    for c in chunks(feats):
        for lane in lanes:
            attended_t[c, lane : lane + 128] = totals[c.start, lane].astype(BF)
    o_o[0] = attended_t[...].T[0:rows]
    product = nn(o_o[0], wproj[...])
    bias, scale, gain, shift = row(projb), row(gamma1), row(n2g), row(n2b)
    for c in chunks(rows):
        u = product[c] + bias
        x1 = pad[c, :] + scale * u
        u_o[0, c, :] = u
        x1_o[0, c, :] = x1
        n, _ = normalized(x1)
        a2_o[0, c, :] = (n * gain + shift).astype(BF)


def store_blocks(count, put):
    mine = lax.axis_index("dp")
    for core in range(2):

        @pl.when(jnp.bitwise_and(mine, 1) == core)
        def _(core=core):
            for b in range(count):
                place = jnp.bitwise_xor(jnp.int32(b >> 1), jnp.right_shift(mine, 1))
                put((b ^ core) & 1, place, b)


def mlp_step(a2, dfs, w1, b1, w2, hids, dzs, at, rows, b1_sum, units=2):
    size = rows // units
    width = w2.shape[0]
    lanes = 256
    places = [pl.ds(pl.multiple_of(at + u * size, 16), size) for u in range(units)]
    sums = {}

    def products(u):
        return nn(a2[places[u], :], w1[...]), nt(dfs[places[u], :], w2[...])

    upcoming = products(0)
    outs = []
    for u in range(units):
        z, grad_hidden = upcoming
        if u + 1 < units:
            upcoming = products(u + 1)
        hid_columns, dz_columns = [], []
        for first in range(0, width, lanes):
            part = slice(first, first + lanes)
            bias = b1[:, part]
            hid_rows, dz_rows = [], []
            for c in chunks(size):
                zc = z[c, part] + bias
                phi, slope = gelu_parts(zc)
                dz = (grad_hidden[c, part] * slope).astype(BF)
                hid_rows.append((zc * phi).astype(BF))
                dz_rows.append(dz)
                more = fold(dz.astype(F32))
                sums[first] = sums[first] + more if first in sums else more
            hid_columns.append(jnp.concatenate(hid_rows, axis=0))
            dz_columns.append(jnp.concatenate(dz_rows, axis=0))
        hid = jnp.concatenate(hid_columns, axis=1)
        dz = jnp.concatenate(dz_columns, axis=1)
        hids[places[u], :] = hid
        dzs[places[u], :] = dz
        outs.append((nn(hid, w2[...]), nt(dz, w1[...])))
    for first, value in sums.items():
        b1_sum[:, first : first + lanes] += colsum(value)
    return outs


def mlp_first_kernel(
    a2, dy, gamma2, w1_own, b1_own, w2_own, near,
    f_o, da2_o, grads, b1_o, a2t, dft,
    w1, w2, b1, hids, dzs, dfs,
):
    i = pl.program_id(0)
    rows, feats = f_o.shape
    at = i * rows

    @pl.when(i == 0)
    def _():
        b1_o[...] = jnp.zeros_like(b1_o)
        w1[:, 0:feats] = w1_own[...]
        w1[:, feats:] = near[0:feats]
        w2[0:feats, :] = w2_own[...]
        w2[feats:, :] = near[feats : 2 * feats]
        b1[:, 0:feats] = row(b1_own)
        b1[:, feats:] = colsum(near[2 * feats : 2 * feats + 16].astype(F32))

    gain = row(gamma2)
    for c in chunks(rows):
        place = pl.ds(pl.multiple_of(at + c.start, 16), 16)
        dfs[place, :] = (dy[place, :].astype(F32) * gain).astype(BF)
    outs = mlp_step(a2, dfs, w1, b1, w2, hids, dzs, at, rows, b1_o)
    size = rows // len(outs)
    for u, (f, da2) in enumerate(outs):
        f_o[u * size : (u + 1) * size, :] = f
        da2_o[u * size : (u + 1) * size, :] = da2

    @pl.when(i == pl.num_programs(0) - 1)
    def _():
        a2t[...] = a2[...].T
        dft[...] = dfs[...].T
        grads[0] = nn(a2t[...], dzs[...]).astype(BF).T
        down = nn(dft[...], hids[...]).astype(BF)
        for c in range(2):
            grads[1, c * feats : (c + 1) * feats, :] = down[:, c * feats : (c + 1) * feats]


def mlp_rest_kernel(
    counts, a2, dy, x1, u, o, f0, da20, near, far, grads, a2t, dft, wproj, gamma1, n2g, fc2b, gamma2,
    out_o, dx1_o, do_o, keep, send, b1_o, acc_o,
    w1, w2, b1, hids, dzs, dfs, dus, ups, downs, projs,
):
    i = pl.program_id(0)
    rows, feats = f0.shape
    group, patches = out_o.shape[:2]
    image_rows = rows // group
    at = i * rows
    here = pl.ds(pl.multiple_of(at, rows), rows)
    m_idx = lax.axis_index("mp")

    @pl.when(i == 0)
    def _():
        b1_o[...] = jnp.zeros_like(b1_o)
        acc_o[...] = jnp.zeros_like(acc_o)
        for c in range(2):
            b1[:, c * feats : (c + 1) * feats] = colsum(near[c, feats : feats + 16].astype(F32))

    for core in range(2):

        @pl.when(jnp.logical_and(i == 0, jnp.bitwise_and(lax.axis_index("dp"), 1) == core))
        def _(core=core):
            first, second = (near, far) if core == 0 else (far, near)
            for c in range(2):
                w1[:, c * feats : (c + 1) * feats] = first[c, 0:feats]
                w2[c * feats : (c + 1) * feats, :] = second[c, 0:feats]

    gain2 = row(gamma2)
    for c in chunks(rows):
        place = pl.ds(pl.multiple_of(at + c.start, 16), 16)
        dfs[place, :] = (dy[place, :].astype(F32) * gain2).astype(BF)
    outs = mlp_step(a2, dfs, w1, b1, w2, hids, dzs, at, rows, b1_o)
    size = rows // len(outs)
    bias, gain, scale = row(fc2b), row(n2g), row(gamma1)
    sums = [jnp.zeros((8, feats), F32) for _ in range(6)]
    for c in chunks(rows):
        place = pl.ds(pl.multiple_of(at + c.start, 16), 16)
        f, da2 = outs[c.start // size]
        inner = slice(c.start % size, c.start % size + 16)
        fc = f[inner] + f0[c, :] + bias
        dac = da2[inner] + da20[c, :]
        x1c = x1[c, :]
        dyc = dy[place, :].astype(F32)
        n, r = normalized(x1c)
        dx1 = dyc + norm_back(dac, n, r, gain)
        dx1_o[c, :] = dx1
        du = (dx1 * scale).astype(BF)
        dus[place, :] = du
        image = c.start // image_rows
        first = c.start - image * image_rows
        live = (m_idx * (group * pl.num_programs(0)) + i * group + image < counts[0]).astype(F32)
        out = ((x1c + gain2 * fc) * live).astype(BF)
        if first + 16 <= patches:
            out_o[image, first : first + 16, :] = out
        else:
            out_o[image, first:patches, :] = out[0 : patches - first]
        terms = (
            du.astype(F32), u[c, :] * dx1, dac * n, dac, dfs[place, :].astype(F32), fc * dyc,
        )
        sums = [s + fold(t) for s, t in zip(sums, terms)]
    for j in range(6):
        acc_o[j : j + 1, :] += colsum(sums[j])
    do = nt(dus[here, :], wproj[...]).astype(BF)
    for j in range(group):
        do_o[j, 0:image_rows] = do[j * image_rows : (j + 1) * image_rows]
        do_o[j, image_rows:] = jnp.zeros((do_o.shape[1] - image_rows, feats), BF)

    @pl.when(i == pl.num_programs(0) - 1)
    def _():
        count = 2 * keep.shape[0]
        size = feats // count
        outs = (keep, send)

        ups[...] = nn(a2t[...], dzs[...]).astype(BF).T
        downs[...] = nn(dft[...], hids[...]).astype(BF)
        projs[...] = tn(dus[...], o[...]).astype(BF)

        def put(which, place, b):
            out = outs[which]
            for c in range(2):
                part = slice(c * feats, (c + 1) * feats)
                up = slice(c * feats + b * size, c * feats + (b + 1) * size)
                down = slice(b * size, (b + 1) * size)
                pieces = (grads[0, up, :], grads[1, c * feats + b * size : c * feats + (b + 1) * size, :])
                for j, piece in enumerate(pieces):
                    out[place, (2 * c + j) * size : (2 * c + j + 1) * size, :] = piece
                pieces = (ups[up, :], downs[down, part])
                for j, piece in enumerate(pieces):
                    out[place, (4 + 2 * c + j) * size : (5 + 2 * c + j) * size, :] = piece
            out[place, 8 * size : 9 * size, :] = projs[b * size : (b + 1) * size, :]

        store_blocks(count, put)


def attn_bwd_kernel(
    pre_s, do_r, q_r, k_r, v_r, p_r, dx1, tok, mpre, mpost, mixb, wqkv, n1g, *refs
):
    dqkv_o, in_o, acc_o, dq_t, pad = refs[-5:]
    i = pl.program_id(0)
    slots, feats = do_r.shape[1:]
    patches = tok.shape[1]
    rows = k_r.shape[1]
    heads = mpre.shape[0]

    @pl.when(i == 0)
    def _():
        acc_o[...] = jnp.zeros_like(acc_o)

    head_dim = feats // heads
    lanes = range(0, slots, 128)
    q = q_r[0]
    do = do_r[0]
    kt = k_r[0].T

    def prob_grad(pair):
        parts = []
        for h in pair:
            for c in chunks(rows):
                parts.append((v_r[0, c, :].astype(F32) * mpost[h : h + 1, :]).astype(BF))
        return nt(jnp.concatenate(parts, axis=0), do)

    dv, dk, dqt = {}, {}, {}

    def add(pair, dvs, dks, dqs):
        for j, h in enumerate(pair):
            post_sum = jnp.zeros((8, feats), F32)
            pre_sum = jnp.zeros((8, feats), F32)
            for c in chunks(rows):
                at = slice(j * rows + c.start, j * rows + c.stop)
                vc, kc = dvs[at], dks[at]
                post_sum = post_sum + fold(v_r[0, c, :].astype(F32) * vc)
                pre_sum = pre_sum + fold(k_r[0, c, :].astype(F32) * kc)
                vc = vc * mpost[h : h + 1, :]
                kc = kc * mpre[h : h + 1, :]
                dv[c.start] = dv[c.start] + vc if c.start in dv else vc
                dk[c.start] = dk[c.start] + kc if c.start in dk else kc
            acc_o[h : h + 1, :] += colsum(post_sum)
            acc_o[heads + h : heads + h + 1, :] += colsum(pre_sum)
            for c in chunks(feats):
                g = c.start // head_dim
                for lane in lanes:
                    more = dqs[j][c, lane : lane + 128] * pre_s[h, g]
                    key = (c.start, lane)
                    dqt[key] = dqt[key] + more if key in dqt else more

    pairs = [(h, h + 1) for h in range(0, heads, 2)]
    upcoming = prob_grad(pairs[0])
    pending = None
    for s, pair in enumerate(pairs):
        current = upcoming
        if s + 1 < len(pairs):
            upcoming = prob_grad(pairs[s + 1])
        dvs = nn(p_r[0, pair[0] : pair[1] + 1].reshape(2 * rows, slots), do)
        dls = []
        for j, h in enumerate(pair):
            columns = []
            for lane in lanes:
                dp = current[j * rows : (j + 1) * rows, lane : lane + 128]
                pf = p_r[0, h, :, lane : lane + 128].astype(F32)
                mean = jnp.sum(dp * pf, axis=0, keepdims=True) / jnp.sum(pf, axis=0, keepdims=True)
                columns.append((pf * (dp - mean)).astype(BF))
            dls.append(jnp.concatenate(columns, axis=1))
        dks = nn(jnp.concatenate(dls, axis=0), q)
        dqs = [nn(kt, dl) for dl in dls]
        if pending is not None:
            add(*pending)
        pending = (pair, dvs, dks, dqs)
    add(*pending)

    do_sum = jnp.zeros((8, feats), F32)
    for c in chunks(rows):
        do_sum = do_sum + fold(do_r[0, c, :].astype(F32))
    do_sum = colsum(do_sum)
    bias_row = mixb[...] * do_sum
    v_sum, dv_sum, dk_sum = (jnp.zeros((8, feats), F32) for _ in range(3))
    for c in chunks(rows):
        vf = v_r[0, c, :].astype(F32)
        whole_dv = dv[c.start] + bias_row
        if c.stop > patches:
            inside = lax.broadcasted_iota(jnp.int32, vf.shape, 0) < patches - c.start
            whole_dv = jnp.where(inside, whole_dv, 0.0)
            vf = jnp.where(inside, vf, 0.0)
        low = whole_dv.astype(BF)
        dqkv_o[0, c, 2 * feats :] = low
        dv_sum = dv_sum + fold(low.astype(F32))
        v_sum = v_sum + fold(vf)
        low = (dk[c.start] * (1.0 / LOG2E)).astype(BF)
        dqkv_o[0, c, feats : 2 * feats] = low
        dk_sum = dk_sum + fold(low.astype(F32))
    for c in chunks(feats):
        for lane in lanes:
            dq_t[c, lane : lane + 128] = (dqt[c.start, lane] * head_dim**-0.5).astype(BF)
    dq = dq_t[...].T[0:rows]
    dqkv_o[0, :, 0:feats] = dq
    acc_o[2 * heads : 2 * heads + 1, :] += do_sum * colsum(v_sum)
    acc_o[2 * heads + 8 : 2 * heads + 9, :] += colsum(dq.astype(F32))
    acc_o[2 * heads + 9 : 2 * heads + 10, :] += colsum(dk_sum)
    acc_o[2 * heads + 10 : 2 * heads + 11, :] += colsum(dv_sum)

    pad[patches:, :] = jnp.zeros((rows - patches, feats), F32)
    pad[0:patches, :] = tok[0].astype(F32)
    da1 = nt(dqkv_o[0], wqkv[...])
    gain = row(n1g)
    sums = [jnp.zeros((8, feats), F32) for _ in range(2)]
    for c in chunks(rows):
        n, r = normalized(pad[c, :])
        cot = da1[c]
        grad = dx1[0, c, :] + norm_back(cot, n, r, gain)
        sums = [sums[0] + fold(cot * n), sums[1] + fold(cot)]
        if c.stop <= patches:
            in_o[0, c, :] = grad
        else:
            in_o[0, c.start : patches, :] = grad[0 : patches - c.start]
    for j in range(2):
        acc_o[2 * heads + 11 + j : 2 * heads + 12 + j, :] += colsum(sums[j])


def qkv_grad_kernel(heads, dqkv, *refs):
    accs = refs[:-8]
    a1, acc_mlp, b1_first, b1_rest, keep, send, small, grads = refs[-8:]
    feats = a1.shape[1]
    count = 2 * keep.shape[0]
    size = 3 * feats // count
    acc = accs[0][...]
    for other in accs[1:]:
        acc = acc + other[...]
    small[...] = jnp.zeros_like(small)
    small[0:2, :] = acc[2 * heads + 11 : 2 * heads + 13]
    small[2:8, :] = acc_mlp[0:6, :]
    small[8:11, :] = acc[2 * heads + 8 : 2 * heads + 11]
    head_dim = feats // heads
    lanes = 2 * heads * heads
    gather = (
        head_of_lane((feats, lanes), 0, head_dim)
        == lax.broadcasted_iota(jnp.int32, (feats, lanes), 1) % heads
    ).astype(F32)
    sums = exact(acc[0 : 2 * heads + 8], gather, ((1,), (0,)))
    place = head_of_lane((2 * heads, lanes), 1, heads) == lax.broadcasted_iota(
        jnp.int32, (2 * heads, lanes), 0
    )
    small[11:12, 0:lanes] = colsum(jnp.where(place, sums[0 : 2 * heads], 0.0))
    small[11:12, lanes : 2 * lanes] = sums[2 * heads : 2 * heads + 1]
    m_idx = lax.axis_index("mp")
    for c, ref in enumerate((b1_first, b1_first, b1_rest, b1_rest)):
        place = 12 + jnp.bitwise_xor(m_idx, c)
        small[pl.ds(place, 1), :] = ref[:, (c % 2) * feats : (c % 2 + 1) * feats]
    low = small[...].astype(BF)
    outs = (keep, send)

    grads[...] = tn(a1[...], dqkv[...]).astype(BF).T

    def put(which, place, b):
        outs[which][place, 0:size, :] = grads[b * size : (b + 1) * size, :]
        outs[which][place, size:, :] = low

    store_blocks(count, put)


def final_kernel(heads, size, many, *refs):
    mine, got = refs[0], refs[1 : 1 + many]
    mlp_mine, got_z = refs[1 + many], refs[2 + many : 2 + 2 * many]
    qkv_o, qkvb_o, pre_o, post_o, postb_o, b1_o, *vecs_o, fc1_o, fc2_o, proj_o = refs[-17:]
    block = fc1_o.shape[0]
    outs = ((fc1_o, 0, 0), (fc2_o, 1, 1), (proj_o, 8, 2))
    for out, first, place in outs:
        total = mlp_mine[first * block : (first + 1) * block, :]
        for part in got_z:
            total = total + part[place * block : (place + 1) * block, :].astype(F32)
        out[...] = total
    total = mine[...]
    for part in got:
        total = total + part[...].astype(F32)
    feats = total.shape[1]
    qkv_o[...] = total[0:size]
    small = total[size:]
    d_idx = lax.axis_index("dp")
    m_idx = lax.axis_index("mp")

    def own(value, width, index):
        lanes = value.shape[1]
        return pltpu.roll(value, lax.rem(lanes - index * width, lanes), axis=1)[:, 0:width]

    width = vecs_o[0].shape[1]
    vecs = own(small[0:8], width, d_idx)
    for j, ref in enumerate(vecs_o):
        ref[...] = vecs[j : j + 1]
    flat = jnp.concatenate([small[8 + j : 9 + j] for j in range(3)], axis=1)
    qkvb_o[...] = own(jnp.broadcast_to(flat, (8, 3 * feats)), qkvb_o.shape[1], d_idx)[0:1]
    b1 = own(small[8:16], b1_o.shape[1], d_idx)[4:8]
    pick = lax.broadcasted_iota(jnp.int32, b1.shape, 0) == m_idx
    b1_o[...] = colsum(jnp.where(pick, b1, 0.0))
    mix = small[11:12]
    hh = heads * heads
    line = lax.broadcasted_iota(jnp.int32, (heads, hh), 0)
    lane = lax.broadcasted_iota(jnp.int32, (heads, hh), 1)
    fold = (
        lax.broadcasted_iota(jnp.int32, (hh, heads), 0) % heads
        == lax.broadcasted_iota(jnp.int32, (hh, heads), 1)
    ).astype(F32)
    head_dim = feats // heads

    def square(values):
        return exact(jnp.where(lane // heads == line, values, 0.0), fold, ((1,), (0,)))

    post_o[...] = square(mix[:, 0:hh]).T
    pre_o[...] = square(mix[:, hh : 2 * hh]) * (head_dim**-0.5)
    postb_o[...] = mix[:, 2 * hh : 2 * hh + heads]


def whole(shape):
    return pl.BlockSpec(shape, lambda i: (0,) * len(shape))


def each(shape, first=0, many=1):
    return pl.BlockSpec((many,) + shape[1:], lambda i: (i + first,) + (0,) * (len(shape) - 1))


SCALARS = pl.BlockSpec(memory_space=pltpu.SMEM)
IN_HBM = pl.BlockSpec(memory_space=pltpu.HBM)


def kept(a):
    return pltpu.with_memory_space_constraint(a, pltpu.HBM)


def sds(shape, dtype):
    return jax.ShapeDtypeStruct(shape, dtype)


def call(
    kernel, grid, ins, in_specs, outs, out_specs, scratch=(), flops=0, name=None, aliases=None
):
    size = lambda a: a.size * a.dtype.itemsize
    return pl.pallas_call(
        kernel,
        grid=grid,
        in_specs=in_specs,
        out_specs=out_specs,
        out_shape=outs,
        scratch_shapes=scratch,
        input_output_aliases=aliases or {},
        compiler_params=pltpu.CompilerParams(vmem_limit_bytes=VMEM_LIMIT),
        cost_estimate=pl.CostEstimate(
            flops=flops,
            bytes_accessed=sum(size(a) for a in ins) + sum(size(a) for a in outs),
            transcendentals=0,
        ),
        name=name,
    )(*ins)


def xor_perm(count, mask):
    return [(j, j ^ mask) for j in range(count)]


def dp_hops(dp):
    bits = dp.bit_length() - 1
    groups = []
    at = 1
    while at < bits:
        groups.append((at, min(2, bits - at)))
        at += groups[-1][1]
    return groups


def dp_scatter(value, dp):
    for at, many in dp_hops(dp):
        value = value.reshape((-1, 1 << many) + value.shape[1:])
        got = [
            lax.ppermute(value[:, j].astype(BF), "dp", xor_perm(dp, j << at))
            for j in range(1, 1 << many)
        ]
        value = value[:, 0] + sum(g.astype(F32) for g in got)
    return value.reshape(value.shape[-2:])


def per_device(
    dp, mp,
    tokens_in, image_counts, norm1_gain, norm1_bias, qkv_weight, qkv_bias,
    mix_pre, mix_post, mix_post_bias, proj_weight, proj_bias, gamma1,
    norm2_gain, norm2_bias, fc1_weight, fc1_bias, fc2_weight, fc2_bias, gamma2, out_grad,
):
    images, patches, feats = tokens_in.shape
    heads = mix_pre.shape[0]
    rows = -(-patches // 16) * 16
    slots = -(-patches // 128) * 128
    hidden = fc1_weight.shape[1]
    ins = [kept(a) for a in (fc1_weight, fc2_weight, fc1_bias)]
    outs = [sds((2 * feats + 16, hidden), BF), sds((feats + 16, hidden), BF)]
    one, other = call(
        pack_kernel,
        (1,),
        ins,
        [IN_HBM] * 3,
        outs,
        [whole(a.shape) for a in outs],
        [pltpu.VMEM(fc1_bias.shape, F32), pltpu.SemaphoreType.DMA((4,))],
        name="pack",
    )
    near_one = lax.ppermute(one, "mp", xor_perm(mp, 1))
    near = [lax.ppermute(other, "mp", xor_perm(mp, j)) for j in range(2, mp)]

    tok_rows = (images, rows, feats)
    slot_rows = (images, slots, feats)
    prob_shape = (images, heads, rows, slots)
    mix_shape = (heads, feats)
    ins = [
        image_counts, mix_post, mix_post_bias, tokens_in, out_grad, norm1_gain, norm1_bias, qkv_bias, mix_pre, mix_post,
        mix_post_bias, proj_bias, gamma1, norm2_gain, norm2_bias, qkv_weight, proj_weight,
    ]
    ins[3:] = [kept(a) for a in ins[3:]]
    a1, q, k, v, prob, o, x1, u, a2, dy, mpre, mpost, mixb = call(
        attn_fwd_kernel,
        (images,),
        ins,
        [SCALARS] * 3 + [IN_HBM] * 14,
        [
            sds(tok_rows, BF), sds(slot_rows, BF), sds(tok_rows, BF), sds(tok_rows, BF),
            sds(prob_shape, BF), sds(tok_rows, BF), sds(tok_rows, F32), sds(tok_rows, F32),
            sds(tok_rows, BF), sds(tok_rows, BF), sds(mix_shape, F32), sds(mix_shape, F32),
            sds((1, feats), F32),
        ],
        [each(s) for s in (tok_rows, slot_rows, tok_rows, tok_rows, prob_shape)]
        + [each(tok_rows)] * 5
        + [whole(mix_shape)] * 2
        + [whole((1, feats))],
        [pltpu.VMEM(a.shape, a.dtype) for a in ins[3:]]
        + [
            pltpu.VMEM((rows, feats), F32), pltpu.VMEM((feats, slots), BF),
            pltpu.SemaphoreType.DMA((2 * images + 14,)),
        ],
        flops=images * 15 * 10**8,
        name="attn_fwd",
    )

    block = feats // dp
    total = images * rows
    group = 2 if images % 2 == 0 else 1
    flat = (total, feats)
    step = (group * rows, feats)
    a2, dy, x1, u, o = (a.reshape(flat) for a in (a2, dy, x1, u, o))
    near_one, near, a2 = lax.optimization_barrier((near_one, near, a2))
    near = jnp.stack(near)
    far = lax.ppermute(near, "dp", xor_perm(dp, 1))
    ins = [a2, dy, gamma2, fc1_weight, fc1_bias, fc2_weight, near_one]
    blocked = pl.BlockSpec(step, lambda i: (i, 0))
    wide = 2 * hidden
    grad_shape = (2, wide, feats)
    f0, da20, grads0, b1_0, a2t, dft = call(
        mlp_first_kernel,
        (images // group,),
        ins,
        [whole(a.shape) for a in ins],
        [
            sds(flat, F32), sds(flat, F32), sds(grad_shape, BF), sds((1, wide), F32),
            sds((feats, total), BF), sds((feats, total), BF),
        ],
        [blocked, blocked, whole(grad_shape), whole((1, wide))] + [whole((feats, total))] * 2,
        [
            pltpu.VMEM((feats, wide), BF), pltpu.VMEM((wide, feats), BF),
            pltpu.VMEM((1, wide), F32), pltpu.VMEM((total, wide), BF),
            pltpu.VMEM((total, wide), BF), pltpu.VMEM(flat, BF),
        ],
        flops=images * 8 * 10**8,
        name="mlp_first",
    )

    grad_rows = 9 * block
    half_shape = (dp // 2, grad_rows, feats)
    ins = [
        image_counts, a2, dy, x1, u, o, f0, da20, near, far, grads0, a2t, dft, proj_weight, gamma1,
        norm2_gain, fc2_bias, gamma2,
    ]
    layer_out, dx1, do, keep, send, b1_1, acc_mlp = call(
        mlp_rest_kernel,
        (images // group,),
        ins,
        [SCALARS, whole(flat), whole(flat), blocked, blocked, whole(flat), blocked, blocked]
        + [whole(a.shape) for a in ins[8:]],
        [
            sds(tokens_in.shape, BF), sds(flat, F32), sds(slot_rows, BF), sds(half_shape, BF),
            sds(half_shape, BF), sds((1, wide), F32), sds((8, feats), F32),
        ],
        [
            each(tokens_in.shape, 0, group), blocked, each(slot_rows, 0, group), whole(half_shape),
            whole(half_shape), whole((1, wide)), whole((8, feats)),
        ],
        [
            pltpu.VMEM((feats, wide), BF), pltpu.VMEM((wide, feats), BF),
            pltpu.VMEM((1, wide), F32), pltpu.VMEM((total, wide), BF),
            pltpu.VMEM((total, wide), BF), pltpu.VMEM(flat, BF), pltpu.VMEM(flat, BF),
            pltpu.VMEM((wide, feats), BF), pltpu.VMEM((feats, wide), BF),
            pltpu.VMEM((feats, feats), BF),
        ],
        flops=images * 9 * 10**8,
        name="mlp_rest",
    )
    got = lax.ppermute(send, "dp", xor_perm(dp, 1))
    dx1 = dx1.reshape(tok_rows)

    shares = [1, images - 1] if images > 1 else [1]
    dqkv_shape = (images, rows, 3 * feats)
    carried, accs = [], []
    for s, share in enumerate(shares):
        first = sum(shares[:s])
        ins = [mix_pre, do, q, k, v, prob, dx1, tokens_in, mpre, mpost, mixb, qkv_weight, norm1_gain]
        *carried, acc = call(
            attn_bwd_kernel,
            (share,),
            ins + carried,
            [SCALARS]
            + [each(a.shape, first) for a in ins[1:8]]
            + [whole(a.shape) for a in ins[8:]]
            + [pl.BlockSpec(memory_space=pl.ANY)] * len(carried),
            [sds(dqkv_shape, BF), sds(tokens_in.shape, F32), sds((2 * heads + 16, feats), F32)],
            [
                each(dqkv_shape, first), each(tokens_in.shape, first),
                whole((2 * heads + 16, feats)),
            ],
            [
                pltpu.VMEM((feats, slots), BF), pltpu.VMEM((rows, feats), F32),
            ],
            flops=share * 20 * 10**8,
            name="attn_bwd",
            aliases={len(ins): 0, len(ins) + 1: 1} if carried else None,
        )
        accs.append(acc)
        if s == 0:
            (keep, got), acc = lax.optimization_barrier(((keep, got), acc))
            mine = dp_scatter(keep.astype(F32) + got.astype(F32), dp)
            accs[0], do = lax.optimization_barrier((acc, do))
    dqkv, in_grad = carried
    mine, dqkv = lax.optimization_barrier((mine, dqkv))
    mlp_mine = mine
    low = mine.astype(BF)
    proj = low[8 * block :]
    got_z = [
        lax.ppermute(
            jnp.concatenate([low[2 * j * block : 2 * (j + 1) * block], proj]), "mp", xor_perm(mp, j)
        )
        for j in range(1, mp)
    ]

    q_block = 3 * feats // dp
    half_shape = (dp // 2, q_block + 16, feats)
    ins = [dqkv.reshape(total, 3 * feats)] + accs + [a1.reshape(flat), acc_mlp, b1_0, b1_1]
    keep, send = call(
        functools.partial(qkv_grad_kernel, heads),
        (1,),
        ins,
        [whole(a.shape) for a in ins],
        [sds(half_shape, BF), sds(half_shape, BF)],
        [whole(half_shape), whole(half_shape)],
        [pltpu.VMEM((16, feats), F32), pltpu.VMEM((3 * feats, feats), BF)],
        flops=11 * 10**8,
        name="qkv_grad",
    )
    got = lax.ppermute(send, "dp", xor_perm(dp, 1))
    mine = dp_scatter(keep.astype(F32) + got.astype(F32), dp)
    low = mine.astype(BF)
    got = [lax.ppermute(low, "mp", xor_perm(mp, j)) for j in range(1, mp)]
    b1_size = hidden // dp
    ins = [mine] + got + [mlp_mine] + got_z
    outs = [
        sds((q_block, feats), F32), sds((1, q_block), F32), sds((heads, heads), F32),
        sds((heads, heads), F32), sds((1, heads), F32), sds((1, b1_size), F32),
    ] + [sds((1, block), F32)] * 8 + [sds((block, feats), F32)] * 3
    qkvw, qkvb, pre, post, postb, b1g, *vecs, fc1g, fc2g, projg = call(
        functools.partial(final_kernel, heads, q_block, mp - 1),
        (1,),
        ins,
        [whole(a.shape) for a in ins],
        outs,
        [whole(a.shape) for a in outs],
        name="final",
    )
    vecs = [a.reshape(-1) for a in vecs]
    return (
        layer_out,
        in_grad,
        vecs[0],
        vecs[1],
        qkvw.T,
        qkvb.reshape(-1),
        pre,
        post,
        postb.reshape(-1),
        projg.T,
        vecs[2],
        vecs[3],
        vecs[4],
        vecs[5],
        fc1g.T,
        b1g.reshape(-1),
        fc2g.T,
        vecs[6],
        vecs[7],
    )


def solution(mesh):
    tokens = P(("dp", "mp"), None, None)
    placed = (
        (tokens, P("dp")) + (P(),) * 12 + (P(None, "mp"), P("mp"), P("mp", None), P(), P(), tokens)
    )
    return jax.shard_map(
        functools.partial(per_device, mesh.shape["dp"], mesh.shape["mp"]),
        mesh=mesh,
        in_specs=placed,
        out_specs=(
            tokens, tokens, P("dp"), P("dp"), P(None, "dp"), P("dp"), P(), P(), P(),
            P(None, "dp"), P("dp"), P("dp"), P("dp"), P("dp"), P(None, ("mp", "dp")),
            P(("mp", "dp")), P("mp", "dp"), P("dp"), P("dp"),
        ),
        check_vma=False,
    )
```

```python
import functools

import jax
import jax.numpy as jnp
from jax import lax
from jax.experimental import pallas as pl
from jax.experimental.pallas import tpu as pltpu
from jax.sharding import PartitionSpec as P

BF = jnp.bfloat16
F32 = jnp.float32
LOG2E = 1.4426950408889634
EPS = 1e-06
VMEM_LIMIT = 20 * 1024 * 1024


def nn(a, b):
    return lax.dot_general(a, b, (((1,), (0,)), ((), ())), preferred_element_type=F32)


def nt(a, b):
    return lax.dot_general(a, b, (((1,), (1,)), ((), ())), preferred_element_type=F32)


def tn(a, b):
    return lax.dot_general(a, b, (((0,), (0,)), ((), ())), preferred_element_type=F32)


def exact(a, b, dims):
    return lax.dot_general(
        a, b, (dims, ((), ())), precision=lax.Precision.HIGHEST, preferred_element_type=F32
    )


def normalized(x):
    mean = jnp.mean(x, axis=-1, keepdims=True)
    c = x - mean
    r = lax.rsqrt(jnp.mean(c * c, axis=-1, keepdims=True) + EPS)
    return c * r, r


def norm_back(cot, n, r, gain):
    cg = cot * gain
    return r * (
        cg
        - jnp.mean(cg, axis=-1, keepdims=True)
        - n * jnp.mean(cg * n, axis=-1, keepdims=True)
    )


def colsum(x):
    return jnp.sum(x, axis=0, keepdims=True)


def split(x):
    hi = x.astype(BF)
    return jnp.concatenate([hi, (x - hi.astype(F32)).astype(BF)], axis=1)


def row(ref):
    return ref[...].reshape(1, ref.shape[0])


def inverse(x):
    near = pl.reciprocal(x, approx=True)
    return near * (2.0 - x * near)


def gelu_parts(z):
    e = jnp.exp2(z * z * (-0.5 * LOG2E))
    t = inverse(1.0 + jnp.abs(z) * (0.3275911 * 0.7071067811865476))
    poly = t * (
        0.5 * 0.254829592
        + t
        * (
            0.5 * -0.284496736
            + t * (0.5 * 1.421413741 + t * (0.5 * -1.453152027 + t * (0.5 * 1.061405429)))
        )
    )
    tail = poly * e
    phi = jnp.where(z >= 0, 1.0 - tail, tail)
    return phi, phi + z * e * 0.3989422804014327


def head_of_lane(shape, axis, head_dim):
    return lax.broadcasted_iota(jnp.int32, shape, axis) // head_dim


def chunks(count, size=16):
    return [slice(at, at + size) for at in range(0, count, size)]


def fold(x):
    return sum(x[at : at + 8] for at in range(8, x.shape[0], 8)) + x[0:8]


def pack_kernel(w1, w2, b1, one, other, b1_v, sems):
    feats = w1.shape[0]
    core = jnp.bitwise_and(lax.axis_index("dp"), 1)
    copies = [
        pltpu.make_async_copy(b1, b1_v, sems.at[0]),
        pltpu.make_async_copy(w1, one.at[0:feats], sems.at[1]),
        pltpu.make_async_copy(w2, one.at[feats : 2 * feats], sems.at[2]),
    ]
    own = [pltpu.make_async_copy(w, other.at[0:feats], sems.at[3]) for w in (w1, w2)]
    for copy in copies:
        copy.start()
    for j in range(2):
        pl.when(core == j)(own[j].start)
    copies[0].wait()
    rest = row(b1_v)
    place = lax.broadcasted_iota(jnp.int32, (16, feats), 0)
    bias = jnp.zeros((16, feats), F32)
    for j in range(3):
        term = rest.astype(BF).astype(F32)
        bias = jnp.where(place == j, term, bias)
        rest = rest - term
    bias = bias.astype(BF)
    one[2 * feats :, :] = bias
    other[feats:, :] = bias
    for copy in copies[1:]:
        copy.wait()
    for j in range(2):
        pl.when(core == j)(own[j].wait)


def attn_fwd_kernel(
    counts, post_s, postb_s, *refs
):
    sources, refs = refs[:14], refs[14:]
    a1_o, q_o, k_o, v_o, p_o, o_o, x1_o, u_o, a2_o, dy_o, mpre, mpost, mixb = refs[:13]
    held, (pad, attended_t, v_pad, probs, scaled_vt, sems) = refs[13:27], refs[27:]
    tok, og, n1g, n1b, qkvb, pre, post, postb, projb, gamma1, n2g, n2b, wqkv, wproj = held
    i = pl.program_id(0)
    images, patches, feats = tok.shape

    def image_copy(which, at):
        return pltpu.make_async_copy(
            sources[which].at[at], held[which].at[at], sems.at[which * images + at]
        )

    @pl.when(i == 0)
    def _():
        shared = [
            pltpu.make_async_copy(sources[j], held[j], sems.at[2 * images + j])
            for j in range(2, 14)
        ]
        image_copy(0, 0).start()
        image_copy(1, 0).start()
        for copy in shared:
            copy.start()
        for at in range(1, images):
            image_copy(0, at).start()
            image_copy(1, at).start()
        for copy in shared:
            copy.wait()

    image_copy(0, i).wait()
    image_copy(1, i).wait()
    rows = pad.shape[0]
    heads = mpre.shape[0]
    head_dim = feats // heads
    slots = q_o.shape[1]

    @pl.when(i == 0)
    def _():
        spread = (
            head_of_lane((heads, feats), 1, head_dim)
            == lax.broadcasted_iota(jnp.int32, (heads, feats), 0)
        ).astype(F32)
        mpre[...] = exact(pre[...], spread, ((1,), (0,))) * (head_dim**-0.5 * LOG2E)
        mpost[...] = exact(post[...], spread, ((0,), (0,)))
        mixb[...] = exact(row(postb), spread, ((1,), (0,)))
        probs[...] = jnp.zeros_like(probs)

    pad[patches:, :] = jnp.zeros((rows - patches, feats), F32)
    live = (lax.axis_index("mp") * images + i < counts[0]).astype(F32)
    pad[0:patches, :] = og[i].astype(F32) * live
    dy_o[0] = pad[...].astype(BF)
    pad[0:patches, :] = tok[i].astype(F32)
    gain, shift = row(n1g), row(n1b)
    for c in chunks(rows):
        n, _ = normalized(pad[c, :])
        a1_o[0, c, :] = (n * gain + shift).astype(BF)
    qkv = nn(a1_o[0], wqkv[...])
    bias = row(qkvb)
    q_o[0, rows:] = jnp.zeros((slots - rows, feats), BF)
    for c in chunks(rows):
        q, k, v = (
            qkv[c, j * feats : (j + 1) * feats] + bias[:, j * feats : (j + 1) * feats]
            for j in range(3)
        )
        q_o[0, c, :] = q.astype(BF)
        v_o[0, c, :] = v.astype(BF)
        k_o[0, c, :] = k.astype(BF)
    q2 = jnp.concatenate([q_o[0], q_o[0]], axis=1)
    v_pad[0:rows, :] = v_o[0]
    v_pad[rows:, :] = jnp.zeros((slots - rows, feats), BF)
    vt = v_pad[...].T
    tail = patches // 8 * 8
    inside = lax.broadcasted_iota(jnp.int32, (rows - tail, 128), 0) < patches - tail
    lanes = range(0, slots, 128)
    real = (lax.broadcasted_iota(jnp.int32, (slots, 128), 0) < patches).astype(BF)
    start = nn(vt, real)

    def logits(pair):
        parts = []
        for g in pair:
            for c in chunks(rows):
                scaled = k_o[0, c, :].astype(F32) * mpre[g : g + 1, :]
                hi = scaled.astype(BF)
                parts.append(jnp.concatenate([hi, (scaled - hi.astype(F32)).astype(BF)], axis=1))
        return nt(jnp.concatenate(parts, axis=0), q2)

    pairs = [(g, g + 1) for g in range(0, heads, 2)]
    upcoming = logits(pairs[0])
    for s, pair in enumerate(pairs):
        current = upcoming
        if s + 1 < len(pairs):
            upcoming = logits(pairs[s + 1])
        for j, g in enumerate(pair):
            for lane in lanes:
                x = current[j * rows : (j + 1) * rows, lane : lane + 128]
                x = jnp.concatenate([x[0:tail], jnp.where(inside, x[tail:], -1e30)], axis=0)
                e = jnp.exp2(x - jnp.max(x, axis=0, keepdims=True))
                inv = 1.0 / jnp.sum(e, axis=0, keepdims=True)
                probs[g * slots : g * slots + rows, lane : lane + 128] = (e * inv).astype(BF)
            p_o[0, g] = probs[g * slots : g * slots + rows, :]
    for c in chunks(feats):
        g = c.start // head_dim
        vc = vt[c].astype(F32)
        for h in range(heads):
            scaled_vt[c, h * slots : (h + 1) * slots] = (vc * post_s[g, h]).astype(BF)
    mixed = nn(scaled_vt[...], probs[...])
    for c in chunks(feats):
        first = start[c] * postb_s[c.start // head_dim]
        for lane in lanes:
            attended_t[c, lane : lane + 128] = (mixed[c, lane : lane + 128] + first).astype(BF)
    o_o[0] = attended_t[...].T[0:rows]
    product = nn(o_o[0], wproj[...])
    bias, scale, gain, shift = row(projb), row(gamma1), row(n2g), row(n2b)
    for c in chunks(rows):
        u = product[c] + bias
        x1 = pad[c, :] + scale * u
        u_o[0, c, :] = u
        x1_o[0, c, :] = x1
        n, _ = normalized(x1)
        a2_o[0, c, :] = (n * gain + shift).astype(BF)


def store_blocks(count, put):
    mine = lax.axis_index("dp")
    for core in range(2):

        @pl.when(jnp.bitwise_and(mine, 1) == core)
        def _(core=core):
            for b in range(count):
                place = jnp.bitwise_xor(jnp.int32(b >> 1), jnp.right_shift(mine, 1))
                put((b ^ core) & 1, place, b)


def mlp_units(a2, dfs, w1, b1, w2, hids, dzs, b1_o, units, use):
    size = a2.shape[0] // units
    width = w2.shape[0]
    lanes = 256
    places = [slice(u * size, (u + 1) * size) for u in range(units)]
    sums = {}

    def products(u):
        return nn(a2[places[u], :], w1[...]), nt(dfs[places[u], :], w2[...])

    upcoming = products(0)
    for u in range(units):
        z, grad_hidden = upcoming
        if u + 1 < units:
            upcoming = products(u + 1)
        for first in range(0, width, lanes):
            part = slice(first, first + lanes)
            bias = b1[:, part]
            for c in chunks(size):
                zc = z[c, part] + bias
                phi, slope = gelu_parts(zc)
                dz = (grad_hidden[c, part] * slope).astype(BF)
                at = slice(places[u].start + c.start, places[u].start + c.stop)
                hids[at, part] = (zc * phi).astype(BF)
                dzs[at, part] = dz
                more = fold(dz.astype(F32))
                sums[first] = sums[first] + more if first in sums else more
        use(places[u], nn(hids[places[u], :], w2[...]), nt(dzs[places[u], :], w1[...]))
    for first, value in sums.items():
        b1_o[:, first : first + lanes] = colsum(value)


def mlp_first_kernel(
    a2, dy, gamma2, w1_own, b1_own, w2_own, near,
    f_o, da2_o, grads, b1_o, a2t, dft,
    w1, w2, b1, hids, dzs, dfs,
):
    total, feats = f_o.shape
    w1[:, 0:feats] = w1_own[...]
    w1[:, feats:] = near[0:feats]
    w2[0:feats, :] = w2_own[...]
    w2[feats:, :] = near[feats : 2 * feats]
    b1[:, 0:feats] = row(b1_own)
    b1[:, feats:] = colsum(near[2 * feats : 2 * feats + 16].astype(F32))
    gain = row(gamma2)
    for c in chunks(total):
        dfs[c, :] = (dy[c, :].astype(F32) * gain).astype(BF)

    def use(rows, f, da2):
        f_o[rows, :] = f
        da2_o[rows, :] = da2

    mlp_units(a2, dfs, w1, b1, w2, hids, dzs, b1_o, 3, use)
    a2t[...] = a2[...].T
    dft[...] = dfs[...].T
    grads[0] = nn(a2t[...], dzs[...]).astype(BF).T
    down = nn(dft[...], hids[...]).astype(BF)
    for c in range(2):
        grads[1, c * feats : (c + 1) * feats, :] = down[:, c * feats : (c + 1) * feats]


def mlp_rest_kernel(
    counts, a2, dy, x1, u, o, f0, da20, near, far, grads, a2t, dft, wproj, gamma1, n2g, fc2b, gamma2,
    out_o, dx1_o, do_o, keep, send, b1_o, acc_o,
    w1, w2, b1, hids, dzs, dfs, dus, ups, downs, projs,
):
    total, feats = f0.shape
    images, patches = out_o.shape[:2]
    image_rows = total // images
    m_idx = lax.axis_index("mp")
    acc_o[...] = jnp.zeros_like(acc_o)
    for c in range(2):
        b1[:, c * feats : (c + 1) * feats] = colsum(near[c, feats : feats + 16].astype(F32))
    for core in range(2):

        @pl.when(jnp.bitwise_and(lax.axis_index("dp"), 1) == core)
        def _(core=core):
            first, second = (near, far) if core == 0 else (far, near)
            for c in range(2):
                w1[:, c * feats : (c + 1) * feats] = first[c, 0:feats]
                w2[c * feats : (c + 1) * feats, :] = second[c, 0:feats]

    gain2 = row(gamma2)
    bias, gain, scale = row(fc2b), row(n2g), row(gamma1)
    for c in chunks(total):
        dfs[c, :] = (dy[c, :].astype(F32) * gain2).astype(BF)

    def use(rows, f, da2):
        sums = [jnp.zeros((8, feats), F32) for _ in range(6)]
        for c in chunks(rows.stop - rows.start):
            at = slice(rows.start + c.start, rows.start + c.stop)
            fc = f[c] + f0[at, :] + bias
            dac = da2[c] + da20[at, :]
            x1c = x1[at, :]
            dyc = dy[at, :].astype(F32)
            n, r = normalized(x1c)
            dx1 = dyc + norm_back(dac, n, r, gain)
            dx1_o[at, :] = dx1
            du = (dx1 * scale).astype(BF)
            dus[at, :] = du
            image = at.start // image_rows
            first = at.start - image * image_rows
            live = (m_idx * images + image < counts[0]).astype(F32)
            out = ((x1c + gain2 * fc) * live).astype(BF)
            if first + 16 <= patches:
                out_o[image, first : first + 16, :] = out
            else:
                out_o[image, first:patches, :] = out[0 : patches - first]
            terms = (
                du.astype(F32), u[at, :] * dx1, dac * n, dac, dfs[at, :].astype(F32), fc * dyc,
            )
            sums = [s + fold(t) for s, t in zip(sums, terms)]
        for j in range(6):
            acc_o[j : j + 1, :] += colsum(sums[j])
        do = nt(dus[rows, :], wproj[...]).astype(BF)
        for at in range(0, rows.stop - rows.start, image_rows):
            image = (rows.start + at) // image_rows
            do_o[image, 0:image_rows] = do[at : at + image_rows]
            do_o[image, image_rows:] = jnp.zeros((do_o.shape[1] - image_rows, feats), BF)

    mlp_units(a2, dfs, w1, b1, w2, hids, dzs, b1_o, 3, use)
    ups[...] = nn(a2t[...], dzs[...]).astype(BF).T
    downs[...] = nn(dft[...], hids[...]).astype(BF)
    projs[...] = tn(dus[...], o[...]).astype(BF)
    count = 2 * keep.shape[0]
    size = feats // count
    outs = (keep, send)

    def put(which, place, b):
        out = outs[which]
        for c in range(2):
            part = slice(c * feats, (c + 1) * feats)
            up = slice(c * feats + b * size, c * feats + (b + 1) * size)
            down = slice(b * size, (b + 1) * size)
            pieces = (grads[0, up, :], grads[1, up, :])
            for j, piece in enumerate(pieces):
                out[place, (2 * c + j) * size : (2 * c + j + 1) * size, :] = piece
            pieces = (ups[up, :], downs[down, part])
            for j, piece in enumerate(pieces):
                out[place, (4 + 2 * c + j) * size : (5 + 2 * c + j) * size, :] = piece
        out[place, 8 * size : 9 * size, :] = projs[b * size : (b + 1) * size, :]

    store_blocks(count, put)


def attn_bwd_kernel(
    pre_s, do_r, q_r, k_r, v_r, p_r, dx1, tok, mpre, mpost, mixb, wqkv, n1g, *refs
):
    dqkv_o, in_o, acc_o, vgs, dls, dq_t, k_pad, scaled_kt, pad = refs[-9:]
    i = pl.program_id(0)
    slots, feats = do_r.shape[1:]
    patches = tok.shape[1]
    rows = k_r.shape[1]
    heads = mpre.shape[0]
    head_dim = feats // heads
    many = heads // 2
    half = many * rows

    @pl.when(i == 0)
    def _():
        acc_o[...] = jnp.zeros_like(acc_o)
        dls[...] = jnp.zeros_like(dls)
        k_pad[...] = jnp.zeros_like(k_pad)

    do_sum = jnp.zeros((8, feats), F32)
    for c in chunks(rows):
        vf = v_r[0, c, :].astype(F32)
        do_sum = do_sum + fold(do_r[0, c, :].astype(F32))
        for h in range(heads):
            vgs[h * rows + c.start : h * rows + c.stop, :] = (vf * mpost[h : h + 1, :]).astype(BF)
    do_sum = colsum(do_sum)
    q = q_r[0]
    do = do_r[0]
    k_pad[0:rows, :] = k_r[0]
    kt = k_pad[...].T
    for c in chunks(feats):
        g = c.start // head_dim
        kc = kt[c].astype(F32) * head_dim**-0.5
        for h in range(heads):
            scaled_kt[c, h * slots : (h + 1) * slots] = (kc * pre_s[h, g]).astype(BF)
    dps = [nt(vgs[s * half : (s + 1) * half, :], do) for s in range(2)]
    dvs = [nn(p_r[0, s * many : (s + 1) * many].reshape(half, slots), do) for s in range(2)]
    dks = []
    for h in range(heads):
        for lane in range(0, slots, 128):
            dp = dps[h // many][h % many * rows : (h % many + 1) * rows, lane : lane + 128]
            pf = p_r[0, h, :, lane : lane + 128].astype(F32)
            mean = jnp.sum(dp * pf, axis=0, keepdims=True) / jnp.sum(pf, axis=0, keepdims=True)
            dls[h * slots : h * slots + rows, lane : lane + 128] = (pf * (dp - mean)).astype(BF)
        if h % many == many - 1:
            mine = range(h + 1 - many, h + 1)
            parts = [dls[j * slots : j * slots + rows, :] for j in mine]
            dks.append(nn(jnp.concatenate(parts, axis=0), q))
    dq_t[...] = nn(scaled_kt[...], dls[...]).astype(BF)

    bias_row = mixb[...] * do_sum
    v_sum = jnp.zeros((8, feats), F32)
    dv_sum = jnp.zeros((8, feats), F32)
    sums = [jnp.zeros((8, feats), F32) for _ in range(heads)]
    for c in chunks(rows):
        vf = v_r[0, c, :].astype(F32)
        dv = bias_row
        for h in range(heads):
            at = (h % many) * rows
            this = dvs[h // many][at + c.start : at + c.stop]
            dv = dv + this * mpost[h : h + 1, :]
            sums[h] = sums[h] + fold(vf * this)
        if c.stop > patches:
            inside = lax.broadcasted_iota(jnp.int32, dv.shape, 0) < patches - c.start
            dv = jnp.where(inside, dv, 0.0)
            vf = jnp.where(inside, vf, 0.0)
        low = dv.astype(BF)
        dqkv_o[0, c, 2 * feats :] = low
        dv_sum = dv_sum + fold(low.astype(F32))
        v_sum = v_sum + fold(vf)
    for h in range(heads):
        acc_o[h : h + 1, :] += colsum(sums[h])
    acc_o[2 * heads : 2 * heads + 1, :] += do_sum * colsum(v_sum)
    acc_o[2 * heads + 10 : 2 * heads + 11, :] += colsum(dv_sum)

    dq = dq_t[...].T[0:rows]
    dqkv_o[0, :, 0:feats] = dq
    dk_sum = jnp.zeros((8, feats), F32)
    sums = [jnp.zeros((8, feats), F32) for _ in range(heads)]
    for c in chunks(rows):
        kf = k_r[0, c, :].astype(F32)
        dk = 0.0
        for h in range(heads):
            at = (h % many) * rows
            this = dks[h // many][at + c.start : at + c.stop]
            dk = dk + this * mpre[h : h + 1, :]
            sums[h] = sums[h] + fold(kf * this)
        low = (dk * (1.0 / LOG2E)).astype(BF)
        dqkv_o[0, c, feats : 2 * feats] = low
        dk_sum = dk_sum + fold(low.astype(F32))
    for h in range(heads):
        acc_o[heads + h : heads + h + 1, :] += colsum(sums[h])
    acc_o[2 * heads + 8 : 2 * heads + 9, :] += colsum(dq.astype(F32))
    acc_o[2 * heads + 9 : 2 * heads + 10, :] += colsum(dk_sum)

    pad[patches:, :] = jnp.zeros((rows - patches, feats), F32)
    pad[0:patches, :] = tok[0].astype(F32)
    da1 = nt(dqkv_o[0], wqkv[...])
    gain = row(n1g)
    sums = [jnp.zeros((8, feats), F32) for _ in range(2)]
    for c in chunks(rows):
        n, r = normalized(pad[c, :])
        cot = da1[c]
        grad = dx1[0, c, :] + norm_back(cot, n, r, gain)
        sums = [sums[0] + fold(cot * n), sums[1] + fold(cot)]
        if c.stop <= patches:
            in_o[0, c, :] = grad
        else:
            in_o[0, c.start : patches, :] = grad[0 : patches - c.start]
    for j in range(2):
        acc_o[2 * heads + 11 + j : 2 * heads + 12 + j, :] += colsum(sums[j])


def qkv_grad_kernel(heads, dqkv, *refs):
    accs = refs[:-8]
    a1, acc_mlp, b1_first, b1_rest, keep, send, small, grads = refs[-8:]
    feats = a1.shape[1]
    count = 2 * keep.shape[0]
    size = 3 * feats // count
    acc = accs[0][...]
    for other in accs[1:]:
        acc = acc + other[...]
    small[...] = jnp.zeros_like(small)
    small[0:2, :] = acc[2 * heads + 11 : 2 * heads + 13]
    small[2:8, :] = acc_mlp[0:6, :]
    small[8:11, :] = acc[2 * heads + 8 : 2 * heads + 11]
    head_dim = feats // heads
    lanes = 2 * heads * heads
    gather = (
        head_of_lane((feats, lanes), 0, head_dim)
        == lax.broadcasted_iota(jnp.int32, (feats, lanes), 1) % heads
    ).astype(F32)
    sums = exact(acc[0 : 2 * heads + 8], gather, ((1,), (0,)))
    place = head_of_lane((2 * heads, lanes), 1, heads) == lax.broadcasted_iota(
        jnp.int32, (2 * heads, lanes), 0
    )
    small[11:12, 0:lanes] = colsum(jnp.where(place, sums[0 : 2 * heads], 0.0))
    small[11:12, lanes : 2 * lanes] = sums[2 * heads : 2 * heads + 1]
    m_idx = lax.axis_index("mp")
    for c, ref in enumerate((b1_first, b1_first, b1_rest, b1_rest)):
        place = 12 + jnp.bitwise_xor(m_idx, c)
        small[pl.ds(place, 1), :] = ref[:, (c % 2) * feats : (c % 2 + 1) * feats]
    low = small[...].astype(BF)
    outs = (keep, send)

    grads[...] = tn(a1[...], dqkv[...]).astype(BF).T

    def put(which, place, b):
        outs[which][place, 0:size, :] = grads[b * size : (b + 1) * size, :]
        outs[which][place, size : size + 16, :] = low
        if outs[which].shape[1] > size + 16:
            outs[which][place, size + 16 :, :] = jnp.zeros_like(outs[which][place, size + 16 :, :])

    store_blocks(count, put)


def final_kernel(heads, size, many, *refs):
    parts = refs[0 : 1 + many]
    mlp_mine, got_z = refs[1 + many], refs[2 + many : 2 + 2 * many]
    qkv_o, qkvb_o, pre_o, post_o, postb_o, b1_o, *vecs_o, fc1_o, fc2_o, proj_o, held = refs[-18:]
    block = fc1_o.shape[0]
    outs = ((fc1_o, 0, 0), (fc2_o, 1, 1), (proj_o, 8, 2))
    for out, first, place in outs:
        total = mlp_mine[first * block : (first + 1) * block, :]
        for part in got_z:
            total = total + part[place * block : (place + 1) * block, :].astype(F32)
        out[...] = total
    d_idx = lax.axis_index("dp")
    m_idx = lax.axis_index("mp")
    quarter, feats = parts[0].shape
    for j, part in enumerate(parts):
        held[jnp.bitwise_xor(m_idx, j)] = part[...].astype(F32)
    total = held[...].reshape(-1, feats)
    qkv_o[...] = total[0:size]
    small = total[size : size + 16]

    def own(value, width, index):
        lanes = value.shape[1]
        return pltpu.roll(value, lax.rem(lanes - index * width, lanes), axis=1)[:, 0:width]

    width = vecs_o[0].shape[1]
    vecs = own(small[0:8], width, d_idx)
    for j, ref in enumerate(vecs_o):
        ref[...] = vecs[j : j + 1]
    flat = jnp.concatenate([small[8 + j : 9 + j] for j in range(3)], axis=1)
    qkvb_o[...] = own(jnp.broadcast_to(flat, (8, 3 * feats)), qkvb_o.shape[1], d_idx)[0:1]
    b1 = own(small[8:16], b1_o.shape[1], d_idx)[4:8]
    pick = lax.broadcasted_iota(jnp.int32, b1.shape, 0) == m_idx
    b1_o[...] = colsum(jnp.where(pick, b1, 0.0))
    mix = small[11:12]
    hh = heads * heads
    line = lax.broadcasted_iota(jnp.int32, (heads, hh), 0)
    lane = lax.broadcasted_iota(jnp.int32, (heads, hh), 1)
    fold = (
        lax.broadcasted_iota(jnp.int32, (hh, heads), 0) % heads
        == lax.broadcasted_iota(jnp.int32, (hh, heads), 1)
    ).astype(F32)
    head_dim = feats // heads

    def square(values):
        return exact(jnp.where(lane // heads == line, values, 0.0), fold, ((1,), (0,)))

    post_o[...] = square(mix[:, 0:hh]).T
    pre_o[...] = square(mix[:, hh : 2 * hh]) * (head_dim**-0.5)
    postb_o[...] = mix[:, 2 * hh : 2 * hh + heads]


def whole(shape):
    return pl.BlockSpec(shape, lambda i: (0,) * len(shape))


def each(shape, first=0, many=1):
    return pl.BlockSpec((many,) + shape[1:], lambda i: (i + first,) + (0,) * (len(shape) - 1))


SCALARS = pl.BlockSpec(memory_space=pltpu.SMEM)
IN_VMEM = pl.BlockSpec(memory_space=pltpu.VMEM)
IN_HBM = pl.BlockSpec(memory_space=pltpu.HBM)


def kept(a):
    return pltpu.with_memory_space_constraint(a, pltpu.HBM)


def sds(shape, dtype):
    return jax.ShapeDtypeStruct(shape, dtype)


def call(
    kernel, grid, ins, in_specs, outs, out_specs, scratch=(), flops=0, name=None, aliases=None
):
    size = lambda a: a.size * a.dtype.itemsize
    return pl.pallas_call(
        kernel,
        grid=grid,
        in_specs=in_specs,
        out_specs=out_specs,
        out_shape=outs,
        scratch_shapes=scratch,
        input_output_aliases=aliases or {},
        compiler_params=pltpu.CompilerParams(vmem_limit_bytes=VMEM_LIMIT),
        cost_estimate=pl.CostEstimate(
            flops=flops,
            bytes_accessed=sum(size(a) for a in ins) + sum(size(a) for a in outs),
            transcendentals=0,
        ),
        name=name,
    )(*ins)


def xor_perm(count, mask):
    return [(j, j ^ mask) for j in range(count)]


def dp_hops(dp):
    bits = dp.bit_length() - 1
    groups = []
    at = 1
    while at < bits:
        groups.append((at, min(2, bits - at)))
        at += groups[-1][1]
    return groups


def dp_scatter(value, dp):
    for at, many in dp_hops(dp):
        value = value.reshape((-1, 1 << many) + value.shape[1:])
        got = [
            lax.ppermute(value[:, j].astype(BF), "dp", xor_perm(dp, j << at))
            for j in range(1, 1 << many)
        ]
        value = value[:, 0] + sum(g.astype(F32) for g in got)
    return value.reshape(value.shape[-2:])


def per_device(
    dp, mp,
    tokens_in, image_counts, norm1_gain, norm1_bias, qkv_weight, qkv_bias,
    mix_pre, mix_post, mix_post_bias, proj_weight, proj_bias, gamma1,
    norm2_gain, norm2_bias, fc1_weight, fc1_bias, fc2_weight, fc2_bias, gamma2, out_grad,
):
    images, patches, feats = tokens_in.shape
    heads = mix_pre.shape[0]
    rows = -(-patches // 16) * 16
    slots = -(-patches // 128) * 128
    hidden = fc1_weight.shape[1]
    ins = [kept(a) for a in (fc1_weight, fc2_weight, fc1_bias)]
    outs = [sds((2 * feats + 16, hidden), BF), sds((feats + 16, hidden), BF)]
    one, other = call(
        pack_kernel,
        (1,),
        ins,
        [IN_HBM] * 3,
        outs,
        [whole(a.shape) for a in outs],
        [pltpu.VMEM(fc1_bias.shape, F32), pltpu.SemaphoreType.DMA((4,))],
        name="pack",
    )
    near_one = lax.ppermute(one, "mp", xor_perm(mp, 1))
    near = [lax.ppermute(other, "mp", xor_perm(mp, j)) for j in range(2, mp)]

    tok_rows = (images, rows, feats)
    slot_rows = (images, slots, feats)
    prob_shape = (images, heads, rows, slots)
    mix_shape = (heads, feats)
    ins = [
        image_counts, mix_post, mix_post_bias, tokens_in, out_grad, norm1_gain, norm1_bias, qkv_bias, mix_pre, mix_post,
        mix_post_bias, proj_bias, gamma1, norm2_gain, norm2_bias, qkv_weight, proj_weight,
    ]
    ins[3:] = [kept(a) for a in ins[3:]]
    a1, q, k, v, prob, o, x1, u, a2, dy, mpre, mpost, mixb = call(
        attn_fwd_kernel,
        (images,),
        ins,
        [SCALARS] * 3 + [IN_HBM] * 14,
        [
            sds(tok_rows, BF), sds(slot_rows, BF), sds(tok_rows, BF), sds(tok_rows, BF),
            sds(prob_shape, BF), sds(tok_rows, BF), sds(tok_rows, F32), sds(tok_rows, F32),
            sds(tok_rows, BF), sds(tok_rows, BF), sds(mix_shape, F32), sds(mix_shape, F32),
            sds((1, feats), F32),
        ],
        [each(s) for s in (tok_rows, slot_rows, tok_rows, tok_rows, prob_shape)]
        + [each(tok_rows)] * 5
        + [whole(mix_shape)] * 2
        + [whole((1, feats))],
        [pltpu.VMEM(a.shape, a.dtype) for a in ins[3:]]
        + [
            pltpu.VMEM((rows, feats), F32), pltpu.VMEM((feats, slots), BF),
            pltpu.VMEM((slots, feats), BF), pltpu.VMEM((heads * slots, slots), BF),
            pltpu.VMEM((feats, heads * slots), BF), pltpu.SemaphoreType.DMA((2 * images + 14,)),
        ],
        flops=images * 15 * 10**8,
        name="attn_fwd",
    )

    block = feats // dp
    total = images * rows
    flat = (total, feats)
    a2, dy, x1, u, o = (a.reshape(flat) for a in (a2, dy, x1, u, o))
    near_one, near, a2 = lax.optimization_barrier((near_one, near, a2))
    near = jnp.stack(near)
    far = lax.ppermute(near, "dp", xor_perm(dp, 1))
    ins = [a2, dy, gamma2, fc1_weight, fc1_bias, fc2_weight, near_one]
    wide = 2 * hidden
    grad_shape = (2, wide, feats)
    f0, da20, grads0, b1_0, a2t, dft = call(
        mlp_first_kernel,
        (),
        ins,
        [IN_VMEM] * len(ins),
        [
            sds(flat, F32), sds(flat, F32), sds(grad_shape, BF), sds((1, wide), F32),
            sds((feats, total), BF), sds((feats, total), BF),
        ],
        [IN_VMEM] * 6,
        [
            pltpu.VMEM((feats, wide), BF), pltpu.VMEM((wide, feats), BF),
            pltpu.VMEM((1, wide), F32), pltpu.VMEM((total, wide), BF),
            pltpu.VMEM((total, wide), BF), pltpu.VMEM(flat, BF),
        ],
        flops=images * 8 * 10**8,
        name="mlp_first",
    )

    grad_rows = 9 * block
    half_shape = (dp // 2, grad_rows, feats)
    ins = [
        image_counts, a2, dy, x1, u, o, f0, da20, near, far, grads0, a2t, dft, proj_weight, gamma1,
        norm2_gain, fc2_bias, gamma2,
    ]
    layer_out, dx1, do, keep, send, b1_1, acc_mlp = call(
        mlp_rest_kernel,
        (),
        ins,
        [SCALARS] + [IN_VMEM] * (len(ins) - 1),
        [
            sds(tokens_in.shape, BF), sds(flat, F32), sds(slot_rows, BF), sds(half_shape, BF),
            sds(half_shape, BF), sds((1, wide), F32), sds((8, feats), F32),
        ],
        [IN_VMEM] * 7,
        [
            pltpu.VMEM((feats, wide), BF), pltpu.VMEM((wide, feats), BF),
            pltpu.VMEM((1, wide), F32), pltpu.VMEM((total, wide), BF),
            pltpu.VMEM((total, wide), BF), pltpu.VMEM(flat, BF), pltpu.VMEM(flat, BF),
            pltpu.VMEM((wide, feats), BF), pltpu.VMEM((feats, wide), BF),
            pltpu.VMEM((feats, feats), BF),
        ],
        flops=images * 9 * 10**8,
        name="mlp_rest",
    )
    got = lax.ppermute(send, "dp", xor_perm(dp, 1))
    dx1 = dx1.reshape(tok_rows)

    shares = [1, images - 1] if images > 1 else [1]
    dqkv_shape = (images, rows, 3 * feats)
    carried, accs = [], []
    for s, share in enumerate(shares):
        first = sum(shares[:s])
        ins = [mix_pre, do, q, k, v, prob, dx1, tokens_in, mpre, mpost, mixb, qkv_weight, norm1_gain]
        *carried, acc = call(
            attn_bwd_kernel,
            (share,),
            ins + carried,
            [SCALARS]
            + [each(a.shape, first) for a in ins[1:8]]
            + [whole(a.shape) for a in ins[8:]]
            + [pl.BlockSpec(memory_space=pl.ANY)] * len(carried),
            [sds(dqkv_shape, BF), sds(tokens_in.shape, F32), sds((2 * heads + 16, feats), F32)],
            [
                each(dqkv_shape, first), each(tokens_in.shape, first),
                whole((2 * heads + 16, feats)),
            ],
            [
                pltpu.VMEM((heads * rows, feats), BF), pltpu.VMEM((heads * slots, slots), BF),
                pltpu.VMEM((feats, slots), BF), pltpu.VMEM((slots, feats), BF),
                pltpu.VMEM((feats, heads * slots), BF), pltpu.VMEM((rows, feats), F32),
            ],
            flops=share * 20 * 10**8,
            name="attn_bwd",
            aliases={len(ins): 0, len(ins) + 1: 1} if carried else None,
        )
        accs.append(acc)
        if s == 0:
            (keep, got), acc = lax.optimization_barrier(((keep, got), acc))
            mine = dp_scatter(keep.astype(F32) + got.astype(F32), dp)
            accs[0], do = lax.optimization_barrier((acc, do))
    dqkv, in_grad = carried
    mine, dqkv = lax.optimization_barrier((mine, dqkv))
    mlp_mine = mine
    low = mine.astype(BF)
    proj = low[8 * block :]
    got_z = [
        lax.ppermute(
            jnp.concatenate([low[2 * j * block : 2 * (j + 1) * block], proj]), "mp", xor_perm(mp, j)
        )
        for j in range(1, mp)
    ]

    q_block = 3 * feats // dp
    quarter = -(-(q_block + 16) // (8 * mp)) * 8
    half_shape = (dp // 2, mp * quarter, feats)
    ins = [dqkv.reshape(total, 3 * feats)] + accs + [a1.reshape(flat), acc_mlp, b1_0, b1_1]
    keep, send = call(
        functools.partial(qkv_grad_kernel, heads),
        (1,),
        ins,
        [whole(a.shape) for a in ins],
        [sds(half_shape, BF), sds(half_shape, BF)],
        [whole(half_shape), whole(half_shape)],
        [pltpu.VMEM((16, feats), F32), pltpu.VMEM((3 * feats, feats), BF)],
        flops=11 * 10**8,
        name="qkv_grad",
    )
    got = lax.ppermute(send, "dp", xor_perm(dp, 1))
    mine = dp_scatter(keep.astype(F32) + got.astype(F32), dp)
    m_idx = lax.axis_index("mp")

    def part(j):
        return lax.dynamic_slice_in_dim(mine, jnp.bitwise_xor(m_idx, j) * quarter, quarter)

    own = part(0)
    for j in range(1, mp):
        own = own + lax.ppermute(part(j).astype(BF), "mp", xor_perm(mp, j)).astype(F32)
    own = own.astype(BF)
    got = [lax.ppermute(own, "mp", xor_perm(mp, j)) for j in range(1, mp)]
    b1_size = hidden // dp
    ins = [own] + got + [mlp_mine] + got_z
    outs = [
        sds((q_block, feats), F32), sds((1, q_block), F32), sds((heads, heads), F32),
        sds((heads, heads), F32), sds((1, heads), F32), sds((1, b1_size), F32),
    ] + [sds((1, block), F32)] * 8 + [sds((block, feats), F32)] * 3
    qkvw, qkvb, pre, post, postb, b1g, *vecs, fc1g, fc2g, projg = call(
        functools.partial(final_kernel, heads, q_block, mp - 1),
        (1,),
        ins,
        [whole(a.shape) for a in ins],
        outs,
        [whole(a.shape) for a in outs],
        [pltpu.VMEM((mp, quarter, feats), F32)],
        name="final",
    )
    vecs = [a.reshape(-1) for a in vecs]
    return (
        layer_out,
        in_grad,
        vecs[0],
        vecs[1],
        qkvw.T,
        qkvb.reshape(-1),
        pre,
        post,
        postb.reshape(-1),
        projg.T,
        vecs[2],
        vecs[3],
        vecs[4],
        vecs[5],
        fc1g.T,
        b1g.reshape(-1),
        fc2g.T,
        vecs[6],
        vecs[7],
    )


def solution(mesh):
    tokens = P(("dp", "mp"), None, None)
    placed = (
        (tokens, P("dp")) + (P(),) * 12 + (P(None, "mp"), P("mp"), P("mp", None), P(), P(), tokens)
    )
    return jax.shard_map(
        functools.partial(per_device, mesh.shape["dp"], mesh.shape["mp"]),
        mesh=mesh,
        in_specs=placed,
        out_specs=(
            tokens, tokens, P("dp"), P("dp"), P(None, "dp"), P("dp"), P(), P(), P(),
            P(None, "dp"), P("dp"), P("dp"), P("dp"), P("dp"), P(None, ("mp", "dp")),
            P(("mp", "dp")), P("mp", "dp"), P("dp"), P("dp"),
        ),
        check_vma=False,
    )
```

```python
import functools

import jax
import jax.numpy as jnp
from jax import lax
from jax.experimental import pallas as pl
from jax.experimental.pallas import tpu as pltpu
from jax.sharding import PartitionSpec as P

BF = jnp.bfloat16
F32 = jnp.float32
LOG2E = 1.4426950408889634
EPS = 1e-06
VMEM_LIMIT = 28 * 1024 * 1024


def nn(a, b):
    return lax.dot_general(a, b, (((1,), (0,)), ((), ())), preferred_element_type=F32)


def nt(a, b):
    return lax.dot_general(a, b, (((1,), (1,)), ((), ())), preferred_element_type=F32)


def tn(a, b):
    return lax.dot_general(a, b, (((0,), (0,)), ((), ())), preferred_element_type=F32)


def exact(a, b, dims):
    return lax.dot_general(
        a, b, (dims, ((), ())), precision=lax.Precision.HIGHEST, preferred_element_type=F32
    )


def normalized(x):
    mean = jnp.mean(x, axis=-1, keepdims=True)
    c = x - mean
    r = lax.rsqrt(jnp.mean(c * c, axis=-1, keepdims=True) + EPS)
    return c * r, r


def norm_back(cot, n, r, gain):
    cg = cot * gain
    return r * (
        cg
        - jnp.mean(cg, axis=-1, keepdims=True)
        - n * jnp.mean(cg * n, axis=-1, keepdims=True)
    )


def colsum(x):
    return jnp.sum(x, axis=0, keepdims=True)


def split(x):
    hi = x.astype(BF)
    return jnp.concatenate([hi, (x - hi.astype(F32)).astype(BF)], axis=1)


def row(ref):
    return ref[...].reshape(1, ref.shape[0])


def inverse(x):
    near = pl.reciprocal(x, approx=True)
    return near * (2.0 - x * near)


def gelu_parts(z):
    e = jnp.exp2(z * z * (-0.5 * LOG2E))
    t = inverse(1.0 + jnp.abs(z) * (0.3275911 * 0.7071067811865476))
    poly = t * (
        0.5 * 0.254829592
        + t
        * (
            0.5 * -0.284496736
            + t * (0.5 * 1.421413741 + t * (0.5 * -1.453152027 + t * (0.5 * 1.061405429)))
        )
    )
    tail = poly * e
    phi = jnp.where(z >= 0, 1.0 - tail, tail)
    return phi, phi + z * e * 0.3989422804014327


def head_of_lane(shape, axis, head_dim):
    return lax.broadcasted_iota(jnp.int32, shape, axis) // head_dim


def chunks(count, size=16):
    return [slice(at, at + size) for at in range(0, count, size)]


def fold(x):
    return sum(x[at : at + 8] for at in range(8, x.shape[0], 8)) + x[0:8]


def pack_kernel(w1, w2, b1, one, other, b1_v, sems):
    feats = w1.shape[0]
    core = jnp.bitwise_and(lax.axis_index("dp"), 1)
    copies = [
        pltpu.make_async_copy(b1, b1_v, sems.at[0]),
        pltpu.make_async_copy(w1, one.at[0:feats], sems.at[1]),
        pltpu.make_async_copy(w2, one.at[feats : 2 * feats], sems.at[2]),
    ]
    own = [pltpu.make_async_copy(w, other.at[0:feats], sems.at[3]) for w in (w1, w2)]
    for copy in copies:
        copy.start()
    for j in range(2):
        pl.when(core == j)(own[j].start)
    copies[0].wait()
    rest = row(b1_v)
    place = lax.broadcasted_iota(jnp.int32, (16, feats), 0)
    bias = jnp.zeros((16, feats), F32)
    for j in range(3):
        term = rest.astype(BF).astype(F32)
        bias = jnp.where(place == j, term, bias)
        rest = rest - term
    bias = bias.astype(BF)
    one[2 * feats :, :] = bias
    other[feats:, :] = bias
    for copy in copies[1:]:
        copy.wait()
    for j in range(2):
        pl.when(core == j)(own[j].wait)


def attn_fwd_kernel(
    counts, post_s, postb_s, *refs
):
    sources, refs = refs[:14], refs[14:]
    a1_o, q_o, k_o, v_o, p_o, o_o, x1_o, u_o, a2_o, dy_o, mpre, mpost, mixb = refs[:13]
    held, (pad, kk, attended_t, probs, wide, logits, mixed, sems) = refs[13:27], refs[27:]
    tok, og, n1g, n1b, qkvb, pre, post, postb, projb, gamma1, n2g, n2b, wqkv, wproj = held
    i = pl.program_id(0)
    images, patches, feats = tok.shape

    def image_copy(which, at):
        return pltpu.make_async_copy(
            sources[which].at[at], held[which].at[at], sems.at[which * images + at]
        )

    @pl.when(i == 0)
    def _():
        shared = [
            pltpu.make_async_copy(sources[j], held[j], sems.at[2 * images + j])
            for j in range(2, 14)
        ]
        image_copy(0, 0).start()
        image_copy(1, 0).start()
        for copy in shared:
            copy.start()
        for at in range(1, images):
            image_copy(0, at).start()
            image_copy(1, at).start()
        for copy in shared:
            copy.wait()

    image_copy(0, i).wait()
    image_copy(1, i).wait()
    rows = pad.shape[0]
    heads = mpre.shape[0]
    head_dim = feats // heads
    slots = q_o.shape[1]

    @pl.when(i == 0)
    def _():
        spread = (
            head_of_lane((heads, feats), 1, head_dim)
            == lax.broadcasted_iota(jnp.int32, (heads, feats), 0)
        ).astype(F32)
        mpre[...] = exact(pre[...], spread, ((1,), (0,))) * (head_dim**-0.5 * LOG2E)
        mpost[...] = exact(post[...], spread, ((0,), (0,)))
        mixb[...] = exact(row(postb), spread, ((1,), (0,)))

    pad[patches:, :] = jnp.zeros((rows - patches, feats), F32)
    live = (lax.axis_index("mp") * images + i < counts[0]).astype(F32)
    pad[0:patches, :] = og[i].astype(F32) * live
    dy_o[0] = pad[...].astype(BF)
    pad[0:patches, :] = tok[i].astype(F32)
    gain, shift = row(n1g), row(n1b)
    for c in chunks(rows):
        n, _ = normalized(pad[c, :])
        a1_o[0, c, :] = (n * gain + shift).astype(BF)
    wide[...] = nn(a1_o[0], wqkv[...])
    bias = row(qkvb)
    q_o[0, rows:] = jnp.zeros((slots - rows, feats), BF)
    for c in chunks(rows):
        q, k, v = (
            wide[c, j * feats : (j + 1) * feats] + bias[:, j * feats : (j + 1) * feats]
            for j in range(3)
        )
        q_o[0, c, :] = q.astype(BF)
        v_o[0, c, :] = v.astype(BF)
        k = k.astype(BF)
        k_o[0, c, :] = k
        kf = k.astype(F32)
        for g in range(heads):
            at = slice(g * rows + c.start, g * rows + c.stop)
            scaled = kf * mpre[g : g + 1, :]
            hi = scaled.astype(BF)
            kk[at, 0:feats] = hi
            kk[at, feats:] = (scaled - hi.astype(F32)).astype(BF)
    q2 = jnp.concatenate([q_o[0], q_o[0]], axis=1)
    vt = v_o[0].T
    many = heads // 2
    half = many * rows
    tail = patches // 8 * 8
    inside = lax.broadcasted_iota(jnp.int32, (rows - tail, 128), 0) < patches - tail
    real = (lax.broadcasted_iota(jnp.int32, (rows, 128), 0) < patches).astype(BF)
    start = nn(vt, real)
    for s in range(2):
        part = slice(s * half, (s + 1) * half)
        logits[part, :] = nt(kk[part, :], q2)
    for g in range(heads):
        for lane in range(0, slots, 128):
            x = logits[g * rows : (g + 1) * rows, lane : lane + 128]
            x = jnp.concatenate([x[0:tail], jnp.where(inside, x[tail:], -1e30)], axis=0)
            e = jnp.exp2(x - jnp.max(x, axis=0, keepdims=True))
            inv = 1.0 / jnp.sum(e, axis=0, keepdims=True)
            p = (e * inv).astype(BF)
            probs[g * rows : (g + 1) * rows, lane : lane + 128] = p
            p_o[0, g, :, lane : lane + 128] = p
        mixed[g] = nn(vt, probs[g * rows : (g + 1) * rows, :])
    for c in chunks(feats):
        g = c.start // head_dim
        first = start[c] * postb_s[g]
        for lane in range(0, slots, 128):
            total = first
            for h in range(heads):
                total = total + mixed[h, c, lane : lane + 128] * post_s[g, h]
            attended_t[c, lane : lane + 128] = total.astype(BF)
    o_o[0] = attended_t[...].T[0:rows]
    wide[:, 0:feats] = nn(o_o[0], wproj[...])
    bias, scale, gain, shift = row(projb), row(gamma1), row(n2g), row(n2b)
    for c in chunks(rows):
        u = wide[c, 0:feats] + bias
        x1 = pad[c, :] + scale * u
        u_o[0, c, :] = u
        x1_o[0, c, :] = x1
        n, _ = normalized(x1)
        a2_o[0, c, :] = (n * gain + shift).astype(BF)


def store_blocks(count, put):
    mine = lax.axis_index("dp")
    for core in range(2):

        @pl.when(jnp.bitwise_and(mine, 1) == core)
        def _(core=core):
            for b in range(count):
                place = jnp.bitwise_xor(jnp.int32(b >> 1), jnp.right_shift(mine, 1))
                put((b ^ core) & 1, place, b)


def mlp_units(a2, dfs, w1, b1, w2, hids, dzs, zs, ghs, b1_o, units, store, use):
    size = a2.shape[0] // units
    width = w2.shape[0]
    lanes = 256
    places = [slice(u * size, (u + 1) * size) for u in range(units)]
    sums = {}

    def products(u):
        zs[u % 2] = nn(a2[places[u], :], w1[...])
        ghs[u % 2] = nt(dfs[places[u], :], w2[...])

    products(0)
    for u in range(units):
        if u + 1 < units:
            products(u + 1)
        for first in range(0, width, lanes):
            part = slice(first, first + lanes)
            bias = b1[:, part]
            for c in chunks(size):
                zc = zs[u % 2, c, part] + bias
                phi, slope = gelu_parts(zc)
                dz = (ghs[u % 2, c, part] * slope).astype(BF)
                at = slice(places[u].start + c.start, places[u].start + c.stop)
                hids[at, part] = (zc * phi).astype(BF)
                dzs[at, part] = dz
                more = fold(dz.astype(F32))
                sums[first] = sums[first] + more if first in sums else more
        store(places[u], nn(hids[places[u], :], w2[...]), nt(dzs[places[u], :], w1[...]))
        if u > 0:
            use(places[u - 1])
    use(places[units - 1])
    for first, value in sums.items():
        b1_o[:, first : first + lanes] = colsum(value)


def mlp_first_kernel(
    a2, dy, gamma2, w1_own, b1_own, w2_own, near,
    f_o, da2_o, grads, b1_o, a2t, dft,
    w1, w2, b1, hids, dzs, dfs, zs, ghs,
):
    total, feats = f_o.shape
    w1[:, 0:feats] = w1_own[...]
    w1[:, feats:] = near[0:feats]
    w2[0:feats, :] = w2_own[...]
    w2[feats:, :] = near[feats : 2 * feats]
    b1[:, 0:feats] = row(b1_own)
    b1[:, feats:] = colsum(near[2 * feats : 2 * feats + 16].astype(F32))
    gain = row(gamma2)
    for c in chunks(total):
        dfs[c, :] = (dy[c, :].astype(F32) * gain).astype(BF)

    def store(rows, f, da2):
        f_o[rows, :] = f
        da2_o[rows, :] = da2

    mlp_units(a2, dfs, w1, b1, w2, hids, dzs, zs, ghs, b1_o, 3, store, lambda rows: None)
    a2t[...] = a2[...].T
    dft[...] = dfs[...].T
    grads[0] = nn(a2t[...], dzs[...]).astype(BF).T
    down = nn(dft[...], hids[...]).astype(BF)
    for c in range(2):
        grads[1, c * feats : (c + 1) * feats, :] = down[:, c * feats : (c + 1) * feats]


def mlp_rest_kernel(
    counts, a2, dy, x1, u, o, f0, da20, near, far, grads, a2t, dft, wproj, gamma1, n2g, fc2b, gamma2,
    out_o, dx1_o, do_o, keep, send, b1_o, acc_o,
    w1, w2, b1, hids, dzs, dfs, zs, ghs, fs, da2s, dus, ups, downs, projs,
):
    total, feats = f0.shape
    images, patches = out_o.shape[:2]
    image_rows = total // images
    m_idx = lax.axis_index("mp")
    acc_o[...] = jnp.zeros_like(acc_o)
    for c in range(2):
        b1[:, c * feats : (c + 1) * feats] = colsum(near[c, feats : feats + 16].astype(F32))
    for core in range(2):

        @pl.when(jnp.bitwise_and(lax.axis_index("dp"), 1) == core)
        def _(core=core):
            first, second = (near, far) if core == 0 else (far, near)
            for c in range(2):
                w1[:, c * feats : (c + 1) * feats] = first[c, 0:feats]
                w2[c * feats : (c + 1) * feats, :] = second[c, 0:feats]

    gain2 = row(gamma2)
    bias, gain, scale = row(fc2b), row(n2g), row(gamma1)
    for c in chunks(total):
        dfs[c, :] = (dy[c, :].astype(F32) * gain2).astype(BF)

    def store(rows, f, da2):
        fs[rows, :] = f
        da2s[rows, :] = da2

    def use(rows):
        sums = [jnp.zeros((8, feats), F32) for _ in range(6)]
        for c in chunks(rows.stop - rows.start):
            at = slice(rows.start + c.start, rows.start + c.stop)
            fc = fs[at, :] + f0[at, :] + bias
            dac = da2s[at, :] + da20[at, :]
            x1c = x1[at, :]
            dyc = dy[at, :].astype(F32)
            n, r = normalized(x1c)
            dx1 = dyc + norm_back(dac, n, r, gain)
            dx1_o[at, :] = dx1
            du = (dx1 * scale).astype(BF)
            dus[at, :] = du
            image = at.start // image_rows
            first = at.start - image * image_rows
            live = (m_idx * images + image < counts[0]).astype(F32)
            out = ((x1c + gain2 * fc) * live).astype(BF)
            if first + 16 <= patches:
                out_o[image, first : first + 16, :] = out
            else:
                out_o[image, first:patches, :] = out[0 : patches - first]
            terms = (
                du.astype(F32), u[at, :] * dx1, dac * n, dac, dfs[at, :].astype(F32), fc * dyc,
            )
            sums = [s + fold(t) for s, t in zip(sums, terms)]
        for j in range(6):
            acc_o[j : j + 1, :] += colsum(sums[j])
        do = nt(dus[rows, :], wproj[...]).astype(BF)
        for at in range(0, rows.stop - rows.start, image_rows):
            image = (rows.start + at) // image_rows
            do_o[image, 0:image_rows] = do[at : at + image_rows]
            do_o[image, image_rows:] = jnp.zeros((do_o.shape[1] - image_rows, feats), BF)

    mlp_units(a2, dfs, w1, b1, w2, hids, dzs, zs, ghs, b1_o, 3, store, use)
    ups[...] = nn(a2t[...], dzs[...]).astype(BF).T
    downs[...] = nn(dft[...], hids[...]).astype(BF)
    projs[...] = tn(dus[...], o[...]).astype(BF)
    count = 2 * keep.shape[0]
    size = feats // count
    outs = (keep, send)

    def put(which, place, b):
        out = outs[which]
        for c in range(2):
            part = slice(c * feats, (c + 1) * feats)
            up = slice(c * feats + b * size, c * feats + (b + 1) * size)
            down = slice(b * size, (b + 1) * size)
            pieces = (grads[0, up, :], grads[1, up, :])
            for j, piece in enumerate(pieces):
                out[place, (2 * c + j) * size : (2 * c + j + 1) * size, :] = piece
            pieces = (ups[up, :], downs[down, part])
            for j, piece in enumerate(pieces):
                out[place, (4 + 2 * c + j) * size : (5 + 2 * c + j) * size, :] = piece
        out[place, 8 * size : 9 * size, :] = projs[b * size : (b + 1) * size, :]

    store_blocks(count, put)


def attn_bwd_kernel(
    pre_s, do_r, q_r, k_r, v_r, p_r, dx1, tok, mpre, mpost, mixb, wqkv, n1g, *refs
):
    dqkv_o, in_o, acc_o, vgs, dls, dq_t, dps, dvs, dks, dqs, da1, pad = refs[-12:]
    i = pl.program_id(0)
    slots, feats = do_r.shape[1:]
    patches = tok.shape[1]
    rows = k_r.shape[1]
    heads = mpre.shape[0]
    head_dim = feats // heads
    many = heads // 2
    half = many * rows

    @pl.when(i == 0)
    def _():
        acc_o[...] = jnp.zeros_like(acc_o)

    do_sum = jnp.zeros((8, feats), F32)
    for c in chunks(rows):
        vf = v_r[0, c, :].astype(F32)
        do_sum = do_sum + fold(do_r[0, c, :].astype(F32))
        for h in range(heads):
            vgs[h * rows + c.start : h * rows + c.stop, :] = (vf * mpost[h : h + 1, :]).astype(BF)
    do_sum = colsum(do_sum)
    q = q_r[0]
    do = do_r[0]
    kt = k_r[0].T
    parts = [slice(s * half, (s + 1) * half) for s in range(2)]
    for part in parts:
        dps[part, :] = nt(vgs[part, :], do)
    for s, part in enumerate(parts):
        dvs[part, :] = nn(p_r[0, s * many : (s + 1) * many].reshape(half, slots), do)
    for s, part in enumerate(parts):
        for h in range(s * many, (s + 1) * many):
            at = slice(h * rows, (h + 1) * rows)
            for lane in range(0, slots, 128):
                dp = dps[at, lane : lane + 128]
                pf = p_r[0, h, :, lane : lane + 128].astype(F32)
                mean = jnp.sum(dp * pf, axis=0, keepdims=True) / jnp.sum(pf, axis=0, keepdims=True)
                dls[at, lane : lane + 128] = (pf * (dp - mean)).astype(BF)
            dqs[h] = nn(kt, dls[at, :])
        dks[part, :] = nn(dls[part, :], q)

    bias_row = mixb[...] * do_sum
    v_sum = jnp.zeros((8, feats), F32)
    dv_sum = jnp.zeros((8, feats), F32)
    sums = [jnp.zeros((8, feats), F32) for _ in range(heads)]
    for c in chunks(rows):
        vf = v_r[0, c, :].astype(F32)
        dv = bias_row
        for h in range(heads):
            this = dvs[h * rows + c.start : h * rows + c.stop, :]
            dv = dv + this * mpost[h : h + 1, :]
            sums[h] = sums[h] + fold(vf * this)
        if c.stop > patches:
            inside = lax.broadcasted_iota(jnp.int32, dv.shape, 0) < patches - c.start
            dv = jnp.where(inside, dv, 0.0)
            vf = jnp.where(inside, vf, 0.0)
        low = dv.astype(BF)
        dqkv_o[0, c, 2 * feats :] = low
        dv_sum = dv_sum + fold(low.astype(F32))
        v_sum = v_sum + fold(vf)
    for h in range(heads):
        acc_o[h : h + 1, :] += colsum(sums[h])
    acc_o[2 * heads : 2 * heads + 1, :] += do_sum * colsum(v_sum)
    acc_o[2 * heads + 10 : 2 * heads + 11, :] += colsum(dv_sum)

    for c in chunks(feats):
        g = c.start // head_dim
        for lane in range(0, slots, 128):
            total = 0.0
            for h in range(heads):
                total = total + dqs[h, c, lane : lane + 128] * pre_s[h, g]
            dq_t[c, lane : lane + 128] = (total * head_dim**-0.5).astype(BF)
    dq = dq_t[...].T[0:rows]
    dqkv_o[0, :, 0:feats] = dq
    dk_sum = jnp.zeros((8, feats), F32)
    sums = [jnp.zeros((8, feats), F32) for _ in range(heads)]
    for c in chunks(rows):
        kf = k_r[0, c, :].astype(F32)
        dk = 0.0
        for h in range(heads):
            this = dks[h * rows + c.start : h * rows + c.stop, :]
            dk = dk + this * mpre[h : h + 1, :]
            sums[h] = sums[h] + fold(kf * this)
        low = (dk * (1.0 / LOG2E)).astype(BF)
        dqkv_o[0, c, feats : 2 * feats] = low
        dk_sum = dk_sum + fold(low.astype(F32))
    for h in range(heads):
        acc_o[heads + h : heads + h + 1, :] += colsum(sums[h])
    acc_o[2 * heads + 8 : 2 * heads + 9, :] += colsum(dq.astype(F32))
    acc_o[2 * heads + 9 : 2 * heads + 10, :] += colsum(dk_sum)

    pad[patches:, :] = jnp.zeros((rows - patches, feats), F32)
    pad[0:patches, :] = tok[0].astype(F32)
    da1[...] = nt(dqkv_o[0], wqkv[...])
    gain = row(n1g)
    sums = [jnp.zeros((8, feats), F32) for _ in range(2)]
    for c in chunks(rows):
        n, r = normalized(pad[c, :])
        cot = da1[c, :]
        grad = dx1[0, c, :] + norm_back(cot, n, r, gain)
        sums = [sums[0] + fold(cot * n), sums[1] + fold(cot)]
        if c.stop <= patches:
            in_o[0, c, :] = grad
        else:
            in_o[0, c.start : patches, :] = grad[0 : patches - c.start]
    for j in range(2):
        acc_o[2 * heads + 11 + j : 2 * heads + 12 + j, :] += colsum(sums[j])


def qkv_grad_kernel(heads, dqkv, *refs):
    accs = refs[:-8]
    a1, acc_mlp, b1_first, b1_rest, keep, send, small, grads = refs[-8:]
    feats = a1.shape[1]
    count = 2 * keep.shape[0]
    size = 3 * feats // count
    acc = accs[0][...]
    for other in accs[1:]:
        acc = acc + other[...]
    small[...] = jnp.zeros_like(small)
    small[0:2, :] = acc[2 * heads + 11 : 2 * heads + 13]
    small[2:8, :] = acc_mlp[0:6, :]
    small[8:11, :] = acc[2 * heads + 8 : 2 * heads + 11]
    head_dim = feats // heads
    lanes = 2 * heads * heads
    gather = (
        head_of_lane((feats, lanes), 0, head_dim)
        == lax.broadcasted_iota(jnp.int32, (feats, lanes), 1) % heads
    ).astype(F32)
    sums = exact(acc[0 : 2 * heads + 8], gather, ((1,), (0,)))
    place = head_of_lane((2 * heads, lanes), 1, heads) == lax.broadcasted_iota(
        jnp.int32, (2 * heads, lanes), 0
    )
    small[11:12, 0:lanes] = colsum(jnp.where(place, sums[0 : 2 * heads], 0.0))
    small[11:12, lanes : 2 * lanes] = sums[2 * heads : 2 * heads + 1]
    m_idx = lax.axis_index("mp")
    for c, ref in enumerate((b1_first, b1_first, b1_rest, b1_rest)):
        place = 12 + jnp.bitwise_xor(m_idx, c)
        small[pl.ds(place, 1), :] = ref[:, (c % 2) * feats : (c % 2 + 1) * feats]
    low = small[...].astype(BF)
    outs = (keep, send)

    grads[...] = tn(a1[...], dqkv[...]).astype(BF).T

    def put(which, place, b):
        outs[which][place, 0:size, :] = grads[b * size : (b + 1) * size, :]
        outs[which][place, size:, :] = low

    store_blocks(count, put)


def final_kernel(heads, size, many, *refs):
    mine, got = refs[0], refs[1 : 1 + many]
    mlp_mine, got_z = refs[1 + many], refs[2 + many : 2 + 2 * many]
    qkv_o, qkvb_o, pre_o, post_o, postb_o, b1_o, *vecs_o, fc1_o, fc2_o, proj_o = refs[-17:]
    block = fc1_o.shape[0]
    outs = ((fc1_o, 0, 0), (fc2_o, 1, 1), (proj_o, 8, 2))
    for out, first, place in outs:
        total = mlp_mine[first * block : (first + 1) * block, :]
        for part in got_z:
            total = total + part[place * block : (place + 1) * block, :].astype(F32)
        out[...] = total
    d_idx = lax.axis_index("dp")
    m_idx = lax.axis_index("mp")
    total = mine[...]
    for part in got:
        total = total + part[...].astype(F32)
    feats = total.shape[1]
    qkv_o[...] = total[0:size]
    small = total[size:]

    def own(value, width, index):
        lanes = value.shape[1]
        return pltpu.roll(value, lax.rem(lanes - index * width, lanes), axis=1)[:, 0:width]

    width = vecs_o[0].shape[1]
    vecs = own(small[0:8], width, d_idx)
    for j, ref in enumerate(vecs_o):
        ref[...] = vecs[j : j + 1]
    flat = jnp.concatenate([small[8 + j : 9 + j] for j in range(3)], axis=1)
    qkvb_o[...] = own(jnp.broadcast_to(flat, (8, 3 * feats)), qkvb_o.shape[1], d_idx)[0:1]
    b1 = own(small[8:16], b1_o.shape[1], d_idx)[4:8]
    pick = lax.broadcasted_iota(jnp.int32, b1.shape, 0) == m_idx
    b1_o[...] = colsum(jnp.where(pick, b1, 0.0))
    mix = small[11:12]
    hh = heads * heads
    line = lax.broadcasted_iota(jnp.int32, (heads, hh), 0)
    lane = lax.broadcasted_iota(jnp.int32, (heads, hh), 1)
    fold = (
        lax.broadcasted_iota(jnp.int32, (hh, heads), 0) % heads
        == lax.broadcasted_iota(jnp.int32, (hh, heads), 1)
    ).astype(F32)
    head_dim = feats // heads

    def square(values):
        return exact(jnp.where(lane // heads == line, values, 0.0), fold, ((1,), (0,)))

    post_o[...] = square(mix[:, 0:hh]).T
    pre_o[...] = square(mix[:, hh : 2 * hh]) * (head_dim**-0.5)
    postb_o[...] = mix[:, 2 * hh : 2 * hh + heads]


def whole(shape):
    return pl.BlockSpec(shape, lambda i: (0,) * len(shape))


def each(shape, first=0, many=1):
    return pl.BlockSpec((many,) + shape[1:], lambda i: (i + first,) + (0,) * (len(shape) - 1))


SCALARS = pl.BlockSpec(memory_space=pltpu.SMEM)
IN_VMEM = pl.BlockSpec(memory_space=pltpu.VMEM)
IN_HBM = pl.BlockSpec(memory_space=pltpu.HBM)


def kept(a):
    return pltpu.with_memory_space_constraint(a, pltpu.HBM)


def sds(shape, dtype):
    return jax.ShapeDtypeStruct(shape, dtype)


def call(
    kernel, grid, ins, in_specs, outs, out_specs, scratch=(), flops=0, name=None, aliases=None
):
    size = lambda a: a.size * a.dtype.itemsize
    return pl.pallas_call(
        kernel,
        grid=grid,
        in_specs=in_specs,
        out_specs=out_specs,
        out_shape=outs,
        scratch_shapes=scratch,
        input_output_aliases=aliases or {},
        compiler_params=pltpu.CompilerParams(vmem_limit_bytes=VMEM_LIMIT),
        cost_estimate=pl.CostEstimate(
            flops=flops,
            bytes_accessed=sum(size(a) for a in ins) + sum(size(a) for a in outs),
            transcendentals=0,
        ),
        name=name,
    )(*ins)


def xor_perm(count, mask):
    return [(j, j ^ mask) for j in range(count)]


def dp_hops(dp):
    bits = dp.bit_length() - 1
    groups = []
    at = 1
    while at < bits:
        groups.append((at, min(2, bits - at)))
        at += groups[-1][1]
    return groups


def dp_scatter(value, dp):
    for at, many in dp_hops(dp):
        value = value.reshape((-1, 1 << many) + value.shape[1:])
        got = [
            lax.ppermute(value[:, j].astype(BF), "dp", xor_perm(dp, j << at))
            for j in range(1, 1 << many)
        ]
        value = value[:, 0] + sum(g.astype(F32) for g in got)
    return value.reshape(value.shape[-2:])


def per_device(
    dp, mp,
    tokens_in, image_counts, norm1_gain, norm1_bias, qkv_weight, qkv_bias,
    mix_pre, mix_post, mix_post_bias, proj_weight, proj_bias, gamma1,
    norm2_gain, norm2_bias, fc1_weight, fc1_bias, fc2_weight, fc2_bias, gamma2, out_grad,
):
    images, patches, feats = tokens_in.shape
    heads = mix_pre.shape[0]
    rows = -(-patches // 16) * 16
    slots = -(-patches // 128) * 128
    hidden = fc1_weight.shape[1]
    ins = [kept(a) for a in (fc1_weight, fc2_weight, fc1_bias)]
    outs = [sds((2 * feats + 16, hidden), BF), sds((feats + 16, hidden), BF)]
    one, other = call(
        pack_kernel,
        (1,),
        ins,
        [IN_HBM] * 3,
        outs,
        [whole(a.shape) for a in outs],
        [pltpu.VMEM(fc1_bias.shape, F32), pltpu.SemaphoreType.DMA((4,))],
        name="pack",
    )
    near_one = lax.ppermute(one, "mp", xor_perm(mp, 1))
    near = [lax.ppermute(other, "mp", xor_perm(mp, j)) for j in range(2, mp)]

    tok_rows = (images, rows, feats)
    slot_rows = (images, slots, feats)
    prob_shape = (images, heads, rows, slots)
    mix_shape = (heads, feats)
    ins = [
        image_counts, mix_post, mix_post_bias, tokens_in, out_grad, norm1_gain, norm1_bias, qkv_bias, mix_pre, mix_post,
        mix_post_bias, proj_bias, gamma1, norm2_gain, norm2_bias, qkv_weight, proj_weight,
    ]
    ins[3:] = [kept(a) for a in ins[3:]]
    a1, q, k, v, prob, o, x1, u, a2, dy, mpre, mpost, mixb = call(
        attn_fwd_kernel,
        (images,),
        ins,
        [SCALARS] * 3 + [IN_HBM] * 14,
        [
            sds(tok_rows, BF), sds(slot_rows, BF), sds(tok_rows, BF), sds(tok_rows, BF),
            sds(prob_shape, BF), sds(tok_rows, BF), sds(tok_rows, F32), sds(tok_rows, F32),
            sds(tok_rows, BF), sds(tok_rows, BF), sds(mix_shape, F32), sds(mix_shape, F32),
            sds((1, feats), F32),
        ],
        [each(s) for s in (tok_rows, slot_rows, tok_rows, tok_rows, prob_shape)]
        + [each(tok_rows)] * 5
        + [whole(mix_shape)] * 2
        + [whole((1, feats))],
        [pltpu.VMEM(a.shape, a.dtype) for a in ins[3:]]
        + [
            pltpu.VMEM((rows, feats), F32), pltpu.VMEM((heads * rows, 2 * feats), BF),
            pltpu.VMEM((feats, slots), BF), pltpu.VMEM((heads * rows, slots), BF),
            pltpu.VMEM((rows, 3 * feats), F32), pltpu.VMEM((heads * rows, slots), F32),
            pltpu.VMEM((heads, feats, slots), F32), pltpu.SemaphoreType.DMA((2 * images + 14,)),
        ],
        flops=images * 15 * 10**8,
        name="attn_fwd",
    )

    block = feats // dp
    total = images * rows
    flat = (total, feats)
    a2, dy, x1, u, o = (a.reshape(flat) for a in (a2, dy, x1, u, o))
    near_one, near, a2 = lax.optimization_barrier((near_one, near, a2))
    near = jnp.stack(near)
    far = lax.ppermute(near, "dp", xor_perm(dp, 1))
    ins = [a2, dy, gamma2, fc1_weight, fc1_bias, fc2_weight, near_one]
    wide = 2 * hidden
    grad_shape = (2, wide, feats)
    f0, da20, grads0, b1_0, a2t, dft = call(
        mlp_first_kernel,
        (),
        ins,
        [IN_VMEM] * len(ins),
        [
            sds(flat, F32), sds(flat, F32), sds(grad_shape, BF), sds((1, wide), F32),
            sds((feats, total), BF), sds((feats, total), BF),
        ],
        [IN_VMEM] * 6,
        [
            pltpu.VMEM((feats, wide), BF), pltpu.VMEM((wide, feats), BF),
            pltpu.VMEM((1, wide), F32), pltpu.VMEM((total, wide), BF),
            pltpu.VMEM((total, wide), BF), pltpu.VMEM(flat, BF),
            pltpu.VMEM((2, total // 3, wide), F32), pltpu.VMEM((2, total // 3, wide), F32),
        ],
        flops=images * 8 * 10**8,
        name="mlp_first",
    )

    grad_rows = 9 * block
    half_shape = (dp // 2, grad_rows, feats)
    ins = [
        image_counts, a2, dy, x1, u, o, f0, da20, near, far, grads0, a2t, dft, proj_weight, gamma1,
        norm2_gain, fc2_bias, gamma2,
    ]
    layer_out, dx1, do, keep, send, b1_1, acc_mlp = call(
        mlp_rest_kernel,
        (),
        ins,
        [SCALARS] + [IN_VMEM] * (len(ins) - 1),
        [
            sds(tokens_in.shape, BF), sds(flat, F32), sds(slot_rows, BF), sds(half_shape, BF),
            sds(half_shape, BF), sds((1, wide), F32), sds((8, feats), F32),
        ],
        [IN_VMEM] * 7,
        [
            pltpu.VMEM((feats, wide), BF), pltpu.VMEM((wide, feats), BF),
            pltpu.VMEM((1, wide), F32), pltpu.VMEM((total, wide), BF),
            pltpu.VMEM((total, wide), BF), pltpu.VMEM(flat, BF),
            pltpu.VMEM((2, total // 3, wide), F32), pltpu.VMEM((2, total // 3, wide), F32),
            pltpu.VMEM(flat, F32), pltpu.VMEM(flat, F32), pltpu.VMEM(flat, BF),
            pltpu.VMEM((wide, feats), BF), pltpu.VMEM((feats, wide), BF),
            pltpu.VMEM((feats, feats), BF),
        ],
        flops=images * 9 * 10**8,
        name="mlp_rest",
    )
    got = lax.ppermute(send, "dp", xor_perm(dp, 1))
    dx1 = dx1.reshape(tok_rows)

    shares = [1, images - 1] if images > 1 else [1]
    dqkv_shape = (images, rows, 3 * feats)
    carried, accs = [], []
    for s, share in enumerate(shares):
        first = sum(shares[:s])
        ins = [mix_pre, do, q, k, v, prob, dx1, tokens_in, mpre, mpost, mixb, qkv_weight, norm1_gain]
        *carried, acc = call(
            attn_bwd_kernel,
            (share,),
            ins + carried,
            [SCALARS]
            + [each(a.shape, first) for a in ins[1:8]]
            + [whole(a.shape) for a in ins[8:]]
            + [pl.BlockSpec(memory_space=pl.ANY)] * len(carried),
            [sds(dqkv_shape, BF), sds(tokens_in.shape, F32), sds((2 * heads + 16, feats), F32)],
            [
                each(dqkv_shape, first), each(tokens_in.shape, first),
                whole((2 * heads + 16, feats)),
            ],
            [
                pltpu.VMEM((heads * rows, feats), BF), pltpu.VMEM((heads * rows, slots), BF),
                pltpu.VMEM((feats, slots), BF), pltpu.VMEM((heads * rows, slots), F32),
                pltpu.VMEM((heads * rows, feats), F32), pltpu.VMEM((heads * rows, feats), F32),
                pltpu.VMEM((heads, feats, slots), F32), pltpu.VMEM((rows, feats), F32),
                pltpu.VMEM((rows, feats), F32),
            ],
            flops=share * 20 * 10**8,
            name="attn_bwd",
            aliases={len(ins): 0, len(ins) + 1: 1} if carried else None,
        )
        accs.append(acc)
        if s == 0:
            (keep, got), acc = lax.optimization_barrier(((keep, got), acc))
            mine = dp_scatter(keep.astype(F32) + got.astype(F32), dp)
            accs[0], do = lax.optimization_barrier((acc, do))
    dqkv, in_grad = carried
    mine, dqkv = lax.optimization_barrier((mine, dqkv))
    mlp_mine = mine
    low = mine.astype(BF)
    proj = low[8 * block :]
    got_z = [
        lax.ppermute(
            jnp.concatenate([low[2 * j * block : 2 * (j + 1) * block], proj]), "mp", xor_perm(mp, j)
        )
        for j in range(1, mp)
    ]

    q_block = 3 * feats // dp
    half_shape = (dp // 2, q_block + 16, feats)
    ins = [dqkv.reshape(total, 3 * feats)] + accs + [a1.reshape(flat), acc_mlp, b1_0, b1_1]
    keep, send = call(
        functools.partial(qkv_grad_kernel, heads),
        (1,),
        ins,
        [whole(a.shape) for a in ins],
        [sds(half_shape, BF), sds(half_shape, BF)],
        [whole(half_shape), whole(half_shape)],
        [pltpu.VMEM((16, feats), F32), pltpu.VMEM((3 * feats, feats), BF)],
        flops=11 * 10**8,
        name="qkv_grad",
    )
    got = lax.ppermute(send, "dp", xor_perm(dp, 1))
    mine = dp_scatter(keep.astype(F32) + got.astype(F32), dp)
    low = mine.astype(BF)
    got = [lax.ppermute(low, "mp", xor_perm(mp, j)) for j in range(1, mp)]
    b1_size = hidden // dp
    ins = [mine] + got + [mlp_mine] + got_z
    outs = [
        sds((q_block, feats), F32), sds((1, q_block), F32), sds((heads, heads), F32),
        sds((heads, heads), F32), sds((1, heads), F32), sds((1, b1_size), F32),
    ] + [sds((1, block), F32)] * 8 + [sds((block, feats), F32)] * 3
    qkvw, qkvb, pre, post, postb, b1g, *vecs, fc1g, fc2g, projg = call(
        functools.partial(final_kernel, heads, q_block, mp - 1),
        (1,),
        ins,
        [whole(a.shape) for a in ins],
        outs,
        [whole(a.shape) for a in outs],
        name="final",
    )
    vecs = [a.reshape(-1) for a in vecs]
    return (
        layer_out,
        in_grad,
        vecs[0],
        vecs[1],
        qkvw.T,
        qkvb.reshape(-1),
        pre,
        post,
        postb.reshape(-1),
        projg.T,
        vecs[2],
        vecs[3],
        vecs[4],
        vecs[5],
        fc1g.T,
        b1g.reshape(-1),
        fc2g.T,
        vecs[6],
        vecs[7],
    )


def solution(mesh):
    tokens = P(("dp", "mp"), None, None)
    placed = (
        (tokens, P("dp")) + (P(),) * 12 + (P(None, "mp"), P("mp"), P("mp", None), P(), P(), tokens)
    )
    return jax.shard_map(
        functools.partial(per_device, mesh.shape["dp"], mesh.shape["mp"]),
        mesh=mesh,
        in_specs=placed,
        out_specs=(
            tokens, tokens, P("dp"), P("dp"), P(None, "dp"), P("dp"), P(), P(), P(),
            P(None, "dp"), P("dp"), P("dp"), P("dp"), P("dp"), P(None, ("mp", "dp")),
            P(("mp", "dp")), P("mp", "dp"), P("dp"), P("dp"),
        ),
        check_vma=False,
    )
```

```python
import functools

import jax
import jax.numpy as jnp
from jax import lax
from jax.experimental import pallas as pl
from jax.experimental.pallas import tpu as pltpu
from jax.sharding import PartitionSpec as P

BF = jnp.bfloat16
F32 = jnp.float32
LOG2E = 1.4426950408889634
EPS = 1e-06
VMEM_LIMIT = 20 * 1024 * 1024
ATTENTION_LIMIT = 28 * 1024 * 1024


def nn(a, b):
    return lax.dot_general(a, b, (((1,), (0,)), ((), ())), preferred_element_type=F32)


def nt(a, b):
    return lax.dot_general(a, b, (((1,), (1,)), ((), ())), preferred_element_type=F32)


def tn(a, b):
    return lax.dot_general(a, b, (((0,), (0,)), ((), ())), preferred_element_type=F32)


def exact(a, b, dims):
    return lax.dot_general(
        a, b, (dims, ((), ())), precision=lax.Precision.HIGHEST, preferred_element_type=F32
    )


def normalized(x):
    mean = jnp.mean(x, axis=-1, keepdims=True)
    c = x - mean
    r = lax.rsqrt(jnp.mean(c * c, axis=-1, keepdims=True) + EPS)
    return c * r, r


def norm_back(cot, n, r, gain):
    cg = cot * gain
    return r * (
        cg
        - jnp.mean(cg, axis=-1, keepdims=True)
        - n * jnp.mean(cg * n, axis=-1, keepdims=True)
    )


def colsum(x):
    return jnp.sum(x, axis=0, keepdims=True)


def split(x):
    hi = x.astype(BF)
    return jnp.concatenate([hi, (x - hi.astype(F32)).astype(BF)], axis=1)


def row(ref):
    return ref[...].reshape(1, ref.shape[0])


def inverse(x):
    near = pl.reciprocal(x, approx=True)
    return near * (2.0 - x * near)


def gelu_parts(z):
    e = jnp.exp2(z * z * (-0.5 * LOG2E))
    t = inverse(1.0 + jnp.abs(z) * (0.3275911 * 0.7071067811865476))
    poly = t * (
        0.5 * 0.254829592
        + t
        * (
            0.5 * -0.284496736
            + t * (0.5 * 1.421413741 + t * (0.5 * -1.453152027 + t * (0.5 * 1.061405429)))
        )
    )
    tail = poly * e
    phi = jnp.where(z >= 0, 1.0 - tail, tail)
    return phi, phi + z * e * 0.3989422804014327


def head_of_lane(shape, axis, head_dim):
    return lax.broadcasted_iota(jnp.int32, shape, axis) // head_dim


def chunks(count, size=16):
    return [slice(at, at + size) for at in range(0, count, size)]


def fold(x):
    return sum(x[at : at + 8] for at in range(8, x.shape[0], 8)) + x[0:8]


def pack_kernel(w1, w2, b1, one, other, b1_v, sems):
    feats = w1.shape[0]
    core = jnp.bitwise_and(lax.axis_index("dp"), 1)
    copies = [
        pltpu.make_async_copy(b1, b1_v, sems.at[0]),
        pltpu.make_async_copy(w1, one.at[0:feats], sems.at[1]),
        pltpu.make_async_copy(w2, one.at[feats : 2 * feats], sems.at[2]),
    ]
    own = [pltpu.make_async_copy(w, other.at[0:feats], sems.at[3]) for w in (w1, w2)]
    for copy in copies:
        copy.start()
    for j in range(2):
        pl.when(core == j)(own[j].start)
    copies[0].wait()
    rest = row(b1_v)
    place = lax.broadcasted_iota(jnp.int32, (16, feats), 0)
    bias = jnp.zeros((16, feats), F32)
    for j in range(3):
        term = rest.astype(BF).astype(F32)
        bias = jnp.where(place == j, term, bias)
        rest = rest - term
    bias = bias.astype(BF)
    one[2 * feats :, :] = bias
    other[feats:, :] = bias
    for copy in copies[1:]:
        copy.wait()
    for j in range(2):
        pl.when(core == j)(own[j].wait)


def attn_fwd_kernel(
    counts, post_s, postb_s, *refs
):
    sources, refs = refs[:14], refs[14:]
    a1_o, q_o, k_o, v_o, p_o, o_o, x1_o, u_o, a2_o, dy_o, mpre, mpost, mixb = refs[:13]
    held, (pad, kk, attended_t, probs, wide, logits, mixed, sems) = refs[13:27], refs[27:]
    tok, og, n1g, n1b, qkvb, pre, post, postb, projb, gamma1, n2g, n2b, wqkv, wproj = held
    i = pl.program_id(0)
    images, patches, feats = tok.shape

    def image_copy(which, at):
        return pltpu.make_async_copy(
            sources[which].at[at], held[which].at[at], sems.at[which * images + at]
        )

    @pl.when(i == 0)
    def _():
        shared = [
            pltpu.make_async_copy(sources[j], held[j], sems.at[2 * images + j])
            for j in range(2, 14)
        ]
        image_copy(0, 0).start()
        image_copy(1, 0).start()
        for copy in shared:
            copy.start()
        for at in range(1, images):
            image_copy(0, at).start()
            image_copy(1, at).start()
        for copy in shared:
            copy.wait()

    image_copy(0, i).wait()
    image_copy(1, i).wait()
    rows = pad.shape[0]
    heads = mpre.shape[0]
    head_dim = feats // heads
    slots = q_o.shape[1]

    @pl.when(i == 0)
    def _():
        spread = (
            head_of_lane((heads, feats), 1, head_dim)
            == lax.broadcasted_iota(jnp.int32, (heads, feats), 0)
        ).astype(F32)
        mpre[...] = exact(pre[...], spread, ((1,), (0,))) * (head_dim**-0.5 * LOG2E)
        mpost[...] = exact(post[...], spread, ((0,), (0,)))
        mixb[...] = exact(row(postb), spread, ((1,), (0,)))

    pad[patches:, :] = jnp.zeros((rows - patches, feats), F32)
    live = (lax.axis_index("mp") * images + i < counts[0]).astype(F32)
    pad[0:patches, :] = og[i].astype(F32) * live
    dy_o[0] = pad[...].astype(BF)
    pad[0:patches, :] = tok[i].astype(F32)
    gain, shift = row(n1g), row(n1b)
    for c in chunks(rows):
        n, _ = normalized(pad[c, :])
        a1_o[0, c, :] = (n * gain + shift).astype(BF)
    wide[...] = nn(a1_o[0], wqkv[...])
    bias = row(qkvb)
    q_o[0, rows:] = jnp.zeros((slots - rows, feats), BF)
    for c in chunks(rows):
        q, k, v = (
            wide[c, j * feats : (j + 1) * feats] + bias[:, j * feats : (j + 1) * feats]
            for j in range(3)
        )
        q_o[0, c, :] = q.astype(BF)
        v_o[0, c, :] = v.astype(BF)
        k = k.astype(BF)
        k_o[0, c, :] = k
        kf = k.astype(F32)
        for g in range(heads):
            at = slice(g * rows + c.start, g * rows + c.stop)
            scaled = kf * mpre[g : g + 1, :]
            hi = scaled.astype(BF)
            kk[at, 0:feats] = hi
            kk[at, feats:] = (scaled - hi.astype(F32)).astype(BF)
    q2 = jnp.concatenate([q_o[0], q_o[0]], axis=1)
    vt = v_o[0].T
    many = heads // 2
    half = many * rows
    tail = patches // 8 * 8
    inside = lax.broadcasted_iota(jnp.int32, (rows - tail, 128), 0) < patches - tail
    real = (lax.broadcasted_iota(jnp.int32, (rows, 128), 0) < patches).astype(BF)
    start = nn(vt, real)
    for s in range(2):
        part = slice(s * half, (s + 1) * half)
        logits[part, :] = nt(kk[part, :], q2)
    for g in range(heads):
        for lane in range(0, slots, 128):
            x = logits[g * rows : (g + 1) * rows, lane : lane + 128]
            x = jnp.concatenate([x[0:tail], jnp.where(inside, x[tail:], -1e30)], axis=0)
            e = jnp.exp2(x - jnp.max(x, axis=0, keepdims=True))
            inv = 1.0 / jnp.sum(e, axis=0, keepdims=True)
            p = (e * inv).astype(BF)
            probs[g * rows : (g + 1) * rows, lane : lane + 128] = p
            p_o[0, g, :, lane : lane + 128] = p
        mixed[g] = nn(vt, probs[g * rows : (g + 1) * rows, :])
    for c in chunks(feats):
        g = c.start // head_dim
        first = start[c] * postb_s[g]
        for lane in range(0, slots, 128):
            total = first
            for h in range(heads):
                total = total + mixed[h, c, lane : lane + 128] * post_s[g, h]
            attended_t[c, lane : lane + 128] = total.astype(BF)
    o_o[0] = attended_t[...].T[0:rows]
    wide[:, 0:feats] = nn(o_o[0], wproj[...])
    bias, scale, gain, shift = row(projb), row(gamma1), row(n2g), row(n2b)
    for c in chunks(rows):
        u = wide[c, 0:feats] + bias
        x1 = pad[c, :] + scale * u
        u_o[0, c, :] = u
        x1_o[0, c, :] = x1
        n, _ = normalized(x1)
        a2_o[0, c, :] = (n * gain + shift).astype(BF)


def store_blocks(count, put):
    mine = lax.axis_index("dp")
    for core in range(2):

        @pl.when(jnp.bitwise_and(mine, 1) == core)
        def _(core=core):
            for b in range(count):
                put((b ^ core) & 1, b >> 1, b)


def mlp_units(a2, dfs, w1, b1, w2, hids, dzs, zs, ghs, b1_o, units, store, use):
    size = a2.shape[0] // units
    width = w2.shape[0]
    lanes = 256
    places = [slice(u * size, (u + 1) * size) for u in range(units)]
    sums = {}

    def products(u):
        zs[u % 2] = nn(a2[places[u], :], w1[...])
        ghs[u % 2] = nt(dfs[places[u], :], w2[...])

    products(0)
    for u in range(units):
        if u + 1 < units:
            products(u + 1)
        for first in range(0, width, lanes):
            part = slice(first, first + lanes)
            bias = b1[:, part]
            for c in chunks(size):
                zc = zs[u % 2, c, part] + bias
                phi, slope = gelu_parts(zc)
                dz = (ghs[u % 2, c, part] * slope).astype(BF)
                at = slice(places[u].start + c.start, places[u].start + c.stop)
                hids[at, part] = (zc * phi).astype(BF)
                dzs[at, part] = dz
                more = fold(dz.astype(F32))
                sums[first] = sums[first] + more if first in sums else more
        store(places[u], nn(hids[places[u], :], w2[...]), nt(dzs[places[u], :], w1[...]))
        if u > 0:
            use(places[u - 1])
    use(places[units - 1])
    for first, value in sums.items():
        b1_o[:, first : first + lanes] = colsum(value)


def mlp_first_kernel(
    a2, dy, gamma2, w1_own, b1_own, w2_own, near,
    f_o, da2_o, grads, b1_o, a2t, dft,
    w1, w2, b1, hids, dzs, dfs, zs, ghs,
):
    total, feats = f_o.shape
    w1[:, 0:feats] = w1_own[...]
    w1[:, feats:] = near[0:feats]
    w2[0:feats, :] = w2_own[...]
    w2[feats:, :] = near[feats : 2 * feats]
    b1[:, 0:feats] = row(b1_own)
    b1[:, feats:] = colsum(near[2 * feats : 2 * feats + 16].astype(F32))
    gain = row(gamma2)
    for c in chunks(total):
        dfs[c, :] = (dy[c, :].astype(F32) * gain).astype(BF)

    def store(rows, f, da2):
        f_o[rows, :] = f
        da2_o[rows, :] = da2

    mlp_units(a2, dfs, w1, b1, w2, hids, dzs, zs, ghs, b1_o, 3, store, lambda rows: None)
    a2t[...] = a2[...].T
    dft[...] = dfs[...].T
    grads[0] = nn(a2t[...], dzs[...]).astype(BF).T
    down = nn(dft[...], hids[...]).astype(BF)
    for c in range(2):
        grads[1, c * feats : (c + 1) * feats, :] = down[:, c * feats : (c + 1) * feats]


def mlp_rest_kernel(
    counts, a2, dy, x1, u, o, f0, da20, near, far, grads, a2t, dft, wproj, gamma1, n2g, fc2b, gamma2,
    out_o, dx1_o, do_o, keep, send, b1_o, acc_o,
    w1, w2, b1, hids, dzs, dfs, zs, ghs, fs, da2s, dus, ups, downs, projs,
):
    total, feats = f0.shape
    images, patches = out_o.shape[:2]
    image_rows = total // images
    m_idx = lax.axis_index("mp")
    acc_o[...] = jnp.zeros_like(acc_o)
    for c in range(2):
        b1[:, c * feats : (c + 1) * feats] = colsum(near[c, feats : feats + 16].astype(F32))
    for core in range(2):

        @pl.when(jnp.bitwise_and(lax.axis_index("dp"), 1) == core)
        def _(core=core):
            first, second = (near, far) if core == 0 else (far, near)
            for c in range(2):
                w1[:, c * feats : (c + 1) * feats] = first[c, 0:feats]
                w2[c * feats : (c + 1) * feats, :] = second[c, 0:feats]

    gain2 = row(gamma2)
    bias, gain, scale = row(fc2b), row(n2g), row(gamma1)
    for c in chunks(total):
        dfs[c, :] = (dy[c, :].astype(F32) * gain2).astype(BF)

    def store(rows, f, da2):
        fs[rows, :] = f
        da2s[rows, :] = da2

    def use(rows):
        sums = [jnp.zeros((8, feats), F32) for _ in range(6)]
        for c in chunks(rows.stop - rows.start):
            at = slice(rows.start + c.start, rows.start + c.stop)
            fc = fs[at, :] + f0[at, :] + bias
            dac = da2s[at, :] + da20[at, :]
            x1c = x1[at, :]
            dyc = dy[at, :].astype(F32)
            n, r = normalized(x1c)
            dx1 = dyc + norm_back(dac, n, r, gain)
            dx1_o[at, :] = dx1
            du = (dx1 * scale).astype(BF)
            dus[at, :] = du
            image = at.start // image_rows
            first = at.start - image * image_rows
            live = (m_idx * images + image < counts[0]).astype(F32)
            out = ((x1c + gain2 * fc) * live).astype(BF)
            if first + 16 <= patches:
                out_o[image, first : first + 16, :] = out
            else:
                out_o[image, first:patches, :] = out[0 : patches - first]
            terms = (
                du.astype(F32), u[at, :] * dx1, dac * n, dac, dfs[at, :].astype(F32), fc * dyc,
            )
            sums = [s + fold(t) for s, t in zip(sums, terms)]
        for j in range(6):
            acc_o[j : j + 1, :] += colsum(sums[j])
        do = nt(dus[rows, :], wproj[...]).astype(BF)
        for at in range(0, rows.stop - rows.start, image_rows):
            image = (rows.start + at) // image_rows
            do_o[image, 0:image_rows] = do[at : at + image_rows]
            do_o[image, image_rows:] = jnp.zeros((do_o.shape[1] - image_rows, feats), BF)

    mlp_units(a2, dfs, w1, b1, w2, hids, dzs, zs, ghs, b1_o, 3, store, use)
    ups[...] = nn(a2t[...], dzs[...]).astype(BF).T
    downs[...] = nn(dft[...], hids[...]).astype(BF)
    projs[...] = tn(dus[...], o[...]).astype(BF)
    count = 2 * keep.shape[0]
    size = feats // count
    outs = (keep, send)

    def put(which, place, b):
        out = outs[which]
        for c in range(2):
            part = slice(c * feats, (c + 1) * feats)
            up = slice(c * feats + b * size, c * feats + (b + 1) * size)
            down = slice(b * size, (b + 1) * size)
            pieces = (grads[0, up, :], grads[1, up, :])
            for j, piece in enumerate(pieces):
                out[place, (2 * c + j) * size : (2 * c + j + 1) * size, :] = piece
            pieces = (ups[up, :], downs[down, part])
            for j, piece in enumerate(pieces):
                out[place, (4 + 2 * c + j) * size : (5 + 2 * c + j) * size, :] = piece
        out[place, 8 * size : 9 * size, :] = projs[b * size : (b + 1) * size, :]

    store_blocks(count, put)


def attn_bwd_kernel(
    pre_s, do_r, q_r, k_r, v_r, p_r, dx1, tok, mpre, mpost, mixb, wqkv, n1g, *refs
):
    dqkv_o, in_o, acc_o, vgs, dls, dq_t, dps, dvs, dks, dqs, da1, pad = refs[-12:]
    i = pl.program_id(0)
    slots, feats = do_r.shape[1:]
    patches = tok.shape[1]
    rows = k_r.shape[1]
    heads = mpre.shape[0]
    head_dim = feats // heads
    many = heads // 2
    half = many * rows

    @pl.when(i == 0)
    def _():
        acc_o[...] = jnp.zeros_like(acc_o)

    do_sum = jnp.zeros((8, feats), F32)
    for c in chunks(rows):
        vf = v_r[0, c, :].astype(F32)
        do_sum = do_sum + fold(do_r[0, c, :].astype(F32))
        for h in range(heads):
            vgs[h * rows + c.start : h * rows + c.stop, :] = (vf * mpost[h : h + 1, :]).astype(BF)
    do_sum = colsum(do_sum)
    q = q_r[0]
    do = do_r[0]
    kt = k_r[0].T
    parts = [slice(s * half, (s + 1) * half) for s in range(2)]
    for part in parts:
        dps[part, :] = nt(vgs[part, :], do)
    for s, part in enumerate(parts):
        dvs[part, :] = nn(p_r[0, s * many : (s + 1) * many].reshape(half, slots), do)
    for s, part in enumerate(parts):
        for h in range(s * many, (s + 1) * many):
            at = slice(h * rows, (h + 1) * rows)
            for lane in range(0, slots, 128):
                dp = dps[at, lane : lane + 128]
                pf = p_r[0, h, :, lane : lane + 128].astype(F32)
                mean = jnp.sum(dp * pf, axis=0, keepdims=True) / jnp.sum(pf, axis=0, keepdims=True)
                dls[at, lane : lane + 128] = (pf * (dp - mean)).astype(BF)
            dqs[h] = nn(kt, dls[at, :])
        dks[part, :] = nn(dls[part, :], q)

    bias_row = mixb[...] * do_sum
    v_sum = jnp.zeros((8, feats), F32)
    dv_sum = jnp.zeros((8, feats), F32)
    sums = [jnp.zeros((8, feats), F32) for _ in range(heads)]
    for c in chunks(rows):
        vf = v_r[0, c, :].astype(F32)
        dv = bias_row
        for h in range(heads):
            this = dvs[h * rows + c.start : h * rows + c.stop, :]
            dv = dv + this * mpost[h : h + 1, :]
            sums[h] = sums[h] + fold(vf * this)
        if c.stop > patches:
            inside = lax.broadcasted_iota(jnp.int32, dv.shape, 0) < patches - c.start
            dv = jnp.where(inside, dv, 0.0)
            vf = jnp.where(inside, vf, 0.0)
        low = dv.astype(BF)
        dqkv_o[0, c, 2 * feats :] = low
        dv_sum = dv_sum + fold(low.astype(F32))
        v_sum = v_sum + fold(vf)
    for h in range(heads):
        acc_o[h : h + 1, :] += colsum(sums[h])
    acc_o[2 * heads : 2 * heads + 1, :] += do_sum * colsum(v_sum)
    acc_o[2 * heads + 10 : 2 * heads + 11, :] += colsum(dv_sum)

    for c in chunks(feats):
        g = c.start // head_dim
        for lane in range(0, slots, 128):
            total = 0.0
            for h in range(heads):
                total = total + dqs[h, c, lane : lane + 128] * pre_s[h, g]
            dq_t[c, lane : lane + 128] = (total * head_dim**-0.5).astype(BF)
    dq = dq_t[...].T[0:rows]
    dqkv_o[0, :, 0:feats] = dq
    dk_sum = jnp.zeros((8, feats), F32)
    sums = [jnp.zeros((8, feats), F32) for _ in range(heads)]
    for c in chunks(rows):
        kf = k_r[0, c, :].astype(F32)
        dk = 0.0
        for h in range(heads):
            this = dks[h * rows + c.start : h * rows + c.stop, :]
            dk = dk + this * mpre[h : h + 1, :]
            sums[h] = sums[h] + fold(kf * this)
        low = (dk * (1.0 / LOG2E)).astype(BF)
        dqkv_o[0, c, feats : 2 * feats] = low
        dk_sum = dk_sum + fold(low.astype(F32))
    for h in range(heads):
        acc_o[heads + h : heads + h + 1, :] += colsum(sums[h])
    acc_o[2 * heads + 8 : 2 * heads + 9, :] += colsum(dq.astype(F32))
    acc_o[2 * heads + 9 : 2 * heads + 10, :] += colsum(dk_sum)

    pad[patches:, :] = jnp.zeros((rows - patches, feats), F32)
    pad[0:patches, :] = tok[0].astype(F32)
    da1[...] = nt(dqkv_o[0], wqkv[...])
    gain = row(n1g)
    sums = [jnp.zeros((8, feats), F32) for _ in range(2)]
    for c in chunks(rows):
        n, r = normalized(pad[c, :])
        cot = da1[c, :]
        grad = dx1[0, c, :] + norm_back(cot, n, r, gain)
        sums = [sums[0] + fold(cot * n), sums[1] + fold(cot)]
        if c.stop <= patches:
            in_o[0, c, :] = grad
        else:
            in_o[0, c.start : patches, :] = grad[0 : patches - c.start]
    for j in range(2):
        acc_o[2 * heads + 11 + j : 2 * heads + 12 + j, :] += colsum(sums[j])


def qkv_grad_kernel(heads, dqkv, *refs):
    accs = refs[:-8]
    a1, acc_mlp, b1_first, b1_rest, keep, send, small, grads = refs[-8:]
    feats = a1.shape[1]
    count = 2 * keep.shape[0]
    size = 3 * feats // count
    acc = accs[0][...]
    for other in accs[1:]:
        acc = acc + other[...]
    small[...] = jnp.zeros_like(small)
    small[0:2, :] = acc[2 * heads + 11 : 2 * heads + 13]
    small[2:8, :] = acc_mlp[0:6, :]
    small[8:11, :] = acc[2 * heads + 8 : 2 * heads + 11]
    head_dim = feats // heads
    lanes = 2 * heads * heads
    gather = (
        head_of_lane((feats, lanes), 0, head_dim)
        == lax.broadcasted_iota(jnp.int32, (feats, lanes), 1) % heads
    ).astype(F32)
    sums = exact(acc[0 : 2 * heads + 8], gather, ((1,), (0,)))
    place = head_of_lane((2 * heads, lanes), 1, heads) == lax.broadcasted_iota(
        jnp.int32, (2 * heads, lanes), 0
    )
    small[11:12, 0:lanes] = colsum(jnp.where(place, sums[0 : 2 * heads], 0.0))
    small[11:12, lanes : 2 * lanes] = sums[2 * heads : 2 * heads + 1]
    m_idx = lax.axis_index("mp")
    for c, ref in enumerate((b1_first, b1_first, b1_rest, b1_rest)):
        place = 12 + jnp.bitwise_xor(m_idx, c)
        small[pl.ds(place, 1), :] = ref[:, (c % 2) * feats : (c % 2 + 1) * feats]
    low = small[...].astype(BF)
    outs = (keep, send)

    grads[...] = tn(a1[...], dqkv[...]).astype(BF).T

    def put(which, place, b):
        outs[which][place, 0:size, :] = grads[b * size : (b + 1) * size, :]
        outs[which][place, size : size + 16, :] = low
        if outs[which].shape[1] > size + 16:
            outs[which][place, size + 16 :, :] = jnp.zeros_like(outs[which][place, size + 16 :, :])

    store_blocks(count, put)


def final_kernel(heads, size, sums, got_z, *refs):
    qkv_o, qkvb_o, pre_o, post_o, postb_o, b1_o, *vecs_o, fc1_o, fc2_o, proj_o = refs
    block = fc1_o.shape[0]
    for place, out in enumerate((fc1_o, fc2_o, proj_o)):
        part = slice(place * block, (place + 1) * block)
        out[...] = sum(got_z[j, part, :].astype(F32) for j in range(got_z.shape[0]))
    d_idx = lax.axis_index("dp")
    m_idx = lax.axis_index("mp")
    total = sums[...].astype(F32).reshape(-1, sums.shape[2])
    feats = total.shape[1]
    qkv_o[...] = total[0:size]
    small = total[size : size + 16]

    def own(value, width, index):
        lanes = value.shape[1]
        return pltpu.roll(value, lax.rem(lanes - index * width, lanes), axis=1)[:, 0:width]

    width = vecs_o[0].shape[1]
    vecs = own(small[0:8], width, d_idx)
    for j, ref in enumerate(vecs_o):
        ref[...] = vecs[j : j + 1]
    flat = jnp.concatenate([small[8 + j : 9 + j] for j in range(3)], axis=1)
    qkvb_o[...] = own(jnp.broadcast_to(flat, (8, 3 * feats)), qkvb_o.shape[1], d_idx)[0:1]
    b1 = own(small[8:16], b1_o.shape[1], d_idx)[4:8]
    pick = lax.broadcasted_iota(jnp.int32, b1.shape, 0) == m_idx
    b1_o[...] = colsum(jnp.where(pick, b1, 0.0))
    mix = small[11:12]
    hh = heads * heads
    line = lax.broadcasted_iota(jnp.int32, (heads, hh), 0)
    lane = lax.broadcasted_iota(jnp.int32, (heads, hh), 1)
    fold = (
        lax.broadcasted_iota(jnp.int32, (hh, heads), 0) % heads
        == lax.broadcasted_iota(jnp.int32, (hh, heads), 1)
    ).astype(F32)
    head_dim = feats // heads

    def square(values):
        return exact(jnp.where(lane // heads == line, values, 0.0), fold, ((1,), (0,)))

    post_o[...] = square(mix[:, 0:hh]).T
    pre_o[...] = square(mix[:, hh : 2 * hh]) * (head_dim**-0.5)
    postb_o[...] = mix[:, 2 * hh : 2 * hh + heads]


def whole(shape):
    return pl.BlockSpec(shape, lambda i: (0,) * len(shape))


def each(shape, first=0, many=1):
    return pl.BlockSpec((many,) + shape[1:], lambda i: (i + first,) + (0,) * (len(shape) - 1))


SCALARS = pl.BlockSpec(memory_space=pltpu.SMEM)
IN_VMEM = pl.BlockSpec(memory_space=pltpu.VMEM)
IN_HBM = pl.BlockSpec(memory_space=pltpu.HBM)


def kept(a):
    return pltpu.with_memory_space_constraint(a, pltpu.HBM)


def sds(shape, dtype):
    return jax.ShapeDtypeStruct(shape, dtype)


def call(
    kernel, grid, ins, in_specs, outs, out_specs, scratch=(), flops=0, name=None, aliases=None,
    limit=VMEM_LIMIT,
):
    size = lambda a: a.size * a.dtype.itemsize
    return pl.pallas_call(
        kernel,
        grid=grid,
        in_specs=in_specs,
        out_specs=out_specs,
        out_shape=outs,
        scratch_shapes=scratch,
        input_output_aliases=aliases or {},
        compiler_params=pltpu.CompilerParams(vmem_limit_bytes=limit),
        cost_estimate=pl.CostEstimate(
            flops=flops,
            bytes_accessed=sum(size(a) for a in ins) + sum(size(a) for a in outs),
            transcendentals=0,
        ),
        name=name,
    )(*ins)


def xor_perm(count, mask):
    return [(j, j ^ mask) for j in range(count)]


def dp_hops(dp):
    bits = dp.bit_length() - 1
    groups = []
    at = 1
    while at < bits:
        groups.append((at, min(2, bits - at)))
        at += groups[-1][1]
    return groups


def dp_scatter(value, dp):
    for at, many in dp_hops(dp):
        size = 1 << many
        value = value.astype(BF).reshape((-1, size) + value.shape[1:])
        groups = [
            [base + (j << at) for j in range(size)]
            for base in range(dp)
            if base >> at & (size - 1) == 0
        ]
        got = lax.all_to_all(value, "dp", 1, 1, axis_index_groups=groups, tiled=True)
        value = jnp.sum(got.astype(F32), axis=1)
    return value.reshape(value.shape[-2:])


def per_device(
    dp, mp,
    tokens_in, image_counts, norm1_gain, norm1_bias, qkv_weight, qkv_bias,
    mix_pre, mix_post, mix_post_bias, proj_weight, proj_bias, gamma1,
    norm2_gain, norm2_bias, fc1_weight, fc1_bias, fc2_weight, fc2_bias, gamma2, out_grad,
):
    images, patches, feats = tokens_in.shape
    heads = mix_pre.shape[0]
    rows = -(-patches // 16) * 16
    slots = -(-patches // 128) * 128
    hidden = fc1_weight.shape[1]
    ins = [kept(a) for a in (fc1_weight, fc2_weight, fc1_bias)]
    outs = [sds((2 * feats + 16, hidden), BF), sds((feats + 16, hidden), BF)]
    one, other = call(
        pack_kernel,
        (1,),
        ins,
        [IN_HBM] * 3,
        outs,
        [whole(a.shape) for a in outs],
        [pltpu.VMEM(fc1_bias.shape, F32), pltpu.SemaphoreType.DMA((4,))],
        name="pack",
    )
    near_one = lax.ppermute(one, "mp", xor_perm(mp, 1))
    near = [lax.ppermute(other, "mp", xor_perm(mp, j)) for j in range(2, mp)]

    tok_rows = (images, rows, feats)
    slot_rows = (images, slots, feats)
    prob_shape = (images, heads, rows, slots)
    mix_shape = (heads, feats)
    ins = [
        image_counts, mix_post, mix_post_bias, tokens_in, out_grad, norm1_gain, norm1_bias, qkv_bias, mix_pre, mix_post,
        mix_post_bias, proj_bias, gamma1, norm2_gain, norm2_bias, qkv_weight, proj_weight,
    ]
    ins[3:] = [kept(a) for a in ins[3:]]
    a1, q, k, v, prob, o, x1, u, a2, dy, mpre, mpost, mixb = call(
        attn_fwd_kernel,
        (images,),
        ins,
        [SCALARS] * 3 + [IN_HBM] * 14,
        [
            sds(tok_rows, BF), sds(slot_rows, BF), sds(tok_rows, BF), sds(tok_rows, BF),
            sds(prob_shape, BF), sds(tok_rows, BF), sds(tok_rows, F32), sds(tok_rows, F32),
            sds(tok_rows, BF), sds(tok_rows, BF), sds(mix_shape, F32), sds(mix_shape, F32),
            sds((1, feats), F32),
        ],
        [each(s) for s in (tok_rows, slot_rows, tok_rows, tok_rows, prob_shape)]
        + [each(tok_rows)] * 5
        + [whole(mix_shape)] * 2
        + [whole((1, feats))],
        [pltpu.VMEM(a.shape, a.dtype) for a in ins[3:]]
        + [
            pltpu.VMEM((rows, feats), F32), pltpu.VMEM((heads * rows, 2 * feats), BF),
            pltpu.VMEM((feats, slots), BF), pltpu.VMEM((heads * rows, slots), BF),
            pltpu.VMEM((rows, 3 * feats), F32), pltpu.VMEM((heads * rows, slots), F32),
            pltpu.VMEM((heads, feats, slots), F32), pltpu.SemaphoreType.DMA((2 * images + 14,)),
        ],
        flops=images * 15 * 10**8,
        name="attn_fwd",
        limit=ATTENTION_LIMIT,
    )

    block = feats // dp
    total = images * rows
    flat = (total, feats)
    a2, dy, x1, u, o = (a.reshape(flat) for a in (a2, dy, x1, u, o))
    near_one, near, a2 = lax.optimization_barrier((near_one, near, a2))
    near = jnp.stack(near)
    far = lax.ppermute(near, "dp", xor_perm(dp, 1))
    ins = [a2, dy, gamma2, fc1_weight, fc1_bias, fc2_weight, near_one]
    wide = 2 * hidden
    grad_shape = (2, wide, feats)
    f0, da20, grads0, b1_0, a2t, dft = call(
        mlp_first_kernel,
        (),
        ins,
        [IN_VMEM] * len(ins),
        [
            sds(flat, F32), sds(flat, F32), sds(grad_shape, BF), sds((1, wide), F32),
            sds((feats, total), BF), sds((feats, total), BF),
        ],
        [IN_VMEM] * 6,
        [
            pltpu.VMEM((feats, wide), BF), pltpu.VMEM((wide, feats), BF),
            pltpu.VMEM((1, wide), F32), pltpu.VMEM((total, wide), BF),
            pltpu.VMEM((total, wide), BF), pltpu.VMEM(flat, BF),
            pltpu.VMEM((2, total // 3, wide), F32), pltpu.VMEM((2, total // 3, wide), F32),
        ],
        flops=images * 8 * 10**8,
        name="mlp_first",
    )

    grad_rows = 9 * block
    half_shape = (dp // 2, grad_rows, feats)
    ins = [
        image_counts, a2, dy, x1, u, o, f0, da20, near, far, grads0, a2t, dft, proj_weight, gamma1,
        norm2_gain, fc2_bias, gamma2,
    ]
    layer_out, dx1, do, keep, send, b1_1, acc_mlp = call(
        mlp_rest_kernel,
        (),
        ins,
        [SCALARS] + [IN_VMEM] * (len(ins) - 1),
        [
            sds(tokens_in.shape, BF), sds(flat, F32), sds(slot_rows, BF), sds(half_shape, BF),
            sds(half_shape, BF), sds((1, wide), F32), sds((8, feats), F32),
        ],
        [IN_VMEM] * 7,
        [
            pltpu.VMEM((feats, wide), BF), pltpu.VMEM((wide, feats), BF),
            pltpu.VMEM((1, wide), F32), pltpu.VMEM((total, wide), BF),
            pltpu.VMEM((total, wide), BF), pltpu.VMEM(flat, BF),
            pltpu.VMEM((2, total // 3, wide), F32), pltpu.VMEM((2, total // 3, wide), F32),
            pltpu.VMEM(flat, F32), pltpu.VMEM(flat, F32), pltpu.VMEM(flat, BF),
            pltpu.VMEM((wide, feats), BF), pltpu.VMEM((feats, wide), BF),
            pltpu.VMEM((feats, feats), BF),
        ],
        flops=images * 9 * 10**8,
        name="mlp_rest",
    )
    got = lax.ppermute(send, "dp", xor_perm(dp, 1))
    dx1 = dx1.reshape(tok_rows)

    shares = [1, images - 1] if images > 1 else [1]
    dqkv_shape = (images, rows, 3 * feats)
    carried, accs = [], []
    for s, share in enumerate(shares):
        first = sum(shares[:s])
        ins = [mix_pre, do, q, k, v, prob, dx1, tokens_in, mpre, mpost, mixb, qkv_weight, norm1_gain]
        *carried, acc = call(
            attn_bwd_kernel,
            (share,),
            ins + carried,
            [SCALARS]
            + [each(a.shape, first) for a in ins[1:8]]
            + [whole(a.shape) for a in ins[8:]]
            + [pl.BlockSpec(memory_space=pl.ANY)] * len(carried),
            [sds(dqkv_shape, BF), sds(tokens_in.shape, F32), sds((2 * heads + 16, feats), F32)],
            [
                each(dqkv_shape, first), each(tokens_in.shape, first),
                whole((2 * heads + 16, feats)),
            ],
            [
                pltpu.VMEM((heads * rows, feats), BF), pltpu.VMEM((heads * rows, slots), BF),
                pltpu.VMEM((feats, slots), BF), pltpu.VMEM((heads * rows, slots), F32),
                pltpu.VMEM((heads * rows, feats), F32), pltpu.VMEM((heads * rows, feats), F32),
                pltpu.VMEM((heads, feats, slots), F32), pltpu.VMEM((rows, feats), F32),
                pltpu.VMEM((rows, feats), F32),
            ],
            flops=share * 20 * 10**8,
            name="attn_bwd",
            limit=ATTENTION_LIMIT,
            aliases={len(ins): 0, len(ins) + 1: 1} if carried else None,
        )
        accs.append(acc)
        if s == 0:
            (keep, got), acc = lax.optimization_barrier(((keep, got), acc))
            mine = dp_scatter(keep.astype(F32) + got.astype(F32), dp)
            accs[0], do = lax.optimization_barrier((acc, do))
    dqkv, in_grad = carried
    mine, dqkv = lax.optimization_barrier((mine, dqkv))
    low = mine.astype(BF)
    proj = low[8 * block :]
    m_idx = lax.axis_index("mp")
    by_distance = low[: 8 * block].reshape(mp, 2 * block, feats)
    payload = jnp.stack(
        [
            jnp.concatenate(
                [lax.dynamic_index_in_dim(by_distance, jnp.bitwise_xor(m_idx, j), 0, False), proj]
            )
            for j in range(mp)
        ]
    )
    got_z = lax.all_to_all(payload, "mp", 0, 0, tiled=True)

    q_block = 3 * feats // dp
    quarter = -(-(q_block + 16) // (8 * mp)) * 8
    half_shape = (dp // 2, mp * quarter, feats)
    ins = [dqkv.reshape(total, 3 * feats)] + accs + [a1.reshape(flat), acc_mlp, b1_0, b1_1]
    keep, send = call(
        functools.partial(qkv_grad_kernel, heads),
        (1,),
        ins,
        [whole(a.shape) for a in ins],
        [sds(half_shape, BF), sds(half_shape, BF)],
        [whole(half_shape), whole(half_shape)],
        [pltpu.VMEM((16, feats), F32), pltpu.VMEM((3 * feats, feats), BF)],
        flops=11 * 10**8,
        name="qkv_grad",
    )
    got = lax.ppermute(send, "dp", xor_perm(dp, 1))
    mine = dp_scatter(keep.astype(F32) + got.astype(F32), dp)
    quarters = mine.astype(BF).reshape(mp, quarter, feats)
    quarters, got_z = lax.optimization_barrier((quarters, got_z))
    got = lax.all_to_all(quarters, "mp", 0, 0, tiled=True)
    own = jnp.sum(got.astype(F32), axis=0).astype(BF)
    sums = lax.all_to_all(
        jnp.broadcast_to(own[None], (mp, quarter, feats)), "mp", 0, 0, tiled=True
    )
    b1_size = hidden // dp
    ins = [sums, got_z]
    outs = [
        sds((q_block, feats), F32), sds((1, q_block), F32), sds((heads, heads), F32),
        sds((heads, heads), F32), sds((1, heads), F32), sds((1, b1_size), F32),
    ] + [sds((1, block), F32)] * 8 + [sds((block, feats), F32)] * 3
    qkvw, qkvb, pre, post, postb, b1g, *vecs, fc1g, fc2g, projg = call(
        functools.partial(final_kernel, heads, q_block),
        (1,),
        ins,
        [whole(a.shape) for a in ins],
        outs,
        [whole(a.shape) for a in outs],
        name="final",
    )
    vecs = [a.reshape(-1) for a in vecs]
    return (
        layer_out,
        in_grad,
        vecs[0],
        vecs[1],
        qkvw.T,
        qkvb.reshape(-1),
        pre,
        post,
        postb.reshape(-1),
        projg.T,
        vecs[2],
        vecs[3],
        vecs[4],
        vecs[5],
        fc1g.T,
        b1g.reshape(-1),
        fc2g.T,
        vecs[6],
        vecs[7],
    )


def solution(mesh):
    tokens = P(("dp", "mp"), None, None)
    placed = (
        (tokens, P("dp")) + (P(),) * 12 + (P(None, "mp"), P("mp"), P("mp", None), P(), P(), tokens)
    )
    return jax.shard_map(
        functools.partial(per_device, mesh.shape["dp"], mesh.shape["mp"]),
        mesh=mesh,
        in_specs=placed,
        out_specs=(
            tokens, tokens, P("dp"), P("dp"), P(None, "dp"), P("dp"), P(), P(), P(),
            P(None, "dp"), P("dp"), P("dp"), P("dp"), P("dp"), P(None, ("mp", "dp")),
            P(("mp", "dp")), P("mp", "dp"), P("dp"), P("dp"),
        ),
        check_vma=False,
    )
```

```python
import functools

import jax
import jax.numpy as jnp
from jax import lax
from jax.experimental import pallas as pl
from jax.experimental.pallas import tpu as pltpu
from jax.sharding import PartitionSpec as P

BF = jnp.bfloat16
F32 = jnp.float32
LOG2E = 1.4426950408889634
EPS = 1e-06
VMEM_LIMIT = 20 * 1024 * 1024
ATTENTION_LIMIT = 28 * 1024 * 1024


def nn(a, b):
    return lax.dot_general(a, b, (((1,), (0,)), ((), ())), preferred_element_type=F32)


def nt(a, b):
    return lax.dot_general(a, b, (((1,), (1,)), ((), ())), preferred_element_type=F32)


def tn(a, b):
    return lax.dot_general(a, b, (((0,), (0,)), ((), ())), preferred_element_type=F32)


def exact(a, b, dims):
    return lax.dot_general(
        a, b, (dims, ((), ())), precision=lax.Precision.HIGHEST, preferred_element_type=F32
    )


def normalized(x):
    mean = jnp.mean(x, axis=-1, keepdims=True)
    c = x - mean
    r = lax.rsqrt(jnp.mean(c * c, axis=-1, keepdims=True) + EPS)
    return c * r, r


def norm_back(cot, n, r, gain):
    cg = cot * gain
    return r * (
        cg
        - jnp.mean(cg, axis=-1, keepdims=True)
        - n * jnp.mean(cg * n, axis=-1, keepdims=True)
    )


def colsum(x):
    return jnp.sum(x, axis=0, keepdims=True)


def split(x):
    hi = x.astype(BF)
    return jnp.concatenate([hi, (x - hi.astype(F32)).astype(BF)], axis=1)


def row(ref):
    return ref[...].reshape(1, ref.shape[0])


def inverse(x):
    near = pl.reciprocal(x, approx=True)
    return near * (2.0 - x * near)


def gelu_parts(z):
    e = jnp.exp2(z * z * (-0.5 * LOG2E))
    t = inverse(1.0 + jnp.abs(z) * (0.3275911 * 0.7071067811865476))
    poly = t * (
        0.5 * 0.254829592
        + t
        * (
            0.5 * -0.284496736
            + t * (0.5 * 1.421413741 + t * (0.5 * -1.453152027 + t * (0.5 * 1.061405429)))
        )
    )
    tail = poly * e
    phi = jnp.where(z >= 0, 1.0 - tail, tail)
    return phi, phi + z * e * 0.3989422804014327


def head_of_lane(shape, axis, head_dim):
    return lax.broadcasted_iota(jnp.int32, shape, axis) // head_dim


def chunks(count, size=16):
    return [slice(at, at + size) for at in range(0, count, size)]


def fold(x):
    return sum(x[at : at + 8] for at in range(8, x.shape[0], 8)) + x[0:8]


def pack_kernel(w1, w2, b1, *refs):
    many = (len(refs) - 3) // 2
    sources, other, held, b1_v, sems = refs[:many], refs[many], refs[many + 1 : -2], refs[-2], refs[-1]
    feats = w1.shape[0]
    core = jnp.bitwise_and(lax.axis_index("dp"), 1)
    bias_copy = pltpu.make_async_copy(b1, b1_v, sems.at[0])
    own = [pltpu.make_async_copy(w, other.at[0:feats], sems.at[1]) for w in (w1, w2)]
    copies = [
        pltpu.make_async_copy(sources[j], held[j], sems.at[2 + j]) for j in range(many)
    ]
    bias_copy.start()
    for j in range(2):
        pl.when(core == j)(own[j].start)
    for copy in copies:
        copy.start()
    bias_copy.wait()
    rest = row(b1_v)
    place = lax.broadcasted_iota(jnp.int32, (16, feats), 0)
    bias = jnp.zeros((16, feats), F32)
    for j in range(3):
        term = rest.astype(BF).astype(F32)
        bias = jnp.where(place == j, term, bias)
        rest = rest - term
    other[feats:, :] = bias.astype(BF)
    for j in range(2):
        pl.when(core == j)(own[j].wait)
    for copy in copies:
        copy.wait()


SHARES = {}


def attn_fwd_kernel(carried, counts, post_s, postb_s, *refs):
    first, refs = (0, refs) if carried is None else (carried, refs)
    sources, refs = refs[:14], refs[14 + (10 if first else 0) :]
    a1_o, q_o, k_o, v_o, p_o, o_o, x1_o, u_o, a2_o, dy_o, mpre, mpost, mixb = refs[:13]
    held, (pad, kk, attended_t, probs, wide, logits, mixed, sems) = refs[13:27], refs[27:]
    tok, og, n1g, n1b, qkvb, pre, post, postb, projb, gamma1, n2g, n2b, wqkv, wproj = held
    i = pl.program_id(0) + first
    images, patches, feats = tok.shape
    share = range(first, first + SHARES[images][first])

    def image_copy(which, at):
        return pltpu.make_async_copy(
            sources[which].at[at], held[which].at[at], sems.at[which * images + at]
        )

    @pl.when(i == first)
    def _():
        shared = [
            pltpu.make_async_copy(sources[j], held[j], sems.at[2 * images + j])
            for j in range(2, 14)
        ]
        image_copy(0, first).start()
        image_copy(1, first).start()
        for copy in shared:
            copy.start()
        for at in share[1:]:
            image_copy(0, at).start()
            image_copy(1, at).start()
        for copy in shared:
            copy.wait()

    image_copy(0, i).wait()
    image_copy(1, i).wait()
    rows = pad.shape[0]
    heads = mpre.shape[0]
    head_dim = feats // heads
    slots = q_o.shape[1]

    @pl.when(i == first)
    def _():
        spread = (
            head_of_lane((heads, feats), 1, head_dim)
            == lax.broadcasted_iota(jnp.int32, (heads, feats), 0)
        ).astype(F32)
        mpre[...] = exact(pre[...], spread, ((1,), (0,))) * (head_dim**-0.5 * LOG2E)
        mpost[...] = exact(post[...], spread, ((0,), (0,)))
        mixb[...] = exact(row(postb), spread, ((1,), (0,)))

    pad[patches:, :] = jnp.zeros((rows - patches, feats), F32)
    live = (lax.axis_index("mp") * images + i < counts[0]).astype(F32)
    pad[0:patches, :] = og[i].astype(F32) * live
    dy_o[0] = pad[...].astype(BF)
    pad[0:patches, :] = tok[i].astype(F32)
    gain, shift = row(n1g), row(n1b)
    for c in chunks(rows):
        n, _ = normalized(pad[c, :])
        a1_o[0, c, :] = (n * gain + shift).astype(BF)
    wide[...] = nn(a1_o[0], wqkv[...])
    bias = row(qkvb)
    q_o[0, rows:] = jnp.zeros((slots - rows, feats), BF)
    for c in chunks(rows):
        q, k, v = (
            wide[c, j * feats : (j + 1) * feats] + bias[:, j * feats : (j + 1) * feats]
            for j in range(3)
        )
        q_o[0, c, :] = q.astype(BF)
        v_o[0, c, :] = v.astype(BF)
        k = k.astype(BF)
        k_o[0, c, :] = k
        kf = k.astype(F32)
        for g in range(heads):
            at = slice(g * rows + c.start, g * rows + c.stop)
            scaled = kf * mpre[g : g + 1, :]
            hi = scaled.astype(BF)
            kk[at, 0:feats] = hi
            kk[at, feats:] = (scaled - hi.astype(F32)).astype(BF)
    q2 = jnp.concatenate([q_o[0], q_o[0]], axis=1)
    vt = v_o[0].T
    many = heads // 2
    half = many * rows
    tail = patches // 8 * 8
    inside = lax.broadcasted_iota(jnp.int32, (rows - tail, 128), 0) < patches - tail
    real = (lax.broadcasted_iota(jnp.int32, (rows, 128), 0) < patches).astype(BF)
    start = nn(vt, real)
    for s in range(2):
        part = slice(s * half, (s + 1) * half)
        logits[part, :] = nt(kk[part, :], q2)
    for g in range(heads):
        for lane in range(0, slots, 128):
            x = logits[g * rows : (g + 1) * rows, lane : lane + 128]
            x = jnp.concatenate([x[0:tail], jnp.where(inside, x[tail:], -1e30)], axis=0)
            e = jnp.exp2(x - jnp.max(x, axis=0, keepdims=True))
            inv = 1.0 / jnp.sum(e, axis=0, keepdims=True)
            p = (e * inv).astype(BF)
            probs[g * rows : (g + 1) * rows, lane : lane + 128] = p
            p_o[0, g, :, lane : lane + 128] = p
        mixed[g] = nn(vt, probs[g * rows : (g + 1) * rows, :])
    for c in chunks(feats):
        g = c.start // head_dim
        first = start[c] * postb_s[g]
        for lane in range(0, slots, 128):
            total = first
            for h in range(heads):
                total = total + mixed[h, c, lane : lane + 128] * post_s[g, h]
            attended_t[c, lane : lane + 128] = total.astype(BF)
    o_o[0] = attended_t[...].T[0:rows]
    wide[:, 0:feats] = nn(o_o[0], wproj[...])
    bias, scale, gain, shift = row(projb), row(gamma1), row(n2g), row(n2b)
    for c in chunks(rows):
        u = wide[c, 0:feats] + bias
        x1 = pad[c, :] + scale * u
        u_o[0, c, :] = u
        x1_o[0, c, :] = x1
        n, _ = normalized(x1)
        a2_o[0, c, :] = (n * gain + shift).astype(BF)


def store_blocks(count, put):
    mine = lax.axis_index("dp")
    for core in range(2):

        @pl.when(jnp.bitwise_and(mine, 1) == core)
        def _(core=core):
            for b in range(count):
                place = jnp.bitwise_xor(jnp.int32(b >> 1), jnp.right_shift(mine, 1))
                put((b ^ core) & 1, place, b)


def mlp_units(a2, dfs, w1, b1, w2, hids, dzs, zs, ghs, b1_o, units, store, use):
    size = a2.shape[0] // units
    width = w2.shape[0]
    lanes = 256
    places = [slice(u * size, (u + 1) * size) for u in range(units)]
    sums = {}

    def products(u):
        zs[u % 2] = nn(a2[places[u], :], w1[...])
        ghs[u % 2] = nt(dfs[places[u], :], w2[...])

    products(0)
    for u in range(units):
        if u + 1 < units:
            products(u + 1)
        for first in range(0, width, lanes):
            part = slice(first, first + lanes)
            bias = b1[:, part]
            for c in chunks(size):
                zc = zs[u % 2, c, part] + bias
                phi, slope = gelu_parts(zc)
                dz = (ghs[u % 2, c, part] * slope).astype(BF)
                at = slice(places[u].start + c.start, places[u].start + c.stop)
                hids[at, part] = (zc * phi).astype(BF)
                dzs[at, part] = dz
                more = fold(dz.astype(F32))
                sums[first] = sums[first] + more if first in sums else more
        store(places[u], nn(hids[places[u], :], w2[...]), nt(dzs[places[u], :], w1[...]))
        if u > 0:
            use(places[u - 1])
    use(places[units - 1])
    for first, value in sums.items():
        b1_o[:, first : first + lanes] = colsum(value)


def mlp_first_kernel(
    a2, dy, gamma2, w1_own, b1_own, w2_own, near, far,
    f_o, da2_o, grads, b1_o, a2t, dft,
    w1, w2, b1, hids, dzs, dfs, zs, ghs,
):
    total, feats = f_o.shape
    w1[:, 0:feats] = w1_own[...]
    w2[0:feats, :] = w2_own[...]
    for core in range(2):

        @pl.when(jnp.bitwise_and(lax.axis_index("dp"), 1) == core)
        def _(core=core):
            one, two = (near, far) if core == 0 else (far, near)
            w1[:, feats:] = one[0, 0:feats]
            w2[feats:, :] = two[0, 0:feats]

    b1[:, 0:feats] = row(b1_own)
    b1[:, feats:] = colsum(near[0, feats : feats + 16].astype(F32))
    gain = row(gamma2)
    for c in chunks(total):
        dfs[c, :] = (dy[c, :].astype(F32) * gain).astype(BF)

    def store(rows, f, da2):
        f_o[rows, :] = f
        da2_o[rows, :] = da2

    mlp_units(a2, dfs, w1, b1, w2, hids, dzs, zs, ghs, b1_o, 3, store, lambda rows: None)
    a2t[...] = a2[...].T
    dft[...] = dfs[...].T
    grads[0] = nn(a2t[...], dzs[...]).astype(BF).T
    down = nn(dft[...], hids[...]).astype(BF)
    for c in range(2):
        grads[1, c * feats : (c + 1) * feats, :] = down[:, c * feats : (c + 1) * feats]


def mlp_rest_kernel(
    counts, a2, dy, x1, u, o, f0, da20, near, far, last, far_last, grads, a2t, dft, wproj, gamma1, n2g, fc2b, gamma2,
    out_o, dx1_o, do_o, keep, send, b1_o, acc_o,
    w1, w2, b1, hids, dzs, dfs, zs, ghs, fs, da2s, dus, ups, downs, projs, out_v, sems,
):
    total, feats = f0.shape
    images, patches = out_o.shape[:2]
    image_rows = total // images
    m_idx = lax.axis_index("mp")
    acc_o[...] = jnp.zeros_like(acc_o)
    b1[:, 0:feats] = colsum(near[1, feats : feats + 16].astype(F32))
    b1[:, feats:] = colsum(last[feats : feats + 16].astype(F32))
    for core in range(2):

        @pl.when(jnp.bitwise_and(lax.axis_index("dp"), 1) == core)
        def _(core=core):
            one, two = (near, far) if core == 0 else (far, near)
            w1[:, 0:feats] = one[1, 0:feats]
            w2[0:feats, :] = two[1, 0:feats]
            one, two = (last, far_last) if core == 0 else (far_last, last)
            w1[:, feats:] = one[0:feats]
            w2[feats:, :] = two[0:feats]

    gain2 = row(gamma2)
    bias, gain, scale = row(fc2b), row(n2g), row(gamma1)
    for c in chunks(total):
        dfs[c, :] = (dy[c, :].astype(F32) * gain2).astype(BF)

    def out_copy(image):
        return pltpu.make_async_copy(out_v.at[image], out_o.at[image], sems.at[image])

    def store(rows, f, da2):
        fs[rows, :] = f
        da2s[rows, :] = da2

    def use(rows):
        sums = [jnp.zeros((8, feats), F32) for _ in range(6)]
        for c in chunks(rows.stop - rows.start):
            at = slice(rows.start + c.start, rows.start + c.stop)
            fc = fs[at, :] + f0[at, :] + bias
            dac = da2s[at, :] + da20[at, :]
            x1c = x1[at, :]
            dyc = dy[at, :].astype(F32)
            n, r = normalized(x1c)
            dx1 = dyc + norm_back(dac, n, r, gain)
            dx1_o[at, :] = dx1
            du = (dx1 * scale).astype(BF)
            dus[at, :] = du
            image = at.start // image_rows
            first = at.start - image * image_rows
            live = (m_idx * images + image < counts[0]).astype(F32)
            out = ((x1c + gain2 * fc) * live).astype(BF)
            if first + 16 <= patches:
                out_v[image, first : first + 16, :] = out
            else:
                out_v[image, first:patches, :] = out[0 : patches - first]
            terms = (
                du.astype(F32), u[at, :] * dx1, dac * n, dac, dfs[at, :].astype(F32), fc * dyc,
            )
            sums = [s + fold(t) for s, t in zip(sums, terms)]
        for j in range(6):
            acc_o[j : j + 1, :] += colsum(sums[j])
        do = nt(dus[rows, :], wproj[...]).astype(BF)
        for at in range(0, rows.stop - rows.start, image_rows):
            image = (rows.start + at) // image_rows
            out_copy(image).start()
            do_o[image, 0:image_rows] = do[at : at + image_rows]
            do_o[image, image_rows:] = jnp.zeros((do_o.shape[1] - image_rows, feats), BF)

    mlp_units(a2, dfs, w1, b1, w2, hids, dzs, zs, ghs, b1_o, 3, store, use)
    ups[...] = nn(a2t[...], dzs[...]).astype(BF).T
    downs[...] = nn(dft[...], hids[...]).astype(BF)
    projs[...] = tn(dus[...], o[...]).astype(BF)
    count = 2 * keep.shape[0]
    size = feats // count
    outs = (keep, send)

    def put(which, place, b):
        out = outs[which]
        for c in range(2):
            part = slice(c * feats, (c + 1) * feats)
            up = slice(c * feats + b * size, c * feats + (b + 1) * size)
            down = slice(b * size, (b + 1) * size)
            pieces = (grads[0, up, :], grads[1, up, :])
            for j, piece in enumerate(pieces):
                out[place, (2 * c + j) * size : (2 * c + j + 1) * size, :] = piece
            pieces = (ups[up, :], downs[down, part])
            for j, piece in enumerate(pieces):
                out[place, (4 + 2 * c + j) * size : (5 + 2 * c + j) * size, :] = piece
        out[place, 8 * size : 9 * size, :] = projs[b * size : (b + 1) * size, :]

    store_blocks(count, put)
    for image in range(images):
        out_copy(image).wait()


def attn_bwd_kernel(
    pre_s, do_r, q_r, k_r, v_r, p_r, dx1, tok, mpre, mpost, mixb, wqkv, n1g, *refs
):
    dqkv_o, in_o, acc_o, vgs, dls, dq_t, dps, dvs, dks, dqs, da1, pad = refs[-12:]
    i = pl.program_id(0)
    slots, feats = do_r.shape[1:]
    patches = tok.shape[1]
    rows = k_r.shape[1]
    heads = mpre.shape[0]
    head_dim = feats // heads
    many = heads // 2
    half = many * rows

    @pl.when(i == 0)
    def _():
        acc_o[...] = jnp.zeros_like(acc_o)

    do_sum = jnp.zeros((8, feats), F32)
    for c in chunks(rows):
        vf = v_r[0, c, :].astype(F32)
        do_sum = do_sum + fold(do_r[0, c, :].astype(F32))
        for h in range(heads):
            vgs[h * rows + c.start : h * rows + c.stop, :] = (vf * mpost[h : h + 1, :]).astype(BF)
    do_sum = colsum(do_sum)
    q = q_r[0]
    do = do_r[0]
    kt = k_r[0].T
    parts = [slice(s * half, (s + 1) * half) for s in range(2)]
    for part in parts:
        dps[part, :] = nt(vgs[part, :], do)
    for s, part in enumerate(parts):
        dvs[part, :] = nn(p_r[0, s * many : (s + 1) * many].reshape(half, slots), do)
    for s, part in enumerate(parts):
        for h in range(s * many, (s + 1) * many):
            at = slice(h * rows, (h + 1) * rows)
            for lane in range(0, slots, 128):
                dp = dps[at, lane : lane + 128]
                pf = p_r[0, h, :, lane : lane + 128].astype(F32)
                mean = jnp.sum(dp * pf, axis=0, keepdims=True) / jnp.sum(pf, axis=0, keepdims=True)
                dls[at, lane : lane + 128] = (pf * (dp - mean)).astype(BF)
            dqs[h] = nn(kt, dls[at, :])
        dks[part, :] = nn(dls[part, :], q)

    bias_row = mixb[...] * do_sum
    v_sum = jnp.zeros((8, feats), F32)
    dv_sum = jnp.zeros((8, feats), F32)
    sums = [jnp.zeros((8, feats), F32) for _ in range(heads)]
    for c in chunks(rows):
        vf = v_r[0, c, :].astype(F32)
        dv = bias_row
        for h in range(heads):
            this = dvs[h * rows + c.start : h * rows + c.stop, :]
            dv = dv + this * mpost[h : h + 1, :]
            sums[h] = sums[h] + fold(vf * this)
        if c.stop > patches:
            inside = lax.broadcasted_iota(jnp.int32, dv.shape, 0) < patches - c.start
            dv = jnp.where(inside, dv, 0.0)
            vf = jnp.where(inside, vf, 0.0)
        low = dv.astype(BF)
        dqkv_o[0, c, 2 * feats :] = low
        dv_sum = dv_sum + fold(low.astype(F32))
        v_sum = v_sum + fold(vf)
    for h in range(heads):
        acc_o[h : h + 1, :] += colsum(sums[h])
    acc_o[2 * heads : 2 * heads + 1, :] += do_sum * colsum(v_sum)
    acc_o[2 * heads + 10 : 2 * heads + 11, :] += colsum(dv_sum)

    for c in chunks(feats):
        g = c.start // head_dim
        for lane in range(0, slots, 128):
            total = 0.0
            for h in range(heads):
                total = total + dqs[h, c, lane : lane + 128] * pre_s[h, g]
            dq_t[c, lane : lane + 128] = (total * head_dim**-0.5).astype(BF)
    dq = dq_t[...].T[0:rows]
    dqkv_o[0, :, 0:feats] = dq
    dk_sum = jnp.zeros((8, feats), F32)
    sums = [jnp.zeros((8, feats), F32) for _ in range(heads)]
    for c in chunks(rows):
        kf = k_r[0, c, :].astype(F32)
        dk = 0.0
        for h in range(heads):
            this = dks[h * rows + c.start : h * rows + c.stop, :]
            dk = dk + this * mpre[h : h + 1, :]
            sums[h] = sums[h] + fold(kf * this)
        low = (dk * (1.0 / LOG2E)).astype(BF)
        dqkv_o[0, c, feats : 2 * feats] = low
        dk_sum = dk_sum + fold(low.astype(F32))
    for h in range(heads):
        acc_o[heads + h : heads + h + 1, :] += colsum(sums[h])
    acc_o[2 * heads + 8 : 2 * heads + 9, :] += colsum(dq.astype(F32))
    acc_o[2 * heads + 9 : 2 * heads + 10, :] += colsum(dk_sum)

    pad[patches:, :] = jnp.zeros((rows - patches, feats), F32)
    pad[0:patches, :] = tok[0].astype(F32)
    da1[...] = nt(dqkv_o[0], wqkv[...])
    gain = row(n1g)
    sums = [jnp.zeros((8, feats), F32) for _ in range(2)]
    for c in chunks(rows):
        n, r = normalized(pad[c, :])
        cot = da1[c, :]
        grad = dx1[0, c, :] + norm_back(cot, n, r, gain)
        sums = [sums[0] + fold(cot * n), sums[1] + fold(cot)]
        if c.stop <= patches:
            in_o[0, c, :] = grad
        else:
            in_o[0, c.start : patches, :] = grad[0 : patches - c.start]
    for j in range(2):
        acc_o[2 * heads + 11 + j : 2 * heads + 12 + j, :] += colsum(sums[j])


def qkv_grad_kernel(heads, dqkv, *refs):
    accs = refs[:-8]
    a1, acc_mlp, b1_first, b1_rest, keep, send, small, grads = refs[-8:]
    feats = a1.shape[1]
    count = 2 * keep.shape[0]
    size = 3 * feats // count
    acc = accs[0][...]
    for other in accs[1:]:
        acc = acc + other[...]
    small[...] = jnp.zeros_like(small)
    small[0:2, :] = acc[2 * heads + 11 : 2 * heads + 13]
    small[2:8, :] = acc_mlp[0:6, :]
    small[8:11, :] = acc[2 * heads + 8 : 2 * heads + 11]
    head_dim = feats // heads
    lanes = 2 * heads * heads
    gather = (
        head_of_lane((feats, lanes), 0, head_dim)
        == lax.broadcasted_iota(jnp.int32, (feats, lanes), 1) % heads
    ).astype(F32)
    sums = exact(acc[0 : 2 * heads + 8], gather, ((1,), (0,)))
    place = head_of_lane((2 * heads, lanes), 1, heads) == lax.broadcasted_iota(
        jnp.int32, (2 * heads, lanes), 0
    )
    small[11:12, 0:lanes] = colsum(jnp.where(place, sums[0 : 2 * heads], 0.0))
    small[11:12, lanes : 2 * lanes] = sums[2 * heads : 2 * heads + 1]
    m_idx = lax.axis_index("mp")
    for c, ref in enumerate((b1_first, b1_first, b1_rest, b1_rest)):
        place = 12 + jnp.bitwise_xor(m_idx, c)
        small[pl.ds(place, 1), :] = ref[:, (c % 2) * feats : (c % 2 + 1) * feats]
    low = small[...].astype(BF)
    outs = (keep, send)

    grads[...] = tn(a1[...], dqkv[...]).astype(BF).T

    def put(which, place, b):
        outs[which][place, 0:size, :] = grads[b * size : (b + 1) * size, :]
        outs[which][place, size : size + 16, :] = low
        if outs[which].shape[1] > size + 16:
            outs[which][place, size + 16 :, :] = jnp.zeros_like(outs[which][place, size + 16 :, :])

    store_blocks(count, put)


def final_kernel(heads, size, many, *refs):
    parts = refs[0 : 1 + many]
    mlp_mine, got_z = refs[1 + many], refs[2 + many : 2 + 2 * many]
    qkv_o, qkvb_o, pre_o, post_o, postb_o, b1_o, *vecs_o, fc1_o, fc2_o, proj_o, held, held_proj = refs[-19:]
    block = fc1_o.shape[0]
    for place, out in enumerate((fc1_o, fc2_o)):
        rows = slice(place * block, (place + 1) * block)
        out[...] = mlp_mine[rows, :] + sum(g[rows, :].astype(F32) for g in got_z)
    d_idx = lax.axis_index("dp")
    m_idx = lax.axis_index("mp")
    quarter, feats = held.shape[1:]
    for j, part in enumerate(parts):
        place = jnp.bitwise_xor(m_idx, j)
        value = part[...].astype(F32)
        held[place] = value[0:quarter]
        held_proj[place] = value[quarter:]
    total = held[...].reshape(-1, feats)
    proj_o[...] = held_proj[...].reshape(-1, feats)[0:block]
    qkv_o[...] = total[0:size]
    small = total[size : size + 16]

    def own(value, width, index):
        lanes = value.shape[1]
        return pltpu.roll(value, lax.rem(lanes - index * width, lanes), axis=1)[:, 0:width]

    width = vecs_o[0].shape[1]
    vecs = own(small[0:8], width, d_idx)
    for j, ref in enumerate(vecs_o):
        ref[...] = vecs[j : j + 1]
    flat = jnp.concatenate([small[8 + j : 9 + j] for j in range(3)], axis=1)
    qkvb_o[...] = own(jnp.broadcast_to(flat, (8, 3 * feats)), qkvb_o.shape[1], d_idx)[0:1]
    b1 = own(small[8:16], b1_o.shape[1], d_idx)[4:8]
    pick = lax.broadcasted_iota(jnp.int32, b1.shape, 0) == m_idx
    b1_o[...] = colsum(jnp.where(pick, b1, 0.0))
    mix = small[11:12]
    hh = heads * heads
    line = lax.broadcasted_iota(jnp.int32, (heads, hh), 0)
    lane = lax.broadcasted_iota(jnp.int32, (heads, hh), 1)
    fold = (
        lax.broadcasted_iota(jnp.int32, (hh, heads), 0) % heads
        == lax.broadcasted_iota(jnp.int32, (hh, heads), 1)
    ).astype(F32)
    head_dim = feats // heads

    def square(values):
        return exact(jnp.where(lane // heads == line, values, 0.0), fold, ((1,), (0,)))

    post_o[...] = square(mix[:, 0:hh]).T
    pre_o[...] = square(mix[:, hh : 2 * hh]) * (head_dim**-0.5)
    postb_o[...] = mix[:, 2 * hh : 2 * hh + heads]


def whole(shape):
    return pl.BlockSpec(shape, lambda i: (0,) * len(shape))


def each(shape, first=0, many=1):
    return pl.BlockSpec((many,) + shape[1:], lambda i: (i + first,) + (0,) * (len(shape) - 1))


SCALARS = pl.BlockSpec(memory_space=pltpu.SMEM)
IN_VMEM = pl.BlockSpec(memory_space=pltpu.VMEM)
IN_HBM = pl.BlockSpec(memory_space=pltpu.HBM)


def kept(a):
    return pltpu.with_memory_space_constraint(a, pltpu.HBM)


def sds(shape, dtype):
    return jax.ShapeDtypeStruct(shape, dtype)


def call(
    kernel, grid, ins, in_specs, outs, out_specs, scratch=(), flops=0, name=None, aliases=None,
    limit=VMEM_LIMIT,
):
    size = lambda a: a.size * a.dtype.itemsize
    return pl.pallas_call(
        kernel,
        grid=grid,
        in_specs=in_specs,
        out_specs=out_specs,
        out_shape=outs,
        scratch_shapes=scratch,
        input_output_aliases=aliases or {},
        compiler_params=pltpu.CompilerParams(vmem_limit_bytes=limit),
        cost_estimate=pl.CostEstimate(
            flops=flops,
            bytes_accessed=sum(size(a) for a in ins) + sum(size(a) for a in outs),
            transcendentals=0,
        ),
        name=name,
    )(*ins)


def xor_perm(count, mask):
    return [(j, j ^ mask) for j in range(count)]


def dp_hops(dp):
    bits = dp.bit_length() - 1
    groups = []
    at = 1
    while at < bits:
        groups.append((at, min(2, bits - at)))
        at += groups[-1][1]
    return groups


def dp_scatter(value, dp):
    for at, many in dp_hops(dp):
        value = value.reshape((-1, 1 << many) + value.shape[1:])
        got = [
            lax.ppermute(value[:, j].astype(BF), "dp", xor_perm(dp, j << at))
            for j in range(1, 1 << many)
        ]
        value = value[:, 0] + sum(g.astype(F32) for g in got)
    return value.reshape(value.shape[-2:])


def per_device(
    dp, mp,
    tokens_in, image_counts, norm1_gain, norm1_bias, qkv_weight, qkv_bias,
    mix_pre, mix_post, mix_post_bias, proj_weight, proj_bias, gamma1,
    norm2_gain, norm2_bias, fc1_weight, fc1_bias, fc2_weight, fc2_bias, gamma2, out_grad,
):
    images, patches, feats = tokens_in.shape
    heads = mix_pre.shape[0]
    rows = -(-patches // 16) * 16
    slots = -(-patches // 128) * 128
    hidden = fc1_weight.shape[1]
    tok_rows = (images, rows, feats)
    slot_rows = (images, slots, feats)
    prob_shape = (images, heads, rows, slots)
    mix_shape = (heads, feats)
    operands = [
        tokens_in, out_grad, norm1_gain, norm1_bias, qkv_bias, mix_pre, mix_post,
        mix_post_bias, proj_bias, gamma1, norm2_gain, norm2_bias, qkv_weight, proj_weight,
    ]

    ins = [kept(a) for a in [fc1_weight, fc2_weight, fc1_bias] + operands]
    outs = [sds((feats + 16, hidden), BF)] + [sds(a.shape, a.dtype) for a in operands]
    other, *held = call(
        pack_kernel,
        (),
        ins,
        [IN_HBM] * len(ins),
        outs,
        [IN_VMEM] * len(outs),
        [pltpu.VMEM(fc1_bias.shape, F32), pltpu.SemaphoreType.DMA((2 + len(operands),))],
        name="pack",
    )
    near = [lax.ppermute(other, "mp", xor_perm(mp, j)) for j in (1, 2)]

    shares = [images - 2, 2] if images > 2 else [images]
    SHARES[images] = {sum(shares[:s]): share for s, share in enumerate(shares)}
    carried = []
    for s, share in enumerate(shares):
        first = sum(shares[:s])
        ins = [image_counts, mix_post, mix_post_bias] + (operands if first else held)
        outs = call(
            functools.partial(attn_fwd_kernel, first),
            (share,),
            ins + carried,
            [SCALARS] * 3 + [IN_HBM] * 14 + [pl.BlockSpec(memory_space=pl.ANY)] * len(carried),
            [
                sds(tok_rows, BF), sds(slot_rows, BF), sds(tok_rows, BF), sds(tok_rows, BF),
                sds(prob_shape, BF), sds(tok_rows, BF), sds(tok_rows, F32), sds(tok_rows, F32),
                sds(tok_rows, BF), sds(tok_rows, BF), sds(mix_shape, F32), sds(mix_shape, F32),
                sds((1, feats), F32),
            ],
            [each(a, first) for a in (tok_rows, slot_rows, tok_rows, tok_rows, prob_shape)]
            + [each(tok_rows, first)] * 5
            + [whole(mix_shape)] * 2
            + [whole((1, feats))],
            [pltpu.VMEM(a.shape, a.dtype) for a in operands]
            + [
                pltpu.VMEM((rows, feats), F32), pltpu.VMEM((heads * rows, 2 * feats), BF),
                pltpu.VMEM((feats, slots), BF), pltpu.VMEM((heads * rows, slots), BF),
                pltpu.VMEM((rows, 3 * feats), F32), pltpu.VMEM((heads * rows, slots), F32),
                pltpu.VMEM((heads, feats, slots), F32),
                pltpu.SemaphoreType.DMA((2 * images + 14,)),
            ],
            flops=share * 15 * 10**8,
            name="attn_fwd",
            aliases={len(ins) + j: j for j in range(10)} if carried else None,
            limit=ATTENTION_LIMIT,
        )
        carried, (mpre, mpost, mixb) = list(outs[:10]), outs[10:]
        if s == 0:
            near, carried[0] = lax.optimization_barrier((near, carried[0]))
            last = lax.ppermute(near[1], "mp", xor_perm(mp, 1))
            near = jnp.stack(near)
            far = lax.ppermute(near, "dp", xor_perm(dp, 1))
    a1, q, k, v, prob, o, x1, u, a2, dy = carried
    far, last, a2 = lax.optimization_barrier((far, last, a2))
    far_last = lax.ppermute(last, "dp", xor_perm(dp, 1))

    block = feats // dp
    total = images * rows
    flat = (total, feats)
    a2, dy, x1, u, o = (a.reshape(flat) for a in (a2, dy, x1, u, o))
    ins = [a2, dy, gamma2, fc1_weight, fc1_bias, fc2_weight, near, far]
    wide = 2 * hidden
    grad_shape = (2, wide, feats)
    f0, da20, grads0, b1_0, a2t, dft = call(
        mlp_first_kernel,
        (),
        ins,
        [IN_VMEM] * len(ins),
        [
            sds(flat, F32), sds(flat, F32), sds(grad_shape, BF), sds((1, wide), F32),
            sds((feats, total), BF), sds((feats, total), BF),
        ],
        [IN_VMEM] * 6,
        [
            pltpu.VMEM((feats, wide), BF), pltpu.VMEM((wide, feats), BF),
            pltpu.VMEM((1, wide), F32), pltpu.VMEM((total, wide), BF),
            pltpu.VMEM((total, wide), BF), pltpu.VMEM(flat, BF),
            pltpu.VMEM((2, total // 3, wide), F32), pltpu.VMEM((2, total // 3, wide), F32),
        ],
        flops=images * 8 * 10**8,
        name="mlp_first",
    )

    grad_rows = 9 * block
    half_shape = (dp // 2, grad_rows, feats)
    ins = [
        image_counts, a2, dy, x1, u, o, f0, da20, near, far, last, far_last, grads0, a2t, dft,
        proj_weight, gamma1,
        norm2_gain, fc2_bias, gamma2,
    ]
    layer_out, dx1, do, keep, send, b1_1, acc_mlp = call(
        mlp_rest_kernel,
        (),
        ins,
        [SCALARS] + [IN_VMEM] * (len(ins) - 1),
        [
            sds(tokens_in.shape, BF), sds(flat, F32), sds(slot_rows, BF), sds(half_shape, BF),
            sds(half_shape, BF), sds((1, wide), F32), sds((8, feats), F32),
        ],
        [IN_HBM] + [IN_VMEM] * 6,
        [
            pltpu.VMEM((feats, wide), BF), pltpu.VMEM((wide, feats), BF),
            pltpu.VMEM((1, wide), F32), pltpu.VMEM((total, wide), BF),
            pltpu.VMEM((total, wide), BF), pltpu.VMEM(flat, BF),
            pltpu.VMEM((2, total // 3, wide), F32), pltpu.VMEM((2, total // 3, wide), F32),
            pltpu.VMEM(flat, F32), pltpu.VMEM(flat, F32), pltpu.VMEM(flat, BF),
            pltpu.VMEM((wide, feats), BF), pltpu.VMEM((feats, wide), BF),
            pltpu.VMEM((feats, feats), BF), pltpu.VMEM(tokens_in.shape, BF),
            pltpu.SemaphoreType.DMA((images,)),
        ],
        flops=images * 9 * 10**8,
        name="mlp_rest",
    )
    got = lax.ppermute(send, "dp", xor_perm(dp, 1))
    dx1 = dx1.reshape(tok_rows)

    shares = [1, images - 1] if images > 1 else [1]
    dqkv_shape = (images, rows, 3 * feats)
    carried, accs = [], []
    for s, share in enumerate(shares):
        first = sum(shares[:s])
        ins = [mix_pre, do, q, k, v, prob, dx1, tokens_in, mpre, mpost, mixb, qkv_weight, norm1_gain]
        *carried, acc = call(
            attn_bwd_kernel,
            (share,),
            ins + carried,
            [SCALARS]
            + [each(a.shape, first) for a in ins[1:8]]
            + [whole(a.shape) for a in ins[8:]]
            + [pl.BlockSpec(memory_space=pl.ANY)] * len(carried),
            [sds(dqkv_shape, BF), sds(tokens_in.shape, F32), sds((2 * heads + 16, feats), F32)],
            [
                each(dqkv_shape, first), each(tokens_in.shape, first),
                whole((2 * heads + 16, feats)),
            ],
            [
                pltpu.VMEM((heads * rows, feats), BF), pltpu.VMEM((heads * rows, slots), BF),
                pltpu.VMEM((feats, slots), BF), pltpu.VMEM((heads * rows, slots), F32),
                pltpu.VMEM((heads * rows, feats), F32), pltpu.VMEM((heads * rows, feats), F32),
                pltpu.VMEM((heads, feats, slots), F32), pltpu.VMEM((rows, feats), F32),
                pltpu.VMEM((rows, feats), F32),
            ],
            flops=share * 20 * 10**8,
            name="attn_bwd",
            limit=ATTENTION_LIMIT,
            aliases={len(ins): 0, len(ins) + 1: 1} if carried else None,
        )
        accs.append(acc)
        if s == 0:
            (keep, got), acc = lax.optimization_barrier(((keep, got), acc))
            mine = dp_scatter(keep.astype(F32) + got.astype(F32), dp)
            accs[0], do = lax.optimization_barrier((acc, do))
    dqkv, in_grad = carried
    mine, dqkv = lax.optimization_barrier((mine, dqkv))
    mlp_mine = mine
    low = mine.astype(BF)
    m_idx = lax.axis_index("mp")
    share_rows = -(-block // (16 * mp)) * 16
    proj = jnp.pad(mine[8 * block :], ((0, mp * share_rows - block), (0, 0)))

    def proj_share(j):
        return lax.dynamic_slice_in_dim(proj, jnp.bitwise_xor(m_idx, j) * share_rows, share_rows)

    got_z = [
        lax.ppermute(
            jnp.concatenate([low[2 * j * block : 2 * (j + 1) * block], proj_share(j).astype(BF)]),
            "mp",
            xor_perm(mp, j),
        )
        for j in range(1, mp)
    ]

    q_block = 3 * feats // dp
    quarter = -(-(q_block + 16) // (8 * mp)) * 8
    half_shape = (dp // 2, mp * quarter, feats)
    ins = [dqkv.reshape(total, 3 * feats)] + accs + [a1.reshape(flat), acc_mlp, b1_0, b1_1]
    keep, send = call(
        functools.partial(qkv_grad_kernel, heads),
        (1,),
        ins,
        [whole(a.shape) for a in ins],
        [sds(half_shape, BF), sds(half_shape, BF)],
        [whole(half_shape), whole(half_shape)],
        [pltpu.VMEM((16, feats), F32), pltpu.VMEM((3 * feats, feats), BF)],
        flops=11 * 10**8,
        name="qkv_grad",
    )
    got = lax.ppermute(send, "dp", xor_perm(dp, 1))
    mine = dp_scatter(keep.astype(F32) + got.astype(F32), dp)
    mine, got_z = lax.optimization_barrier((mine, got_z))

    def part(j):
        return lax.dynamic_slice_in_dim(mine, jnp.bitwise_xor(m_idx, j) * quarter, quarter)

    own = part(0)
    for j in range(1, mp):
        own = own + lax.ppermute(part(j).astype(BF), "mp", xor_perm(mp, j)).astype(F32)
    proj_own = proj_share(0) + sum(g[2 * block :].astype(F32) for g in got_z)
    own = jnp.concatenate([own, proj_own]).astype(BF)
    got = [lax.ppermute(own, "mp", xor_perm(mp, j)) for j in range(1, mp)]
    b1_size = hidden // dp
    ins = [own] + got + [mlp_mine] + got_z
    outs = [
        sds((q_block, feats), F32), sds((1, q_block), F32), sds((heads, heads), F32),
        sds((heads, heads), F32), sds((1, heads), F32), sds((1, b1_size), F32),
    ] + [sds((1, block), F32)] * 8 + [sds((block, feats), F32)] * 3
    qkvw, qkvb, pre, post, postb, b1g, *vecs, fc1g, fc2g, projg = call(
        functools.partial(final_kernel, heads, q_block, mp - 1),
        (1,),
        ins,
        [whole(a.shape) for a in ins],
        outs,
        [whole(a.shape) for a in outs],
        [pltpu.VMEM((mp, quarter, feats), F32), pltpu.VMEM((mp, share_rows, feats), F32)],
        name="final",
    )
    vecs = [a.reshape(-1) for a in vecs]
    return (
        layer_out,
        in_grad,
        vecs[0],
        vecs[1],
        qkvw.T,
        qkvb.reshape(-1),
        pre,
        post,
        postb.reshape(-1),
        projg.T,
        vecs[2],
        vecs[3],
        vecs[4],
        vecs[5],
        fc1g.T,
        b1g.reshape(-1),
        fc2g.T,
        vecs[6],
        vecs[7],
    )


def solution(mesh):
    tokens = P(("dp", "mp"), None, None)
    placed = (
        (tokens, P("dp")) + (P(),) * 12 + (P(None, "mp"), P("mp"), P("mp", None), P(), P(), tokens)
    )
    return jax.shard_map(
        functools.partial(per_device, mesh.shape["dp"], mesh.shape["mp"]),
        mesh=mesh,
        in_specs=placed,
        out_specs=(
            tokens, tokens, P("dp"), P("dp"), P(None, "dp"), P("dp"), P(), P(), P(),
            P(None, "dp"), P("dp"), P("dp"), P("dp"), P("dp"), P(None, ("mp", "dp")),
            P(("mp", "dp")), P("mp", "dp"), P("dp"), P("dp"),
        ),
        check_vma=False,
    )
```

```python
import functools

import jax
import jax.numpy as jnp
from jax import lax
from jax.experimental import pallas as pl
from jax.experimental.pallas import tpu as pltpu
from jax.sharding import PartitionSpec as P

BF = jnp.bfloat16
F32 = jnp.float32
LOG2E = 1.4426950408889634
EPS = 1e-06
VMEM_LIMIT = 20 * 1024 * 1024


def nn(a, b):
    return lax.dot_general(a, b, (((1,), (0,)), ((), ())), preferred_element_type=F32)


def nt(a, b):
    return lax.dot_general(a, b, (((1,), (1,)), ((), ())), preferred_element_type=F32)


def tn(a, b):
    return lax.dot_general(a, b, (((0,), (0,)), ((), ())), preferred_element_type=F32)


def exact(a, b, dims):
    return lax.dot_general(
        a, b, (dims, ((), ())), precision=lax.Precision.HIGHEST, preferred_element_type=F32
    )


def normalized(x):
    mean = jnp.mean(x, axis=-1, keepdims=True)
    c = x - mean
    r = lax.rsqrt(jnp.mean(c * c, axis=-1, keepdims=True) + EPS)
    return c * r, r


def norm_back(cot, n, r, gain):
    cg = cot * gain
    return r * (
        cg
        - jnp.mean(cg, axis=-1, keepdims=True)
        - n * jnp.mean(cg * n, axis=-1, keepdims=True)
    )


def colsum(x):
    return jnp.sum(x, axis=0, keepdims=True)


def split(x):
    hi = x.astype(BF)
    return jnp.concatenate([hi, (x - hi.astype(F32)).astype(BF)], axis=1)


def row(ref):
    return ref[...].reshape(1, ref.shape[0])


def inverse(x):
    near = pl.reciprocal(x, approx=True)
    return near * (2.0 - x * near)


def gelu_parts(z):
    e = jnp.exp2(z * z * (-0.5 * LOG2E))
    t = inverse(1.0 + jnp.abs(z) * (0.3275911 * 0.7071067811865476))
    poly = t * (
        0.5 * 0.254829592
        + t
        * (
            0.5 * -0.284496736
            + t * (0.5 * 1.421413741 + t * (0.5 * -1.453152027 + t * (0.5 * 1.061405429)))
        )
    )
    tail = poly * e
    phi = jnp.where(z >= 0, 1.0 - tail, tail)
    return phi, phi + z * e * 0.3989422804014327


def head_of_lane(shape, axis, head_dim):
    return lax.broadcasted_iota(jnp.int32, shape, axis) // head_dim


def chunks(count, size=16):
    return [slice(at, at + size) for at in range(0, count, size)]


def fold(x):
    return sum(x[at : at + 8] for at in range(8, x.shape[0], 8)) + x[0:8]


def pack_kernel(w1, w2, b1, *refs):
    many = (len(refs) - 3) // 2
    sources, other, held, b1_v, sems = refs[:many], refs[many], refs[many + 1 : -2], refs[-2], refs[-1]
    feats = w1.shape[0]
    core = jnp.bitwise_and(lax.axis_index("dp"), 1)
    bias_copy = pltpu.make_async_copy(b1, b1_v, sems.at[0])
    own = [pltpu.make_async_copy(w, other.at[0:feats], sems.at[1]) for w in (w1, w2)]
    copies = [
        pltpu.make_async_copy(sources[j], held[j], sems.at[2 + j]) for j in range(many)
    ]
    bias_copy.start()
    for j in range(2):
        pl.when(core == j)(own[j].start)
    for copy in copies:
        copy.start()
    bias_copy.wait()
    rest = row(b1_v)
    place = lax.broadcasted_iota(jnp.int32, (16, feats), 0)
    bias = jnp.zeros((16, feats), F32)
    for j in range(3):
        term = rest.astype(BF).astype(F32)
        bias = jnp.where(place == j, term, bias)
        rest = rest - term
    other[feats:, :] = bias.astype(BF)
    for j in range(2):
        pl.when(core == j)(own[j].wait)
    for copy in copies:
        copy.wait()


def attn_fwd_kernel(first, share, *refs):
    counts, post_s, postb_s, tok, og, n1g, n1b, qkvb, pre, post, postb, projb = refs[:12]
    gamma1, n2g, n2b, wqkv, wproj = refs[12:17]
    a1_o, q_o, k_o, v_o, p_o, o_o, x1_o, u_o, a2_o, dy_o, mpre, mpost, mixb = refs[-20:-7]
    pad, kk, attended_t, probs, wide, logits, mixed = refs[-7:]
    images, patches, feats = tok.shape
    rows = pad.shape[0]
    heads = mpre.shape[0]
    head_dim = feats // heads
    slots = q_o.shape[1]

    spread = (
        head_of_lane((heads, feats), 1, head_dim)
        == lax.broadcasted_iota(jnp.int32, (heads, feats), 0)
    ).astype(F32)
    mpre[...] = exact(pre[...], spread, ((1,), (0,))) * (head_dim**-0.5 * LOG2E)
    mpost[...] = exact(post[...], spread, ((0,), (0,)))
    mixb[...] = exact(row(postb), spread, ((1,), (0,)))

    @pl.loop(first, first + share)
    def _(i):
        pad[patches:, :] = jnp.zeros((rows - patches, feats), F32)
        live = (lax.axis_index("mp") * images + i < counts[0]).astype(F32)
        pad[0:patches, :] = og[i].astype(F32) * live
        dy_o[i] = pad[...].astype(BF)
        pad[0:patches, :] = tok[i].astype(F32)
        gain, shift = row(n1g), row(n1b)
        for c in chunks(rows):
            n, _ = normalized(pad[c, :])
            a1_o[i, c, :] = (n * gain + shift).astype(BF)
        wide[...] = nn(a1_o[i], wqkv[...])
        bias = row(qkvb)
        q_o[i, rows:] = jnp.zeros((slots - rows, feats), BF)
        for c in chunks(rows):
            q, k, v = (
                wide[c, j * feats : (j + 1) * feats] + bias[:, j * feats : (j + 1) * feats]
                for j in range(3)
            )
            q_o[i, c, :] = q.astype(BF)
            v_o[i, c, :] = v.astype(BF)
            k = k.astype(BF)
            k_o[i, c, :] = k
            kf = k.astype(F32)
            for g in range(heads):
                at = slice(g * rows + c.start, g * rows + c.stop)
                scaled = kf * mpre[g : g + 1, :]
                hi = scaled.astype(BF)
                kk[at, 0:feats] = hi
                kk[at, feats:] = (scaled - hi.astype(F32)).astype(BF)
        q2 = jnp.concatenate([q_o[i], q_o[i]], axis=1)
        vt = v_o[i].T
        many = heads // 2
        half = many * rows
        tail = patches // 8 * 8
        inside = lax.broadcasted_iota(jnp.int32, (rows - tail, 128), 0) < patches - tail
        real = (lax.broadcasted_iota(jnp.int32, (rows, 128), 0) < patches).astype(BF)
        start = nn(vt, real)
        for s in range(2):
            part = slice(s * half, (s + 1) * half)
            logits[part, :] = nt(kk[part, :], q2)
        for g in range(heads):
            for lane in range(0, slots, 128):
                x = logits[g * rows : (g + 1) * rows, lane : lane + 128]
                x = jnp.concatenate([x[0:tail], jnp.where(inside, x[tail:], -1e30)], axis=0)
                e = jnp.exp2(x - jnp.max(x, axis=0, keepdims=True))
                inv = 1.0 / jnp.sum(e, axis=0, keepdims=True)
                p = (e * inv).astype(BF)
                probs[g * rows : (g + 1) * rows, lane : lane + 128] = p
                p_o[i, g, :, lane : lane + 128] = p
            mixed[g] = nn(vt, probs[g * rows : (g + 1) * rows, :])
        for c in chunks(feats):
            g = c.start // head_dim
            first = start[c] * postb_s[g]
            for lane in range(0, slots, 128):
                total = first
                for h in range(heads):
                    total = total + mixed[h, c, lane : lane + 128] * post_s[g, h]
                attended_t[c, lane : lane + 128] = total.astype(BF)
        o_o[i] = attended_t[...].T[0:rows]
        wide[:, 0:feats] = nn(o_o[i], wproj[...])
        bias, scale, gain, shift = row(projb), row(gamma1), row(n2g), row(n2b)
        for c in chunks(rows):
            u = wide[c, 0:feats] + bias
            x1 = pad[c, :] + scale * u
            u_o[i, c, :] = u
            x1_o[i, c, :] = x1
            n, _ = normalized(x1)
            a2_o[i, c, :] = (n * gain + shift).astype(BF)


def store_blocks(count, put):
    mine = lax.axis_index("dp")
    for core in range(2):

        @pl.when(jnp.bitwise_and(mine, 1) == core)
        def _(core=core):
            for b in range(count):
                place = jnp.bitwise_xor(jnp.int32(b >> 1), jnp.right_shift(mine, 1))
                put((b ^ core) & 1, place, b)


def mlp_units(a2, dfs, w1, b1, w2, hids, dzs, zs, ghs, b1_o, units, store, use):
    size = a2.shape[0] // units
    width = w2.shape[0]
    lanes = 256
    places = [slice(u * size, (u + 1) * size) for u in range(units)]
    sums = {}

    def products(u):
        zs[u % 2] = nn(a2[places[u], :], w1[...])
        ghs[u % 2] = nt(dfs[places[u], :], w2[...])

    products(0)
    for u in range(units):
        if u + 1 < units:
            products(u + 1)
        for first in range(0, width, lanes):
            part = slice(first, first + lanes)
            bias = b1[:, part]
            for c in chunks(size):
                zc = zs[u % 2, c, part] + bias
                phi, slope = gelu_parts(zc)
                dz = (ghs[u % 2, c, part] * slope).astype(BF)
                at = slice(places[u].start + c.start, places[u].start + c.stop)
                hids[at, part] = (zc * phi).astype(BF)
                dzs[at, part] = dz
                more = fold(dz.astype(F32))
                sums[first] = sums[first] + more if first in sums else more
        store(places[u], nn(hids[places[u], :], w2[...]), nt(dzs[places[u], :], w1[...]))
        if u > 0:
            use(places[u - 1])
    use(places[units - 1])
    for first, value in sums.items():
        b1_o[:, first : first + lanes] = colsum(value)


def mlp_first_kernel(
    a2, dy, gamma2, w1_own, b1_own, w2_own, near, far,
    f_o, da2_o, grads, b1_o, a2t, dft,
    w1, w2, b1, hids, dzs, dfs, zs, ghs,
):
    total, feats = f_o.shape
    w1[:, 0:feats] = w1_own[...]
    w2[0:feats, :] = w2_own[...]
    for core in range(2):

        @pl.when(jnp.bitwise_and(lax.axis_index("dp"), 1) == core)
        def _(core=core):
            one, two = (near, far) if core == 0 else (far, near)
            w1[:, feats:] = one[0, 0:feats]
            w2[feats:, :] = two[0, 0:feats]

    b1[:, 0:feats] = row(b1_own)
    b1[:, feats:] = colsum(near[0, feats : feats + 16].astype(F32))
    gain = row(gamma2)
    for c in chunks(total):
        dfs[c, :] = (dy[c, :].astype(F32) * gain).astype(BF)

    def store(rows, f, da2):
        f_o[rows, :] = f
        da2_o[rows, :] = da2

    mlp_units(a2, dfs, w1, b1, w2, hids, dzs, zs, ghs, b1_o, 3, store, lambda rows: None)
    a2t[...] = a2[...].T
    dft[...] = dfs[...].T
    grads[0] = nn(a2t[...], dzs[...]).astype(BF).T
    down = nn(dft[...], hids[...]).astype(BF)
    for c in range(2):
        grads[1, c * feats : (c + 1) * feats, :] = down[:, c * feats : (c + 1) * feats]


def mlp_rest_kernel(
    counts, a2, dy, x1, u, o, f0, da20, near, far, last, far_last, grads, a2t, dft, wproj, gamma1, n2g, fc2b, gamma2,
    out_o, dx1_o, do_o, keep, send, b1_o, acc_o,
    w1, w2, b1, hids, dzs, dfs, zs, ghs, fs, da2s, dus, ups, downs, projs, out_v, sems,
):
    total, feats = f0.shape
    images, patches = out_o.shape[:2]
    image_rows = total // images
    m_idx = lax.axis_index("mp")
    acc_o[...] = jnp.zeros_like(acc_o)
    b1[:, 0:feats] = colsum(near[1, feats : feats + 16].astype(F32))
    b1[:, feats:] = colsum(last[feats : feats + 16].astype(F32))
    for core in range(2):

        @pl.when(jnp.bitwise_and(lax.axis_index("dp"), 1) == core)
        def _(core=core):
            one, two = (near, far) if core == 0 else (far, near)
            w1[:, 0:feats] = one[1, 0:feats]
            w2[0:feats, :] = two[1, 0:feats]
            one, two = (last, far_last) if core == 0 else (far_last, last)
            w1[:, feats:] = one[0:feats]
            w2[feats:, :] = two[0:feats]

    gain2 = row(gamma2)
    bias, gain, scale = row(fc2b), row(n2g), row(gamma1)
    for c in chunks(total):
        dfs[c, :] = (dy[c, :].astype(F32) * gain2).astype(BF)

    def out_copy(image):
        return pltpu.make_async_copy(out_v.at[image], out_o.at[image], sems.at[image])

    def store(rows, f, da2):
        fs[rows, :] = f
        da2s[rows, :] = da2

    def use(rows):
        sums = [jnp.zeros((8, feats), F32) for _ in range(6)]
        for c in chunks(rows.stop - rows.start):
            at = slice(rows.start + c.start, rows.start + c.stop)
            fc = fs[at, :] + f0[at, :] + bias
            dac = da2s[at, :] + da20[at, :]
            x1c = x1[at, :]
            dyc = dy[at, :].astype(F32)
            n, r = normalized(x1c)
            dx1 = dyc + norm_back(dac, n, r, gain)
            dx1_o[at, :] = dx1
            du = (dx1 * scale).astype(BF)
            dus[at, :] = du
            image = at.start // image_rows
            first = at.start - image * image_rows
            live = (m_idx * images + image < counts[0]).astype(F32)
            out = ((x1c + gain2 * fc) * live).astype(BF)
            if first + 16 <= patches:
                out_v[image, first : first + 16, :] = out
            else:
                out_v[image, first:patches, :] = out[0 : patches - first]
            terms = (
                du.astype(F32), u[at, :] * dx1, dac * n, dac, dfs[at, :].astype(F32), fc * dyc,
            )
            sums = [s + fold(t) for s, t in zip(sums, terms)]
        for j in range(6):
            acc_o[j : j + 1, :] += colsum(sums[j])
        do = nt(dus[rows, :], wproj[...]).astype(BF)
        for at in range(0, rows.stop - rows.start, image_rows):
            image = (rows.start + at) // image_rows
            out_copy(image).start()
            do_o[image, 0:image_rows] = do[at : at + image_rows]
            do_o[image, image_rows:] = jnp.zeros((do_o.shape[1] - image_rows, feats), BF)

    mlp_units(a2, dfs, w1, b1, w2, hids, dzs, zs, ghs, b1_o, 3, store, use)
    ups[...] = nn(a2t[...], dzs[...]).astype(BF).T
    downs[...] = nn(dft[...], hids[...]).astype(BF)
    projs[...] = tn(dus[...], o[...]).astype(BF)
    count = 2 * keep.shape[0]
    size = feats // count
    outs = (keep, send)

    def put(which, place, b):
        out = outs[which]
        for c in range(2):
            part = slice(c * feats, (c + 1) * feats)
            up = slice(c * feats + b * size, c * feats + (b + 1) * size)
            down = slice(b * size, (b + 1) * size)
            pieces = (grads[0, up, :], grads[1, up, :])
            for j, piece in enumerate(pieces):
                out[place, (2 * c + j) * size : (2 * c + j + 1) * size, :] = piece
            pieces = (ups[up, :], downs[down, part])
            for j, piece in enumerate(pieces):
                out[place, (4 + 2 * c + j) * size : (5 + 2 * c + j) * size, :] = piece
        out[place, 8 * size : 9 * size, :] = projs[b * size : (b + 1) * size, :]

    store_blocks(count, put)
    for image in range(images):
        out_copy(image).wait()


def attn_bwd_kernel(first, share, *refs):
    pre_s, do_r, q_r, k_r, v_r, p_r, dx1, tok, mpre, mpost, mixb, wqkv, n1g = refs[:13]
    dqkv_o, in_o, acc_o, vgs, dls, dq_t, dps, dvs, dks, dqs, da1, pad, in_v, sems = refs[-14:]
    slots, feats = do_r.shape[1:]
    patches = tok.shape[1]
    rows = k_r.shape[1]
    heads = mpre.shape[0]
    head_dim = feats // heads
    many = heads // 2
    half = many * rows
    acc_o[...] = jnp.zeros_like(acc_o)

    def in_copy(i):
        return pltpu.make_async_copy(in_v.at[i - first], in_o.at[i], sems.at[i - first])

    @pl.loop(first, first + share)
    def _(i):
        do_sum = jnp.zeros((8, feats), F32)
        for c in chunks(rows):
            vf = v_r[i, c, :].astype(F32)
            do_sum = do_sum + fold(do_r[i, c, :].astype(F32))
            for h in range(heads):
                vgs[h * rows + c.start : h * rows + c.stop, :] = (vf * mpost[h : h + 1, :]).astype(BF)
        do_sum = colsum(do_sum)
        q = q_r[i]
        do = do_r[i]
        kt = k_r[i].T
        parts = [slice(s * half, (s + 1) * half) for s in range(2)]
        for part in parts:
            dps[part, :] = nt(vgs[part, :], do)
        for s, part in enumerate(parts):
            dvs[part, :] = nn(p_r[i, s * many : (s + 1) * many].reshape(half, slots), do)
        for s, part in enumerate(parts):
            for h in range(s * many, (s + 1) * many):
                at = slice(h * rows, (h + 1) * rows)
                for lane in range(0, slots, 128):
                    dp = dps[at, lane : lane + 128]
                    pf = p_r[i, h, :, lane : lane + 128].astype(F32)
                    mean = jnp.sum(dp * pf, axis=0, keepdims=True) / jnp.sum(pf, axis=0, keepdims=True)
                    dls[at, lane : lane + 128] = (pf * (dp - mean)).astype(BF)
                dqs[h] = nn(kt, dls[at, :])
            dks[part, :] = nn(dls[part, :], q)

        bias_row = mixb[...] * do_sum
        v_sum = jnp.zeros((8, feats), F32)
        dv_sum = jnp.zeros((8, feats), F32)
        sums = [jnp.zeros((8, feats), F32) for _ in range(heads)]
        for c in chunks(rows):
            vf = v_r[i, c, :].astype(F32)
            dv = bias_row
            for h in range(heads):
                this = dvs[h * rows + c.start : h * rows + c.stop, :]
                dv = dv + this * mpost[h : h + 1, :]
                sums[h] = sums[h] + fold(vf * this)
            if c.stop > patches:
                inside = lax.broadcasted_iota(jnp.int32, dv.shape, 0) < patches - c.start
                dv = jnp.where(inside, dv, 0.0)
                vf = jnp.where(inside, vf, 0.0)
            low = dv.astype(BF)
            dqkv_o[i, c, 2 * feats :] = low
            dv_sum = dv_sum + fold(low.astype(F32))
            v_sum = v_sum + fold(vf)
        for h in range(heads):
            acc_o[h : h + 1, :] += colsum(sums[h])
        acc_o[2 * heads : 2 * heads + 1, :] += do_sum * colsum(v_sum)
        acc_o[2 * heads + 10 : 2 * heads + 11, :] += colsum(dv_sum)

        for c in chunks(feats):
            g = c.start // head_dim
            for lane in range(0, slots, 128):
                total = 0.0
                for h in range(heads):
                    total = total + dqs[h, c, lane : lane + 128] * pre_s[h, g]
                dq_t[c, lane : lane + 128] = (total * head_dim**-0.5).astype(BF)
        dq = dq_t[...].T[0:rows]
        dqkv_o[i, :, 0:feats] = dq
        dk_sum = jnp.zeros((8, feats), F32)
        sums = [jnp.zeros((8, feats), F32) for _ in range(heads)]
        for c in chunks(rows):
            kf = k_r[i, c, :].astype(F32)
            dk = 0.0
            for h in range(heads):
                this = dks[h * rows + c.start : h * rows + c.stop, :]
                dk = dk + this * mpre[h : h + 1, :]
                sums[h] = sums[h] + fold(kf * this)
            low = (dk * (1.0 / LOG2E)).astype(BF)
            dqkv_o[i, c, feats : 2 * feats] = low
            dk_sum = dk_sum + fold(low.astype(F32))
        for h in range(heads):
            acc_o[heads + h : heads + h + 1, :] += colsum(sums[h])
        acc_o[2 * heads + 8 : 2 * heads + 9, :] += colsum(dq.astype(F32))
        acc_o[2 * heads + 9 : 2 * heads + 10, :] += colsum(dk_sum)

        pad[patches:, :] = jnp.zeros((rows - patches, feats), F32)
        pad[0:patches, :] = tok[i].astype(F32)
        da1[...] = nt(dqkv_o[i], wqkv[...])
        gain = row(n1g)
        sums = [jnp.zeros((8, feats), F32) for _ in range(2)]
        for c in chunks(rows):
            n, r = normalized(pad[c, :])
            cot = da1[c, :]
            grad = dx1[i, c, :] + norm_back(cot, n, r, gain)
            sums = [sums[0] + fold(cot * n), sums[1] + fold(cot)]
            if c.stop <= patches:
                in_v[i - first, c, :] = grad
            else:
                in_v[i - first, c.start : patches, :] = grad[0 : patches - c.start]
        for j in range(2):
            acc_o[2 * heads + 11 + j : 2 * heads + 12 + j, :] += colsum(sums[j])
        in_copy(i).start()

    @pl.loop(first, first + share)
    def _(i):
        in_copy(i).wait()


def qkv_grad_kernel(heads, dqkv, *refs):
    accs = refs[:-8]
    a1, acc_mlp, b1_first, b1_rest, keep, send, small, grads = refs[-8:]
    feats = a1.shape[1]
    count = 2 * keep.shape[0]
    size = 3 * feats // count
    acc = accs[0][...]
    for other in accs[1:]:
        acc = acc + other[...]
    small[...] = jnp.zeros_like(small)
    small[0:2, :] = acc[2 * heads + 11 : 2 * heads + 13]
    small[2:8, :] = acc_mlp[0:6, :]
    small[8:11, :] = acc[2 * heads + 8 : 2 * heads + 11]
    head_dim = feats // heads
    lanes = 2 * heads * heads
    gather = (
        head_of_lane((feats, lanes), 0, head_dim)
        == lax.broadcasted_iota(jnp.int32, (feats, lanes), 1) % heads
    ).astype(F32)
    sums = exact(acc[0 : 2 * heads + 8], gather, ((1,), (0,)))
    place = head_of_lane((2 * heads, lanes), 1, heads) == lax.broadcasted_iota(
        jnp.int32, (2 * heads, lanes), 0
    )
    small[11:12, 0:lanes] = colsum(jnp.where(place, sums[0 : 2 * heads], 0.0))
    small[11:12, lanes : 2 * lanes] = sums[2 * heads : 2 * heads + 1]
    m_idx = lax.axis_index("mp")
    for c, ref in enumerate((b1_first, b1_first, b1_rest, b1_rest)):
        place = 12 + jnp.bitwise_xor(m_idx, c)
        small[pl.ds(place, 1), :] = ref[:, (c % 2) * feats : (c % 2 + 1) * feats]
    low = small[...].astype(BF)
    outs = (keep, send)

    grads[...] = tn(a1[...], dqkv[...]).astype(BF).T

    def put(which, place, b):
        outs[which][place, 0:size, :] = grads[b * size : (b + 1) * size, :]
        outs[which][place, size : size + 16, :] = low
        if outs[which].shape[1] > size + 16:
            outs[which][place, size + 16 :, :] = jnp.zeros_like(outs[which][place, size + 16 :, :])

    store_blocks(count, put)


def final_kernel(heads, size, many, *refs):
    parts = refs[0 : 1 + many]
    mlp_mine, got_z = refs[1 + many], refs[2 + many : 2 + 2 * many]
    qkv_o, qkvb_o, pre_o, post_o, postb_o, b1_o, *vecs_o, fc1_o, fc2_o, proj_o, held, held_proj = refs[-19:]
    block = fc1_o.shape[0]
    for place, out in enumerate((fc1_o, fc2_o)):
        rows = slice(place * block, (place + 1) * block)
        out[...] = mlp_mine[rows, :] + sum(g[rows, :].astype(F32) for g in got_z)
    d_idx = lax.axis_index("dp")
    m_idx = lax.axis_index("mp")
    quarter, feats = held.shape[1:]
    for j, part in enumerate(parts):
        place = jnp.bitwise_xor(m_idx, j)
        value = part[...].astype(F32)
        held[place] = value[0:quarter]
        held_proj[place] = value[quarter:]
    total = held[...].reshape(-1, feats)
    proj_o[...] = held_proj[...].reshape(-1, feats)[0:block]
    qkv_o[...] = total[0:size]
    small = total[size : size + 16]

    def own(value, width, index):
        lanes = value.shape[1]
        return pltpu.roll(value, lax.rem(lanes - index * width, lanes), axis=1)[:, 0:width]

    width = vecs_o[0].shape[1]
    vecs = own(small[0:8], width, d_idx)
    for j, ref in enumerate(vecs_o):
        ref[...] = vecs[j : j + 1]
    flat = jnp.concatenate([small[8 + j : 9 + j] for j in range(3)], axis=1)
    qkvb_o[...] = own(jnp.broadcast_to(flat, (8, 3 * feats)), qkvb_o.shape[1], d_idx)[0:1]
    b1 = own(small[8:16], b1_o.shape[1], d_idx)[4:8]
    pick = lax.broadcasted_iota(jnp.int32, b1.shape, 0) == m_idx
    b1_o[...] = colsum(jnp.where(pick, b1, 0.0))
    mix = small[11:12]
    hh = heads * heads
    line = lax.broadcasted_iota(jnp.int32, (heads, hh), 0)
    lane = lax.broadcasted_iota(jnp.int32, (heads, hh), 1)
    fold = (
        lax.broadcasted_iota(jnp.int32, (hh, heads), 0) % heads
        == lax.broadcasted_iota(jnp.int32, (hh, heads), 1)
    ).astype(F32)
    head_dim = feats // heads

    def square(values):
        return exact(jnp.where(lane // heads == line, values, 0.0), fold, ((1,), (0,)))

    post_o[...] = square(mix[:, 0:hh]).T
    pre_o[...] = square(mix[:, hh : 2 * hh]) * (head_dim**-0.5)
    postb_o[...] = mix[:, 2 * hh : 2 * hh + heads]


def whole(shape):
    return pl.BlockSpec(shape, lambda i: (0,) * len(shape))


def each(shape, first=0, many=1):
    return pl.BlockSpec((many,) + shape[1:], lambda i: (i + first,) + (0,) * (len(shape) - 1))


SCALARS = pl.BlockSpec(memory_space=pltpu.SMEM)
IN_VMEM = pl.BlockSpec(memory_space=pltpu.VMEM)
IN_HBM = pl.BlockSpec(memory_space=pltpu.HBM)


def kept(a):
    return pltpu.with_memory_space_constraint(a, pltpu.HBM)


def sds(shape, dtype):
    return jax.ShapeDtypeStruct(shape, dtype)


def call(
    kernel, grid, ins, in_specs, outs, out_specs, scratch=(), flops=0, name=None, aliases=None,
    limit=VMEM_LIMIT,
):
    size = lambda a: a.size * a.dtype.itemsize
    return pl.pallas_call(
        kernel,
        grid=grid,
        in_specs=in_specs,
        out_specs=out_specs,
        out_shape=outs,
        scratch_shapes=scratch,
        input_output_aliases=aliases or {},
        compiler_params=pltpu.CompilerParams(vmem_limit_bytes=limit),
        cost_estimate=pl.CostEstimate(
            flops=flops,
            bytes_accessed=sum(size(a) for a in ins) + sum(size(a) for a in outs),
            transcendentals=0,
        ),
        name=name,
    )(*ins)


def xor_perm(count, mask):
    return [(j, j ^ mask) for j in range(count)]


def dp_hops(dp):
    bits = dp.bit_length() - 1
    groups = []
    at = 1
    while at < bits:
        groups.append((at, min(2, bits - at)))
        at += groups[-1][1]
    return groups


def dp_scatter(value, dp):
    for at, many in dp_hops(dp):
        value = value.reshape((-1, 1 << many) + value.shape[1:])
        got = [
            lax.ppermute(value[:, j].astype(BF), "dp", xor_perm(dp, j << at))
            for j in range(1, 1 << many)
        ]
        value = value[:, 0] + sum(g.astype(F32) for g in got)
    return value.reshape(value.shape[-2:])


def per_device(
    dp, mp,
    tokens_in, image_counts, norm1_gain, norm1_bias, qkv_weight, qkv_bias,
    mix_pre, mix_post, mix_post_bias, proj_weight, proj_bias, gamma1,
    norm2_gain, norm2_bias, fc1_weight, fc1_bias, fc2_weight, fc2_bias, gamma2, out_grad,
):
    images, patches, feats = tokens_in.shape
    heads = mix_pre.shape[0]
    rows = -(-patches // 16) * 16
    slots = -(-patches // 128) * 128
    hidden = fc1_weight.shape[1]
    tok_rows = (images, rows, feats)
    slot_rows = (images, slots, feats)
    prob_shape = (images, heads, rows, slots)
    mix_shape = (heads, feats)
    operands = [
        tokens_in, out_grad, norm1_gain, norm1_bias, qkv_bias, mix_pre, mix_post,
        mix_post_bias, proj_bias, gamma1, norm2_gain, norm2_bias, qkv_weight, proj_weight,
    ]

    ins = [kept(a) for a in [fc1_weight, fc2_weight, fc1_bias] + operands]
    outs = [sds((feats + 16, hidden), BF)] + [sds(a.shape, a.dtype) for a in operands]
    other, *held = call(
        pack_kernel,
        (),
        ins,
        [IN_HBM] * len(ins),
        outs,
        [IN_VMEM] * len(outs),
        [pltpu.VMEM(fc1_bias.shape, F32), pltpu.SemaphoreType.DMA((2 + len(operands),))],
        name="pack",
    )
    near = [lax.ppermute(other, "mp", xor_perm(mp, j)) for j in (1, 2)]

    shares = [images - 2, 2] if images > 2 else [images]
    carried = []
    for s, share in enumerate(shares):
        first = sum(shares[:s])
        ins = [image_counts, mix_post, mix_post_bias] + held
        outs = call(
            functools.partial(attn_fwd_kernel, first, share),
            (),
            ins + carried,
            [SCALARS] * 3
            + [IN_VMEM] * 14
            + [pl.BlockSpec(memory_space=pl.ANY)] * len(carried),
            [
                sds(tok_rows, BF), sds(slot_rows, BF), sds(tok_rows, BF), sds(tok_rows, BF),
                sds(prob_shape, BF), sds(tok_rows, BF), sds(tok_rows, F32), sds(tok_rows, F32),
                sds(tok_rows, BF), sds(tok_rows, BF), sds(mix_shape, F32), sds(mix_shape, F32),
                sds((1, feats), F32),
            ],
            [IN_VMEM] * 13,
            [
                pltpu.VMEM((rows, feats), F32), pltpu.VMEM((heads * rows, 2 * feats), BF),
                pltpu.VMEM((feats, slots), BF), pltpu.VMEM((heads * rows, slots), BF),
                pltpu.VMEM((rows, 3 * feats), F32), pltpu.VMEM((heads * rows, slots), F32),
                pltpu.VMEM((heads, feats, slots), F32),
            ],
            flops=share * 15 * 10**8,
            name="attn_fwd",
            aliases={len(ins) + j: j for j in range(10)} if carried else None,
        )
        carried, (mpre, mpost, mixb) = list(outs[:10]), outs[10:]
        if s == 0:
            near, carried[0] = lax.optimization_barrier((near, carried[0]))
            last = lax.ppermute(near[1], "mp", xor_perm(mp, 1))
            near = jnp.stack(near)
            far = lax.ppermute(near, "dp", xor_perm(dp, 1))
    a1, q, k, v, prob, o, x1, u, a2, dy = carried
    far, a2 = lax.optimization_barrier((far, a2))

    block = feats // dp
    total = images * rows
    flat = (total, feats)
    a2, dy, x1, u, o = (a.reshape(flat) for a in (a2, dy, x1, u, o))
    ins = [a2, dy, gamma2, fc1_weight, fc1_bias, fc2_weight, near, far]
    wide = 2 * hidden
    grad_shape = (2, wide, feats)
    f0, da20, grads0, b1_0, a2t, dft = call(
        mlp_first_kernel,
        (),
        ins,
        [IN_VMEM] * len(ins),
        [
            sds(flat, F32), sds(flat, F32), sds(grad_shape, BF), sds((1, wide), F32),
            sds((feats, total), BF), sds((feats, total), BF),
        ],
        [IN_VMEM] * 6,
        [
            pltpu.VMEM((feats, wide), BF), pltpu.VMEM((wide, feats), BF),
            pltpu.VMEM((1, wide), F32), pltpu.VMEM((total, wide), BF),
            pltpu.VMEM((total, wide), BF), pltpu.VMEM(flat, BF),
            pltpu.VMEM((2, total // 3, wide), F32), pltpu.VMEM((2, total // 3, wide), F32),
        ],
        flops=images * 8 * 10**8,
        name="mlp_first",
    )

    last, f0 = lax.optimization_barrier((last, f0))
    far_last = lax.ppermute(last, "dp", xor_perm(dp, 1))

    grad_rows = 9 * block
    half_shape = (dp // 2, grad_rows, feats)
    ins = [
        image_counts, a2, dy, x1, u, o, f0, da20, near, far, last, far_last, grads0, a2t, dft,
        proj_weight, gamma1,
        norm2_gain, fc2_bias, gamma2,
    ]
    layer_out, dx1, do, keep, send, b1_1, acc_mlp = call(
        mlp_rest_kernel,
        (),
        ins,
        [SCALARS] + [IN_VMEM] * (len(ins) - 1),
        [
            sds(tokens_in.shape, BF), sds(flat, F32), sds(slot_rows, BF), sds(half_shape, BF),
            sds(half_shape, BF), sds((1, wide), F32), sds((8, feats), F32),
        ],
        [IN_HBM] + [IN_VMEM] * 6,
        [
            pltpu.VMEM((feats, wide), BF), pltpu.VMEM((wide, feats), BF),
            pltpu.VMEM((1, wide), F32), pltpu.VMEM((total, wide), BF),
            pltpu.VMEM((total, wide), BF), pltpu.VMEM(flat, BF),
            pltpu.VMEM((2, total // 3, wide), F32), pltpu.VMEM((2, total // 3, wide), F32),
            pltpu.VMEM(flat, F32), pltpu.VMEM(flat, F32), pltpu.VMEM(flat, BF),
            pltpu.VMEM((wide, feats), BF), pltpu.VMEM((feats, wide), BF),
            pltpu.VMEM((feats, feats), BF), pltpu.VMEM(tokens_in.shape, BF),
            pltpu.SemaphoreType.DMA((images,)),
        ],
        flops=images * 9 * 10**8,
        name="mlp_rest",
    )
    got = lax.ppermute(send, "dp", xor_perm(dp, 1))
    dx1 = dx1.reshape(tok_rows)

    shares = [1, images - 1] if images > 1 else [1]
    dqkv_shape = (images, rows, 3 * feats)
    carried, accs = [], []
    for s, share in enumerate(shares):
        first = sum(shares[:s])
        ins = [mix_pre, do, q, k, v, prob, dx1, tokens_in, mpre, mpost, mixb, qkv_weight, norm1_gain]
        *carried, acc = call(
            functools.partial(attn_bwd_kernel, first, share),
            (),
            ins + carried,
            [SCALARS]
            + [IN_VMEM] * (len(ins) - 1)
            + [pl.BlockSpec(memory_space=pl.ANY)] * len(carried),
            [sds(dqkv_shape, BF), sds(tokens_in.shape, F32), sds((2 * heads + 16, feats), F32)],
            [IN_VMEM, IN_HBM, IN_VMEM],
            [
                pltpu.VMEM((heads * rows, feats), BF), pltpu.VMEM((heads * rows, slots), BF),
                pltpu.VMEM((feats, slots), BF), pltpu.VMEM((heads * rows, slots), F32),
                pltpu.VMEM((heads * rows, feats), F32), pltpu.VMEM((heads * rows, feats), F32),
                pltpu.VMEM((heads, feats, slots), F32), pltpu.VMEM((rows, feats), F32),
                pltpu.VMEM((rows, feats), F32), pltpu.VMEM((share, patches, feats), F32),
                pltpu.SemaphoreType.DMA((share,)),
            ],
            flops=share * 20 * 10**8,
            name="attn_bwd",
            aliases={len(ins): 0, len(ins) + 1: 1} if carried else None,
        )
        accs.append(acc)
        if s == 0:
            (keep, got), acc = lax.optimization_barrier(((keep, got), acc))
            mine = dp_scatter(keep.astype(F32) + got.astype(F32), dp)
            accs[0], do = lax.optimization_barrier((acc, do))
    dqkv, in_grad = carried
    mine, dqkv = lax.optimization_barrier((mine, dqkv))
    mlp_mine = mine
    low = mine.astype(BF)
    m_idx = lax.axis_index("mp")
    share_rows = -(-block // (16 * mp)) * 16
    proj = jnp.pad(mine[8 * block :], ((0, mp * share_rows - block), (0, 0)))

    def proj_share(j):
        return lax.dynamic_slice_in_dim(proj, jnp.bitwise_xor(m_idx, j) * share_rows, share_rows)

    got_z = [
        lax.ppermute(
            jnp.concatenate([low[2 * j * block : 2 * (j + 1) * block], proj_share(j).astype(BF)]),
            "mp",
            xor_perm(mp, j),
        )
        for j in range(1, mp)
    ]

    q_block = 3 * feats // dp
    quarter = -(-(q_block + 16) // (8 * mp)) * 8
    half_shape = (dp // 2, mp * quarter, feats)
    ins = [dqkv.reshape(total, 3 * feats)] + accs + [a1.reshape(flat), acc_mlp, b1_0, b1_1]
    keep, send = call(
        functools.partial(qkv_grad_kernel, heads),
        (1,),
        ins,
        [whole(a.shape) for a in ins],
        [sds(half_shape, BF), sds(half_shape, BF)],
        [whole(half_shape), whole(half_shape)],
        [pltpu.VMEM((16, feats), F32), pltpu.VMEM((3 * feats, feats), BF)],
        flops=11 * 10**8,
        name="qkv_grad",
    )
    got = lax.ppermute(send, "dp", xor_perm(dp, 1))
    mine = dp_scatter(keep.astype(F32) + got.astype(F32), dp)
    mine, got_z = lax.optimization_barrier((mine, got_z))

    def part(j):
        return lax.dynamic_slice_in_dim(mine, jnp.bitwise_xor(m_idx, j) * quarter, quarter)

    own = part(0)
    for j in range(1, mp):
        own = own + lax.ppermute(part(j).astype(BF), "mp", xor_perm(mp, j)).astype(F32)
    proj_own = proj_share(0) + sum(g[2 * block :].astype(F32) for g in got_z)
    own = jnp.concatenate([own, proj_own]).astype(BF)
    got = [lax.ppermute(own, "mp", xor_perm(mp, j)) for j in range(1, mp)]
    b1_size = hidden // dp
    ins = [own] + got + [mlp_mine] + got_z
    outs = [
        sds((q_block, feats), F32), sds((1, q_block), F32), sds((heads, heads), F32),
        sds((heads, heads), F32), sds((1, heads), F32), sds((1, b1_size), F32),
    ] + [sds((1, block), F32)] * 8 + [sds((block, feats), F32)] * 3
    qkvw, qkvb, pre, post, postb, b1g, *vecs, fc1g, fc2g, projg = call(
        functools.partial(final_kernel, heads, q_block, mp - 1),
        (1,),
        ins,
        [whole(a.shape) for a in ins],
        outs,
        [whole(a.shape) for a in outs],
        [pltpu.VMEM((mp, quarter, feats), F32), pltpu.VMEM((mp, share_rows, feats), F32)],
        name="final",
    )
    vecs = [a.reshape(-1) for a in vecs]
    return (
        layer_out,
        in_grad,
        vecs[0],
        vecs[1],
        qkvw.T,
        qkvb.reshape(-1),
        pre,
        post,
        postb.reshape(-1),
        projg.T,
        vecs[2],
        vecs[3],
        vecs[4],
        vecs[5],
        fc1g.T,
        b1g.reshape(-1),
        fc2g.T,
        vecs[6],
        vecs[7],
    )


def solution(mesh):
    tokens = P(("dp", "mp"), None, None)
    placed = (
        (tokens, P("dp")) + (P(),) * 12 + (P(None, "mp"), P("mp"), P("mp", None), P(), P(), tokens)
    )
    return jax.shard_map(
        functools.partial(per_device, mesh.shape["dp"], mesh.shape["mp"]),
        mesh=mesh,
        in_specs=placed,
        out_specs=(
            tokens, tokens, P("dp"), P("dp"), P(None, "dp"), P("dp"), P(), P(), P(),
            P(None, "dp"), P("dp"), P("dp"), P("dp"), P("dp"), P(None, ("mp", "dp")),
            P(("mp", "dp")), P("mp", "dp"), P("dp"), P("dp"),
        ),
        check_vma=False,
    )
```

```python
import functools

import jax
import jax.numpy as jnp
from jax import lax
from jax.experimental import pallas as pl
from jax.experimental.pallas import tpu as pltpu
from jax.sharding import PartitionSpec as P

BF = jnp.bfloat16
F32 = jnp.float32
LOG2E = 1.4426950408889634
EPS = 1e-06
VMEM_LIMIT = 20 * 1024 * 1024


def nn(a, b):
    return lax.dot_general(a, b, (((1,), (0,)), ((), ())), preferred_element_type=F32)


def nt(a, b):
    return lax.dot_general(a, b, (((1,), (1,)), ((), ())), preferred_element_type=F32)


def tn(a, b):
    return lax.dot_general(a, b, (((0,), (0,)), ((), ())), preferred_element_type=F32)


def exact(a, b, dims):
    return lax.dot_general(
        a, b, (dims, ((), ())), precision=lax.Precision.HIGHEST, preferred_element_type=F32
    )


def normalized(x):
    mean = jnp.mean(x, axis=-1, keepdims=True)
    c = x - mean
    r = lax.rsqrt(jnp.mean(c * c, axis=-1, keepdims=True) + EPS)
    return c * r, r


def norm_back(cot, n, r, gain):
    cg = cot * gain
    return r * (
        cg
        - jnp.mean(cg, axis=-1, keepdims=True)
        - n * jnp.mean(cg * n, axis=-1, keepdims=True)
    )


def colsum(x):
    return jnp.sum(x, axis=0, keepdims=True)


def split(x):
    hi = x.astype(BF)
    return jnp.concatenate([hi, (x - hi.astype(F32)).astype(BF)], axis=1)


def row(ref):
    return ref[...].reshape(1, ref.shape[0])


def inverse(x):
    near = pl.reciprocal(x, approx=True)
    return near * (2.0 - x * near)


def gelu_parts(z):
    e = jnp.exp2(z * z * (-0.5 * LOG2E))
    t = inverse(1.0 + jnp.abs(z) * (0.3275911 * 0.7071067811865476))
    poly = t * (
        0.5 * 0.254829592
        + t
        * (
            0.5 * -0.284496736
            + t * (0.5 * 1.421413741 + t * (0.5 * -1.453152027 + t * (0.5 * 1.061405429)))
        )
    )
    tail = poly * e
    phi = jnp.where(z >= 0, 1.0 - tail, tail)
    return phi, phi + z * e * 0.3989422804014327


def head_of_lane(shape, axis, head_dim):
    return lax.broadcasted_iota(jnp.int32, shape, axis) // head_dim


def chunks(count, size=16):
    return [slice(at, at + size) for at in range(0, count, size)]


def fold(x):
    return sum(x[at : at + 8] for at in range(8, x.shape[0], 8)) + x[0:8]


def pack_kernel(w1, w2, b1, *refs):
    many = (len(refs) - 3) // 2
    sources, other, held, b1_v, sems = refs[:many], refs[many], refs[many + 1 : -2], refs[-2], refs[-1]
    feats = w1.shape[0]
    core = jnp.bitwise_and(lax.axis_index("dp"), 1)
    bias_copy = pltpu.make_async_copy(b1, b1_v, sems.at[0])
    own = [pltpu.make_async_copy(w, other.at[0:feats], sems.at[1]) for w in (w1, w2)]
    copies = [
        pltpu.make_async_copy(sources[j], held[j], sems.at[2 + j]) for j in range(many)
    ]
    bias_copy.start()
    for j in range(2):
        pl.when(core == j)(own[j].start)
    for copy in copies:
        copy.start()
    bias_copy.wait()
    rest = row(b1_v)
    place = lax.broadcasted_iota(jnp.int32, (16, feats), 0)
    bias = jnp.zeros((16, feats), F32)
    for j in range(3):
        term = rest.astype(BF).astype(F32)
        bias = jnp.where(place == j, term, bias)
        rest = rest - term
    other[feats:, :] = bias.astype(BF)
    for j in range(2):
        pl.when(core == j)(own[j].wait)
    for copy in copies:
        copy.wait()


def attn_fwd_kernel(first, share, *refs):
    counts, pre_s, post_s, postb_s, tok, og, n1g, n1b, qkvb, pre, post, postb, projb = refs[:13]
    gamma1, n2g, n2b, wqkv, wproj = refs[13:18]
    a1_o, q_o, k_o, v_o, p_o, o_o, x1_o, u_o, a2_o, dy_o, mpre, mpost, mixb = refs[-21:-8]
    pad, kk, attended_t, probs, wide, scores, logits, mixed = refs[-8:]
    images, patches, feats = tok.shape
    rows = pad.shape[0]
    heads = mpre.shape[0]
    head_dim = feats // heads
    slots = q_o.shape[1]

    spread = (
        head_of_lane((heads, feats), 1, head_dim)
        == lax.broadcasted_iota(jnp.int32, (heads, feats), 0)
    ).astype(F32)
    mpre[...] = exact(pre[...], spread, ((1,), (0,))) * (head_dim**-0.5 * LOG2E)
    mpost[...] = exact(post[...], spread, ((0,), (0,)))
    mixb[...] = exact(row(postb), spread, ((1,), (0,)))

    tiles = [
        (h * head_dim // 128 * 128, -(-(h + 1) * head_dim // 128) * 128) for h in range(heads)
    ]
    masks = []
    for h, (low, high) in enumerate(tiles):
        lane = lax.broadcasted_iota(jnp.int32, (1, high - low), 1) + low
        masks.append((lane // head_dim == h).astype(F32))
    runs = []
    for h in range(heads):
        if runs and tiles[runs[-1][0]] == tiles[h]:
            runs[-1] = (runs[-1][0], h + 1)
        else:
            runs.append((h, h + 1))

    @pl.loop(first, first + share)
    def _(i):
        pad[patches:, :] = jnp.zeros((rows - patches, feats), F32)
        live = (lax.axis_index("mp") * images + i < counts[0]).astype(F32)
        pad[0:patches, :] = og[i].astype(F32) * live
        dy_o[i] = pad[...].astype(BF)
        pad[0:patches, :] = tok[i].astype(F32)
        gain, shift = row(n1g), row(n1b)
        for c in chunks(rows):
            n, _ = normalized(pad[c, :])
            a1_o[i, c, :] = (n * gain + shift).astype(BF)
        wide[...] = nn(a1_o[i], wqkv[...])
        bias = row(qkvb)
        q_o[i, rows:] = jnp.zeros((slots - rows, feats), BF)
        for c in chunks(rows):
            q, k, v = (
                wide[c, j * feats : (j + 1) * feats] + bias[:, j * feats : (j + 1) * feats]
                for j in range(3)
            )
            q_o[i, c, :] = q.astype(BF)
            v_o[i, c, :] = v.astype(BF)
            k = k.astype(BF)
            k_o[i, c, :] = k
            kf = k.astype(F32)
            for h, (low, high) in enumerate(tiles):
                at = slice(h * rows + c.start, h * rows + c.stop)
                kk[at, 0 : high - low] = (kf[:, low:high] * masks[h]).astype(BF)
        vt = v_o[i].T
        tail = patches // 8 * 8
        inside = lax.broadcasted_iota(jnp.int32, (rows - tail, 128), 0) < patches - tail
        real = (lax.broadcasted_iota(jnp.int32, (rows, 128), 0) < patches).astype(BF)
        start = nn(vt, real)
        for first_head, last_head in runs:
            low, high = tiles[first_head]
            part = slice(first_head * rows, last_head * rows)
            scores[part, :] = nt(kk[part, 0 : high - low], q_o[i, :, low:high])
        factors = [
            [pre_s[g, h] * (head_dim**-0.5 * LOG2E) for h in range(heads)] for g in range(heads)
        ]
        for c in chunks(rows):
            each_head = [scores[h * rows + c.start : h * rows + c.stop, :] for h in range(heads)]
            for g in range(heads):
                total = each_head[0] * factors[g][0]
                for h in range(1, heads):
                    total = total + each_head[h] * factors[g][h]
                logits[g * rows + c.start : g * rows + c.stop, :] = total
        for g in range(heads):
            for lane in range(0, slots, 128):
                x = logits[g * rows : (g + 1) * rows, lane : lane + 128]
                x = jnp.concatenate([x[0:tail], jnp.where(inside, x[tail:], -1e30)], axis=0)
                e = jnp.exp2(x - jnp.max(x, axis=0, keepdims=True))
                inv = 1.0 / jnp.sum(e, axis=0, keepdims=True)
                p = (e * inv).astype(BF)
                probs[g * rows : (g + 1) * rows, lane : lane + 128] = p
                p_o[i, g, :, lane : lane + 128] = p
            mixed[g] = nn(vt, probs[g * rows : (g + 1) * rows, :])
        for c in chunks(feats):
            g = c.start // head_dim
            first = start[c] * postb_s[g]
            for lane in range(0, slots, 128):
                total = first
                for h in range(heads):
                    total = total + mixed[h, c, lane : lane + 128] * post_s[g, h]
                attended_t[c, lane : lane + 128] = total.astype(BF)
        o_o[i] = attended_t[...].T[0:rows]
        wide[:, 0:feats] = nn(o_o[i], wproj[...])
        bias, scale, gain, shift = row(projb), row(gamma1), row(n2g), row(n2b)
        for c in chunks(rows):
            u = wide[c, 0:feats] + bias
            x1 = pad[c, :] + scale * u
            u_o[i, c, :] = u
            x1_o[i, c, :] = x1
            n, _ = normalized(x1)
            a2_o[i, c, :] = (n * gain + shift).astype(BF)


def store_blocks(count, put):
    mine = lax.axis_index("dp")
    for core in range(2):

        @pl.when(jnp.bitwise_and(mine, 1) == core)
        def _(core=core):
            for b in range(count):
                place = jnp.bitwise_xor(jnp.int32(b >> 1), jnp.right_shift(mine, 1))
                put((b ^ core) & 1, place, b)


def mlp_units(a2, dfs, w1, b1, w2, hids, dzs, zs, ghs, b1_o, units, store, use):
    size = a2.shape[0] // units
    width = w2.shape[0]
    lanes = 256
    places = [slice(u * size, (u + 1) * size) for u in range(units)]
    sums = {}

    def products(u):
        zs[u % 2] = nn(a2[places[u], :], w1[...])
        ghs[u % 2] = nt(dfs[places[u], :], w2[...])

    products(0)
    for u in range(units):
        if u + 1 < units:
            products(u + 1)
        for first in range(0, width, lanes):
            part = slice(first, first + lanes)
            bias = b1[:, part]
            for c in chunks(size):
                zc = zs[u % 2, c, part] + bias
                phi, slope = gelu_parts(zc)
                dz = (ghs[u % 2, c, part] * slope).astype(BF)
                at = slice(places[u].start + c.start, places[u].start + c.stop)
                hids[at, part] = (zc * phi).astype(BF)
                dzs[at, part] = dz
                more = fold(dz.astype(F32))
                sums[first] = sums[first] + more if first in sums else more
        store(places[u], nn(hids[places[u], :], w2[...]), nt(dzs[places[u], :], w1[...]))
        if u > 0:
            use(places[u - 1])
    use(places[units - 1])
    for first, value in sums.items():
        b1_o[:, first : first + lanes] = colsum(value)


def mlp_first_kernel(
    a2, dy, gamma2, w1_own, b1_own, w2_own, near, far,
    f_o, da2_o, grads, b1_o, a2t, dft,
    w1, w2, b1, hids, dzs, dfs, zs, ghs,
):
    total, feats = f_o.shape
    w1[:, 0:feats] = w1_own[...]
    w2[0:feats, :] = w2_own[...]
    for core in range(2):

        @pl.when(jnp.bitwise_and(lax.axis_index("dp"), 1) == core)
        def _(core=core):
            one, two = (near, far) if core == 0 else (far, near)
            w1[:, feats:] = one[0, 0:feats]
            w2[feats:, :] = two[0, 0:feats]

    b1[:, 0:feats] = row(b1_own)
    b1[:, feats:] = colsum(near[0, feats : feats + 16].astype(F32))
    gain = row(gamma2)
    for c in chunks(total):
        dfs[c, :] = (dy[c, :].astype(F32) * gain).astype(BF)

    def store(rows, f, da2):
        f_o[rows, :] = f
        da2_o[rows, :] = da2

    mlp_units(a2, dfs, w1, b1, w2, hids, dzs, zs, ghs, b1_o, 3, store, lambda rows: None)
    a2t[...] = a2[...].T
    dft[...] = dfs[...].T
    grads[0] = nn(a2t[...], dzs[...]).astype(BF).T
    down = nn(dft[...], hids[...]).astype(BF)
    for c in range(2):
        grads[1, c * feats : (c + 1) * feats, :] = down[:, c * feats : (c + 1) * feats]


def mlp_rest_kernel(
    counts, a2, dy, x1, u, o, f0, da20, near, far, last, far_last, grads, a2t, dft, wproj, gamma1, n2g, fc2b, gamma2,
    out_o, dx1_o, do_o, keep, send, b1_o, acc_o,
    w1, w2, b1, hids, dzs, dfs, zs, ghs, fs, da2s, dus, ups, downs, projs, out_v, sems,
):
    total, feats = f0.shape
    images, patches = out_o.shape[:2]
    image_rows = total // images
    m_idx = lax.axis_index("mp")
    acc_o[...] = jnp.zeros_like(acc_o)
    b1[:, 0:feats] = colsum(near[1, feats : feats + 16].astype(F32))
    b1[:, feats:] = colsum(last[feats : feats + 16].astype(F32))
    for core in range(2):

        @pl.when(jnp.bitwise_and(lax.axis_index("dp"), 1) == core)
        def _(core=core):
            one, two = (near, far) if core == 0 else (far, near)
            w1[:, 0:feats] = one[1, 0:feats]
            w2[0:feats, :] = two[1, 0:feats]
            one, two = (last, far_last) if core == 0 else (far_last, last)
            w1[:, feats:] = one[0:feats]
            w2[feats:, :] = two[0:feats]

    gain2 = row(gamma2)
    bias, gain, scale = row(fc2b), row(n2g), row(gamma1)
    for c in chunks(total):
        dfs[c, :] = (dy[c, :].astype(F32) * gain2).astype(BF)

    def out_copy(image):
        return pltpu.make_async_copy(out_v.at[image], out_o.at[image], sems.at[image])

    def store(rows, f, da2):
        fs[rows, :] = f
        da2s[rows, :] = da2

    def use(rows):
        sums = [jnp.zeros((8, feats), F32) for _ in range(6)]
        for c in chunks(rows.stop - rows.start):
            at = slice(rows.start + c.start, rows.start + c.stop)
            fc = fs[at, :] + f0[at, :] + bias
            dac = da2s[at, :] + da20[at, :]
            x1c = x1[at, :]
            dyc = dy[at, :].astype(F32)
            n, r = normalized(x1c)
            dx1 = dyc + norm_back(dac, n, r, gain)
            dx1_o[at, :] = dx1
            du = (dx1 * scale).astype(BF)
            dus[at, :] = du
            image = at.start // image_rows
            first = at.start - image * image_rows
            live = (m_idx * images + image < counts[0]).astype(F32)
            out = ((x1c + gain2 * fc) * live).astype(BF)
            if first + 16 <= patches:
                out_v[image, first : first + 16, :] = out
            else:
                out_v[image, first:patches, :] = out[0 : patches - first]
            terms = (
                du.astype(F32), u[at, :] * dx1, dac * n, dac, dfs[at, :].astype(F32), fc * dyc,
            )
            sums = [s + fold(t) for s, t in zip(sums, terms)]
        for j in range(6):
            acc_o[j : j + 1, :] += colsum(sums[j])
        do = nt(dus[rows, :], wproj[...]).astype(BF)
        for at in range(0, rows.stop - rows.start, image_rows):
            image = (rows.start + at) // image_rows
            out_copy(image).start()
            do_o[image, 0:image_rows] = do[at : at + image_rows]
            do_o[image, image_rows:] = jnp.zeros((do_o.shape[1] - image_rows, feats), BF)

    mlp_units(a2, dfs, w1, b1, w2, hids, dzs, zs, ghs, b1_o, 3, store, use)
    ups[...] = nn(a2t[...], dzs[...]).astype(BF).T
    downs[...] = nn(dft[...], hids[...]).astype(BF)
    projs[...] = tn(dus[...], o[...]).astype(BF)
    count = 2 * keep.shape[0]
    size = feats // count
    outs = (keep, send)

    def put(which, place, b):
        out = outs[which]
        for c in range(2):
            part = slice(c * feats, (c + 1) * feats)
            up = slice(c * feats + b * size, c * feats + (b + 1) * size)
            down = slice(b * size, (b + 1) * size)
            pieces = (grads[0, up, :], grads[1, up, :])
            for j, piece in enumerate(pieces):
                out[place, (2 * c + j) * size : (2 * c + j + 1) * size, :] = piece
            pieces = (ups[up, :], downs[down, part])
            for j, piece in enumerate(pieces):
                out[place, (4 + 2 * c + j) * size : (5 + 2 * c + j) * size, :] = piece
        out[place, 8 * size : 9 * size, :] = projs[b * size : (b + 1) * size, :]

    store_blocks(count, put)
    for image in range(images):
        out_copy(image).wait()


def attn_bwd_kernel(first, share, *refs):
    pre_s, do_r, q_r, k_r, v_r, p_r, dx1, tok, mpre, mpost, mixb, wqkv, n1g = refs[:13]
    dqkv_o, in_o, acc_o, vgs, dls, dq_t, dps, dvs, dks, dqs, da1, pad, in_v, sems = refs[-14:]
    slots, feats = do_r.shape[1:]
    patches = tok.shape[1]
    rows = k_r.shape[1]
    heads = mpre.shape[0]
    head_dim = feats // heads
    many = heads // 2
    half = many * rows
    acc_o[...] = jnp.zeros_like(acc_o)

    def in_copy(i):
        return pltpu.make_async_copy(in_v.at[i - first], in_o.at[i], sems.at[i - first])

    @pl.loop(first, first + share)
    def _(i):
        do_sum = jnp.zeros((8, feats), F32)
        for c in chunks(rows):
            vf = v_r[i, c, :].astype(F32)
            do_sum = do_sum + fold(do_r[i, c, :].astype(F32))
            for h in range(heads):
                vgs[h * rows + c.start : h * rows + c.stop, :] = (vf * mpost[h : h + 1, :]).astype(BF)
        do_sum = colsum(do_sum)
        q = q_r[i]
        do = do_r[i]
        kt = k_r[i].T
        parts = [slice(s * half, (s + 1) * half) for s in range(2)]
        for part in parts:
            dps[part, :] = nt(vgs[part, :], do)
        for s, part in enumerate(parts):
            dvs[part, :] = nn(p_r[i, s * many : (s + 1) * many].reshape(half, slots), do)
        for s, part in enumerate(parts):
            for h in range(s * many, (s + 1) * many):
                at = slice(h * rows, (h + 1) * rows)
                for lane in range(0, slots, 128):
                    dp = dps[at, lane : lane + 128]
                    pf = p_r[i, h, :, lane : lane + 128].astype(F32)
                    mean = jnp.sum(dp * pf, axis=0, keepdims=True) / jnp.sum(pf, axis=0, keepdims=True)
                    dls[at, lane : lane + 128] = (pf * (dp - mean)).astype(BF)
                dqs[h] = nn(kt, dls[at, :])
            dks[part, :] = nn(dls[part, :], q)

        bias_row = mixb[...] * do_sum
        v_sum = jnp.zeros((8, feats), F32)
        dv_sum = jnp.zeros((8, feats), F32)
        sums = [jnp.zeros((8, feats), F32) for _ in range(heads)]
        for c in chunks(rows):
            vf = v_r[i, c, :].astype(F32)
            dv = bias_row
            for h in range(heads):
                this = dvs[h * rows + c.start : h * rows + c.stop, :]
                dv = dv + this * mpost[h : h + 1, :]
                sums[h] = sums[h] + fold(vf * this)
            if c.stop > patches:
                inside = lax.broadcasted_iota(jnp.int32, dv.shape, 0) < patches - c.start
                dv = jnp.where(inside, dv, 0.0)
                vf = jnp.where(inside, vf, 0.0)
            low = dv.astype(BF)
            dqkv_o[i, c, 2 * feats :] = low
            dv_sum = dv_sum + fold(low.astype(F32))
            v_sum = v_sum + fold(vf)
        for h in range(heads):
            acc_o[h : h + 1, :] += colsum(sums[h])
        acc_o[2 * heads : 2 * heads + 1, :] += do_sum * colsum(v_sum)
        acc_o[2 * heads + 10 : 2 * heads + 11, :] += colsum(dv_sum)

        for c in chunks(feats):
            g = c.start // head_dim
            for lane in range(0, slots, 128):
                total = 0.0
                for h in range(heads):
                    total = total + dqs[h, c, lane : lane + 128] * pre_s[h, g]
                dq_t[c, lane : lane + 128] = (total * head_dim**-0.5).astype(BF)
        dq = dq_t[...].T[0:rows]
        dqkv_o[i, :, 0:feats] = dq
        dk_sum = jnp.zeros((8, feats), F32)
        sums = [jnp.zeros((8, feats), F32) for _ in range(heads)]
        for c in chunks(rows):
            kf = k_r[i, c, :].astype(F32)
            dk = 0.0
            for h in range(heads):
                this = dks[h * rows + c.start : h * rows + c.stop, :]
                dk = dk + this * mpre[h : h + 1, :]
                sums[h] = sums[h] + fold(kf * this)
            low = (dk * (1.0 / LOG2E)).astype(BF)
            dqkv_o[i, c, feats : 2 * feats] = low
            dk_sum = dk_sum + fold(low.astype(F32))
        for h in range(heads):
            acc_o[heads + h : heads + h + 1, :] += colsum(sums[h])
        acc_o[2 * heads + 8 : 2 * heads + 9, :] += colsum(dq.astype(F32))
        acc_o[2 * heads + 9 : 2 * heads + 10, :] += colsum(dk_sum)

        pad[patches:, :] = jnp.zeros((rows - patches, feats), F32)
        pad[0:patches, :] = tok[i].astype(F32)
        da1[...] = nt(dqkv_o[i], wqkv[...])
        gain = row(n1g)
        sums = [jnp.zeros((8, feats), F32) for _ in range(2)]
        for c in chunks(rows):
            n, r = normalized(pad[c, :])
            cot = da1[c, :]
            grad = dx1[i, c, :] + norm_back(cot, n, r, gain)
            sums = [sums[0] + fold(cot * n), sums[1] + fold(cot)]
            if c.stop <= patches:
                in_v[i - first, c, :] = grad
            else:
                in_v[i - first, c.start : patches, :] = grad[0 : patches - c.start]
        for j in range(2):
            acc_o[2 * heads + 11 + j : 2 * heads + 12 + j, :] += colsum(sums[j])
        in_copy(i).start()

    @pl.loop(first, first + share)
    def _(i):
        in_copy(i).wait()


def qkv_grad_kernel(heads, dqkv, *refs):
    accs = refs[:-8]
    a1, acc_mlp, b1_first, b1_rest, keep, send, small, grads = refs[-8:]
    feats = a1.shape[1]
    count = 2 * keep.shape[0]
    size = 3 * feats // count
    acc = accs[0][...]
    for other in accs[1:]:
        acc = acc + other[...]
    small[...] = jnp.zeros_like(small)
    small[0:2, :] = acc[2 * heads + 11 : 2 * heads + 13]
    small[2:8, :] = acc_mlp[0:6, :]
    small[8:11, :] = acc[2 * heads + 8 : 2 * heads + 11]
    head_dim = feats // heads
    lanes = 2 * heads * heads
    gather = (
        head_of_lane((feats, lanes), 0, head_dim)
        == lax.broadcasted_iota(jnp.int32, (feats, lanes), 1) % heads
    ).astype(F32)
    sums = exact(acc[0 : 2 * heads + 8], gather, ((1,), (0,)))
    place = head_of_lane((2 * heads, lanes), 1, heads) == lax.broadcasted_iota(
        jnp.int32, (2 * heads, lanes), 0
    )
    small[11:12, 0:lanes] = colsum(jnp.where(place, sums[0 : 2 * heads], 0.0))
    small[11:12, lanes : 2 * lanes] = sums[2 * heads : 2 * heads + 1]
    m_idx = lax.axis_index("mp")
    for c, ref in enumerate((b1_first, b1_first, b1_rest, b1_rest)):
        place = 12 + jnp.bitwise_xor(m_idx, c)
        small[pl.ds(place, 1), :] = ref[:, (c % 2) * feats : (c % 2 + 1) * feats]
    low = small[...].astype(BF)
    outs = (keep, send)

    grads[...] = tn(a1[...], dqkv[...]).astype(BF).T

    def put(which, place, b):
        outs[which][place, 0:size, :] = grads[b * size : (b + 1) * size, :]
        outs[which][place, size : size + 16, :] = low
        if outs[which].shape[1] > size + 16:
            outs[which][place, size + 16 :, :] = jnp.zeros_like(outs[which][place, size + 16 :, :])

    store_blocks(count, put)


def final_kernel(heads, size, many, mine, proj_own, *refs):
    got = refs[:many]
    mlp_mine, got_z = refs[many], refs[1 + many : 1 + 2 * many]
    qkv_o, qkvb_o, pre_o, post_o, postb_o, b1_o, *vecs_o, fc1_o, fc2_o, proj_o, held = refs[-18:]
    block, feats = fc1_o.shape
    for place, out in enumerate((fc1_o, fc2_o)):
        rows = slice(place * block, (place + 1) * block)
        out[...] = mlp_mine[rows, :] + sum(g[rows, :].astype(F32) for g in got_z)
    d_idx = lax.axis_index("dp")
    m_idx = lax.axis_index("mp")
    total = mine[...]
    held[m_idx] = proj_own[...].astype(F32)
    for j, part in enumerate(got):
        value = part[...].astype(F32)
        total = total + value[0 : size + 16]
        held[jnp.bitwise_xor(m_idx, j + 1)] = value[size + 16 :]
    proj_o[...] = held[...].reshape(-1, feats)[0:block]
    qkv_o[...] = total[0:size]
    small = total[size : size + 16]

    def own(value, width, index):
        lanes = value.shape[1]
        return pltpu.roll(value, lax.rem(lanes - index * width, lanes), axis=1)[:, 0:width]

    width = vecs_o[0].shape[1]
    vecs = own(small[0:8], width, d_idx)
    for j, ref in enumerate(vecs_o):
        ref[...] = vecs[j : j + 1]
    flat = jnp.concatenate([small[8 + j : 9 + j] for j in range(3)], axis=1)
    qkvb_o[...] = own(jnp.broadcast_to(flat, (8, 3 * feats)), qkvb_o.shape[1], d_idx)[0:1]
    b1 = own(small[8:16], b1_o.shape[1], d_idx)[4:8]
    pick = lax.broadcasted_iota(jnp.int32, b1.shape, 0) == m_idx
    b1_o[...] = colsum(jnp.where(pick, b1, 0.0))
    mix = small[11:12]
    hh = heads * heads
    line = lax.broadcasted_iota(jnp.int32, (heads, hh), 0)
    lane = lax.broadcasted_iota(jnp.int32, (heads, hh), 1)
    fold = (
        lax.broadcasted_iota(jnp.int32, (hh, heads), 0) % heads
        == lax.broadcasted_iota(jnp.int32, (hh, heads), 1)
    ).astype(F32)
    head_dim = feats // heads

    def square(values):
        return exact(jnp.where(lane // heads == line, values, 0.0), fold, ((1,), (0,)))

    post_o[...] = square(mix[:, 0:hh]).T
    pre_o[...] = square(mix[:, hh : 2 * hh]) * (head_dim**-0.5)
    postb_o[...] = mix[:, 2 * hh : 2 * hh + heads]


def whole(shape):
    return pl.BlockSpec(shape, lambda i: (0,) * len(shape))


def each(shape, first=0, many=1):
    return pl.BlockSpec((many,) + shape[1:], lambda i: (i + first,) + (0,) * (len(shape) - 1))


SCALARS = pl.BlockSpec(memory_space=pltpu.SMEM)
IN_VMEM = pl.BlockSpec(memory_space=pltpu.VMEM)
IN_HBM = pl.BlockSpec(memory_space=pltpu.HBM)


def kept(a):
    return pltpu.with_memory_space_constraint(a, pltpu.HBM)


def sds(shape, dtype):
    return jax.ShapeDtypeStruct(shape, dtype)


def call(
    kernel, grid, ins, in_specs, outs, out_specs, scratch=(), flops=0, name=None, aliases=None,
    limit=VMEM_LIMIT,
):
    size = lambda a: a.size * a.dtype.itemsize
    return pl.pallas_call(
        kernel,
        grid=grid,
        in_specs=in_specs,
        out_specs=out_specs,
        out_shape=outs,
        scratch_shapes=scratch,
        input_output_aliases=aliases or {},
        compiler_params=pltpu.CompilerParams(vmem_limit_bytes=limit),
        cost_estimate=pl.CostEstimate(
            flops=flops,
            bytes_accessed=sum(size(a) for a in ins) + sum(size(a) for a in outs),
            transcendentals=0,
        ),
        name=name,
    )(*ins)


def xor_perm(count, mask):
    return [(j, j ^ mask) for j in range(count)]


def dp_hops(dp):
    bits = dp.bit_length() - 1
    groups = []
    at = 1
    while at < bits:
        groups.append((at, min(2, bits - at)))
        at += groups[-1][1]
    return groups


def dp_scatter(value, dp):
    for at, many in dp_hops(dp):
        value = value.reshape((-1, 1 << many) + value.shape[1:])
        got = [
            lax.ppermute(value[:, j].astype(BF), "dp", xor_perm(dp, j << at))
            for j in range(1, 1 << many)
        ]
        value = value[:, 0] + sum(g.astype(F32) for g in got)
    return value.reshape(value.shape[-2:])


def per_device(
    dp, mp,
    tokens_in, image_counts, norm1_gain, norm1_bias, qkv_weight, qkv_bias,
    mix_pre, mix_post, mix_post_bias, proj_weight, proj_bias, gamma1,
    norm2_gain, norm2_bias, fc1_weight, fc1_bias, fc2_weight, fc2_bias, gamma2, out_grad,
):
    images, patches, feats = tokens_in.shape
    heads = mix_pre.shape[0]
    rows = -(-patches // 16) * 16
    slots = -(-patches // 128) * 128
    hidden = fc1_weight.shape[1]
    tok_rows = (images, rows, feats)
    slot_rows = (images, slots, feats)
    prob_shape = (images, heads, rows, slots)
    mix_shape = (heads, feats)
    operands = [
        tokens_in, out_grad, norm1_gain, norm1_bias, qkv_bias, mix_pre, mix_post,
        mix_post_bias, proj_bias, gamma1, norm2_gain, norm2_bias, qkv_weight, proj_weight,
    ]

    ins = [kept(a) for a in [fc1_weight, fc2_weight, fc1_bias] + operands]
    outs = [sds((feats + 16, hidden), BF)] + [sds(a.shape, a.dtype) for a in operands]
    other, *held = call(
        pack_kernel,
        (),
        ins,
        [IN_HBM] * len(ins),
        outs,
        [IN_VMEM] * len(outs),
        [pltpu.VMEM(fc1_bias.shape, F32), pltpu.SemaphoreType.DMA((2 + len(operands),))],
        name="pack",
    )
    near = [lax.ppermute(other, "mp", xor_perm(mp, j)) for j in (1, 2)]

    shares = [images - 1, 1] if images > 1 else [images]
    carried = []
    for s, share in enumerate(shares):
        first = sum(shares[:s])
        ins = [image_counts, mix_pre, mix_post, mix_post_bias] + held
        outs = call(
            functools.partial(attn_fwd_kernel, first, share),
            (),
            ins + carried,
            [SCALARS] * 4
            + [IN_VMEM] * 14
            + [pl.BlockSpec(memory_space=pl.ANY)] * len(carried),
            [
                sds(tok_rows, BF), sds(slot_rows, BF), sds(tok_rows, BF), sds(tok_rows, BF),
                sds(prob_shape, BF), sds(tok_rows, BF), sds(tok_rows, F32), sds(tok_rows, F32),
                sds(tok_rows, BF), sds(tok_rows, BF), sds(mix_shape, F32), sds(mix_shape, F32),
                sds((1, feats), F32),
            ],
            [IN_VMEM] * 13,
            [
                pltpu.VMEM((rows, feats), F32), pltpu.VMEM((heads * rows, 256), BF),
                pltpu.VMEM((feats, slots), BF), pltpu.VMEM((heads * rows, slots), BF),
                pltpu.VMEM((rows, 3 * feats), F32), pltpu.VMEM((heads * rows, slots), F32),
                pltpu.VMEM((heads * rows, slots), F32),
                pltpu.VMEM((heads, feats, slots), F32),
            ],
            flops=share * 15 * 10**8,
            name="attn_fwd",
            aliases={len(ins) + j: j for j in range(10)} if carried else None,
        )
        carried, (mpre, mpost, mixb) = list(outs[:10]), outs[10:]
        if s == 0:
            near, carried[0] = lax.optimization_barrier((near, carried[0]))
            last = lax.ppermute(near[1], "mp", xor_perm(mp, 1))
            near = jnp.stack(near)
            far = lax.ppermute(near, "dp", xor_perm(dp, 1))
    a1, q, k, v, prob, o, x1, u, a2, dy = carried
    far, a2 = lax.optimization_barrier((far, a2))

    block = feats // dp
    total = images * rows
    flat = (total, feats)
    a2, dy, x1, u, o = (a.reshape(flat) for a in (a2, dy, x1, u, o))
    ins = [a2, dy, gamma2, fc1_weight, fc1_bias, fc2_weight, near, far]
    wide = 2 * hidden
    grad_shape = (2, wide, feats)
    f0, da20, grads0, b1_0, a2t, dft = call(
        mlp_first_kernel,
        (),
        ins,
        [IN_VMEM] * len(ins),
        [
            sds(flat, F32), sds(flat, F32), sds(grad_shape, BF), sds((1, wide), F32),
            sds((feats, total), BF), sds((feats, total), BF),
        ],
        [IN_VMEM] * 6,
        [
            pltpu.VMEM((feats, wide), BF), pltpu.VMEM((wide, feats), BF),
            pltpu.VMEM((1, wide), F32), pltpu.VMEM((total, wide), BF),
            pltpu.VMEM((total, wide), BF), pltpu.VMEM(flat, BF),
            pltpu.VMEM((2, total // 3, wide), F32), pltpu.VMEM((2, total // 3, wide), F32),
        ],
        flops=images * 8 * 10**8,
        name="mlp_first",
    )

    last, f0 = lax.optimization_barrier((last, f0))
    far_last = lax.ppermute(last, "dp", xor_perm(dp, 1))

    grad_rows = 9 * block
    half_shape = (dp // 2, grad_rows, feats)
    ins = [
        image_counts, a2, dy, x1, u, o, f0, da20, near, far, last, far_last, grads0, a2t, dft,
        proj_weight, gamma1,
        norm2_gain, fc2_bias, gamma2,
    ]
    layer_out, dx1, do, keep, send, b1_1, acc_mlp = call(
        mlp_rest_kernel,
        (),
        ins,
        [SCALARS] + [IN_VMEM] * (len(ins) - 1),
        [
            sds(tokens_in.shape, BF), sds(flat, F32), sds(slot_rows, BF), sds(half_shape, BF),
            sds(half_shape, BF), sds((1, wide), F32), sds((8, feats), F32),
        ],
        [IN_HBM] + [IN_VMEM] * 6,
        [
            pltpu.VMEM((feats, wide), BF), pltpu.VMEM((wide, feats), BF),
            pltpu.VMEM((1, wide), F32), pltpu.VMEM((total, wide), BF),
            pltpu.VMEM((total, wide), BF), pltpu.VMEM(flat, BF),
            pltpu.VMEM((2, total // 3, wide), F32), pltpu.VMEM((2, total // 3, wide), F32),
            pltpu.VMEM(flat, F32), pltpu.VMEM(flat, F32), pltpu.VMEM(flat, BF),
            pltpu.VMEM((wide, feats), BF), pltpu.VMEM((feats, wide), BF),
            pltpu.VMEM((feats, feats), BF), pltpu.VMEM(tokens_in.shape, BF),
            pltpu.SemaphoreType.DMA((images,)),
        ],
        flops=images * 9 * 10**8,
        name="mlp_rest",
    )
    got = lax.ppermute(send, "dp", xor_perm(dp, 1))
    dx1 = dx1.reshape(tok_rows)

    shares = [1, images - 1] if images > 1 else [1]
    dqkv_shape = (images, rows, 3 * feats)
    carried, accs = [], []
    for s, share in enumerate(shares):
        first = sum(shares[:s])
        ins = [mix_pre, do, q, k, v, prob, dx1, tokens_in, mpre, mpost, mixb, qkv_weight, norm1_gain]
        *carried, acc = call(
            functools.partial(attn_bwd_kernel, first, share),
            (),
            ins + carried,
            [SCALARS]
            + [IN_VMEM] * (len(ins) - 1)
            + [pl.BlockSpec(memory_space=pl.ANY)] * len(carried),
            [sds(dqkv_shape, BF), sds(tokens_in.shape, F32), sds((2 * heads + 16, feats), F32)],
            [IN_VMEM, IN_HBM, IN_VMEM],
            [
                pltpu.VMEM((heads * rows, feats), BF), pltpu.VMEM((heads * rows, slots), BF),
                pltpu.VMEM((feats, slots), BF), pltpu.VMEM((heads * rows, slots), F32),
                pltpu.VMEM((heads * rows, feats), F32), pltpu.VMEM((heads * rows, feats), F32),
                pltpu.VMEM((heads, feats, slots), F32), pltpu.VMEM((rows, feats), F32),
                pltpu.VMEM((rows, feats), F32), pltpu.VMEM((share, patches, feats), F32),
                pltpu.SemaphoreType.DMA((share,)),
            ],
            flops=share * 20 * 10**8,
            name="attn_bwd",
            aliases={len(ins): 0, len(ins) + 1: 1} if carried else None,
        )
        accs.append(acc)
        if s == 0:
            (keep, got), acc = lax.optimization_barrier(((keep, got), acc))
            mine = dp_scatter(keep.astype(F32) + got.astype(F32), dp)
            accs[0], do = lax.optimization_barrier((acc, do))
    dqkv, in_grad = carried
    mine, dqkv = lax.optimization_barrier((mine, dqkv))
    mlp_mine = mine
    low = mine.astype(BF)
    m_idx = lax.axis_index("mp")
    share_rows = -(-block // (16 * mp)) * 16
    proj = jnp.pad(mine[8 * block :], ((0, mp * share_rows - block), (0, 0)))

    def proj_share(j):
        return lax.dynamic_slice_in_dim(proj, jnp.bitwise_xor(m_idx, j) * share_rows, share_rows)

    got_z = [
        lax.ppermute(
            jnp.concatenate([low[2 * j * block : 2 * (j + 1) * block], proj_share(j).astype(BF)]),
            "mp",
            xor_perm(mp, j),
        )
        for j in range(1, mp)
    ]

    q_block = 3 * feats // dp
    half_shape = (dp // 2, q_block + 16, feats)
    ins = [dqkv.reshape(total, 3 * feats)] + accs + [a1.reshape(flat), acc_mlp, b1_0, b1_1]
    keep, send = call(
        functools.partial(qkv_grad_kernel, heads),
        (1,),
        ins,
        [whole(a.shape) for a in ins],
        [sds(half_shape, BF), sds(half_shape, BF)],
        [whole(half_shape), whole(half_shape)],
        [pltpu.VMEM((16, feats), F32), pltpu.VMEM((3 * feats, feats), BF)],
        flops=11 * 10**8,
        name="qkv_grad",
    )
    got = lax.ppermute(send, "dp", xor_perm(dp, 1))
    mine = dp_scatter(keep.astype(F32) + got.astype(F32), dp)
    mine, got_z = lax.optimization_barrier((mine, got_z))

    proj_own = (proj_share(0) + sum(g[2 * block :].astype(F32) for g in got_z)).astype(BF)
    payload = jnp.concatenate([mine.astype(BF), proj_own])
    got = [lax.ppermute(payload, "mp", xor_perm(mp, j)) for j in range(1, mp)]
    b1_size = hidden // dp
    ins = [mine, proj_own] + got + [mlp_mine] + got_z
    outs = [
        sds((q_block, feats), F32), sds((1, q_block), F32), sds((heads, heads), F32),
        sds((heads, heads), F32), sds((1, heads), F32), sds((1, b1_size), F32),
    ] + [sds((1, block), F32)] * 8 + [sds((block, feats), F32)] * 3
    qkvw, qkvb, pre, post, postb, b1g, *vecs, fc1g, fc2g, projg = call(
        functools.partial(final_kernel, heads, q_block, mp - 1),
        (1,),
        ins,
        [whole(a.shape) for a in ins],
        outs,
        [whole(a.shape) for a in outs],
        [pltpu.VMEM((mp, share_rows, feats), F32)],
        name="final",
    )
    vecs = [a.reshape(-1) for a in vecs]
    return (
        layer_out,
        in_grad,
        vecs[0],
        vecs[1],
        qkvw.T,
        qkvb.reshape(-1),
        pre,
        post,
        postb.reshape(-1),
        projg.T,
        vecs[2],
        vecs[3],
        vecs[4],
        vecs[5],
        fc1g.T,
        b1g.reshape(-1),
        fc2g.T,
        vecs[6],
        vecs[7],
    )


def solution(mesh):
    tokens = P(("dp", "mp"), None, None)
    placed = (
        (tokens, P("dp")) + (P(),) * 12 + (P(None, "mp"), P("mp"), P("mp", None), P(), P(), tokens)
    )
    return jax.shard_map(
        functools.partial(per_device, mesh.shape["dp"], mesh.shape["mp"]),
        mesh=mesh,
        in_specs=placed,
        out_specs=(
            tokens, tokens, P("dp"), P("dp"), P(None, "dp"), P("dp"), P(), P(), P(),
            P(None, "dp"), P("dp"), P("dp"), P("dp"), P("dp"), P(None, ("mp", "dp")),
            P(("mp", "dp")), P("mp", "dp"), P("dp"), P("dp"),
        ),
        check_vma=False,
    )
```

```python
import functools

import jax
import jax.numpy as jnp
from jax import lax
from jax.experimental import pallas as pl
from jax.experimental.pallas import tpu as pltpu
from jax.sharding import PartitionSpec as P

BF = jnp.bfloat16
F32 = jnp.float32
LOG2E = 1.4426950408889634
EPS = 1e-06
VMEM_LIMIT = 20 * 1024 * 1024


def nn(a, b):
    return lax.dot_general(a, b, (((1,), (0,)), ((), ())), preferred_element_type=F32)


def nt(a, b):
    return lax.dot_general(a, b, (((1,), (1,)), ((), ())), preferred_element_type=F32)


def tn(a, b):
    return lax.dot_general(a, b, (((0,), (0,)), ((), ())), preferred_element_type=F32)


def exact(a, b, dims):
    return lax.dot_general(
        a, b, (dims, ((), ())), precision=lax.Precision.HIGHEST, preferred_element_type=F32
    )


def normalized(x):
    mean = jnp.mean(x, axis=-1, keepdims=True)
    c = x - mean
    r = lax.rsqrt(jnp.mean(c * c, axis=-1, keepdims=True) + EPS)
    return c * r, r


def norm_back(cot, n, r, gain):
    cg = cot * gain
    return r * (
        cg
        - jnp.mean(cg, axis=-1, keepdims=True)
        - n * jnp.mean(cg * n, axis=-1, keepdims=True)
    )


def colsum(x):
    return jnp.sum(x, axis=0, keepdims=True)


def split(x):
    hi = x.astype(BF)
    return jnp.concatenate([hi, (x - hi.astype(F32)).astype(BF)], axis=1)


def row(ref):
    return ref[...].reshape(1, ref.shape[0])


def inverse(x):
    near = pl.reciprocal(x, approx=True)
    return near * (2.0 - x * near)


def gelu_parts(z):
    e = jnp.exp2(z * z * (-0.5 * LOG2E))
    t = inverse(1.0 + jnp.abs(z) * (0.3275911 * 0.7071067811865476))
    poly = t * (
        0.5 * 0.254829592
        + t
        * (
            0.5 * -0.284496736
            + t * (0.5 * 1.421413741 + t * (0.5 * -1.453152027 + t * (0.5 * 1.061405429)))
        )
    )
    tail = poly * e
    phi = jnp.where(z >= 0, 1.0 - tail, tail)
    return phi, phi + z * e * 0.3989422804014327


def head_of_lane(shape, axis, head_dim):
    return lax.broadcasted_iota(jnp.int32, shape, axis) // head_dim


def chunks(count, size=16):
    return [slice(at, at + size) for at in range(0, count, size)]


def fold(x):
    return sum(x[at : at + 8] for at in range(8, x.shape[0], 8)) + x[0:8]


def pack_kernel(w1, w2, b1, *refs):
    many = (len(refs) - 3) // 2
    sources, other, held, b1_v, sems = refs[:many], refs[many], refs[many + 1 : -2], refs[-2], refs[-1]
    feats = w1.shape[0]
    core = jnp.bitwise_and(lax.axis_index("dp"), 1)
    bias_copy = pltpu.make_async_copy(b1, b1_v, sems.at[0])
    own = [pltpu.make_async_copy(w, other.at[0:feats], sems.at[1]) for w in (w1, w2)]
    copies = [
        pltpu.make_async_copy(sources[j], held[j], sems.at[2 + j]) for j in range(many)
    ]
    bias_copy.start()
    for j in range(2):
        pl.when(core == j)(own[j].start)
    for copy in copies:
        copy.start()
    bias_copy.wait()
    rest = row(b1_v)
    place = lax.broadcasted_iota(jnp.int32, (16, feats), 0)
    bias = jnp.zeros((16, feats), F32)
    for j in range(3):
        term = rest.astype(BF).astype(F32)
        bias = jnp.where(place == j, term, bias)
        rest = rest - term
    other[feats:, :] = bias.astype(BF)
    for j in range(2):
        pl.when(core == j)(own[j].wait)
    for copy in copies:
        copy.wait()


def attn_fwd_kernel(first, share, *refs):
    counts, post_s, postb_s, tok, og, n1g, n1b, qkvb, pre, post, postb, projb = refs[:12]
    gamma1, n2g, n2b, wqkv, wproj = refs[12:17]
    a1_o, q_o, k_o, v_o, p_o, o_o, x1_o, u_o, a2_o, dy_o, mpre, mpost, mixb = refs[-20:-7]
    pad, kk, attended_t, probs, wide, logits, mixed = refs[-7:]
    images, patches, feats = tok.shape
    rows = pad.shape[0]
    heads = mpre.shape[0]
    head_dim = feats // heads
    slots = q_o.shape[1]

    spread = (
        head_of_lane((heads, feats), 1, head_dim)
        == lax.broadcasted_iota(jnp.int32, (heads, feats), 0)
    ).astype(F32)
    mpre[...] = exact(pre[...], spread, ((1,), (0,))) * (head_dim**-0.5 * LOG2E)
    mpost[...] = exact(post[...], spread, ((0,), (0,)))
    mixb[...] = exact(row(postb), spread, ((1,), (0,)))

    @pl.loop(first, first + share)
    def _(i):
        pad[patches:, :] = jnp.zeros((rows - patches, feats), F32)
        live = (lax.axis_index("mp") * images + i < counts[0]).astype(F32)
        pad[0:patches, :] = og[i].astype(F32) * live
        dy_o[i] = pad[...].astype(BF)
        pad[0:patches, :] = tok[i].astype(F32)
        gain, shift = row(n1g), row(n1b)
        for c in chunks(rows):
            n, _ = normalized(pad[c, :])
            a1_o[i, c, :] = (n * gain + shift).astype(BF)
        wide[...] = nn(a1_o[i], wqkv[...])
        bias = row(qkvb)
        q_o[i, rows:] = jnp.zeros((slots - rows, feats), BF)
        for c in chunks(rows):
            q, k, v = (
                wide[c, j * feats : (j + 1) * feats] + bias[:, j * feats : (j + 1) * feats]
                for j in range(3)
            )
            q_o[i, c, :] = q.astype(BF)
            v_o[i, c, :] = v.astype(BF)
            k = k.astype(BF)
            k_o[i, c, :] = k
            kf = k.astype(F32)
            for g in range(heads):
                at = slice(g * rows + c.start, g * rows + c.stop)
                scaled = kf * mpre[g : g + 1, :]
                hi = scaled.astype(BF)
                kk[at, 0:feats] = hi
                kk[at, feats:] = (scaled - hi.astype(F32)).astype(BF)
        q2 = jnp.concatenate([q_o[i], q_o[i]], axis=1)
        vt = v_o[i].T
        many = heads // 2
        half = many * rows
        tail = patches // 8 * 8
        inside = lax.broadcasted_iota(jnp.int32, (rows - tail, 128), 0) < patches - tail
        real = (lax.broadcasted_iota(jnp.int32, (rows, 128), 0) < patches).astype(BF)
        start = nn(vt, real)
        for s in range(2):
            part = slice(s * half, (s + 1) * half)
            logits[part, :] = nt(kk[part, :], q2)
        for g in range(heads):
            for lane in range(0, slots, 128):
                x = logits[g * rows : (g + 1) * rows, lane : lane + 128]
                x = jnp.concatenate([x[0:tail], jnp.where(inside, x[tail:], -1e30)], axis=0)
                e = jnp.exp2(x - jnp.max(x, axis=0, keepdims=True))
                inv = 1.0 / jnp.sum(e, axis=0, keepdims=True)
                p = (e * inv).astype(BF)
                probs[g * rows : (g + 1) * rows, lane : lane + 128] = p
                p_o[i, g, :, lane : lane + 128] = p
            mixed[g] = nn(vt, probs[g * rows : (g + 1) * rows, :])
        for c in chunks(feats):
            g = c.start // head_dim
            first = start[c] * postb_s[g]
            for lane in range(0, slots, 128):
                total = first
                for h in range(heads):
                    total = total + mixed[h, c, lane : lane + 128] * post_s[g, h]
                attended_t[c, lane : lane + 128] = total.astype(BF)
        o_o[i] = attended_t[...].T[0:rows]
        wide[:, 0:feats] = nn(o_o[i], wproj[...])
        bias, scale, gain, shift = row(projb), row(gamma1), row(n2g), row(n2b)
        for c in chunks(rows):
            u = wide[c, 0:feats] + bias
            x1 = pad[c, :] + scale * u
            u_o[i, c, :] = u
            x1_o[i, c, :] = x1
            n, _ = normalized(x1)
            a2_o[i, c, :] = (n * gain + shift).astype(BF)


def store_blocks(count, put):
    mine = lax.axis_index("dp")
    for core in range(2):

        @pl.when(jnp.bitwise_and(mine, 1) == core)
        def _(core=core):
            for b in range(count):
                place = jnp.bitwise_xor(jnp.int32(b >> 1), jnp.right_shift(mine, 1))
                put((b ^ core) & 1, place, b)


def mlp_units(a2, dfs, w1, b1, w2, hids, dzs, zs, ghs, b1_o, units, store, use):
    size = a2.shape[0] // units
    width = w2.shape[0]
    lanes = 256
    places = [slice(u * size, (u + 1) * size) for u in range(units)]
    sums = {}

    def products(u):
        zs[u % 2] = nn(a2[places[u], :], w1[...])
        ghs[u % 2] = nt(dfs[places[u], :], w2[...])

    products(0)
    for u in range(units):
        if u + 1 < units:
            products(u + 1)
        for first in range(0, width, lanes):
            part = slice(first, first + lanes)
            bias = b1[:, part]
            for c in chunks(size):
                zc = zs[u % 2, c, part] + bias
                phi, slope = gelu_parts(zc)
                dz = (ghs[u % 2, c, part] * slope).astype(BF)
                at = slice(places[u].start + c.start, places[u].start + c.stop)
                hids[at, part] = (zc * phi).astype(BF)
                dzs[at, part] = dz
                more = fold(dz.astype(F32))
                sums[first] = sums[first] + more if first in sums else more
        store(places[u], nn(hids[places[u], :], w2[...]), nt(dzs[places[u], :], w1[...]))
        if u > 0:
            use(places[u - 1])
    use(places[units - 1])
    for first, value in sums.items():
        b1_o[:, first : first + lanes] = colsum(value)


def mlp_first_kernel(
    a2, dy, gamma2, w1_own, b1_own, w2_own, near, far,
    f_o, da2_o, b1_o, hids, dzs, dfs,
    w1, w2, b1, zs, ghs,
):
    total, feats = f_o.shape
    w1[:, 0:feats] = w1_own[...]
    w2[0:feats, :] = w2_own[...]
    for core in range(2):

        @pl.when(jnp.bitwise_and(lax.axis_index("dp"), 1) == core)
        def _(core=core):
            one, two = (near, far) if core == 0 else (far, near)
            w1[:, feats:] = one[0, 0:feats]
            w2[feats:, :] = two[0, 0:feats]

    b1[:, 0:feats] = row(b1_own)
    b1[:, feats:] = colsum(near[0, feats : feats + 16].astype(F32))
    gain = row(gamma2)
    for c in chunks(total):
        dfs[c, :] = (dy[c, :].astype(F32) * gain).astype(BF)

    def store(rows, f, da2):
        f_o[rows, :] = f
        da2_o[rows, :] = da2

    mlp_units(a2, dfs, w1, b1, w2, hids, dzs, zs, ghs, b1_o, 3, store, lambda rows: None)


def mlp_grad_kernel(a2, hids, dzs, dfs, grads, a2t, dft):
    feats = a2.shape[1]
    a2t[...] = a2[...].T
    dft[...] = dfs[...].T
    grads[0] = nn(a2t[...], dzs[...]).astype(BF).T
    down = nn(dft[...], hids[...]).astype(BF)
    for c in range(2):
        grads[1, c * feats : (c + 1) * feats, :] = down[:, c * feats : (c + 1) * feats]


def mlp_rest_kernel(
    counts, a2, dy, dfs, x1, u, o, f0, da20, near, far, last, far_last, grads, a2t, dft, wproj,
    gamma1, n2g, fc2b, gamma2,
    out_o, dx1_o, do_o, keep, send, b1_o, acc_o,
    w1, w2, b1, hids, dzs, zs, ghs, fs, da2s, dus, ups, downs, projs, out_v, sems,
):
    total, feats = f0.shape
    images, patches = out_o.shape[:2]
    image_rows = total // images
    m_idx = lax.axis_index("mp")
    acc_o[...] = jnp.zeros_like(acc_o)
    b1[:, 0:feats] = colsum(near[1, feats : feats + 16].astype(F32))
    b1[:, feats:] = colsum(last[feats : feats + 16].astype(F32))
    for core in range(2):

        @pl.when(jnp.bitwise_and(lax.axis_index("dp"), 1) == core)
        def _(core=core):
            one, two = (near, far) if core == 0 else (far, near)
            w1[:, 0:feats] = one[1, 0:feats]
            w2[0:feats, :] = two[1, 0:feats]
            one, two = (last, far_last) if core == 0 else (far_last, last)
            w1[:, feats:] = one[0:feats]
            w2[feats:, :] = two[0:feats]

    gain2 = row(gamma2)
    bias, gain, scale = row(fc2b), row(n2g), row(gamma1)

    def out_copy(image):
        return pltpu.make_async_copy(out_v.at[image], out_o.at[image], sems.at[image])

    def store(rows, f, da2):
        fs[rows, :] = f
        da2s[rows, :] = da2

    def use(rows):
        sums = [jnp.zeros((8, feats), F32) for _ in range(6)]
        for c in chunks(rows.stop - rows.start):
            at = slice(rows.start + c.start, rows.start + c.stop)
            fc = fs[at, :] + f0[at, :] + bias
            dac = da2s[at, :] + da20[at, :]
            x1c = x1[at, :]
            dyc = dy[at, :].astype(F32)
            n, r = normalized(x1c)
            dx1 = dyc + norm_back(dac, n, r, gain)
            dx1_o[at, :] = dx1
            du = (dx1 * scale).astype(BF)
            dus[at, :] = du
            image = at.start // image_rows
            first = at.start - image * image_rows
            live = (m_idx * images + image < counts[0]).astype(F32)
            out = ((x1c + gain2 * fc) * live).astype(BF)
            if first + 16 <= patches:
                out_v[image, first : first + 16, :] = out
            else:
                out_v[image, first:patches, :] = out[0 : patches - first]
            terms = (
                du.astype(F32), u[at, :] * dx1, dac * n, dac, dfs[at, :].astype(F32), fc * dyc,
            )
            sums = [s + fold(t) for s, t in zip(sums, terms)]
        for j in range(6):
            acc_o[j : j + 1, :] += colsum(sums[j])
        do = nt(dus[rows, :], wproj[...]).astype(BF)
        for at in range(0, rows.stop - rows.start, image_rows):
            image = (rows.start + at) // image_rows
            out_copy(image).start()
            do_o[image, 0:image_rows] = do[at : at + image_rows]
            do_o[image, image_rows:] = jnp.zeros((do_o.shape[1] - image_rows, feats), BF)

    mlp_units(a2, dfs, w1, b1, w2, hids, dzs, zs, ghs, b1_o, 3, store, use)
    ups[...] = nn(a2t[...], dzs[...]).astype(BF).T
    downs[...] = nn(dft[...], hids[...]).astype(BF)
    projs[...] = tn(dus[...], o[...]).astype(BF)
    count = 2 * keep.shape[0]
    size = feats // count
    outs = (keep, send)

    def put(which, place, b):
        out = outs[which]
        for c in range(2):
            part = slice(c * feats, (c + 1) * feats)
            up = slice(c * feats + b * size, c * feats + (b + 1) * size)
            down = slice(b * size, (b + 1) * size)
            pieces = (grads[0, up, :], grads[1, up, :])
            for j, piece in enumerate(pieces):
                out[place, (2 * c + j) * size : (2 * c + j + 1) * size, :] = piece
            pieces = (ups[up, :], downs[down, part])
            for j, piece in enumerate(pieces):
                out[place, (4 + 2 * c + j) * size : (5 + 2 * c + j) * size, :] = piece
        out[place, 8 * size : 9 * size, :] = projs[b * size : (b + 1) * size, :]

    store_blocks(count, put)
    for image in range(images):
        out_copy(image).wait()


def attn_bwd_kernel(first, share, *refs):
    pre_s, do_r, q_r, k_r, v_r, p_r, dx1, tok, mpre, mpost, mixb, wqkv, n1g = refs[:13]
    dqkv_o, in_o, acc_o, vgs, dls, dq_t, dps, dvs, dks, dqs, da1, pad, in_v, sems = refs[-14:]
    slots, feats = do_r.shape[1:]
    patches = tok.shape[1]
    rows = k_r.shape[1]
    heads = mpre.shape[0]
    head_dim = feats // heads
    many = heads // 2
    half = many * rows
    acc_o[...] = jnp.zeros_like(acc_o)

    def in_copy(i):
        return pltpu.make_async_copy(in_v.at[i - first], in_o.at[i], sems.at[i - first])

    @pl.loop(first, first + share)
    def _(i):
        do_sum = jnp.zeros((8, feats), F32)
        for c in chunks(rows):
            vf = v_r[i, c, :].astype(F32)
            do_sum = do_sum + fold(do_r[i, c, :].astype(F32))
            for h in range(heads):
                vgs[h * rows + c.start : h * rows + c.stop, :] = (vf * mpost[h : h + 1, :]).astype(BF)
        do_sum = colsum(do_sum)
        q = q_r[i]
        do = do_r[i]
        kt = k_r[i].T
        parts = [slice(s * half, (s + 1) * half) for s in range(2)]
        for part in parts:
            dps[part, :] = nt(vgs[part, :], do)
        for s, part in enumerate(parts):
            dvs[part, :] = nn(p_r[i, s * many : (s + 1) * many].reshape(half, slots), do)
        for s, part in enumerate(parts):
            for h in range(s * many, (s + 1) * many):
                at = slice(h * rows, (h + 1) * rows)
                for lane in range(0, slots, 128):
                    dp = dps[at, lane : lane + 128]
                    pf = p_r[i, h, :, lane : lane + 128].astype(F32)
                    mean = jnp.sum(dp * pf, axis=0, keepdims=True) / jnp.sum(pf, axis=0, keepdims=True)
                    dls[at, lane : lane + 128] = (pf * (dp - mean)).astype(BF)
                dqs[h] = nn(kt, dls[at, :])
            dks[part, :] = nn(dls[part, :], q)

        bias_row = mixb[...] * do_sum
        v_sum = jnp.zeros((8, feats), F32)
        dv_sum = jnp.zeros((8, feats), F32)
        sums = [jnp.zeros((8, feats), F32) for _ in range(heads)]
        for c in chunks(rows):
            vf = v_r[i, c, :].astype(F32)
            dv = bias_row
            for h in range(heads):
                this = dvs[h * rows + c.start : h * rows + c.stop, :]
                dv = dv + this * mpost[h : h + 1, :]
                sums[h] = sums[h] + fold(vf * this)
            if c.stop > patches:
                inside = lax.broadcasted_iota(jnp.int32, dv.shape, 0) < patches - c.start
                dv = jnp.where(inside, dv, 0.0)
                vf = jnp.where(inside, vf, 0.0)
            low = dv.astype(BF)
            dqkv_o[i, c, 2 * feats :] = low
            dv_sum = dv_sum + fold(low.astype(F32))
            v_sum = v_sum + fold(vf)
        for h in range(heads):
            acc_o[h : h + 1, :] += colsum(sums[h])
        acc_o[2 * heads : 2 * heads + 1, :] += do_sum * colsum(v_sum)
        acc_o[2 * heads + 10 : 2 * heads + 11, :] += colsum(dv_sum)

        for c in chunks(feats):
            g = c.start // head_dim
            for lane in range(0, slots, 128):
                total = 0.0
                for h in range(heads):
                    total = total + dqs[h, c, lane : lane + 128] * pre_s[h, g]
                dq_t[c, lane : lane + 128] = (total * head_dim**-0.5).astype(BF)
        dq = dq_t[...].T[0:rows]
        dqkv_o[i, :, 0:feats] = dq
        dk_sum = jnp.zeros((8, feats), F32)
        sums = [jnp.zeros((8, feats), F32) for _ in range(heads)]
        for c in chunks(rows):
            kf = k_r[i, c, :].astype(F32)
            dk = 0.0
            for h in range(heads):
                this = dks[h * rows + c.start : h * rows + c.stop, :]
                dk = dk + this * mpre[h : h + 1, :]
                sums[h] = sums[h] + fold(kf * this)
            low = (dk * (1.0 / LOG2E)).astype(BF)
            dqkv_o[i, c, feats : 2 * feats] = low
            dk_sum = dk_sum + fold(low.astype(F32))
        for h in range(heads):
            acc_o[heads + h : heads + h + 1, :] += colsum(sums[h])
        acc_o[2 * heads + 8 : 2 * heads + 9, :] += colsum(dq.astype(F32))
        acc_o[2 * heads + 9 : 2 * heads + 10, :] += colsum(dk_sum)

        pad[patches:, :] = jnp.zeros((rows - patches, feats), F32)
        pad[0:patches, :] = tok[i].astype(F32)
        da1[...] = nt(dqkv_o[i], wqkv[...])
        gain = row(n1g)
        sums = [jnp.zeros((8, feats), F32) for _ in range(2)]
        for c in chunks(rows):
            n, r = normalized(pad[c, :])
            cot = da1[c, :]
            grad = dx1[i, c, :] + norm_back(cot, n, r, gain)
            sums = [sums[0] + fold(cot * n), sums[1] + fold(cot)]
            if c.stop <= patches:
                in_v[i - first, c, :] = grad
            else:
                in_v[i - first, c.start : patches, :] = grad[0 : patches - c.start]
        for j in range(2):
            acc_o[2 * heads + 11 + j : 2 * heads + 12 + j, :] += colsum(sums[j])
        in_copy(i).start()

    @pl.loop(first, first + share)
    def _(i):
        in_copy(i).wait()


def qkv_grad_kernel(heads, dqkv, *refs):
    accs = refs[:-8]
    a1, acc_mlp, b1_first, b1_rest, keep, send, small, grads = refs[-8:]
    feats = a1.shape[1]
    count = 2 * keep.shape[0]
    size = 3 * feats // count
    acc = accs[0][...]
    for other in accs[1:]:
        acc = acc + other[...]
    small[...] = jnp.zeros_like(small)
    small[0:2, :] = acc[2 * heads + 11 : 2 * heads + 13]
    small[2:8, :] = acc_mlp[0:6, :]
    small[8:11, :] = acc[2 * heads + 8 : 2 * heads + 11]
    head_dim = feats // heads
    lanes = 2 * heads * heads
    gather = (
        head_of_lane((feats, lanes), 0, head_dim)
        == lax.broadcasted_iota(jnp.int32, (feats, lanes), 1) % heads
    ).astype(F32)
    sums = exact(acc[0 : 2 * heads + 8], gather, ((1,), (0,)))
    place = head_of_lane((2 * heads, lanes), 1, heads) == lax.broadcasted_iota(
        jnp.int32, (2 * heads, lanes), 0
    )
    small[11:12, 0:lanes] = colsum(jnp.where(place, sums[0 : 2 * heads], 0.0))
    small[11:12, lanes : 2 * lanes] = sums[2 * heads : 2 * heads + 1]
    m_idx = lax.axis_index("mp")
    for c, ref in enumerate((b1_first, b1_first, b1_rest, b1_rest)):
        place = 12 + jnp.bitwise_xor(m_idx, c)
        small[pl.ds(place, 1), :] = ref[:, (c % 2) * feats : (c % 2 + 1) * feats]
    low = small[...].astype(BF)
    outs = (keep, send)

    grads[...] = tn(a1[...], dqkv[...]).astype(BF).T

    def put(which, place, b):
        outs[which][place, 0:size, :] = grads[b * size : (b + 1) * size, :]
        outs[which][place, size : size + 16, :] = low
        if outs[which].shape[1] > size + 16:
            outs[which][place, size + 16 :, :] = jnp.zeros_like(outs[which][place, size + 16 :, :])

    store_blocks(count, put)


def final_kernel(heads, size, many, mine, proj_own, *refs):
    got = refs[:many]
    mlp_mine, got_z = refs[many], refs[1 + many : 1 + 2 * many]
    qkv_o, qkvb_o, pre_o, post_o, postb_o, b1_o, *vecs_o, fc1_o, fc2_o, proj_o, held = refs[-18:]
    block, feats = fc1_o.shape
    for place, out in enumerate((fc1_o, fc2_o)):
        rows = slice(place * block, (place + 1) * block)
        out[...] = mlp_mine[rows, :] + sum(g[rows, :].astype(F32) for g in got_z)
    d_idx = lax.axis_index("dp")
    m_idx = lax.axis_index("mp")
    total = mine[...]
    held[m_idx] = proj_own[...].astype(F32)
    for j, part in enumerate(got):
        value = part[...].astype(F32)
        total = total + value[0 : size + 16]
        held[jnp.bitwise_xor(m_idx, j + 1)] = value[size + 16 :]
    proj_o[...] = held[...].reshape(-1, feats)[0:block]
    qkv_o[...] = total[0:size]
    small = total[size : size + 16]

    def own(value, width, index):
        lanes = value.shape[1]
        return pltpu.roll(value, lax.rem(lanes - index * width, lanes), axis=1)[:, 0:width]

    width = vecs_o[0].shape[1]
    vecs = own(small[0:8], width, d_idx)
    for j, ref in enumerate(vecs_o):
        ref[...] = vecs[j : j + 1]
    flat = jnp.concatenate([small[8 + j : 9 + j] for j in range(3)], axis=1)
    qkvb_o[...] = own(jnp.broadcast_to(flat, (8, 3 * feats)), qkvb_o.shape[1], d_idx)[0:1]
    b1 = own(small[8:16], b1_o.shape[1], d_idx)[4:8]
    pick = lax.broadcasted_iota(jnp.int32, b1.shape, 0) == m_idx
    b1_o[...] = colsum(jnp.where(pick, b1, 0.0))
    mix = small[11:12]
    hh = heads * heads
    line = lax.broadcasted_iota(jnp.int32, (heads, hh), 0)
    lane = lax.broadcasted_iota(jnp.int32, (heads, hh), 1)
    fold = (
        lax.broadcasted_iota(jnp.int32, (hh, heads), 0) % heads
        == lax.broadcasted_iota(jnp.int32, (hh, heads), 1)
    ).astype(F32)
    head_dim = feats // heads

    def square(values):
        return exact(jnp.where(lane // heads == line, values, 0.0), fold, ((1,), (0,)))

    post_o[...] = square(mix[:, 0:hh]).T
    pre_o[...] = square(mix[:, hh : 2 * hh]) * (head_dim**-0.5)
    postb_o[...] = mix[:, 2 * hh : 2 * hh + heads]


def whole(shape):
    return pl.BlockSpec(shape, lambda i: (0,) * len(shape))


def each(shape, first=0, many=1):
    return pl.BlockSpec((many,) + shape[1:], lambda i: (i + first,) + (0,) * (len(shape) - 1))


SCALARS = pl.BlockSpec(memory_space=pltpu.SMEM)
IN_VMEM = pl.BlockSpec(memory_space=pltpu.VMEM)
IN_HBM = pl.BlockSpec(memory_space=pltpu.HBM)


def kept(a):
    return pltpu.with_memory_space_constraint(a, pltpu.HBM)


def sds(shape, dtype):
    return jax.ShapeDtypeStruct(shape, dtype)


def call(
    kernel, grid, ins, in_specs, outs, out_specs, scratch=(), flops=0, name=None, aliases=None,
    limit=VMEM_LIMIT,
):
    size = lambda a: a.size * a.dtype.itemsize
    return pl.pallas_call(
        kernel,
        grid=grid,
        in_specs=in_specs,
        out_specs=out_specs,
        out_shape=outs,
        scratch_shapes=scratch,
        input_output_aliases=aliases or {},
        compiler_params=pltpu.CompilerParams(vmem_limit_bytes=limit),
        cost_estimate=pl.CostEstimate(
            flops=flops,
            bytes_accessed=sum(size(a) for a in ins) + sum(size(a) for a in outs),
            transcendentals=0,
        ),
        name=name,
    )(*ins)


def xor_perm(count, mask):
    return [(j, j ^ mask) for j in range(count)]


def dp_hops(dp):
    bits = dp.bit_length() - 1
    groups = []
    at = 1
    while at < bits:
        groups.append((at, min(2, bits - at)))
        at += groups[-1][1]
    return groups


def dp_scatter(value, dp):
    for at, many in dp_hops(dp):
        value = value.reshape((-1, 1 << many) + value.shape[1:])
        got = [
            lax.ppermute(value[:, j].astype(BF), "dp", xor_perm(dp, j << at))
            for j in range(1, 1 << many)
        ]
        value = value[:, 0] + sum(g.astype(F32) for g in got)
    return value.reshape(value.shape[-2:])


def per_device(
    dp, mp,
    tokens_in, image_counts, norm1_gain, norm1_bias, qkv_weight, qkv_bias,
    mix_pre, mix_post, mix_post_bias, proj_weight, proj_bias, gamma1,
    norm2_gain, norm2_bias, fc1_weight, fc1_bias, fc2_weight, fc2_bias, gamma2, out_grad,
):
    images, patches, feats = tokens_in.shape
    heads = mix_pre.shape[0]
    rows = -(-patches // 16) * 16
    slots = -(-patches // 128) * 128
    hidden = fc1_weight.shape[1]
    tok_rows = (images, rows, feats)
    slot_rows = (images, slots, feats)
    prob_shape = (images, heads, rows, slots)
    mix_shape = (heads, feats)
    operands = [
        tokens_in, out_grad, norm1_gain, norm1_bias, qkv_bias, mix_pre, mix_post,
        mix_post_bias, proj_bias, gamma1, norm2_gain, norm2_bias, qkv_weight, proj_weight,
    ]

    ins = [kept(a) for a in [fc1_weight, fc2_weight, fc1_bias] + operands]
    outs = [sds((feats + 16, hidden), BF)] + [sds(a.shape, a.dtype) for a in operands]
    other, *held = call(
        pack_kernel,
        (),
        ins,
        [IN_HBM] * len(ins),
        outs,
        [IN_VMEM] * len(outs),
        [pltpu.VMEM(fc1_bias.shape, F32), pltpu.SemaphoreType.DMA((2 + len(operands),))],
        name="pack",
    )
    near = [lax.ppermute(other, "mp", xor_perm(mp, j)) for j in (1, 2)]

    shares = [images - 1, 1] if images > 1 else [images]
    carried = []
    for s, share in enumerate(shares):
        first = sum(shares[:s])
        ins = [image_counts, mix_post, mix_post_bias] + held
        outs = call(
            functools.partial(attn_fwd_kernel, first, share),
            (),
            ins + carried,
            [SCALARS] * 3
            + [IN_VMEM] * 14
            + [pl.BlockSpec(memory_space=pl.ANY)] * len(carried),
            [
                sds(tok_rows, BF), sds(slot_rows, BF), sds(tok_rows, BF), sds(tok_rows, BF),
                sds(prob_shape, BF), sds(tok_rows, BF), sds(tok_rows, F32), sds(tok_rows, F32),
                sds(tok_rows, BF), sds(tok_rows, BF), sds(mix_shape, F32), sds(mix_shape, F32),
                sds((1, feats), F32),
            ],
            [IN_VMEM] * 13,
            [
                pltpu.VMEM((rows, feats), F32), pltpu.VMEM((heads * rows, 2 * feats), BF),
                pltpu.VMEM((feats, slots), BF), pltpu.VMEM((heads * rows, slots), BF),
                pltpu.VMEM((rows, 3 * feats), F32), pltpu.VMEM((heads * rows, slots), F32),
                pltpu.VMEM((heads, feats, slots), F32),
            ],
            flops=share * 15 * 10**8,
            name="attn_fwd",
            aliases={len(ins) + j: j for j in range(10)} if carried else None,
        )
        carried, (mpre, mpost, mixb) = list(outs[:10]), outs[10:]
        if s == 0:
            near, carried[0] = lax.optimization_barrier((near, carried[0]))
            last = lax.ppermute(near[1], "mp", xor_perm(mp, 1))
            near = jnp.stack(near)
            far = lax.ppermute(near, "dp", xor_perm(dp, 1))
    a1, q, k, v, prob, o, x1, u, a2, dy = carried
    far, a2 = lax.optimization_barrier((far, a2))

    block = feats // dp
    total = images * rows
    flat = (total, feats)
    a2, dy, x1, u, o = (a.reshape(flat) for a in (a2, dy, x1, u, o))
    ins = [a2, dy, gamma2, fc1_weight, fc1_bias, fc2_weight, near, far]
    wide = 2 * hidden
    grad_shape = (2, wide, feats)
    f0, da20, b1_0, hids, dzs, dfs = call(
        mlp_first_kernel,
        (),
        ins,
        [IN_VMEM] * len(ins),
        [
            sds(flat, F32), sds(flat, F32), sds((1, wide), F32), sds((total, wide), BF),
            sds((total, wide), BF), sds(flat, BF),
        ],
        [IN_VMEM] * 6,
        [
            pltpu.VMEM((feats, wide), BF), pltpu.VMEM((wide, feats), BF),
            pltpu.VMEM((1, wide), F32),
            pltpu.VMEM((2, total // 3, wide), F32), pltpu.VMEM((2, total // 3, wide), F32),
        ],
        flops=images * 5 * 10**8,
        name="mlp_first",
    )

    last, f0 = lax.optimization_barrier((last, f0))
    far_last = lax.ppermute(last, "dp", xor_perm(dp, 1))
    ins = [a2, hids, dzs, dfs]
    grads0, a2t, dft = call(
        mlp_grad_kernel,
        (),
        ins,
        [IN_VMEM] * 4,
        [sds(grad_shape, BF), sds((feats, total), BF), sds((feats, total), BF)],
        [IN_VMEM] * 3,
        flops=images * 3 * 10**8,
        name="mlp_grad",
    )

    grad_rows = 9 * block
    half_shape = (dp // 2, grad_rows, feats)
    ins = [
        image_counts, a2, dy, dfs, x1, u, o, f0, da20, near, far, last, far_last, grads0, a2t, dft,
        proj_weight, gamma1,
        norm2_gain, fc2_bias, gamma2,
    ]
    layer_out, dx1, do, keep, send, b1_1, acc_mlp = call(
        mlp_rest_kernel,
        (),
        ins,
        [SCALARS] + [IN_VMEM] * (len(ins) - 1),
        [
            sds(tokens_in.shape, BF), sds(flat, F32), sds(slot_rows, BF), sds(half_shape, BF),
            sds(half_shape, BF), sds((1, wide), F32), sds((8, feats), F32),
        ],
        [IN_HBM] + [IN_VMEM] * 6,
        [
            pltpu.VMEM((feats, wide), BF), pltpu.VMEM((wide, feats), BF),
            pltpu.VMEM((1, wide), F32), pltpu.VMEM((total, wide), BF),
            pltpu.VMEM((total, wide), BF),
            pltpu.VMEM((2, total // 3, wide), F32), pltpu.VMEM((2, total // 3, wide), F32),
            pltpu.VMEM(flat, F32), pltpu.VMEM(flat, F32), pltpu.VMEM(flat, BF),
            pltpu.VMEM((wide, feats), BF), pltpu.VMEM((feats, wide), BF),
            pltpu.VMEM((feats, feats), BF), pltpu.VMEM(tokens_in.shape, BF),
            pltpu.SemaphoreType.DMA((images,)),
        ],
        flops=images * 9 * 10**8,
        name="mlp_rest",
    )
    got = lax.ppermute(send, "dp", xor_perm(dp, 1))
    dx1 = dx1.reshape(tok_rows)

    shares = [1, images - 1] if images > 1 else [1]
    dqkv_shape = (images, rows, 3 * feats)
    carried, accs = [], []
    for s, share in enumerate(shares):
        first = sum(shares[:s])
        ins = [mix_pre, do, q, k, v, prob, dx1, tokens_in, mpre, mpost, mixb, qkv_weight, norm1_gain]
        *carried, acc = call(
            functools.partial(attn_bwd_kernel, first, share),
            (),
            ins + carried,
            [SCALARS]
            + [IN_VMEM] * (len(ins) - 1)
            + [pl.BlockSpec(memory_space=pl.ANY)] * len(carried),
            [sds(dqkv_shape, BF), sds(tokens_in.shape, F32), sds((2 * heads + 16, feats), F32)],
            [IN_VMEM, IN_HBM, IN_VMEM],
            [
                pltpu.VMEM((heads * rows, feats), BF), pltpu.VMEM((heads * rows, slots), BF),
                pltpu.VMEM((feats, slots), BF), pltpu.VMEM((heads * rows, slots), F32),
                pltpu.VMEM((heads * rows, feats), F32), pltpu.VMEM((heads * rows, feats), F32),
                pltpu.VMEM((heads, feats, slots), F32), pltpu.VMEM((rows, feats), F32),
                pltpu.VMEM((rows, feats), F32), pltpu.VMEM((share, patches, feats), F32),
                pltpu.SemaphoreType.DMA((share,)),
            ],
            flops=share * 20 * 10**8,
            name="attn_bwd",
            aliases={len(ins): 0, len(ins) + 1: 1} if carried else None,
        )
        accs.append(acc)
        if s == 0:
            (keep, got), acc = lax.optimization_barrier(((keep, got), acc))
            mine = dp_scatter(keep.astype(F32) + got.astype(F32), dp)
            accs[0], do = lax.optimization_barrier((acc, do))
    dqkv, in_grad = carried
    mine, dqkv = lax.optimization_barrier((mine, dqkv))
    mlp_mine = mine
    low = mine.astype(BF)
    m_idx = lax.axis_index("mp")
    share_rows = -(-block // (16 * mp)) * 16
    proj = jnp.pad(mine[8 * block :], ((0, mp * share_rows - block), (0, 0)))

    def proj_share(j):
        return lax.dynamic_slice_in_dim(proj, jnp.bitwise_xor(m_idx, j) * share_rows, share_rows)

    got_z = [
        lax.ppermute(
            jnp.concatenate([low[2 * j * block : 2 * (j + 1) * block], proj_share(j).astype(BF)]),
            "mp",
            xor_perm(mp, j),
        )
        for j in range(1, mp)
    ]

    q_block = 3 * feats // dp
    half_shape = (dp // 2, q_block + 16, feats)
    ins = [dqkv.reshape(total, 3 * feats)] + accs + [a1.reshape(flat), acc_mlp, b1_0, b1_1]
    keep, send = call(
        functools.partial(qkv_grad_kernel, heads),
        (),
        ins,
        [IN_VMEM] * len(ins),
        [sds(half_shape, BF), sds(half_shape, BF)],
        [IN_VMEM] * 2,
        [pltpu.VMEM((16, feats), F32), pltpu.VMEM((3 * feats, feats), BF)],
        flops=11 * 10**8,
        name="qkv_grad",
    )
    got = lax.ppermute(send, "dp", xor_perm(dp, 1))
    mine = dp_scatter(keep.astype(F32) + got.astype(F32), dp)
    mine, got_z = lax.optimization_barrier((mine, got_z))

    proj_own = (proj_share(0) + sum(g[2 * block :].astype(F32) for g in got_z)).astype(BF)
    payload = jnp.concatenate([mine.astype(BF), proj_own])
    got = [lax.ppermute(payload, "mp", xor_perm(mp, j)) for j in range(1, mp)]
    b1_size = hidden // dp
    ins = [mine, proj_own] + got + [mlp_mine] + got_z
    outs = [
        sds((q_block, feats), F32), sds((1, q_block), F32), sds((heads, heads), F32),
        sds((heads, heads), F32), sds((1, heads), F32), sds((1, b1_size), F32),
    ] + [sds((1, block), F32)] * 8 + [sds((block, feats), F32)] * 3
    qkvw, qkvb, pre, post, postb, b1g, *vecs, fc1g, fc2g, projg = call(
        functools.partial(final_kernel, heads, q_block, mp - 1),
        (),
        ins,
        [IN_VMEM] * len(ins),
        outs,
        [IN_VMEM] * len(outs),
        [pltpu.VMEM((mp, share_rows, feats), F32)],
        name="final",
    )
    vecs = [a.reshape(-1) for a in vecs]
    return (
        layer_out,
        in_grad,
        vecs[0],
        vecs[1],
        qkvw.T,
        qkvb.reshape(-1),
        pre,
        post,
        postb.reshape(-1),
        projg.T,
        vecs[2],
        vecs[3],
        vecs[4],
        vecs[5],
        fc1g.T,
        b1g.reshape(-1),
        fc2g.T,
        vecs[6],
        vecs[7],
    )


def solution(mesh):
    tokens = P(("dp", "mp"), None, None)
    placed = (
        (tokens, P("dp")) + (P(),) * 12 + (P(None, "mp"), P("mp"), P("mp", None), P(), P(), tokens)
    )
    return jax.shard_map(
        functools.partial(per_device, mesh.shape["dp"], mesh.shape["mp"]),
        mesh=mesh,
        in_specs=placed,
        out_specs=(
            tokens, tokens, P("dp"), P("dp"), P(None, "dp"), P("dp"), P(), P(), P(),
            P(None, "dp"), P("dp"), P("dp"), P("dp"), P("dp"), P(None, ("mp", "dp")),
            P(("mp", "dp")), P("mp", "dp"), P("dp"), P("dp"),
        ),
        check_vma=False,
    )
```

```python
import functools

import jax
import jax.numpy as jnp
from jax import lax
from jax.experimental import pallas as pl
from jax.experimental.pallas import tpu as pltpu
from jax.sharding import PartitionSpec as P

BF = jnp.bfloat16
F32 = jnp.float32
LOG2E = 1.4426950408889634
EPS = 1e-06
VMEM_LIMIT = 20 * 1024 * 1024


def nn(a, b):
    return lax.dot_general(a, b, (((1,), (0,)), ((), ())), preferred_element_type=F32)


def nt(a, b):
    return lax.dot_general(a, b, (((1,), (1,)), ((), ())), preferred_element_type=F32)


def tn(a, b):
    return lax.dot_general(a, b, (((0,), (0,)), ((), ())), preferred_element_type=F32)


def exact(a, b, dims):
    return lax.dot_general(
        a, b, (dims, ((), ())), precision=lax.Precision.HIGHEST, preferred_element_type=F32
    )


def normalized(x):
    mean = jnp.mean(x, axis=-1, keepdims=True)
    c = x - mean
    r = lax.rsqrt(jnp.mean(c * c, axis=-1, keepdims=True) + EPS)
    return c * r, r


def norm_back(cot, n, r, gain):
    cg = cot * gain
    return r * (
        cg
        - jnp.mean(cg, axis=-1, keepdims=True)
        - n * jnp.mean(cg * n, axis=-1, keepdims=True)
    )


def colsum(x):
    return jnp.sum(x, axis=0, keepdims=True)


def split(x):
    hi = x.astype(BF)
    return jnp.concatenate([hi, (x - hi.astype(F32)).astype(BF)], axis=1)


def row(ref):
    return ref[...].reshape(1, ref.shape[0])


def gelu_parts(z):
    e = jnp.exp2(z * z * (-0.5 * LOG2E))
    t = pl.reciprocal(1.0 + jnp.abs(z) * (0.3275911 * 0.7071067811865476), approx=True)
    poly = t * (
        0.5 * 0.254829592
        + t
        * (
            0.5 * -0.284496736
            + t * (0.5 * 1.421413741 + t * (0.5 * -1.453152027 + t * (0.5 * 1.061405429)))
        )
    )
    tail = poly * e
    phi = jnp.where(z >= 0, 1.0 - tail, tail)
    return phi, phi + z * e * 0.3989422804014327


def head_of_lane(shape, axis, head_dim):
    return lax.broadcasted_iota(jnp.int32, shape, axis) // head_dim


def chunks(count, size=16):
    return [slice(at, at + size) for at in range(0, count, size)]


def fold(x):
    return sum(x[at : at + 8] for at in range(8, x.shape[0], 8)) + x[0:8]


def pack_kernel(w1, w2, b1, *refs):
    many = (len(refs) - 3) // 2
    sources, other, held, b1_v, sems = refs[:many], refs[many], refs[many + 1 : -2], refs[-2], refs[-1]
    feats = w1.shape[0]
    core = jnp.bitwise_and(lax.axis_index("dp"), 1)
    bias_copy = pltpu.make_async_copy(b1, b1_v, sems.at[0])
    own = [pltpu.make_async_copy(w, other.at[0:feats], sems.at[1]) for w in (w1, w2)]
    copies = [
        pltpu.make_async_copy(sources[j], held[j], sems.at[2 + j]) for j in range(many)
    ]
    bias_copy.start()
    for j in range(2):
        pl.when(core == j)(own[j].start)
    for copy in copies:
        copy.start()
    bias_copy.wait()
    rest = row(b1_v)
    place = lax.broadcasted_iota(jnp.int32, (16, feats), 0)
    bias = jnp.zeros((16, feats), F32)
    for j in range(3):
        term = rest.astype(BF).astype(F32)
        bias = jnp.where(place == j, term, bias)
        rest = rest - term
    other[feats:, :] = bias.astype(BF)
    for j in range(2):
        pl.when(core == j)(own[j].wait)
    for copy in copies:
        copy.wait()


def attn_fwd_kernel(first, share, *refs):
    counts, post_s, postb_s, tok, og, n1g, n1b, qkvb, pre, post, postb, projb = refs[:12]
    gamma1, n2g, n2b, wqkv, wproj = refs[12:17]
    a1_o, q_o, k_o, v_o, p_o, o_o, x1_o, u_o, a2_o, dy_o, mpre, mpost, mixb = refs[-20:-7]
    pad, kk, attended_t, probs, wide, logits, mixed = refs[-7:]
    images, patches, feats = tok.shape
    rows = pad.shape[0]
    heads = mpre.shape[0]
    head_dim = feats // heads
    slots = q_o.shape[1]

    spread = (
        head_of_lane((heads, feats), 1, head_dim)
        == lax.broadcasted_iota(jnp.int32, (heads, feats), 0)
    ).astype(F32)
    mpre[...] = exact(pre[...], spread, ((1,), (0,))) * (head_dim**-0.5 * LOG2E)
    mpost[...] = exact(post[...], spread, ((0,), (0,)))
    mixb[...] = exact(row(postb), spread, ((1,), (0,)))

    @pl.loop(first, first + share)
    def _(i):
        pad[patches:, :] = jnp.zeros((rows - patches, feats), F32)
        live = (lax.axis_index("mp") * images + i < counts[0]).astype(F32)
        pad[0:patches, :] = og[i].astype(F32) * live
        dy_o[i] = pad[...].astype(BF)
        pad[0:patches, :] = tok[i].astype(F32)
        gain, shift = row(n1g), row(n1b)
        for c in chunks(rows):
            n, _ = normalized(pad[c, :])
            a1_o[i, c, :] = (n * gain + shift).astype(BF)
        wide[...] = nn(a1_o[i], wqkv[...])
        bias = row(qkvb)
        q_o[i, rows:] = jnp.zeros((slots - rows, feats), BF)
        for c in chunks(rows):
            q, k, v = (
                wide[c, j * feats : (j + 1) * feats] + bias[:, j * feats : (j + 1) * feats]
                for j in range(3)
            )
            q_o[i, c, :] = q.astype(BF)
            v_o[i, c, :] = v.astype(BF)
            k = k.astype(BF)
            k_o[i, c, :] = k
            kf = k.astype(F32)
            for g in range(heads):
                at = slice(g * rows + c.start, g * rows + c.stop)
                scaled = kf * mpre[g : g + 1, :]
                hi = scaled.astype(BF)
                kk[at, 0:feats] = hi
                kk[at, feats:] = (scaled - hi.astype(F32)).astype(BF)
        q2 = jnp.concatenate([q_o[i], q_o[i]], axis=1)
        vt = v_o[i].T
        many = heads // 2
        half = many * rows
        tail = patches // 8 * 8
        inside = lax.broadcasted_iota(jnp.int32, (rows - tail, 128), 0) < patches - tail
        real = (lax.broadcasted_iota(jnp.int32, (rows, 128), 0) < patches).astype(BF)
        start = nn(vt, real)
        for s in range(2):
            part = slice(s * half, (s + 1) * half)
            logits[part, :] = nt(kk[part, :], q2)
        for g in range(heads):
            for lane in range(0, slots, 128):
                x = logits[g * rows : (g + 1) * rows, lane : lane + 128]
                x = jnp.concatenate([x[0:tail], jnp.where(inside, x[tail:], -1e30)], axis=0)
                e = jnp.exp2(x - jnp.max(x, axis=0, keepdims=True))
                inv = 1.0 / jnp.sum(e, axis=0, keepdims=True)
                p = (e * inv).astype(BF)
                probs[g * rows : (g + 1) * rows, lane : lane + 128] = p
                p_o[i, g, :, lane : lane + 128] = p
            mixed[g] = nn(vt, probs[g * rows : (g + 1) * rows, :])
        for c in chunks(feats):
            g = c.start // head_dim
            first = start[c] * postb_s[g]
            for lane in range(0, slots, 128):
                total = first
                for h in range(heads):
                    total = total + mixed[h, c, lane : lane + 128] * post_s[g, h]
                attended_t[c, lane : lane + 128] = total.astype(BF)
        o_o[i] = attended_t[...].T[0:rows]
        wide[:, 0:feats] = nn(o_o[i], wproj[...])
        bias, scale, gain, shift = row(projb), row(gamma1), row(n2g), row(n2b)
        for c in chunks(rows):
            u = wide[c, 0:feats] + bias
            x1 = pad[c, :] + scale * u
            u_o[i, c, :] = u
            x1_o[i, c, :] = x1
            n, _ = normalized(x1)
            a2_o[i, c, :] = (n * gain + shift).astype(BF)


def store_blocks(count, put):
    mine = lax.axis_index("dp")
    for core in range(2):

        @pl.when(jnp.bitwise_and(mine, 1) == core)
        def _(core=core):
            for b in range(count):
                place = jnp.bitwise_xor(jnp.int32(b >> 1), jnp.right_shift(mine, 1))
                put((b ^ core) & 1, place, b)


def mlp_units(a2, dfs, w1, b1, w2, hids, dzs, zs, ghs, units, store, use):
    size = a2.shape[0] // units
    width = w2.shape[0]
    lanes = zs.shape[2]
    places = [slice(u * size, (u + 1) * size) for u in range(units)]
    blocks = [(u, at) for u in range(units) for at in range(0, width, lanes)]

    def products(j):
        u, at = blocks[j]
        part = slice(at, at + lanes)
        zs[j % 2] = nn(a2[places[u], :], w1[:, part])
        ghs[j % 2] = nt(dfs[places[u], :], w2[part, :])

    def activation(j):
        u, at = blocks[j]
        part = slice(at, at + lanes)
        bias = b1[:, part]
        for c in chunks(size):
            zc = zs[j % 2, c, :] + bias
            phi, slope = gelu_parts(zc)
            rows = slice(places[u].start + c.start, places[u].start + c.stop)
            hids[rows, part] = (zc * phi).astype(BF)
            dzs[rows, part] = (ghs[j % 2, c, :] * slope).astype(BF)

    def finish(u):
        store(places[u], nn(hids[places[u], :], w2[...]), nt(dzs[places[u], :], w1[...]))

    products(0)
    for j, (u, at) in enumerate(blocks):
        if j + 1 < len(blocks):
            products(j + 1)
        if at == lanes and u > 0:
            finish(u - 1)
        activation(j)
        if at == 2 * lanes and u > 0:
            use(places[u - 1])
    finish(units - 1)
    use(places[units - 1])


def mlp_first_kernel(
    a2, dy, gamma2, w1_own, b1_own, w2_own, near, far,
    f_o, da2_o, hids, dzs, dfs,
    w1, w2, b1, zs, ghs,
):
    total, feats = f_o.shape
    w1[:, 0:feats] = w1_own[...]
    w2[0:feats, :] = w2_own[...]
    for core in range(2):

        @pl.when(jnp.bitwise_and(lax.axis_index("dp"), 1) == core)
        def _(core=core):
            one, two = (near, far) if core == 0 else (far, near)
            w1[:, feats:] = one[0, 0:feats]
            w2[feats:, :] = two[0, 0:feats]

    b1[:, 0:feats] = row(b1_own)
    b1[:, feats:] = colsum(near[0, feats : feats + 16].astype(F32))
    gain = row(gamma2)
    for c in chunks(total):
        dfs[c, :] = (dy[c, :].astype(F32) * gain).astype(BF)

    def store(rows, f, da2):
        f_o[rows, :] = f
        da2_o[rows, :] = da2

    mlp_units(a2, dfs, w1, b1, w2, hids, dzs, zs, ghs, 3, store, lambda rows: None)


def mlp_grad_kernel(a2, hids, dzs, dfs, grads, b1_o, a2t, dft):
    feats = a2.shape[1]
    a2t[0:feats, :] = a2[...].T
    a2t[feats:, :] = jnp.ones((a2t.shape[0] - feats, a2t.shape[1]), BF)
    dft[...] = dfs[...].T
    up = nn(a2t[...], dzs[...])
    b1_o[...] = up[feats : feats + 1]
    grads[0] = up[0:feats].astype(BF).T
    down = nn(dft[...], hids[...]).astype(BF)
    for c in range(2):
        grads[1, c * feats : (c + 1) * feats, :] = down[:, c * feats : (c + 1) * feats]


def mlp_rest_kernel(
    counts, a2, dy, dfs, x1, u, o, f0, da20, near, far, last, far_last, grads, a2t, dft, wproj,
    gamma1, n2g, fc2b, gamma2,
    out_o, dx1_o, do_o, keep, send, b1_o, acc_o,
    w1, w2, b1, hids, dzs, zs, ghs, fs, da2s, dus, ups, downs, projs, out_v, sems,
):
    total, feats = f0.shape
    images, patches = out_o.shape[:2]
    image_rows = total // images
    m_idx = lax.axis_index("mp")
    acc_o[...] = jnp.zeros_like(acc_o)
    b1[:, 0:feats] = colsum(near[1, feats : feats + 16].astype(F32))
    b1[:, feats:] = colsum(last[feats : feats + 16].astype(F32))
    for core in range(2):

        @pl.when(jnp.bitwise_and(lax.axis_index("dp"), 1) == core)
        def _(core=core):
            one, two = (near, far) if core == 0 else (far, near)
            w1[:, 0:feats] = one[1, 0:feats]
            w2[0:feats, :] = two[1, 0:feats]
            one, two = (last, far_last) if core == 0 else (far_last, last)
            w1[:, feats:] = one[0:feats]
            w2[feats:, :] = two[0:feats]

    gain2 = row(gamma2)
    bias, gain, scale = row(fc2b), row(n2g), row(gamma1)

    def out_copy(image):
        return pltpu.make_async_copy(out_v.at[image], out_o.at[image], sems.at[image])

    def store(rows, f, da2):
        fs[rows, :] = f
        da2s[rows, :] = da2

    def use(rows):
        sums = [jnp.zeros((8, feats), F32) for _ in range(6)]
        for c in chunks(rows.stop - rows.start):
            at = slice(rows.start + c.start, rows.start + c.stop)
            fc = fs[at, :] + f0[at, :] + bias
            dac = da2s[at, :] + da20[at, :]
            x1c = x1[at, :]
            dyc = dy[at, :].astype(F32)
            n, r = normalized(x1c)
            dx1 = dyc + norm_back(dac, n, r, gain)
            dx1_o[at, :] = dx1
            du = (dx1 * scale).astype(BF)
            dus[at, :] = du
            image = at.start // image_rows
            first = at.start - image * image_rows
            live = (m_idx * images + image < counts[0]).astype(F32)
            out = ((x1c + gain2 * fc) * live).astype(BF)
            if first + 16 <= patches:
                out_v[image, first : first + 16, :] = out
            else:
                out_v[image, first:patches, :] = out[0 : patches - first]
            terms = (
                du.astype(F32), u[at, :] * dx1, dac * n, dac, dfs[at, :].astype(F32), fc * dyc,
            )
            sums = [s + fold(t) for s, t in zip(sums, terms)]
        for j in range(6):
            acc_o[j : j + 1, :] += colsum(sums[j])
        do = nt(dus[rows, :], wproj[...]).astype(BF)
        for at in range(0, rows.stop - rows.start, image_rows):
            image = (rows.start + at) // image_rows
            out_copy(image).start()
            do_o[image, 0:image_rows] = do[at : at + image_rows]
            do_o[image, image_rows:] = jnp.zeros((do_o.shape[1] - image_rows, feats), BF)

    mlp_units(a2, dfs, w1, b1, w2, hids, dzs, zs, ghs, 3, store, use)
    up = nn(a2t[...], dzs[...])
    b1_o[...] = up[feats : feats + 1]
    ups[...] = up[0:feats].astype(BF).T
    downs[...] = nn(dft[...], hids[...]).astype(BF)
    projs[...] = tn(dus[...], o[...]).astype(BF)
    count = 2 * keep.shape[0]
    size = feats // count
    outs = (keep, send)

    def put(which, place, b):
        out = outs[which]
        for c in range(2):
            part = slice(c * feats, (c + 1) * feats)
            up = slice(c * feats + b * size, c * feats + (b + 1) * size)
            down = slice(b * size, (b + 1) * size)
            pieces = (grads[0, up, :], grads[1, up, :])
            for j, piece in enumerate(pieces):
                out[place, (2 * c + j) * size : (2 * c + j + 1) * size, :] = piece
            pieces = (ups[up, :], downs[down, part])
            for j, piece in enumerate(pieces):
                out[place, (4 + 2 * c + j) * size : (5 + 2 * c + j) * size, :] = piece
        out[place, 8 * size : 9 * size, :] = projs[b * size : (b + 1) * size, :]

    store_blocks(count, put)
    for image in range(images):
        out_copy(image).wait()


def attn_bwd_kernel(first, share, *refs):
    pre_s, do_r, q_r, k_r, v_r, p_r, dx1, tok, mpre, mpost, mixb, wqkv, n1g = refs[:13]
    dqkv_o, in_o, acc_o, vgs, dls, dq_t, dps, dvs, dks, dqs, da1, pad, in_v, sems = refs[-14:]
    slots, feats = do_r.shape[1:]
    patches = tok.shape[1]
    rows = k_r.shape[1]
    heads = mpre.shape[0]
    head_dim = feats // heads
    many = heads // 2
    half = many * rows
    acc_o[...] = jnp.zeros_like(acc_o)

    def in_copy(i):
        return pltpu.make_async_copy(in_v.at[i - first], in_o.at[i], sems.at[i - first])

    @pl.loop(first, first + share)
    def _(i):
        do_sum = jnp.zeros((8, feats), F32)
        for c in chunks(rows):
            vf = v_r[i, c, :].astype(F32)
            do_sum = do_sum + fold(do_r[i, c, :].astype(F32))
            for h in range(heads):
                vgs[h * rows + c.start : h * rows + c.stop, :] = (vf * mpost[h : h + 1, :]).astype(BF)
        do_sum = colsum(do_sum)
        q = q_r[i]
        do = do_r[i]
        kt = k_r[i].T
        parts = [slice(s * half, (s + 1) * half) for s in range(2)]
        for part in parts:
            dps[part, :] = nt(vgs[part, :], do)
        for s, part in enumerate(parts):
            dvs[part, :] = nn(p_r[i, s * many : (s + 1) * many].reshape(half, slots), do)
        for s, part in enumerate(parts):
            for h in range(s * many, (s + 1) * many):
                at = slice(h * rows, (h + 1) * rows)
                for lane in range(0, slots, 128):
                    dp = dps[at, lane : lane + 128]
                    pf = p_r[i, h, :, lane : lane + 128].astype(F32)
                    mean = jnp.sum(dp * pf, axis=0, keepdims=True) / jnp.sum(pf, axis=0, keepdims=True)
                    dls[at, lane : lane + 128] = (pf * (dp - mean)).astype(BF)
                dqs[h] = nn(kt, dls[at, :])
            dks[part, :] = nn(dls[part, :], q)

        bias_row = mixb[...] * do_sum
        v_sum = jnp.zeros((8, feats), F32)
        dv_sum = jnp.zeros((8, feats), F32)
        sums = [jnp.zeros((8, feats), F32) for _ in range(heads)]
        for c in chunks(rows):
            vf = v_r[i, c, :].astype(F32)
            dv = bias_row
            for h in range(heads):
                this = dvs[h * rows + c.start : h * rows + c.stop, :]
                dv = dv + this * mpost[h : h + 1, :]
                sums[h] = sums[h] + fold(vf * this)
            if c.stop > patches:
                inside = lax.broadcasted_iota(jnp.int32, dv.shape, 0) < patches - c.start
                dv = jnp.where(inside, dv, 0.0)
                vf = jnp.where(inside, vf, 0.0)
            low = dv.astype(BF)
            dqkv_o[i, c, 2 * feats :] = low
            dv_sum = dv_sum + fold(low.astype(F32))
            v_sum = v_sum + fold(vf)
        for h in range(heads):
            acc_o[h : h + 1, :] += colsum(sums[h])
        acc_o[2 * heads : 2 * heads + 1, :] += do_sum * colsum(v_sum)
        acc_o[2 * heads + 10 : 2 * heads + 11, :] += colsum(dv_sum)

        for c in chunks(feats):
            g = c.start // head_dim
            for lane in range(0, slots, 128):
                total = 0.0
                for h in range(heads):
                    total = total + dqs[h, c, lane : lane + 128] * pre_s[h, g]
                dq_t[c, lane : lane + 128] = (total * head_dim**-0.5).astype(BF)
        dq = dq_t[...].T[0:rows]
        dqkv_o[i, :, 0:feats] = dq
        dk_sum = jnp.zeros((8, feats), F32)
        sums = [jnp.zeros((8, feats), F32) for _ in range(heads)]
        for c in chunks(rows):
            kf = k_r[i, c, :].astype(F32)
            dk = 0.0
            for h in range(heads):
                this = dks[h * rows + c.start : h * rows + c.stop, :]
                dk = dk + this * mpre[h : h + 1, :]
                sums[h] = sums[h] + fold(kf * this)
            low = (dk * (1.0 / LOG2E)).astype(BF)
            dqkv_o[i, c, feats : 2 * feats] = low
            dk_sum = dk_sum + fold(low.astype(F32))
        for h in range(heads):
            acc_o[heads + h : heads + h + 1, :] += colsum(sums[h])
        acc_o[2 * heads + 8 : 2 * heads + 9, :] += colsum(dq.astype(F32))
        acc_o[2 * heads + 9 : 2 * heads + 10, :] += colsum(dk_sum)

        pad[patches:, :] = jnp.zeros((rows - patches, feats), F32)
        pad[0:patches, :] = tok[i].astype(F32)
        da1[...] = nt(dqkv_o[i], wqkv[...])
        gain = row(n1g)
        sums = [jnp.zeros((8, feats), F32) for _ in range(2)]
        for c in chunks(rows):
            n, r = normalized(pad[c, :])
            cot = da1[c, :]
            grad = dx1[i, c, :] + norm_back(cot, n, r, gain)
            sums = [sums[0] + fold(cot * n), sums[1] + fold(cot)]
            if c.stop <= patches:
                in_v[i - first, c, :] = grad
            else:
                in_v[i - first, c.start : patches, :] = grad[0 : patches - c.start]
        for j in range(2):
            acc_o[2 * heads + 11 + j : 2 * heads + 12 + j, :] += colsum(sums[j])
        in_copy(i).start()

    @pl.loop(first, first + share)
    def _(i):
        in_copy(i).wait()


def qkv_grad_kernel(heads, dqkv, *refs):
    accs = refs[:-8]
    a1, acc_mlp, b1_first, b1_rest, keep, send, small, grads = refs[-8:]
    feats = a1.shape[1]
    count = 2 * keep.shape[0]
    size = 3 * feats // count
    acc = accs[0][...]
    for other in accs[1:]:
        acc = acc + other[...]
    small[...] = jnp.zeros_like(small)
    small[0:2, :] = acc[2 * heads + 11 : 2 * heads + 13]
    small[2:8, :] = acc_mlp[0:6, :]
    small[8:11, :] = acc[2 * heads + 8 : 2 * heads + 11]
    head_dim = feats // heads
    lanes = 2 * heads * heads
    gather = (
        head_of_lane((feats, lanes), 0, head_dim)
        == lax.broadcasted_iota(jnp.int32, (feats, lanes), 1) % heads
    ).astype(F32)
    sums = exact(acc[0 : 2 * heads + 8], gather, ((1,), (0,)))
    place = head_of_lane((2 * heads, lanes), 1, heads) == lax.broadcasted_iota(
        jnp.int32, (2 * heads, lanes), 0
    )
    small[11:12, 0:lanes] = colsum(jnp.where(place, sums[0 : 2 * heads], 0.0))
    small[11:12, lanes : 2 * lanes] = sums[2 * heads : 2 * heads + 1]
    m_idx = lax.axis_index("mp")
    for c, ref in enumerate((b1_first, b1_first, b1_rest, b1_rest)):
        place = 12 + jnp.bitwise_xor(m_idx, c)
        small[pl.ds(place, 1), :] = ref[:, (c % 2) * feats : (c % 2 + 1) * feats]
    low = small[...].astype(BF)
    outs = (keep, send)

    grads[...] = tn(a1[...], dqkv[...]).astype(BF).T

    def put(which, place, b):
        outs[which][place, 0:size, :] = grads[b * size : (b + 1) * size, :]
        outs[which][place, size : size + 16, :] = low
        if outs[which].shape[1] > size + 16:
            outs[which][place, size + 16 :, :] = jnp.zeros_like(outs[which][place, size + 16 :, :])

    store_blocks(count, put)


def final_kernel(heads, size, many, mine, proj_own, *refs):
    got = refs[:many]
    mlp_mine, got_z = refs[many], refs[1 + many : 1 + 2 * many]
    qkv_o, qkvb_o, pre_o, post_o, postb_o, b1_o, *vecs_o, fc1_o, fc2_o, proj_o, held = refs[-18:]
    block, feats = fc1_o.shape
    for place, out in enumerate((fc1_o, fc2_o)):
        rows = slice(place * block, (place + 1) * block)
        out[...] = mlp_mine[rows, :] + sum(g[rows, :].astype(F32) for g in got_z)
    d_idx = lax.axis_index("dp")
    m_idx = lax.axis_index("mp")
    total = mine[...]
    held[m_idx] = proj_own[...].astype(F32)
    for j, part in enumerate(got):
        value = part[...].astype(F32)
        total = total + value[0 : size + 16]
        held[jnp.bitwise_xor(m_idx, j + 1)] = value[size + 16 :]
    proj_o[...] = held[...].reshape(-1, feats)[0:block]
    qkv_o[...] = total[0:size]
    small = total[size : size + 16]

    def own(value, width, index):
        lanes = value.shape[1]
        return pltpu.roll(value, lax.rem(lanes - index * width, lanes), axis=1)[:, 0:width]

    width = vecs_o[0].shape[1]
    vecs = own(small[0:8], width, d_idx)
    for j, ref in enumerate(vecs_o):
        ref[...] = vecs[j : j + 1]
    flat = jnp.concatenate([small[8 + j : 9 + j] for j in range(3)], axis=1)
    qkvb_o[...] = own(jnp.broadcast_to(flat, (8, 3 * feats)), qkvb_o.shape[1], d_idx)[0:1]
    b1 = own(small[8:16], b1_o.shape[1], d_idx)[4:8]
    pick = lax.broadcasted_iota(jnp.int32, b1.shape, 0) == m_idx
    b1_o[...] = colsum(jnp.where(pick, b1, 0.0))
    mix = small[11:12]
    hh = heads * heads
    line = lax.broadcasted_iota(jnp.int32, (heads, hh), 0)
    lane = lax.broadcasted_iota(jnp.int32, (heads, hh), 1)
    fold = (
        lax.broadcasted_iota(jnp.int32, (hh, heads), 0) % heads
        == lax.broadcasted_iota(jnp.int32, (hh, heads), 1)
    ).astype(F32)
    head_dim = feats // heads

    def square(values):
        return exact(jnp.where(lane // heads == line, values, 0.0), fold, ((1,), (0,)))

    post_o[...] = square(mix[:, 0:hh]).T
    pre_o[...] = square(mix[:, hh : 2 * hh]) * (head_dim**-0.5)
    postb_o[...] = mix[:, 2 * hh : 2 * hh + heads]


def whole(shape):
    return pl.BlockSpec(shape, lambda i: (0,) * len(shape))


def each(shape, first=0, many=1):
    return pl.BlockSpec((many,) + shape[1:], lambda i: (i + first,) + (0,) * (len(shape) - 1))


SCALARS = pl.BlockSpec(memory_space=pltpu.SMEM)
IN_VMEM = pl.BlockSpec(memory_space=pltpu.VMEM)
IN_HBM = pl.BlockSpec(memory_space=pltpu.HBM)


def kept(a):
    return pltpu.with_memory_space_constraint(a, pltpu.HBM)


def sds(shape, dtype):
    return jax.ShapeDtypeStruct(shape, dtype)


def call(
    kernel, grid, ins, in_specs, outs, out_specs, scratch=(), flops=0, name=None, aliases=None,
    limit=VMEM_LIMIT,
):
    size = lambda a: a.size * a.dtype.itemsize
    return pl.pallas_call(
        kernel,
        grid=grid,
        in_specs=in_specs,
        out_specs=out_specs,
        out_shape=outs,
        scratch_shapes=scratch,
        input_output_aliases=aliases or {},
        compiler_params=pltpu.CompilerParams(vmem_limit_bytes=limit),
        cost_estimate=pl.CostEstimate(
            flops=flops,
            bytes_accessed=sum(size(a) for a in ins) + sum(size(a) for a in outs),
            transcendentals=0,
        ),
        name=name,
    )(*ins)


def xor_perm(count, mask):
    return [(j, j ^ mask) for j in range(count)]


def dp_hops(dp):
    bits = dp.bit_length() - 1
    groups = []
    at = 1
    while at < bits:
        groups.append((at, min(2, bits - at)))
        at += groups[-1][1]
    return groups


def dp_scatter(value, dp):
    for at, many in dp_hops(dp):
        value = value.reshape((-1, 1 << many) + value.shape[1:])
        got = [
            lax.ppermute(value[:, j].astype(BF), "dp", xor_perm(dp, j << at))
            for j in range(1, 1 << many)
        ]
        value = value[:, 0] + sum(g.astype(F32) for g in got)
    return value.reshape(value.shape[-2:])


def per_device(
    dp, mp,
    tokens_in, image_counts, norm1_gain, norm1_bias, qkv_weight, qkv_bias,
    mix_pre, mix_post, mix_post_bias, proj_weight, proj_bias, gamma1,
    norm2_gain, norm2_bias, fc1_weight, fc1_bias, fc2_weight, fc2_bias, gamma2, out_grad,
):
    images, patches, feats = tokens_in.shape
    heads = mix_pre.shape[0]
    rows = -(-patches // 16) * 16
    slots = -(-patches // 128) * 128
    hidden = fc1_weight.shape[1]
    tok_rows = (images, rows, feats)
    slot_rows = (images, slots, feats)
    prob_shape = (images, heads, rows, slots)
    mix_shape = (heads, feats)
    operands = [
        tokens_in, out_grad, norm1_gain, norm1_bias, qkv_bias, mix_pre, mix_post,
        mix_post_bias, proj_bias, gamma1, norm2_gain, norm2_bias, qkv_weight, proj_weight,
    ]

    ins = [kept(a) for a in [fc1_weight, fc2_weight, fc1_bias] + operands]
    outs = [sds((feats + 16, hidden), BF)] + [sds(a.shape, a.dtype) for a in operands]
    other, *held = call(
        pack_kernel,
        (),
        ins,
        [IN_HBM] * len(ins),
        outs,
        [IN_VMEM] * len(outs),
        [pltpu.VMEM(fc1_bias.shape, F32), pltpu.SemaphoreType.DMA((2 + len(operands),))],
        name="pack",
    )
    near = [lax.ppermute(other, "mp", xor_perm(mp, j)) for j in (1, 2)]

    shares = [images - 1, 1] if images > 1 else [images]
    carried = []
    for s, share in enumerate(shares):
        first = sum(shares[:s])
        ins = [image_counts, mix_post, mix_post_bias] + held
        outs = call(
            functools.partial(attn_fwd_kernel, first, share),
            (),
            ins + carried,
            [SCALARS] * 3
            + [IN_VMEM] * 14
            + [pl.BlockSpec(memory_space=pl.ANY)] * len(carried),
            [
                sds(tok_rows, BF), sds(slot_rows, BF), sds(tok_rows, BF), sds(tok_rows, BF),
                sds(prob_shape, BF), sds(tok_rows, BF), sds(tok_rows, F32), sds(tok_rows, F32),
                sds(tok_rows, BF), sds(tok_rows, BF), sds(mix_shape, F32), sds(mix_shape, F32),
                sds((1, feats), F32),
            ],
            [IN_VMEM] * 13,
            [
                pltpu.VMEM((rows, feats), F32), pltpu.VMEM((heads * rows, 2 * feats), BF),
                pltpu.VMEM((feats, slots), BF), pltpu.VMEM((heads * rows, slots), BF),
                pltpu.VMEM((rows, 3 * feats), F32), pltpu.VMEM((heads * rows, slots), F32),
                pltpu.VMEM((heads, feats, slots), F32),
            ],
            flops=share * 15 * 10**8,
            name="attn_fwd",
            aliases={len(ins) + j: j for j in range(10)} if carried else None,
        )
        carried, (mpre, mpost, mixb) = list(outs[:10]), outs[10:]
        if s == 0:
            near, carried[0] = lax.optimization_barrier((near, carried[0]))
            last = lax.ppermute(near[1], "mp", xor_perm(mp, 1))
            near = jnp.stack(near)
            far = lax.ppermute(near, "dp", xor_perm(dp, 1))
    a1, q, k, v, prob, o, x1, u, a2, dy = carried
    far, a2 = lax.optimization_barrier((far, a2))

    block = feats // dp
    total = images * rows
    flat = (total, feats)
    a2, dy, x1, u, o = (a.reshape(flat) for a in (a2, dy, x1, u, o))
    ins = [a2, dy, gamma2, fc1_weight, fc1_bias, fc2_weight, near, far]
    wide = 2 * hidden
    grad_shape = (2, wide, feats)
    f0, da20, hids, dzs, dfs = call(
        mlp_first_kernel,
        (),
        ins,
        [IN_VMEM] * len(ins),
        [
            sds(flat, F32), sds(flat, F32), sds((total, wide), BF), sds((total, wide), BF),
            sds(flat, BF),
        ],
        [IN_VMEM] * 5,
        [
            pltpu.VMEM((feats, wide), BF), pltpu.VMEM((wide, feats), BF),
            pltpu.VMEM((1, wide), F32),
            pltpu.VMEM((2, total // 3, 256), F32), pltpu.VMEM((2, total // 3, 256), F32),
        ],
        flops=images * 5 * 10**8,
        name="mlp_first",
    )

    last, f0 = lax.optimization_barrier((last, f0))
    far_last = lax.ppermute(last, "dp", xor_perm(dp, 1))
    ins = [a2, hids, dzs, dfs]
    grads0, b1_0, a2t, dft = call(
        mlp_grad_kernel,
        (),
        ins,
        [IN_VMEM] * 4,
        [
            sds(grad_shape, BF), sds((1, wide), F32), sds((feats + 16, total), BF),
            sds((feats, total), BF),
        ],
        [IN_VMEM] * 4,
        flops=images * 3 * 10**8,
        name="mlp_grad",
    )

    grad_rows = 9 * block
    half_shape = (dp // 2, grad_rows, feats)
    ins = [
        image_counts, a2, dy, dfs, x1, u, o, f0, da20, near, far, last, far_last, grads0, a2t, dft,
        proj_weight, gamma1,
        norm2_gain, fc2_bias, gamma2,
    ]
    layer_out, dx1, do, keep, send, b1_1, acc_mlp = call(
        mlp_rest_kernel,
        (),
        ins,
        [SCALARS] + [IN_VMEM] * (len(ins) - 1),
        [
            sds(tokens_in.shape, BF), sds(flat, F32), sds(slot_rows, BF), sds(half_shape, BF),
            sds(half_shape, BF), sds((1, wide), F32), sds((8, feats), F32),
        ],
        [IN_HBM] + [IN_VMEM] * 6,
        [
            pltpu.VMEM((feats, wide), BF), pltpu.VMEM((wide, feats), BF),
            pltpu.VMEM((1, wide), F32), pltpu.VMEM((total, wide), BF),
            pltpu.VMEM((total, wide), BF),
            pltpu.VMEM((2, total // 3, 256), F32), pltpu.VMEM((2, total // 3, 256), F32),
            pltpu.VMEM(flat, F32), pltpu.VMEM(flat, F32), pltpu.VMEM(flat, BF),
            pltpu.VMEM((wide, feats), BF), pltpu.VMEM((feats, wide), BF),
            pltpu.VMEM((feats, feats), BF), pltpu.VMEM(tokens_in.shape, BF),
            pltpu.SemaphoreType.DMA((images,)),
        ],
        flops=images * 9 * 10**8,
        name="mlp_rest",
    )
    got = lax.ppermute(send, "dp", xor_perm(dp, 1))
    dx1 = dx1.reshape(tok_rows)

    shares = [1, images - 1] if images > 1 else [1]
    dqkv_shape = (images, rows, 3 * feats)
    carried, accs = [], []
    for s, share in enumerate(shares):
        first = sum(shares[:s])
        ins = [mix_pre, do, q, k, v, prob, dx1, tokens_in, mpre, mpost, mixb, qkv_weight, norm1_gain]
        *carried, acc = call(
            functools.partial(attn_bwd_kernel, first, share),
            (),
            ins + carried,
            [SCALARS]
            + [IN_VMEM] * (len(ins) - 1)
            + [pl.BlockSpec(memory_space=pl.ANY)] * len(carried),
            [sds(dqkv_shape, BF), sds(tokens_in.shape, F32), sds((2 * heads + 16, feats), F32)],
            [IN_VMEM, IN_HBM, IN_VMEM],
            [
                pltpu.VMEM((heads * rows, feats), BF), pltpu.VMEM((heads * rows, slots), BF),
                pltpu.VMEM((feats, slots), BF), pltpu.VMEM((heads * rows, slots), F32),
                pltpu.VMEM((heads * rows, feats), F32), pltpu.VMEM((heads * rows, feats), F32),
                pltpu.VMEM((heads, feats, slots), F32), pltpu.VMEM((rows, feats), F32),
                pltpu.VMEM((rows, feats), F32), pltpu.VMEM((share, patches, feats), F32),
                pltpu.SemaphoreType.DMA((share,)),
            ],
            flops=share * 20 * 10**8,
            name="attn_bwd",
            aliases={len(ins): 0, len(ins) + 1: 1} if carried else None,
        )
        accs.append(acc)
        if s == 0:
            (keep, got), acc = lax.optimization_barrier(((keep, got), acc))
            mine = dp_scatter(keep.astype(F32) + got.astype(F32), dp)
            accs[0], do = lax.optimization_barrier((acc, do))
    dqkv, in_grad = carried
    mine, dqkv = lax.optimization_barrier((mine, dqkv))
    mlp_mine = mine
    low = mine.astype(BF)
    m_idx = lax.axis_index("mp")
    share_rows = -(-block // (16 * mp)) * 16
    proj = jnp.pad(mine[8 * block :], ((0, mp * share_rows - block), (0, 0)))

    def proj_share(j):
        return lax.dynamic_slice_in_dim(proj, jnp.bitwise_xor(m_idx, j) * share_rows, share_rows)

    got_z = [
        lax.ppermute(
            jnp.concatenate([low[2 * j * block : 2 * (j + 1) * block], proj_share(j).astype(BF)]),
            "mp",
            xor_perm(mp, j),
        )
        for j in range(1, mp)
    ]

    q_block = 3 * feats // dp
    half_shape = (dp // 2, q_block + 16, feats)
    ins = [dqkv.reshape(total, 3 * feats)] + accs + [a1.reshape(flat), acc_mlp, b1_0, b1_1]
    keep, send = call(
        functools.partial(qkv_grad_kernel, heads),
        (),
        ins,
        [IN_VMEM] * len(ins),
        [sds(half_shape, BF), sds(half_shape, BF)],
        [IN_VMEM] * 2,
        [pltpu.VMEM((16, feats), F32), pltpu.VMEM((3 * feats, feats), BF)],
        flops=11 * 10**8,
        name="qkv_grad",
    )
    got = lax.ppermute(send, "dp", xor_perm(dp, 1))
    mine = dp_scatter(keep.astype(F32) + got.astype(F32), dp)
    mine, got_z = lax.optimization_barrier((mine, got_z))

    proj_own = (proj_share(0) + sum(g[2 * block :].astype(F32) for g in got_z)).astype(BF)
    payload = jnp.concatenate([mine.astype(BF), proj_own])
    got = [lax.ppermute(payload, "mp", xor_perm(mp, j)) for j in range(1, mp)]
    b1_size = hidden // dp
    ins = [mine, proj_own] + got + [mlp_mine] + got_z
    outs = [
        sds((q_block, feats), F32), sds((1, q_block), F32), sds((heads, heads), F32),
        sds((heads, heads), F32), sds((1, heads), F32), sds((1, b1_size), F32),
    ] + [sds((1, block), F32)] * 8 + [sds((block, feats), F32)] * 3
    qkvw, qkvb, pre, post, postb, b1g, *vecs, fc1g, fc2g, projg = call(
        functools.partial(final_kernel, heads, q_block, mp - 1),
        (),
        ins,
        [IN_VMEM] * len(ins),
        outs,
        [IN_VMEM] * len(outs),
        [pltpu.VMEM((mp, share_rows, feats), F32)],
        name="final",
    )
    vecs = [a.reshape(-1) for a in vecs]
    return (
        layer_out,
        in_grad,
        vecs[0],
        vecs[1],
        qkvw.T,
        qkvb.reshape(-1),
        pre,
        post,
        postb.reshape(-1),
        projg.T,
        vecs[2],
        vecs[3],
        vecs[4],
        vecs[5],
        fc1g.T,
        b1g.reshape(-1),
        fc2g.T,
        vecs[6],
        vecs[7],
    )


def solution(mesh):
    tokens = P(("dp", "mp"), None, None)
    placed = (
        (tokens, P("dp")) + (P(),) * 12 + (P(None, "mp"), P("mp"), P("mp", None), P(), P(), tokens)
    )
    return jax.shard_map(
        functools.partial(per_device, mesh.shape["dp"], mesh.shape["mp"]),
        mesh=mesh,
        in_specs=placed,
        out_specs=(
            tokens, tokens, P("dp"), P("dp"), P(None, "dp"), P("dp"), P(), P(), P(),
            P(None, "dp"), P("dp"), P("dp"), P("dp"), P("dp"), P(None, ("mp", "dp")),
            P(("mp", "dp")), P("mp", "dp"), P("dp"), P("dp"),
        ),
        check_vma=False,
    )
```

```python
import functools

import jax
import jax.numpy as jnp
from jax import lax
from jax.experimental import pallas as pl
from jax.experimental.pallas import tpu as pltpu
from jax.sharding import PartitionSpec as P

BF = jnp.bfloat16
F32 = jnp.float32
LOG2E = 1.4426950408889634
EPS = 1e-06
VMEM_LIMIT = 20 * 1024 * 1024


def nn(a, b):
    return lax.dot_general(a, b, (((1,), (0,)), ((), ())), preferred_element_type=F32)


def nt(a, b):
    return lax.dot_general(a, b, (((1,), (1,)), ((), ())), preferred_element_type=F32)


def tn(a, b):
    return lax.dot_general(a, b, (((0,), (0,)), ((), ())), preferred_element_type=F32)


def exact(a, b, dims):
    return lax.dot_general(
        a, b, (dims, ((), ())), precision=lax.Precision.HIGHEST, preferred_element_type=F32
    )


def normalized(x):
    mean = jnp.mean(x, axis=-1, keepdims=True)
    c = x - mean
    r = lax.rsqrt(jnp.mean(c * c, axis=-1, keepdims=True) + EPS)
    return c * r, r


def norm_back(cot, n, r, gain):
    cg = cot * gain
    return r * (
        cg
        - jnp.mean(cg, axis=-1, keepdims=True)
        - n * jnp.mean(cg * n, axis=-1, keepdims=True)
    )


def colsum(x):
    return jnp.sum(x, axis=0, keepdims=True)


def split(x):
    hi = x.astype(BF)
    return jnp.concatenate([hi, (x - hi.astype(F32)).astype(BF)], axis=1)


def row(ref):
    return ref[...].reshape(1, ref.shape[0])


def gelu_parts(z):
    e = jnp.exp2(z * z * (-0.5 * LOG2E))
    t = pl.reciprocal(1.0 + jnp.abs(z) * (0.3275911 * 0.7071067811865476), approx=True)
    poly = t * (
        0.5 * 0.254829592
        + t
        * (
            0.5 * -0.284496736
            + t * (0.5 * 1.421413741 + t * (0.5 * -1.453152027 + t * (0.5 * 1.061405429)))
        )
    )
    tail = poly * e
    phi = jnp.where(z >= 0, 1.0 - tail, tail)
    return phi, phi + z * e * 0.3989422804014327


def head_of_lane(shape, axis, head_dim):
    return lax.broadcasted_iota(jnp.int32, shape, axis) // head_dim


def chunks(count, size=16):
    return [slice(at, at + size) for at in range(0, count, size)]


def fold(x):
    return sum(x[at : at + 8] for at in range(8, x.shape[0], 8)) + x[0:8]


def pack_kernel(w1, w2, b1, other, b1_v, sems):
    feats = w1.shape[0]
    core = jnp.bitwise_and(lax.axis_index("dp"), 1)
    bias_copy = pltpu.make_async_copy(b1, b1_v, sems.at[0])
    own = [pltpu.make_async_copy(w, other.at[0:feats], sems.at[1]) for w in (w1, w2)]
    bias_copy.start()
    for j in range(2):
        pl.when(core == j)(own[j].start)
    bias_copy.wait()
    rest = row(b1_v)
    place = lax.broadcasted_iota(jnp.int32, (16, feats), 0)
    bias = jnp.zeros((16, feats), F32)
    for j in range(3):
        term = rest.astype(BF).astype(F32)
        bias = jnp.where(place == j, term, bias)
        rest = rest - term
    other[feats:, :] = bias.astype(BF)
    for j in range(2):
        pl.when(core == j)(own[j].wait)


def load_kernel(*refs):
    many = (len(refs) - 2) // 2
    sources, held, sems = refs[:many], refs[many + 1 : -1], refs[-1]
    copies = [pltpu.make_async_copy(sources[j], held[j], sems.at[j]) for j in range(many)]
    for copy in copies:
        copy.start()
    for copy in copies:
        copy.wait()


def attn_fwd_kernel(first, share, *refs):
    counts, post_s, postb_s, tok, og, n1g, n1b, qkvb, pre, post, postb, projb = refs[:12]
    gamma1, n2g, n2b, wqkv, wproj = refs[12:17]
    a1_o, q_o, k_o, v_o, p_o, o_o, x1_o, u_o, a2_o, dy_o, mpre, mpost, mixb = refs[-20:-7]
    pad, kk, attended_t, probs, wide, logits, mixed = refs[-7:]
    images, patches, feats = tok.shape
    rows = pad.shape[0]
    heads = mpre.shape[0]
    head_dim = feats // heads
    slots = q_o.shape[1]

    spread = (
        head_of_lane((heads, feats), 1, head_dim)
        == lax.broadcasted_iota(jnp.int32, (heads, feats), 0)
    ).astype(F32)
    mpre[...] = exact(pre[...], spread, ((1,), (0,))) * (head_dim**-0.5 * LOG2E)
    mpost[...] = exact(post[...], spread, ((0,), (0,)))
    mixb[...] = exact(row(postb), spread, ((1,), (0,)))
    mix_top = jnp.max(mpre[...] * mpre[...])

    @pl.loop(first, first + share)
    def _(i):
        pad[patches:, :] = jnp.zeros((rows - patches, feats), F32)
        live = (lax.axis_index("mp") * images + i < counts[0]).astype(F32)
        pad[0:patches, :] = og[i].astype(F32) * live
        dy_o[i] = pad[...].astype(BF)
        pad[0:patches, :] = tok[i].astype(F32)
        gain, shift = row(n1g), row(n1b)
        for c in chunks(rows):
            n, _ = normalized(pad[c, :])
            a1_o[i, c, :] = (n * gain + shift).astype(BF)
        wide[...] = nn(a1_o[i], wqkv[...])
        bias = row(qkvb)
        q_o[i, rows:] = jnp.zeros((slots - rows, feats), BF)
        q_top = k_top = jnp.zeros((16, 1), F32)
        for c in chunks(rows):
            q, k, v = (
                wide[c, j * feats : (j + 1) * feats] + bias[:, j * feats : (j + 1) * feats]
                for j in range(3)
            )
            q_o[i, c, :] = q.astype(BF)
            v_o[i, c, :] = v.astype(BF)
            k_o[i, c, :] = k.astype(BF)
            q_top = jnp.maximum(q_top, jnp.sum(q * q, axis=-1, keepdims=True))
            k_top = jnp.maximum(k_top, jnp.sum(k * k, axis=-1, keepdims=True))
        vt = v_o[i].T
        many = heads // 2
        half = many * rows
        tail = patches // 8 * 8
        inside = lax.broadcasted_iota(jnp.int32, (rows - tail, 128), 0) < patches - tail
        real = (lax.broadcasted_iota(jnp.int32, (rows, 128), 0) < patches).astype(BF)
        start = nn(vt, real)

        small = mix_top * jnp.max(q_top) * jnp.max(k_top) <= 512.0**2

        def scaled_keys(g, c):
            return k_o[i, c, :].astype(F32) * mpre[g : g + 1, :]

        def places(g, c):
            return slice(g * rows + c.start, g * rows + c.stop)

        @pl.when(small)
        def _():
            for c in chunks(rows):
                for g in range(heads):
                    kk[places(g, c), 0:feats] = scaled_keys(g, c).astype(BF)
            for s in range(2):
                part = slice(s * half, (s + 1) * half)
                logits[part, :] = nt(kk[part, 0:feats], q_o[i])

        @pl.when(jnp.logical_not(small))
        def _():
            for c in chunks(rows):
                for g in range(heads):
                    scaled = scaled_keys(g, c)
                    hi = scaled.astype(BF)
                    kk[places(g, c), 0:feats] = hi
                    kk[places(g, c), feats:] = (scaled - hi.astype(F32)).astype(BF)
            q2 = jnp.concatenate([q_o[i], q_o[i]], axis=1)
            for s in range(2):
                part = slice(s * half, (s + 1) * half)
                logits[part, :] = nt(kk[part, :], q2)

        for g in range(heads):
            for lane in range(0, slots, 128):
                x = logits[g * rows : (g + 1) * rows, lane : lane + 128]
                x = jnp.concatenate([x[0:tail], jnp.where(inside, x[tail:], -1e30)], axis=0)
                e = jnp.exp2(x - jnp.max(x, axis=0, keepdims=True))
                inv = 1.0 / jnp.sum(e, axis=0, keepdims=True)
                p = (e * inv).astype(BF)
                probs[g * rows : (g + 1) * rows, lane : lane + 128] = p
                p_o[i, g, :, lane : lane + 128] = p
            mixed[g] = nn(vt, probs[g * rows : (g + 1) * rows, :])
        for c in chunks(feats):
            g = c.start // head_dim
            first = start[c] * postb_s[g]
            for lane in range(0, slots, 128):
                total = first
                for h in range(heads):
                    total = total + mixed[h, c, lane : lane + 128] * post_s[g, h]
                attended_t[c, lane : lane + 128] = total.astype(BF)
        o_o[i] = attended_t[...].T[0:rows]
        wide[:, 0:feats] = nn(o_o[i], wproj[...])
        bias, scale, gain, shift = row(projb), row(gamma1), row(n2g), row(n2b)
        for c in chunks(rows):
            u = wide[c, 0:feats] + bias
            x1 = pad[c, :] + scale * u
            u_o[i, c, :] = u
            x1_o[i, c, :] = x1
            n, _ = normalized(x1)
            a2_o[i, c, :] = (n * gain + shift).astype(BF)


def store_blocks(count, put):
    mine = lax.axis_index("dp")
    for core in range(2):

        @pl.when(jnp.bitwise_and(mine, 1) == core)
        def _(core=core):
            for b in range(count):
                place = jnp.bitwise_xor(jnp.int32(b >> 1), jnp.right_shift(mine, 1))
                put((b ^ core) & 1, place, b)


def mlp_units(a2, dfs, w1, b1, w2, hids, dzs, zs, ghs, units, store, use):
    size = a2.shape[0] // units
    width = w2.shape[0]
    lanes = zs.shape[2]
    places = [slice(u * size, (u + 1) * size) for u in range(units)]
    blocks = [(u, at) for u in range(units) for at in range(0, width, lanes)]

    def products(j):
        u, at = blocks[j]
        part = slice(at, at + lanes)
        zs[j % 2] = nn(a2[places[u], :], w1[:, part])
        ghs[j % 2] = nt(dfs[places[u], :], w2[part, :])

    def activation(j):
        u, at = blocks[j]
        part = slice(at, at + lanes)
        bias = b1[:, part]
        for c in chunks(size):
            zc = zs[j % 2, c, :] + bias
            phi, slope = gelu_parts(zc)
            rows = slice(places[u].start + c.start, places[u].start + c.stop)
            hids[rows, part] = (zc * phi).astype(BF)
            dzs[rows, part] = (ghs[j % 2, c, :] * slope).astype(BF)

    def finish(u):
        store(places[u], nn(hids[places[u], :], w2[...]), nt(dzs[places[u], :], w1[...]))

    products(0)
    for j, (u, at) in enumerate(blocks):
        if j + 1 < len(blocks):
            products(j + 1)
        if at == lanes and u > 0:
            finish(u - 1)
        activation(j)
        if at == 2 * lanes and u > 0:
            use(places[u - 1])
    finish(units - 1)
    use(places[units - 1])


def mlp_first_kernel(
    a2, dy, gamma2, w1_own, b1_own, w2_own, near, far,
    f_o, da2_o, hids, dzs, dfs,
    w1, w2, b1, zs, ghs,
):
    total, feats = f_o.shape
    w1[:, 0:feats] = w1_own[...]
    w2[0:feats, :] = w2_own[...]
    for core in range(2):

        @pl.when(jnp.bitwise_and(lax.axis_index("dp"), 1) == core)
        def _(core=core):
            one, two = (near, far) if core == 0 else (far, near)
            w1[:, feats:] = one[0, 0:feats]
            w2[feats:, :] = two[0, 0:feats]

    b1[:, 0:feats] = row(b1_own)
    b1[:, feats:] = colsum(near[0, feats : feats + 16].astype(F32))
    gain = row(gamma2)
    for c in chunks(total):
        dfs[c, :] = (dy[c, :].astype(F32) * gain).astype(BF)

    def store(rows, f, da2):
        f_o[rows, :] = f
        da2_o[rows, :] = da2

    mlp_units(a2, dfs, w1, b1, w2, hids, dzs, zs, ghs, 3, store, lambda rows: None)


def mlp_grad_kernel(a2, hids, dzs, dfs, grads, b1_o, a2t, dft):
    feats = a2.shape[1]
    a2t[0:feats, :] = a2[...].T
    a2t[feats:, :] = jnp.ones((a2t.shape[0] - feats, a2t.shape[1]), BF)
    dft[...] = dfs[...].T
    up = nn(a2t[...], dzs[...])
    b1_o[...] = up[feats : feats + 1]
    grads[0] = up[0:feats].astype(BF).T
    down = nn(dft[...], hids[...]).astype(BF)
    for c in range(2):
        grads[1, c * feats : (c + 1) * feats, :] = down[:, c * feats : (c + 1) * feats]


def mlp_rest_kernel(
    counts, a2, dy, dfs, x1, u, o, f0, da20, near, far, last, far_last, grads, a2t, dft, wproj,
    gamma1, n2g, fc2b, gamma2,
    out_o, dx1_o, do_o, keep, send, b1_o, acc_o,
    w1, w2, b1, hids, dzs, zs, ghs, fs, da2s, dus, ups, downs, projs, out_v, sems,
):
    total, feats = f0.shape
    images, patches = out_o.shape[:2]
    image_rows = total // images
    m_idx = lax.axis_index("mp")
    acc_o[...] = jnp.zeros_like(acc_o)
    b1[:, 0:feats] = colsum(near[1, feats : feats + 16].astype(F32))
    b1[:, feats:] = colsum(last[feats : feats + 16].astype(F32))
    for core in range(2):

        @pl.when(jnp.bitwise_and(lax.axis_index("dp"), 1) == core)
        def _(core=core):
            one, two = (near, far) if core == 0 else (far, near)
            w1[:, 0:feats] = one[1, 0:feats]
            w2[0:feats, :] = two[1, 0:feats]
            one, two = (last, far_last) if core == 0 else (far_last, last)
            w1[:, feats:] = one[0:feats]
            w2[feats:, :] = two[0:feats]

    gain2 = row(gamma2)
    bias, gain, scale = row(fc2b), row(n2g), row(gamma1)

    def out_copy(image):
        return pltpu.make_async_copy(out_v.at[image], out_o.at[image], sems.at[image])

    def store(rows, f, da2):
        fs[rows, :] = f
        da2s[rows, :] = da2

    def use(rows):
        sums = [jnp.zeros((8, feats), F32) for _ in range(6)]
        for c in chunks(rows.stop - rows.start):
            at = slice(rows.start + c.start, rows.start + c.stop)
            fc = fs[at, :] + f0[at, :] + bias
            dac = da2s[at, :] + da20[at, :]
            x1c = x1[at, :]
            dyc = dy[at, :].astype(F32)
            n, r = normalized(x1c)
            dx1 = dyc + norm_back(dac, n, r, gain)
            dx1_o[at, :] = dx1
            du = (dx1 * scale).astype(BF)
            dus[at, :] = du
            image = at.start // image_rows
            first = at.start - image * image_rows
            live = (m_idx * images + image < counts[0]).astype(F32)
            out = ((x1c + gain2 * fc) * live).astype(BF)
            if first + 16 <= patches:
                out_v[image, first : first + 16, :] = out
            else:
                out_v[image, first:patches, :] = out[0 : patches - first]
            terms = (
                du.astype(F32), u[at, :] * dx1, dac * n, dac, dfs[at, :].astype(F32), fc * dyc,
            )
            sums = [s + fold(t) for s, t in zip(sums, terms)]
        for j in range(6):
            acc_o[j : j + 1, :] += colsum(sums[j])
        do = nt(dus[rows, :], wproj[...]).astype(BF)
        for at in range(0, rows.stop - rows.start, image_rows):
            image = (rows.start + at) // image_rows
            out_copy(image).start()
            do_o[image, 0:image_rows] = do[at : at + image_rows]
            do_o[image, image_rows:] = jnp.zeros((do_o.shape[1] - image_rows, feats), BF)

    mlp_units(a2, dfs, w1, b1, w2, hids, dzs, zs, ghs, 3, store, use)
    up = nn(a2t[...], dzs[...])
    b1_o[...] = up[feats : feats + 1]
    ups[...] = up[0:feats].astype(BF).T
    downs[...] = nn(dft[...], hids[...]).astype(BF)
    projs[...] = tn(dus[...], o[...]).astype(BF)
    count = 2 * keep.shape[0]
    size = feats // count
    outs = (keep, send)

    def put(which, place, b):
        out = outs[which]
        for c in range(2):
            part = slice(c * feats, (c + 1) * feats)
            up = slice(c * feats + b * size, c * feats + (b + 1) * size)
            down = slice(b * size, (b + 1) * size)
            pieces = (grads[0, up, :], grads[1, up, :])
            for j, piece in enumerate(pieces):
                out[place, (2 * c + j) * size : (2 * c + j + 1) * size, :] = piece
            pieces = (ups[up, :], downs[down, part])
            for j, piece in enumerate(pieces):
                out[place, (4 + 2 * c + j) * size : (5 + 2 * c + j) * size, :] = piece
        out[place, 8 * size : 9 * size, :] = projs[b * size : (b + 1) * size, :]

    store_blocks(count, put)
    for image in range(images):
        out_copy(image).wait()


def attn_bwd_kernel(first, share, *refs):
    pre_s, do_r, q_r, k_r, v_r, p_r, dx1, tok, mpre, mpost, mixb, wqkv, n1g = refs[:13]
    dqkv_o, in_o, acc_o, vgs, dls, dq_t, dps, dvs, dks, dqs, da1, pad, in_v, sems = refs[-14:]
    slots, feats = do_r.shape[1:]
    patches = tok.shape[1]
    rows = k_r.shape[1]
    heads = mpre.shape[0]
    head_dim = feats // heads
    many = heads // 2
    half = many * rows
    acc_o[...] = jnp.zeros_like(acc_o)

    def in_copy(i):
        return pltpu.make_async_copy(in_v.at[i - first], in_o.at[i], sems.at[i - first])

    @pl.loop(first, first + share)
    def _(i):
        do_sum = jnp.zeros((8, feats), F32)
        for c in chunks(rows):
            vf = v_r[i, c, :].astype(F32)
            do_sum = do_sum + fold(do_r[i, c, :].astype(F32))
            for h in range(heads):
                vgs[h * rows + c.start : h * rows + c.stop, :] = (vf * mpost[h : h + 1, :]).astype(BF)
        do_sum = colsum(do_sum)
        q = q_r[i]
        do = do_r[i]
        kt = k_r[i].T
        parts = [slice(s * half, (s + 1) * half) for s in range(2)]
        for part in parts:
            dps[part, :] = nt(vgs[part, :], do)
        for s, part in enumerate(parts):
            dvs[part, :] = nn(p_r[i, s * many : (s + 1) * many].reshape(half, slots), do)
        for s, part in enumerate(parts):
            for h in range(s * many, (s + 1) * many):
                at = slice(h * rows, (h + 1) * rows)
                for lane in range(0, slots, 128):
                    dp = dps[at, lane : lane + 128]
                    pf = p_r[i, h, :, lane : lane + 128].astype(F32)
                    mean = jnp.sum(dp * pf, axis=0, keepdims=True) / jnp.sum(pf, axis=0, keepdims=True)
                    dls[at, lane : lane + 128] = (pf * (dp - mean)).astype(BF)
                dqs[h] = nn(kt, dls[at, :])
            dks[part, :] = nn(dls[part, :], q)

        bias_row = mixb[...] * do_sum
        v_sum = jnp.zeros((8, feats), F32)
        dv_sum = jnp.zeros((8, feats), F32)
        sums = [jnp.zeros((8, feats), F32) for _ in range(heads)]
        for c in chunks(rows):
            vf = v_r[i, c, :].astype(F32)
            dv = bias_row
            for h in range(heads):
                this = dvs[h * rows + c.start : h * rows + c.stop, :]
                dv = dv + this * mpost[h : h + 1, :]
                sums[h] = sums[h] + fold(vf * this)
            if c.stop > patches:
                inside = lax.broadcasted_iota(jnp.int32, dv.shape, 0) < patches - c.start
                dv = jnp.where(inside, dv, 0.0)
                vf = jnp.where(inside, vf, 0.0)
            low = dv.astype(BF)
            dqkv_o[i, c, 2 * feats :] = low
            dv_sum = dv_sum + fold(low.astype(F32))
            v_sum = v_sum + fold(vf)
        for h in range(heads):
            acc_o[h : h + 1, :] += colsum(sums[h])
        acc_o[2 * heads : 2 * heads + 1, :] += do_sum * colsum(v_sum)
        acc_o[2 * heads + 10 : 2 * heads + 11, :] += colsum(dv_sum)

        for c in chunks(feats):
            g = c.start // head_dim
            for lane in range(0, slots, 128):
                total = 0.0
                for h in range(heads):
                    total = total + dqs[h, c, lane : lane + 128] * pre_s[h, g]
                dq_t[c, lane : lane + 128] = (total * head_dim**-0.5).astype(BF)
        dq = dq_t[...].T[0:rows]
        dqkv_o[i, :, 0:feats] = dq
        dk_sum = jnp.zeros((8, feats), F32)
        sums = [jnp.zeros((8, feats), F32) for _ in range(heads)]
        for c in chunks(rows):
            kf = k_r[i, c, :].astype(F32)
            dk = 0.0
            for h in range(heads):
                this = dks[h * rows + c.start : h * rows + c.stop, :]
                dk = dk + this * mpre[h : h + 1, :]
                sums[h] = sums[h] + fold(kf * this)
            low = (dk * (1.0 / LOG2E)).astype(BF)
            dqkv_o[i, c, feats : 2 * feats] = low
            dk_sum = dk_sum + fold(low.astype(F32))
        for h in range(heads):
            acc_o[heads + h : heads + h + 1, :] += colsum(sums[h])
        acc_o[2 * heads + 8 : 2 * heads + 9, :] += colsum(dq.astype(F32))
        acc_o[2 * heads + 9 : 2 * heads + 10, :] += colsum(dk_sum)

        pad[patches:, :] = jnp.zeros((rows - patches, feats), F32)
        pad[0:patches, :] = tok[i].astype(F32)
        da1[...] = nt(dqkv_o[i], wqkv[...])
        gain = row(n1g)
        sums = [jnp.zeros((8, feats), F32) for _ in range(2)]
        for c in chunks(rows):
            n, r = normalized(pad[c, :])
            cot = da1[c, :]
            grad = dx1[i, c, :] + norm_back(cot, n, r, gain)
            sums = [sums[0] + fold(cot * n), sums[1] + fold(cot)]
            if c.stop <= patches:
                in_v[i - first, c, :] = grad
            else:
                in_v[i - first, c.start : patches, :] = grad[0 : patches - c.start]
        for j in range(2):
            acc_o[2 * heads + 11 + j : 2 * heads + 12 + j, :] += colsum(sums[j])
        in_copy(i).start()

    @pl.loop(first, first + share)
    def _(i):
        in_copy(i).wait()


def qkv_grad_kernel(heads, dqkv, *refs):
    accs = refs[:-8]
    a1, acc_mlp, b1_first, b1_rest, keep, send, small, grads = refs[-8:]
    feats = a1.shape[1]
    count = 2 * keep.shape[0]
    size = 3 * feats // count
    acc = accs[0][...]
    for other in accs[1:]:
        acc = acc + other[...]
    small[...] = jnp.zeros_like(small)
    small[0:2, :] = acc[2 * heads + 11 : 2 * heads + 13]
    small[2:8, :] = acc_mlp[0:6, :]
    small[8:11, :] = acc[2 * heads + 8 : 2 * heads + 11]
    head_dim = feats // heads
    lanes = 2 * heads * heads
    gather = (
        head_of_lane((feats, lanes), 0, head_dim)
        == lax.broadcasted_iota(jnp.int32, (feats, lanes), 1) % heads
    ).astype(F32)
    sums = exact(acc[0 : 2 * heads + 8], gather, ((1,), (0,)))
    place = head_of_lane((2 * heads, lanes), 1, heads) == lax.broadcasted_iota(
        jnp.int32, (2 * heads, lanes), 0
    )
    small[11:12, 0:lanes] = colsum(jnp.where(place, sums[0 : 2 * heads], 0.0))
    small[11:12, lanes : 2 * lanes] = sums[2 * heads : 2 * heads + 1]
    m_idx = lax.axis_index("mp")
    for c, ref in enumerate((b1_first, b1_first, b1_rest, b1_rest)):
        place = 12 + jnp.bitwise_xor(m_idx, c)
        small[pl.ds(place, 1), :] = ref[:, (c % 2) * feats : (c % 2 + 1) * feats]
    low = small[...].astype(BF)
    outs = (keep, send)

    grads[...] = tn(a1[...], dqkv[...]).astype(BF).T

    def put(which, place, b):
        outs[which][place, 0:size, :] = grads[b * size : (b + 1) * size, :]
        outs[which][place, size : size + 16, :] = low
        if outs[which].shape[1] > size + 16:
            outs[which][place, size + 16 :, :] = jnp.zeros_like(outs[which][place, size + 16 :, :])

    store_blocks(count, put)


def final_kernel(heads, size, many, mine, proj_own, *refs):
    got = refs[:many]
    mlp_mine, got_z = refs[many], refs[1 + many : 1 + 2 * many]
    qkv_o, qkvb_o, pre_o, post_o, postb_o, b1_o, *vecs_o, fc1_o, fc2_o, proj_o, held = refs[-18:]
    block, feats = fc1_o.shape
    for place, out in enumerate((fc1_o, fc2_o)):
        rows = slice(place * block, (place + 1) * block)
        out[...] = mlp_mine[rows, :] + sum(g[rows, :].astype(F32) for g in got_z)
    d_idx = lax.axis_index("dp")
    m_idx = lax.axis_index("mp")
    total = mine[...]
    held[m_idx] = proj_own[...].astype(F32)
    for j, part in enumerate(got):
        value = part[...].astype(F32)
        total = total + value[0 : size + 16]
        held[jnp.bitwise_xor(m_idx, j + 1)] = value[size + 16 :]
    proj_o[...] = held[...].reshape(-1, feats)[0:block]
    qkv_o[...] = total[0:size]
    small = total[size : size + 16]

    def own(value, width, index):
        lanes = value.shape[1]
        return pltpu.roll(value, lax.rem(lanes - index * width, lanes), axis=1)[:, 0:width]

    width = vecs_o[0].shape[1]
    vecs = own(small[0:8], width, d_idx)
    for j, ref in enumerate(vecs_o):
        ref[...] = vecs[j : j + 1]
    flat = jnp.concatenate([small[8 + j : 9 + j] for j in range(3)], axis=1)
    qkvb_o[...] = own(jnp.broadcast_to(flat, (8, 3 * feats)), qkvb_o.shape[1], d_idx)[0:1]
    b1 = own(small[8:16], b1_o.shape[1], d_idx)[4:8]
    pick = lax.broadcasted_iota(jnp.int32, b1.shape, 0) == m_idx
    b1_o[...] = colsum(jnp.where(pick, b1, 0.0))
    mix = small[11:12]
    hh = heads * heads
    line = lax.broadcasted_iota(jnp.int32, (heads, hh), 0)
    lane = lax.broadcasted_iota(jnp.int32, (heads, hh), 1)
    fold = (
        lax.broadcasted_iota(jnp.int32, (hh, heads), 0) % heads
        == lax.broadcasted_iota(jnp.int32, (hh, heads), 1)
    ).astype(F32)
    head_dim = feats // heads

    def square(values):
        return exact(jnp.where(lane // heads == line, values, 0.0), fold, ((1,), (0,)))

    post_o[...] = square(mix[:, 0:hh]).T
    pre_o[...] = square(mix[:, hh : 2 * hh]) * (head_dim**-0.5)
    postb_o[...] = mix[:, 2 * hh : 2 * hh + heads]


def whole(shape):
    return pl.BlockSpec(shape, lambda i: (0,) * len(shape))


def each(shape, first=0, many=1):
    return pl.BlockSpec((many,) + shape[1:], lambda i: (i + first,) + (0,) * (len(shape) - 1))


SCALARS = pl.BlockSpec(memory_space=pltpu.SMEM)
IN_VMEM = pl.BlockSpec(memory_space=pltpu.VMEM)
IN_HBM = pl.BlockSpec(memory_space=pltpu.HBM)


def kept(a):
    return pltpu.with_memory_space_constraint(a, pltpu.HBM)


def sds(shape, dtype):
    return jax.ShapeDtypeStruct(shape, dtype)


def call(
    kernel, grid, ins, in_specs, outs, out_specs, scratch=(), flops=0, name=None, aliases=None,
    limit=VMEM_LIMIT,
):
    size = lambda a: a.size * a.dtype.itemsize
    return pl.pallas_call(
        kernel,
        grid=grid,
        in_specs=in_specs,
        out_specs=out_specs,
        out_shape=outs,
        scratch_shapes=scratch,
        input_output_aliases=aliases or {},
        compiler_params=pltpu.CompilerParams(vmem_limit_bytes=limit),
        cost_estimate=pl.CostEstimate(
            flops=flops,
            bytes_accessed=sum(size(a) for a in ins) + sum(size(a) for a in outs),
            transcendentals=0,
        ),
        name=name,
    )(*ins)


def xor_perm(count, mask):
    return [(j, j ^ mask) for j in range(count)]


def dp_hops(dp):
    bits = dp.bit_length() - 1
    groups = []
    at = 1
    while at < bits:
        groups.append((at, min(2, bits - at)))
        at += groups[-1][1]
    return groups


def dp_scatter(value, dp):
    for at, many in dp_hops(dp):
        value = value.reshape((-1, 1 << many) + value.shape[1:])
        got = [
            lax.ppermute(value[:, j].astype(BF), "dp", xor_perm(dp, j << at))
            for j in range(1, 1 << many)
        ]
        value = value[:, 0] + sum(g.astype(F32) for g in got)
    return value.reshape(value.shape[-2:])


def per_device(
    dp, mp,
    tokens_in, image_counts, norm1_gain, norm1_bias, qkv_weight, qkv_bias,
    mix_pre, mix_post, mix_post_bias, proj_weight, proj_bias, gamma1,
    norm2_gain, norm2_bias, fc1_weight, fc1_bias, fc2_weight, fc2_bias, gamma2, out_grad,
):
    images, patches, feats = tokens_in.shape
    heads = mix_pre.shape[0]
    rows = -(-patches // 16) * 16
    slots = -(-patches // 128) * 128
    hidden = fc1_weight.shape[1]
    tok_rows = (images, rows, feats)
    slot_rows = (images, slots, feats)
    prob_shape = (images, heads, rows, slots)
    mix_shape = (heads, feats)
    operands = [
        tokens_in, out_grad, norm1_gain, norm1_bias, qkv_bias, mix_pre, mix_post,
        mix_post_bias, proj_bias, gamma1, norm2_gain, norm2_bias, qkv_weight, proj_weight,
    ]

    ins = [kept(a) for a in (fc1_weight, fc2_weight, fc1_bias)]
    other = call(
        pack_kernel,
        (),
        ins,
        [IN_HBM] * 3,
        [sds((feats + 16, hidden), BF)],
        [IN_VMEM],
        [pltpu.VMEM(fc1_bias.shape, F32), pltpu.SemaphoreType.DMA((2,))],
        name="pack",
    )[0]
    near = [lax.ppermute(other, "mp", xor_perm(mp, j)) for j in (2, 1)][::-1]
    outs = [sds(a.shape, a.dtype) for a in operands]
    held = call(
        load_kernel,
        (),
        [kept(a) for a in operands] + [other],
        [IN_HBM] * len(operands) + [pl.BlockSpec(memory_space=pl.ANY)],
        outs,
        [IN_VMEM] * len(outs),
        [pltpu.SemaphoreType.DMA((len(operands),))],
        name="load",
    )

    shares = [images - 1, 1] if images > 1 else [images]
    carried = []
    for s, share in enumerate(shares):
        first = sum(shares[:s])
        ins = [image_counts, mix_post, mix_post_bias] + list(held)
        outs = call(
            functools.partial(attn_fwd_kernel, first, share),
            (),
            ins + carried,
            [SCALARS] * 3
            + [IN_VMEM] * 14
            + [pl.BlockSpec(memory_space=pl.ANY)] * len(carried),
            [
                sds(tok_rows, BF), sds(slot_rows, BF), sds(tok_rows, BF), sds(tok_rows, BF),
                sds(prob_shape, BF), sds(tok_rows, BF), sds(tok_rows, F32), sds(tok_rows, F32),
                sds(tok_rows, BF), sds(tok_rows, BF), sds(mix_shape, F32), sds(mix_shape, F32),
                sds((1, feats), F32),
            ],
            [IN_VMEM] * 13,
            [
                pltpu.VMEM((rows, feats), F32), pltpu.VMEM((heads * rows, 2 * feats), BF),
                pltpu.VMEM((feats, slots), BF), pltpu.VMEM((heads * rows, slots), BF),
                pltpu.VMEM((rows, 3 * feats), F32), pltpu.VMEM((heads * rows, slots), F32),
                pltpu.VMEM((heads, feats, slots), F32),
            ],
            flops=share * 15 * 10**8,
            name="attn_fwd",
            aliases={len(ins) + j: j for j in range(10)} if carried else None,
        )
        carried, (mpre, mpost, mixb) = list(outs[:10]), outs[10:]
        if s == 0:
            near, carried[0] = lax.optimization_barrier((near, carried[0]))
            last = lax.ppermute(near[1], "mp", xor_perm(mp, 1))
            near = jnp.stack(near)
            far = lax.ppermute(near, "dp", xor_perm(dp, 1))
    a1, q, k, v, prob, o, x1, u, a2, dy = carried
    far, a2 = lax.optimization_barrier((far, a2))

    block = feats // dp
    total = images * rows
    flat = (total, feats)
    a2, dy, x1, u, o = (a.reshape(flat) for a in (a2, dy, x1, u, o))
    ins = [a2, dy, gamma2, fc1_weight, fc1_bias, fc2_weight, near, far]
    wide = 2 * hidden
    grad_shape = (2, wide, feats)
    f0, da20, hids, dzs, dfs = call(
        mlp_first_kernel,
        (),
        ins,
        [IN_VMEM] * len(ins),
        [
            sds(flat, F32), sds(flat, F32), sds((total, wide), BF), sds((total, wide), BF),
            sds(flat, BF),
        ],
        [IN_VMEM] * 5,
        [
            pltpu.VMEM((feats, wide), BF), pltpu.VMEM((wide, feats), BF),
            pltpu.VMEM((1, wide), F32),
            pltpu.VMEM((2, total // 3, 256), F32), pltpu.VMEM((2, total // 3, 256), F32),
        ],
        flops=images * 5 * 10**8,
        name="mlp_first",
    )

    last, f0 = lax.optimization_barrier((last, f0))
    far_last = lax.ppermute(last, "dp", xor_perm(dp, 1))
    ins = [a2, hids, dzs, dfs]
    grads0, b1_0, a2t, dft = call(
        mlp_grad_kernel,
        (),
        ins,
        [IN_VMEM] * 4,
        [
            sds(grad_shape, BF), sds((1, wide), F32), sds((feats + 16, total), BF),
            sds((feats, total), BF),
        ],
        [IN_VMEM] * 4,
        flops=images * 3 * 10**8,
        name="mlp_grad",
    )

    grad_rows = 9 * block
    half_shape = (dp // 2, grad_rows, feats)
    ins = [
        image_counts, a2, dy, dfs, x1, u, o, f0, da20, near, far, last, far_last, grads0, a2t, dft,
        proj_weight, gamma1,
        norm2_gain, fc2_bias, gamma2,
    ]
    layer_out, dx1, do, keep, send, b1_1, acc_mlp = call(
        mlp_rest_kernel,
        (),
        ins,
        [SCALARS] + [IN_VMEM] * (len(ins) - 1),
        [
            sds(tokens_in.shape, BF), sds(flat, F32), sds(slot_rows, BF), sds(half_shape, BF),
            sds(half_shape, BF), sds((1, wide), F32), sds((8, feats), F32),
        ],
        [IN_HBM] + [IN_VMEM] * 6,
        [
            pltpu.VMEM((feats, wide), BF), pltpu.VMEM((wide, feats), BF),
            pltpu.VMEM((1, wide), F32), pltpu.VMEM((total, wide), BF),
            pltpu.VMEM((total, wide), BF),
            pltpu.VMEM((2, total // 3, 256), F32), pltpu.VMEM((2, total // 3, 256), F32),
            pltpu.VMEM(flat, F32), pltpu.VMEM(flat, F32), pltpu.VMEM(flat, BF),
            pltpu.VMEM((wide, feats), BF), pltpu.VMEM((feats, wide), BF),
            pltpu.VMEM((feats, feats), BF), pltpu.VMEM(tokens_in.shape, BF),
            pltpu.SemaphoreType.DMA((images,)),
        ],
        flops=images * 9 * 10**8,
        name="mlp_rest",
    )
    got = lax.ppermute(send, "dp", xor_perm(dp, 1))
    dx1 = dx1.reshape(tok_rows)

    shares = [1, images - 1] if images > 1 else [1]
    dqkv_shape = (images, rows, 3 * feats)
    carried, accs = [], []
    for s, share in enumerate(shares):
        first = sum(shares[:s])
        ins = [mix_pre, do, q, k, v, prob, dx1, tokens_in, mpre, mpost, mixb, qkv_weight, norm1_gain]
        *carried, acc = call(
            functools.partial(attn_bwd_kernel, first, share),
            (),
            ins + carried,
            [SCALARS]
            + [IN_VMEM] * (len(ins) - 1)
            + [pl.BlockSpec(memory_space=pl.ANY)] * len(carried),
            [sds(dqkv_shape, BF), sds(tokens_in.shape, F32), sds((2 * heads + 16, feats), F32)],
            [IN_VMEM, IN_HBM, IN_VMEM],
            [
                pltpu.VMEM((heads * rows, feats), BF), pltpu.VMEM((heads * rows, slots), BF),
                pltpu.VMEM((feats, slots), BF), pltpu.VMEM((heads * rows, slots), F32),
                pltpu.VMEM((heads * rows, feats), F32), pltpu.VMEM((heads * rows, feats), F32),
                pltpu.VMEM((heads, feats, slots), F32), pltpu.VMEM((rows, feats), F32),
                pltpu.VMEM((rows, feats), F32), pltpu.VMEM((share, patches, feats), F32),
                pltpu.SemaphoreType.DMA((share,)),
            ],
            flops=share * 20 * 10**8,
            name="attn_bwd",
            aliases={len(ins): 0, len(ins) + 1: 1} if carried else None,
        )
        accs.append(acc)
        if s == 0:
            (keep, got), acc = lax.optimization_barrier(((keep, got), acc))
            mine = dp_scatter(keep.astype(F32) + got.astype(F32), dp)
            accs[0], do = lax.optimization_barrier((acc, do))
    dqkv, in_grad = carried
    mine, dqkv = lax.optimization_barrier((mine, dqkv))
    mlp_mine = mine
    low = mine.astype(BF)
    m_idx = lax.axis_index("mp")
    share_rows = -(-block // (16 * mp)) * 16
    proj = jnp.pad(mine[8 * block :], ((0, mp * share_rows - block), (0, 0)))

    def proj_share(j):
        return lax.dynamic_slice_in_dim(proj, jnp.bitwise_xor(m_idx, j) * share_rows, share_rows)

    got_z = [
        lax.ppermute(
            jnp.concatenate([low[2 * j * block : 2 * (j + 1) * block], proj_share(j).astype(BF)]),
            "mp",
            xor_perm(mp, j),
        )
        for j in range(1, mp)
    ]

    q_block = 3 * feats // dp
    half_shape = (dp // 2, q_block + 16, feats)
    ins = [dqkv.reshape(total, 3 * feats)] + accs + [a1.reshape(flat), acc_mlp, b1_0, b1_1]
    keep, send = call(
        functools.partial(qkv_grad_kernel, heads),
        (),
        ins,
        [IN_VMEM] * len(ins),
        [sds(half_shape, BF), sds(half_shape, BF)],
        [IN_VMEM] * 2,
        [pltpu.VMEM((16, feats), F32), pltpu.VMEM((3 * feats, feats), BF)],
        flops=11 * 10**8,
        name="qkv_grad",
    )
    got = lax.ppermute(send, "dp", xor_perm(dp, 1))
    mine = dp_scatter(keep.astype(F32) + got.astype(F32), dp)
    mine, got_z = lax.optimization_barrier((mine, got_z))

    proj_own = (proj_share(0) + sum(g[2 * block :].astype(F32) for g in got_z)).astype(BF)
    payload = jnp.concatenate([mine.astype(BF), proj_own])
    got = [lax.ppermute(payload, "mp", xor_perm(mp, j)) for j in range(mp - 1, 0, -1)][::-1]
    b1_size = hidden // dp
    ins = [mine, proj_own] + got + [mlp_mine] + got_z
    outs = [
        sds((q_block, feats), F32), sds((1, q_block), F32), sds((heads, heads), F32),
        sds((heads, heads), F32), sds((1, heads), F32), sds((1, b1_size), F32),
    ] + [sds((1, block), F32)] * 8 + [sds((block, feats), F32)] * 3
    qkvw, qkvb, pre, post, postb, b1g, *vecs, fc1g, fc2g, projg = call(
        functools.partial(final_kernel, heads, q_block, mp - 1),
        (),
        ins,
        [IN_VMEM] * len(ins),
        outs,
        [IN_VMEM] * len(outs),
        [pltpu.VMEM((mp, share_rows, feats), F32)],
        name="final",
    )
    vecs = [a.reshape(-1) for a in vecs]
    return (
        layer_out,
        in_grad,
        vecs[0],
        vecs[1],
        qkvw.T,
        qkvb.reshape(-1),
        pre,
        post,
        postb.reshape(-1),
        projg.T,
        vecs[2],
        vecs[3],
        vecs[4],
        vecs[5],
        fc1g.T,
        b1g.reshape(-1),
        fc2g.T,
        vecs[6],
        vecs[7],
    )


def solution(mesh):
    tokens = P(("dp", "mp"), None, None)
    placed = (
        (tokens, P("dp")) + (P(),) * 12 + (P(None, "mp"), P("mp"), P("mp", None), P(), P(), tokens)
    )
    return jax.shard_map(
        functools.partial(per_device, mesh.shape["dp"], mesh.shape["mp"]),
        mesh=mesh,
        in_specs=placed,
        out_specs=(
            tokens, tokens, P("dp"), P("dp"), P(None, "dp"), P("dp"), P(), P(), P(),
            P(None, "dp"), P("dp"), P("dp"), P("dp"), P("dp"), P(None, ("mp", "dp")),
            P(("mp", "dp")), P("mp", "dp"), P("dp"), P("dp"),
        ),
        check_vma=False,
    )
```

```python
import functools

import jax
import jax.numpy as jnp
from jax import lax
from jax.experimental import pallas as pl
from jax.experimental.pallas import tpu as pltpu
from jax.sharding import PartitionSpec as P

BF = jnp.bfloat16
F32 = jnp.float32
LOG2E = 1.4426950408889634
EPS = 1e-06
VMEM_LIMIT = 20 * 1024 * 1024


def nn(a, b):
    return lax.dot_general(a, b, (((1,), (0,)), ((), ())), preferred_element_type=F32)


def nt(a, b):
    return lax.dot_general(a, b, (((1,), (1,)), ((), ())), preferred_element_type=F32)


def tn(a, b):
    return lax.dot_general(a, b, (((0,), (0,)), ((), ())), preferred_element_type=F32)


def exact(a, b, dims):
    return lax.dot_general(
        a, b, (dims, ((), ())), precision=lax.Precision.HIGHEST, preferred_element_type=F32
    )


def normalized(x):
    mean = jnp.mean(x, axis=-1, keepdims=True)
    c = x - mean
    r = lax.rsqrt(jnp.mean(c * c, axis=-1, keepdims=True) + EPS)
    return c * r, r


def norm_back(cot, n, r, gain):
    cg = cot * gain
    return r * (
        cg
        - jnp.mean(cg, axis=-1, keepdims=True)
        - n * jnp.mean(cg * n, axis=-1, keepdims=True)
    )


def colsum(x):
    return jnp.sum(x, axis=0, keepdims=True)


def split(x):
    hi = x.astype(BF)
    return jnp.concatenate([hi, (x - hi.astype(F32)).astype(BF)], axis=1)


def row(ref):
    return ref[...].reshape(1, ref.shape[0])


def gelu_parts(z):
    e = jnp.exp2(z * z * (-0.5 * LOG2E))
    t = pl.reciprocal(1.0 + jnp.abs(z) * (0.3275911 * 0.7071067811865476), approx=True)
    poly = t * (
        0.5 * 0.254829592
        + t
        * (
            0.5 * -0.284496736
            + t * (0.5 * 1.421413741 + t * (0.5 * -1.453152027 + t * (0.5 * 1.061405429)))
        )
    )
    tail = poly * e
    phi = jnp.where(z >= 0, 1.0 - tail, tail)
    return phi, phi + z * e * 0.3989422804014327


def head_of_lane(shape, axis, head_dim):
    return lax.broadcasted_iota(jnp.int32, shape, axis) // head_dim


def chunks(count, size=16):
    return [slice(at, at + size) for at in range(0, count, size)]


def fold(x):
    return sum(x[at : at + 8] for at in range(8, x.shape[0], 8)) + x[0:8]


def pack_kernel(w1, w2, b1, *refs):
    many = (len(refs) - 3) // 2
    sources, other, held, b1_v, sems = refs[:many], refs[many], refs[many + 1 : -2], refs[-2], refs[-1]
    feats = w1.shape[0]
    core = jnp.bitwise_and(lax.axis_index("dp"), 1)
    bias_copy = pltpu.make_async_copy(b1, b1_v, sems.at[0])
    own = [pltpu.make_async_copy(w, other.at[0:feats], sems.at[1]) for w in (w1, w2)]
    copies = [
        pltpu.make_async_copy(sources[j], held[j], sems.at[2 + j]) for j in range(many)
    ]
    bias_copy.start()
    for j in range(2):
        pl.when(core == j)(own[j].start)
    for copy in copies:
        copy.start()
    bias_copy.wait()
    rest = row(b1_v)
    place = lax.broadcasted_iota(jnp.int32, (16, feats), 0)
    bias = jnp.zeros((16, feats), F32)
    for j in range(3):
        term = rest.astype(BF).astype(F32)
        bias = jnp.where(place == j, term, bias)
        rest = rest - term
    other[feats:, :] = bias.astype(BF)
    for j in range(2):
        pl.when(core == j)(own[j].wait)
    for copy in copies:
        copy.wait()


def attn_fwd_kernel(first, share, *refs):
    counts, post_s, postb_s, tok, og, n1g, n1b, qkvb, pre, post, postb, projb = refs[:12]
    gamma1, n2g, n2b, wqkv, wproj = refs[12:17]
    a1_o, q_o, k_o, v_o, p_o, o_o, x1_o, u_o, a2_o, dy_o, mpre, mpost, mixb = refs[-20:-7]
    pad, kk, attended_t, probs, wide, logits, mixed = refs[-7:]
    images, patches, feats = tok.shape
    rows = pad.shape[0]
    heads = mpre.shape[0]
    head_dim = feats // heads
    slots = q_o.shape[1]

    spread = (
        head_of_lane((heads, feats), 1, head_dim)
        == lax.broadcasted_iota(jnp.int32, (heads, feats), 0)
    ).astype(F32)
    mpre[...] = exact(pre[...], spread, ((1,), (0,))) * (head_dim**-0.5 * LOG2E)
    mpost[...] = exact(post[...], spread, ((0,), (0,)))
    mixb[...] = exact(row(postb), spread, ((1,), (0,)))

    @pl.loop(first, first + share)
    def _(i):
        pad[patches:, :] = jnp.zeros((rows - patches, feats), F32)
        live = (lax.axis_index("mp") * images + i < counts[0]).astype(F32)
        pad[0:patches, :] = og[i].astype(F32) * live
        dy_o[i] = pad[...].astype(BF)
        pad[0:patches, :] = tok[i].astype(F32)
        gain, shift = row(n1g), row(n1b)
        for c in chunks(rows):
            n, _ = normalized(pad[c, :])
            a1_o[i, c, :] = (n * gain + shift).astype(BF)
        wide[...] = nn(a1_o[i], wqkv[...])
        bias = row(qkvb)
        q_o[i, rows:] = jnp.zeros((slots - rows, feats), BF)
        for c in chunks(rows):
            q, k, v = (
                wide[c, j * feats : (j + 1) * feats] + bias[:, j * feats : (j + 1) * feats]
                for j in range(3)
            )
            q_o[i, c, :] = q.astype(BF)
            v_o[i, c, :] = v.astype(BF)
            k_o[i, c, :] = k.astype(BF)
        q2 = jnp.concatenate([q_o[i], q_o[i]], axis=1)
        vt = v_o[i].T
        tail = patches // 8 * 8
        inside = lax.broadcasted_iota(jnp.int32, (rows - tail, 128), 0) < patches - tail
        real = (lax.broadcasted_iota(jnp.int32, (rows, 128), 0) < patches).astype(BF)
        start = nn(vt, real)

        def products(pair):
            for c in chunks(rows):
                kf = k_o[i, c, :].astype(F32)
                for g in pair:
                    at = slice(g * rows + c.start, g * rows + c.stop)
                    scaled = kf * mpre[g : g + 1, :]
                    hi = scaled.astype(BF)
                    kk[at, 0:feats] = hi
                    kk[at, feats:] = (scaled - hi.astype(F32)).astype(BF)
            part = slice(pair[0] * rows, (pair[1] + 1) * rows)
            logits[part, :] = nt(kk[part, :], q2)

        products((0, 1))
        for g in range(heads):
            if g % 2 == 0 and g + 2 < heads:
                products((g + 2, g + 3))
            for lane in range(0, slots, 128):
                x = logits[g * rows : (g + 1) * rows, lane : lane + 128]
                x = jnp.concatenate([x[0:tail], jnp.where(inside, x[tail:], -1e30)], axis=0)
                e = jnp.exp2(x - jnp.max(x, axis=0, keepdims=True))
                inv = 1.0 / jnp.sum(e, axis=0, keepdims=True)
                p = (e * inv).astype(BF)
                probs[g * rows : (g + 1) * rows, lane : lane + 128] = p
                p_o[i, g, :, lane : lane + 128] = p
            mixed[g] = nn(vt, probs[g * rows : (g + 1) * rows, :])
        for c in chunks(feats):
            g = c.start // head_dim
            first = start[c] * postb_s[g]
            for lane in range(0, slots, 128):
                total = first
                for h in range(heads):
                    total = total + mixed[h, c, lane : lane + 128] * post_s[g, h]
                attended_t[c, lane : lane + 128] = total.astype(BF)
        o_o[i] = attended_t[...].T[0:rows]
        wide[:, 0:feats] = nn(o_o[i], wproj[...])
        bias, scale, gain, shift = row(projb), row(gamma1), row(n2g), row(n2b)
        for c in chunks(rows):
            u = wide[c, 0:feats] + bias
            x1 = pad[c, :] + scale * u
            u_o[i, c, :] = u
            x1_o[i, c, :] = x1
            n, _ = normalized(x1)
            a2_o[i, c, :] = (n * gain + shift).astype(BF)


def store_blocks(count, put):
    mine = lax.axis_index("dp")
    for core in range(2):

        @pl.when(jnp.bitwise_and(mine, 1) == core)
        def _(core=core):
            for b in range(count):
                place = jnp.bitwise_xor(jnp.int32(b >> 1), jnp.right_shift(mine, 1))
                put((b ^ core) & 1, place, b)


def mlp_units(a2, dfs, w1, b1, w2, hids, dzs, zs, ghs, units, store, use):
    size = a2.shape[0] // units
    width = w2.shape[0]
    lanes = zs.shape[2]
    places = [slice(u * size, (u + 1) * size) for u in range(units)]
    blocks = [(u, at) for u in range(units) for at in range(0, width, lanes)]

    def products(j):
        u, at = blocks[j]
        part = slice(at, at + lanes)
        zs[j % 2] = nn(a2[places[u], :], w1[:, part])
        ghs[j % 2] = nt(dfs[places[u], :], w2[part, :])

    def activation(j):
        u, at = blocks[j]
        part = slice(at, at + lanes)
        bias = b1[:, part]
        for c in chunks(size):
            zc = zs[j % 2, c, :] + bias
            phi, slope = gelu_parts(zc)
            rows = slice(places[u].start + c.start, places[u].start + c.stop)
            hids[rows, part] = (zc * phi).astype(BF)
            dzs[rows, part] = (ghs[j % 2, c, :] * slope).astype(BF)

    def finish(u):
        store(places[u], nn(hids[places[u], :], w2[...]), nt(dzs[places[u], :], w1[...]))

    products(0)
    for j, (u, at) in enumerate(blocks):
        if j + 1 < len(blocks):
            products(j + 1)
        if at == lanes and u > 0:
            finish(u - 1)
        activation(j)
        if at == 2 * lanes and u > 0:
            use(places[u - 1])
    finish(units - 1)
    use(places[units - 1])


def mlp_first_kernel(
    a2, dy, gamma2, w1_own, b1_own, w2_own, near, far,
    f_o, da2_o, hids, dzs, dfs,
    w1, w2, b1, zs, ghs,
):
    total, feats = f_o.shape
    w1[:, 0:feats] = w1_own[...]
    w2[0:feats, :] = w2_own[...]
    for core in range(2):

        @pl.when(jnp.bitwise_and(lax.axis_index("dp"), 1) == core)
        def _(core=core):
            one, two = (near, far) if core == 0 else (far, near)
            w1[:, feats:] = one[0, 0:feats]
            w2[feats:, :] = two[0, 0:feats]

    b1[:, 0:feats] = row(b1_own)
    b1[:, feats:] = colsum(near[0, feats : feats + 16].astype(F32))
    gain = row(gamma2)
    for c in chunks(total):
        dfs[c, :] = (dy[c, :].astype(F32) * gain).astype(BF)

    def store(rows, f, da2):
        f_o[rows, :] = f
        da2_o[rows, :] = da2

    mlp_units(a2, dfs, w1, b1, w2, hids, dzs, zs, ghs, 3, store, lambda rows: None)


def mlp_grad_kernel(a2, hids, dzs, dfs, grads, b1_o, a2t, dft):
    feats = a2.shape[1]
    a2t[0:feats, :] = a2[...].T
    a2t[feats:, :] = jnp.ones((a2t.shape[0] - feats, a2t.shape[1]), BF)
    dft[...] = dfs[...].T
    up = nn(a2t[...], dzs[...])
    b1_o[...] = up[feats : feats + 1]
    grads[0] = up[0:feats].astype(BF).T
    down = nn(dft[...], hids[...]).astype(BF)
    for c in range(2):
        grads[1, c * feats : (c + 1) * feats, :] = down[:, c * feats : (c + 1) * feats]


def mlp_rest_kernel(
    counts, a2, dy, dfs, x1, u, o, f0, da20, near, far, last, far_last, grads, a2t, dft, wproj,
    gamma1, n2g, fc2b, gamma2,
    out_o, dx1_o, do_o, keep, send, b1_o, acc_o,
    w1, w2, b1, hids, dzs, zs, ghs, fs, da2s, dus, ups, downs, projs, out_v, sems,
):
    total, feats = f0.shape
    images, patches = out_o.shape[:2]
    image_rows = total // images
    m_idx = lax.axis_index("mp")
    acc_o[...] = jnp.zeros_like(acc_o)
    b1[:, 0:feats] = colsum(near[1, feats : feats + 16].astype(F32))
    b1[:, feats:] = colsum(last[feats : feats + 16].astype(F32))
    for core in range(2):

        @pl.when(jnp.bitwise_and(lax.axis_index("dp"), 1) == core)
        def _(core=core):
            one, two = (near, far) if core == 0 else (far, near)
            w1[:, 0:feats] = one[1, 0:feats]
            w2[0:feats, :] = two[1, 0:feats]
            one, two = (last, far_last) if core == 0 else (far_last, last)
            w1[:, feats:] = one[0:feats]
            w2[feats:, :] = two[0:feats]

    gain2 = row(gamma2)
    bias, gain, scale = row(fc2b), row(n2g), row(gamma1)

    def out_copy(image):
        return pltpu.make_async_copy(out_v.at[image], out_o.at[image], sems.at[image])

    def store(rows, f, da2):
        fs[rows, :] = f
        da2s[rows, :] = da2

    def use(rows):
        sums = [jnp.zeros((8, feats), F32) for _ in range(6)]
        for c in chunks(rows.stop - rows.start):
            at = slice(rows.start + c.start, rows.start + c.stop)
            fc = fs[at, :] + f0[at, :] + bias
            dac = da2s[at, :] + da20[at, :]
            x1c = x1[at, :]
            dyc = dy[at, :].astype(F32)
            n, r = normalized(x1c)
            dx1 = dyc + norm_back(dac, n, r, gain)
            dx1_o[at, :] = dx1
            du = (dx1 * scale).astype(BF)
            dus[at, :] = du
            image = at.start // image_rows
            first = at.start - image * image_rows
            live = (m_idx * images + image < counts[0]).astype(F32)
            out = ((x1c + gain2 * fc) * live).astype(BF)
            if first + 16 <= patches:
                out_v[image, first : first + 16, :] = out
            else:
                out_v[image, first:patches, :] = out[0 : patches - first]
            terms = (
                du.astype(F32), u[at, :] * dx1, dac * n, dac, dfs[at, :].astype(F32), fc * dyc,
            )
            sums = [s + fold(t) for s, t in zip(sums, terms)]
        for j in range(6):
            acc_o[j : j + 1, :] += colsum(sums[j])
        do = nt(dus[rows, :], wproj[...]).astype(BF)
        for at in range(0, rows.stop - rows.start, image_rows):
            image = (rows.start + at) // image_rows
            out_copy(image).start()
            do_o[image, 0:image_rows] = do[at : at + image_rows]
            do_o[image, image_rows:] = jnp.zeros((do_o.shape[1] - image_rows, feats), BF)

    mlp_units(a2, dfs, w1, b1, w2, hids, dzs, zs, ghs, 3, store, use)
    up = nn(a2t[...], dzs[...])
    b1_o[...] = up[feats : feats + 1]
    ups[...] = up[0:feats].astype(BF).T
    downs[...] = nn(dft[...], hids[...]).astype(BF)
    projs[...] = tn(dus[...], o[...]).astype(BF)
    count = 2 * keep.shape[0]
    size = feats // count
    outs = (keep, send)

    def put(which, place, b):
        out = outs[which]
        for c in range(2):
            part = slice(c * feats, (c + 1) * feats)
            up = slice(c * feats + b * size, c * feats + (b + 1) * size)
            down = slice(b * size, (b + 1) * size)
            pieces = (grads[0, up, :], grads[1, up, :])
            for j, piece in enumerate(pieces):
                out[place, (2 * c + j) * size : (2 * c + j + 1) * size, :] = piece
            pieces = (ups[up, :], downs[down, part])
            for j, piece in enumerate(pieces):
                out[place, (4 + 2 * c + j) * size : (5 + 2 * c + j) * size, :] = piece
        out[place, 8 * size : 9 * size, :] = projs[b * size : (b + 1) * size, :]

    store_blocks(count, put)
    for image in range(images):
        out_copy(image).wait()


def attn_bwd_kernel(first, share, *refs):
    pre_s, do_r, q_r, k_r, v_r, p_r, dx1, tok, mpre, mpost, mixb, wqkv, n1g = refs[:13]
    if first:
        before, in_o = refs[14], refs[-13]
        dqkv_o, acc_o = refs[-14], refs[-12]
        vgs, dls, dq_t, dps, dvs, dks, dqs, da1, pad, in_v, sems = refs[-11:]
    else:
        dqkv_o, in_v, acc_o, vgs, dls, dq_t, dps, dvs, dks, dqs, da1, pad = refs[-12:]
    slots, feats = do_r.shape[1:]
    patches = tok.shape[1]
    rows = k_r.shape[1]
    heads = mpre.shape[0]
    head_dim = feats // heads
    acc_o[...] = jnp.zeros_like(acc_o)

    def in_copy(i):
        return pltpu.make_async_copy(in_v.at[i - first], in_o.at[i], sems.at[i])

    def early_copy(i):
        return pltpu.make_async_copy(before.at[i], in_o.at[i], sems.at[i])

    for i in range(first):
        early_copy(i).start()

    @pl.loop(first, first + share)
    def _(i):
        do_sum = jnp.zeros((8, feats), F32)
        for c in chunks(rows):
            do_sum = do_sum + fold(do_r[i, c, :].astype(F32))
        do_sum = colsum(do_sum)
        q = q_r[i]
        do = do_r[i]
        kt = k_r[i].T

        def products(pair):
            for c in chunks(rows):
                vf = v_r[i, c, :].astype(F32)
                for h in pair:
                    at = slice(h * rows + c.start, h * rows + c.stop)
                    vgs[at, :] = (vf * mpost[h : h + 1, :]).astype(BF)
            part = slice(pair[0] * rows, (pair[1] + 1) * rows)
            dps[part, :] = nt(vgs[part, :], do)
            dvs[part, :] = nn(p_r[i, pair[0] : pair[1] + 1].reshape(2 * rows, slots), do)

        products((0, 1))
        for h in range(heads):
            if h % 2 == 0 and h + 2 < heads:
                products((h + 2, h + 3))
            at = slice(h * rows, (h + 1) * rows)
            for lane in range(0, slots, 128):
                dp = dps[at, lane : lane + 128]
                pf = p_r[i, h, :, lane : lane + 128].astype(F32)
                mean = jnp.sum(dp * pf, axis=0, keepdims=True) / jnp.sum(
                    pf, axis=0, keepdims=True
                )
                dls[at, lane : lane + 128] = (pf * (dp - mean)).astype(BF)
            dqs[h] = nn(kt, dls[at, :])
            if h % 2 == 1:
                part = slice((h - 1) * rows, (h + 1) * rows)
                dks[part, :] = nn(dls[part, :], q)

        bias_row = mixb[...] * do_sum
        v_sum = jnp.zeros((8, feats), F32)
        dv_sum = jnp.zeros((8, feats), F32)
        sums = [jnp.zeros((8, feats), F32) for _ in range(heads)]
        for c in chunks(rows):
            vf = v_r[i, c, :].astype(F32)
            dv = bias_row
            for h in range(heads):
                this = dvs[h * rows + c.start : h * rows + c.stop, :]
                dv = dv + this * mpost[h : h + 1, :]
                sums[h] = sums[h] + fold(vf * this)
            if c.stop > patches:
                inside = lax.broadcasted_iota(jnp.int32, dv.shape, 0) < patches - c.start
                dv = jnp.where(inside, dv, 0.0)
                vf = jnp.where(inside, vf, 0.0)
            low = dv.astype(BF)
            dqkv_o[i, c, 2 * feats :] = low
            dv_sum = dv_sum + fold(low.astype(F32))
            v_sum = v_sum + fold(vf)
        for h in range(heads):
            acc_o[h : h + 1, :] += colsum(sums[h])
        acc_o[2 * heads : 2 * heads + 1, :] += do_sum * colsum(v_sum)
        acc_o[2 * heads + 10 : 2 * heads + 11, :] += colsum(dv_sum)

        for c in chunks(feats):
            g = c.start // head_dim
            for lane in range(0, slots, 128):
                total = 0.0
                for h in range(heads):
                    total = total + dqs[h, c, lane : lane + 128] * pre_s[h, g]
                dq_t[c, lane : lane + 128] = (total * head_dim**-0.5).astype(BF)
        dq = dq_t[...].T[0:rows]
        dqkv_o[i, :, 0:feats] = dq
        dk_sum = jnp.zeros((8, feats), F32)
        sums = [jnp.zeros((8, feats), F32) for _ in range(heads)]
        for c in chunks(rows):
            kf = k_r[i, c, :].astype(F32)
            dk = 0.0
            for h in range(heads):
                this = dks[h * rows + c.start : h * rows + c.stop, :]
                dk = dk + this * mpre[h : h + 1, :]
                sums[h] = sums[h] + fold(kf * this)
            low = (dk * (1.0 / LOG2E)).astype(BF)
            dqkv_o[i, c, feats : 2 * feats] = low
            dk_sum = dk_sum + fold(low.astype(F32))
        for h in range(heads):
            acc_o[heads + h : heads + h + 1, :] += colsum(sums[h])
        acc_o[2 * heads + 8 : 2 * heads + 9, :] += colsum(dq.astype(F32))
        acc_o[2 * heads + 9 : 2 * heads + 10, :] += colsum(dk_sum)

        pad[patches:, :] = jnp.zeros((rows - patches, feats), F32)
        pad[0:patches, :] = tok[i].astype(F32)
        da1[...] = nt(dqkv_o[i], wqkv[...])
        gain = row(n1g)
        sums = [jnp.zeros((8, feats), F32) for _ in range(2)]
        for c in chunks(rows):
            n, r = normalized(pad[c, :])
            cot = da1[c, :]
            grad = dx1[i, c, :] + norm_back(cot, n, r, gain)
            sums = [sums[0] + fold(cot * n), sums[1] + fold(cot)]
            if c.stop <= patches:
                in_v[i - first, c, :] = grad
            else:
                in_v[i - first, c.start : patches, :] = grad[0 : patches - c.start]
        for j in range(2):
            acc_o[2 * heads + 11 + j : 2 * heads + 12 + j, :] += colsum(sums[j])
        if first:
            in_copy(i).start()

    if first:
        for i in range(first):
            early_copy(i).wait()

        @pl.loop(first, first + share)
        def _(i):
            in_copy(i).wait()


def qkv_grad_kernel(heads, dqkv, *refs):
    accs = refs[:-8]
    a1, acc_mlp, b1_first, b1_rest, keep, send, small, grads = refs[-8:]
    feats = a1.shape[1]
    count = 2 * keep.shape[0]
    size = 3 * feats // count
    acc = accs[0][...]
    for other in accs[1:]:
        acc = acc + other[...]
    small[...] = jnp.zeros_like(small)
    small[0:2, :] = acc[2 * heads + 11 : 2 * heads + 13]
    small[2:8, :] = acc_mlp[0:6, :]
    small[8:11, :] = acc[2 * heads + 8 : 2 * heads + 11]
    head_dim = feats // heads
    lanes = 2 * heads * heads
    gather = (
        head_of_lane((feats, lanes), 0, head_dim)
        == lax.broadcasted_iota(jnp.int32, (feats, lanes), 1) % heads
    ).astype(F32)
    sums = exact(acc[0 : 2 * heads + 8], gather, ((1,), (0,)))
    place = head_of_lane((2 * heads, lanes), 1, heads) == lax.broadcasted_iota(
        jnp.int32, (2 * heads, lanes), 0
    )
    small[11:12, 0:lanes] = colsum(jnp.where(place, sums[0 : 2 * heads], 0.0))
    small[11:12, lanes : 2 * lanes] = sums[2 * heads : 2 * heads + 1]
    m_idx = lax.axis_index("mp")
    for c, ref in enumerate((b1_first, b1_first, b1_rest, b1_rest)):
        place = 12 + jnp.bitwise_xor(m_idx, c)
        small[pl.ds(place, 1), :] = ref[:, (c % 2) * feats : (c % 2 + 1) * feats]
    low = small[...].astype(BF)
    outs = (keep, send)

    grads[...] = tn(a1[...], dqkv[...]).astype(BF).T

    def put(which, place, b):
        outs[which][place, 0:size, :] = grads[b * size : (b + 1) * size, :]
        outs[which][place, size : size + 16, :] = low
        if outs[which].shape[1] > size + 16:
            outs[which][place, size + 16 :, :] = jnp.zeros_like(outs[which][place, size + 16 :, :])

    store_blocks(count, put)


def final_kernel(heads, size, many, mine, proj_own, *refs):
    got = refs[:many]
    mlp_mine, got_z = refs[many], refs[1 + many : 1 + 2 * many]
    qkv_o, qkvb_o, pre_o, post_o, postb_o, b1_o, *vecs_o, fc1_o, fc2_o, proj_o, held = refs[-18:]
    block, feats = fc1_o.shape
    for place, out in enumerate((fc1_o, fc2_o)):
        rows = slice(place * block, (place + 1) * block)
        out[...] = mlp_mine[rows, :] + sum(g[rows, :].astype(F32) for g in got_z)
    d_idx = lax.axis_index("dp")
    m_idx = lax.axis_index("mp")
    total = mine[...]
    held[m_idx] = proj_own[...].astype(F32)
    for j, part in enumerate(got):
        value = part[...].astype(F32)
        total = total + value[0 : size + 16]
        held[jnp.bitwise_xor(m_idx, j + 1)] = value[size + 16 :]
    proj_o[...] = held[...].reshape(-1, feats)[0:block]
    qkv_o[...] = total[0:size]
    small = total[size : size + 16]

    def own(value, width, index):
        lanes = value.shape[1]
        return pltpu.roll(value, lax.rem(lanes - index * width, lanes), axis=1)[:, 0:width]

    width = vecs_o[0].shape[1]
    vecs = own(small[0:8], width, d_idx)
    for j, ref in enumerate(vecs_o):
        ref[...] = vecs[j : j + 1]
    flat = jnp.concatenate([small[8 + j : 9 + j] for j in range(3)], axis=1)
    qkvb_o[...] = own(jnp.broadcast_to(flat, (8, 3 * feats)), qkvb_o.shape[1], d_idx)[0:1]
    b1 = own(small[8:16], b1_o.shape[1], d_idx)[4:8]
    pick = lax.broadcasted_iota(jnp.int32, b1.shape, 0) == m_idx
    b1_o[...] = colsum(jnp.where(pick, b1, 0.0))
    mix = small[11:12]
    hh = heads * heads
    line = lax.broadcasted_iota(jnp.int32, (heads, hh), 0)
    lane = lax.broadcasted_iota(jnp.int32, (heads, hh), 1)
    fold = (
        lax.broadcasted_iota(jnp.int32, (hh, heads), 0) % heads
        == lax.broadcasted_iota(jnp.int32, (hh, heads), 1)
    ).astype(F32)
    head_dim = feats // heads

    def square(values):
        return exact(jnp.where(lane // heads == line, values, 0.0), fold, ((1,), (0,)))

    post_o[...] = square(mix[:, 0:hh]).T
    pre_o[...] = square(mix[:, hh : 2 * hh]) * (head_dim**-0.5)
    postb_o[...] = mix[:, 2 * hh : 2 * hh + heads]


def whole(shape):
    return pl.BlockSpec(shape, lambda i: (0,) * len(shape))


def each(shape, first=0, many=1):
    return pl.BlockSpec((many,) + shape[1:], lambda i: (i + first,) + (0,) * (len(shape) - 1))


SCALARS = pl.BlockSpec(memory_space=pltpu.SMEM)
IN_VMEM = pl.BlockSpec(memory_space=pltpu.VMEM)
IN_HBM = pl.BlockSpec(memory_space=pltpu.HBM)


def kept(a):
    return pltpu.with_memory_space_constraint(a, pltpu.HBM)


def sds(shape, dtype):
    return jax.ShapeDtypeStruct(shape, dtype)


def call(
    kernel, grid, ins, in_specs, outs, out_specs, scratch=(), flops=0, name=None, aliases=None,
    limit=VMEM_LIMIT,
):
    size = lambda a: a.size * a.dtype.itemsize
    return pl.pallas_call(
        kernel,
        grid=grid,
        in_specs=in_specs,
        out_specs=out_specs,
        out_shape=outs,
        scratch_shapes=scratch,
        input_output_aliases=aliases or {},
        compiler_params=pltpu.CompilerParams(vmem_limit_bytes=limit),
        cost_estimate=pl.CostEstimate(
            flops=flops,
            bytes_accessed=sum(size(a) for a in ins) + sum(size(a) for a in outs),
            transcendentals=0,
        ),
        name=name,
    )(*ins)


def xor_perm(count, mask):
    return [(j, j ^ mask) for j in range(count)]


def dp_hops(dp):
    bits = dp.bit_length() - 1
    groups = []
    at = 1
    while at < bits:
        groups.append((at, min(2, bits - at)))
        at += groups[-1][1]
    return groups


def dp_scatter(value, dp):
    for at, many in dp_hops(dp):
        value = value.reshape((-1, 1 << many) + value.shape[1:])
        got = [
            lax.ppermute(value[:, j].astype(BF), "dp", xor_perm(dp, j << at))
            for j in range(1, 1 << many)
        ]
        value = value[:, 0] + sum(g.astype(F32) for g in got)
    return value.reshape(value.shape[-2:])


def per_device(
    dp, mp,
    tokens_in, image_counts, norm1_gain, norm1_bias, qkv_weight, qkv_bias,
    mix_pre, mix_post, mix_post_bias, proj_weight, proj_bias, gamma1,
    norm2_gain, norm2_bias, fc1_weight, fc1_bias, fc2_weight, fc2_bias, gamma2, out_grad,
):
    images, patches, feats = tokens_in.shape
    heads = mix_pre.shape[0]
    rows = -(-patches // 16) * 16
    slots = -(-patches // 128) * 128
    hidden = fc1_weight.shape[1]
    tok_rows = (images, rows, feats)
    slot_rows = (images, slots, feats)
    prob_shape = (images, heads, rows, slots)
    mix_shape = (heads, feats)
    operands = [
        tokens_in, out_grad, norm1_gain, norm1_bias, qkv_bias, mix_pre, mix_post,
        mix_post_bias, proj_bias, gamma1, norm2_gain, norm2_bias, qkv_weight, proj_weight,
    ]

    ins = [kept(a) for a in [fc1_weight, fc2_weight, fc1_bias] + operands]
    outs = [sds((feats + 16, hidden), BF)] + [sds(a.shape, a.dtype) for a in operands]
    other, *held = call(
        pack_kernel,
        (),
        ins,
        [IN_HBM] * len(ins),
        outs,
        [IN_VMEM] * len(outs),
        [pltpu.VMEM(fc1_bias.shape, F32), pltpu.SemaphoreType.DMA((2 + len(operands),))],
        name="pack",
    )
    near = [lax.ppermute(other, "mp", xor_perm(mp, j)) for j in (1, 2)]

    shares = [images - 1, 1] if images > 1 else [images]
    carried = []
    for s, share in enumerate(shares):
        first = sum(shares[:s])
        ins = [image_counts, mix_post, mix_post_bias] + held
        outs = call(
            functools.partial(attn_fwd_kernel, first, share),
            (),
            ins + carried,
            [SCALARS] * 3
            + [IN_VMEM] * 14
            + [pl.BlockSpec(memory_space=pl.ANY)] * len(carried),
            [
                sds(tok_rows, BF), sds(slot_rows, BF), sds(tok_rows, BF), sds(tok_rows, BF),
                sds(prob_shape, BF), sds(tok_rows, BF), sds(tok_rows, F32), sds(tok_rows, F32),
                sds(tok_rows, BF), sds(tok_rows, BF), sds(mix_shape, F32), sds(mix_shape, F32),
                sds((1, feats), F32),
            ],
            [IN_VMEM] * 13,
            [
                pltpu.VMEM((rows, feats), F32), pltpu.VMEM((heads * rows, 2 * feats), BF),
                pltpu.VMEM((feats, slots), BF), pltpu.VMEM((heads * rows, slots), BF),
                pltpu.VMEM((rows, 3 * feats), F32), pltpu.VMEM((heads * rows, slots), F32),
                pltpu.VMEM((heads, feats, slots), F32),
            ],
            flops=share * 15 * 10**8,
            name="attn_fwd",
            aliases={len(ins) + j: j for j in range(10)} if carried else None,
        )
        carried, (mpre, mpost, mixb) = list(outs[:10]), outs[10:]
        if s == 0:
            near, carried[0] = lax.optimization_barrier((near, carried[0]))
            last = lax.ppermute(near[1], "mp", xor_perm(mp, 1))
            near = jnp.stack(near)
            far = lax.ppermute(near, "dp", xor_perm(dp, 1))
    a1, q, k, v, prob, o, x1, u, a2, dy = carried
    far, a2 = lax.optimization_barrier((far, a2))

    block = feats // dp
    total = images * rows
    flat = (total, feats)
    a2, dy, x1, u, o = (a.reshape(flat) for a in (a2, dy, x1, u, o))
    ins = [a2, dy, gamma2, fc1_weight, fc1_bias, fc2_weight, near, far]
    wide = 2 * hidden
    grad_shape = (2, wide, feats)
    f0, da20, hids, dzs, dfs = call(
        mlp_first_kernel,
        (),
        ins,
        [IN_VMEM] * len(ins),
        [
            sds(flat, F32), sds(flat, F32), sds((total, wide), BF), sds((total, wide), BF),
            sds(flat, BF),
        ],
        [IN_VMEM] * 5,
        [
            pltpu.VMEM((feats, wide), BF), pltpu.VMEM((wide, feats), BF),
            pltpu.VMEM((1, wide), F32),
            pltpu.VMEM((2, total // 3, 256), F32), pltpu.VMEM((2, total // 3, 256), F32),
        ],
        flops=images * 5 * 10**8,
        name="mlp_first",
    )

    last, f0 = lax.optimization_barrier((last, f0))
    far_last = lax.ppermute(last, "dp", xor_perm(dp, 1))
    ins = [a2, hids, dzs, dfs]
    grads0, b1_0, a2t, dft = call(
        mlp_grad_kernel,
        (),
        ins,
        [IN_VMEM] * 4,
        [
            sds(grad_shape, BF), sds((1, wide), F32), sds((feats + 16, total), BF),
            sds((feats, total), BF),
        ],
        [IN_VMEM] * 4,
        flops=images * 3 * 10**8,
        name="mlp_grad",
    )

    grad_rows = 9 * block
    half_shape = (dp // 2, grad_rows, feats)
    ins = [
        image_counts, a2, dy, dfs, x1, u, o, f0, da20, near, far, last, far_last, grads0, a2t, dft,
        proj_weight, gamma1,
        norm2_gain, fc2_bias, gamma2,
    ]
    layer_out, dx1, do, keep, send, b1_1, acc_mlp = call(
        mlp_rest_kernel,
        (),
        ins,
        [SCALARS] + [IN_VMEM] * (len(ins) - 1),
        [
            sds(tokens_in.shape, BF), sds(flat, F32), sds(slot_rows, BF), sds(half_shape, BF),
            sds(half_shape, BF), sds((1, wide), F32), sds((8, feats), F32),
        ],
        [IN_HBM] + [IN_VMEM] * 6,
        [
            pltpu.VMEM((feats, wide), BF), pltpu.VMEM((wide, feats), BF),
            pltpu.VMEM((1, wide), F32), pltpu.VMEM((total, wide), BF),
            pltpu.VMEM((total, wide), BF),
            pltpu.VMEM((2, total // 3, 256), F32), pltpu.VMEM((2, total // 3, 256), F32),
            pltpu.VMEM(flat, F32), pltpu.VMEM(flat, F32), pltpu.VMEM(flat, BF),
            pltpu.VMEM((wide, feats), BF), pltpu.VMEM((feats, wide), BF),
            pltpu.VMEM((feats, feats), BF), pltpu.VMEM(tokens_in.shape, BF),
            pltpu.SemaphoreType.DMA((images,)),
        ],
        flops=images * 9 * 10**8,
        name="mlp_rest",
    )
    got = lax.ppermute(send, "dp", xor_perm(dp, 1))
    dx1 = dx1.reshape(tok_rows)

    shares = [1, images - 1] if images > 1 else [1]
    dqkv_shape = (images, rows, 3 * feats)
    carried, accs = [], []
    for s, share in enumerate(shares):
        first = sum(shares[:s])
        ins = [mix_pre, do, q, k, v, prob, dx1, tokens_in, mpre, mpost, mixb, qkv_weight, norm1_gain]
        in_shape = tokens_in.shape if first or share == images else (share,) + tokens_in.shape[1:]
        *carried, acc = call(
            functools.partial(attn_bwd_kernel, first, share),
            (),
            ins + carried,
            [SCALARS]
            + [IN_VMEM] * (len(ins) - 1)
            + [pl.BlockSpec(memory_space=pl.ANY), IN_VMEM][: len(carried)],
            [sds(dqkv_shape, BF), sds(in_shape, F32), sds((2 * heads + 16, feats), F32)],
            [IN_VMEM, IN_HBM if first else IN_VMEM, IN_VMEM],
            [
                pltpu.VMEM((heads * rows, feats), BF), pltpu.VMEM((heads * rows, slots), BF),
                pltpu.VMEM((feats, slots), BF), pltpu.VMEM((heads * rows, slots), F32),
                pltpu.VMEM((heads * rows, feats), F32), pltpu.VMEM((heads * rows, feats), F32),
                pltpu.VMEM((heads, feats, slots), F32), pltpu.VMEM((rows, feats), F32),
                pltpu.VMEM((rows, feats), F32),
            ]
            + [pltpu.VMEM((share, patches, feats), F32), pltpu.SemaphoreType.DMA((images,))]
            * bool(first),
            flops=share * 20 * 10**8,
            name="attn_bwd",
            aliases={len(ins): 0} if carried else None,
        )
        accs.append(acc)
        if s == 0:
            (keep, got), acc = lax.optimization_barrier(((keep, got), acc))
            mine = dp_scatter(keep.astype(F32) + got.astype(F32), dp)
            accs[0], do = lax.optimization_barrier((acc, do))
    dqkv, in_grad = carried
    mine, dqkv = lax.optimization_barrier((mine, dqkv))
    mlp_mine = mine
    low = mine.astype(BF)
    m_idx = lax.axis_index("mp")
    share_rows = -(-block // (16 * mp)) * 16
    proj = jnp.pad(mine[8 * block :], ((0, mp * share_rows - block), (0, 0)))

    def proj_share(j):
        return lax.dynamic_slice_in_dim(proj, jnp.bitwise_xor(m_idx, j) * share_rows, share_rows)

    got_z = [
        lax.ppermute(
            jnp.concatenate([low[2 * j * block : 2 * (j + 1) * block], proj_share(j).astype(BF)]),
            "mp",
            xor_perm(mp, j),
        )
        for j in range(1, mp)
    ]

    q_block = 3 * feats // dp
    half_shape = (dp // 2, q_block + 16, feats)
    ins = [dqkv.reshape(total, 3 * feats)] + accs + [a1.reshape(flat), acc_mlp, b1_0, b1_1]
    keep, send = call(
        functools.partial(qkv_grad_kernel, heads),
        (),
        ins,
        [IN_VMEM] * len(ins),
        [sds(half_shape, BF), sds(half_shape, BF)],
        [IN_VMEM] * 2,
        [pltpu.VMEM((16, feats), F32), pltpu.VMEM((3 * feats, feats), BF)],
        flops=11 * 10**8,
        name="qkv_grad",
    )
    got = lax.ppermute(send, "dp", xor_perm(dp, 1))
    mine = dp_scatter(keep.astype(F32) + got.astype(F32), dp)
    mine, got_z = lax.optimization_barrier((mine, got_z))

    proj_own = (proj_share(0) + sum(g[2 * block :].astype(F32) for g in got_z)).astype(BF)
    payload = jnp.concatenate([mine.astype(BF), proj_own])
    got = [lax.ppermute(payload, "mp", xor_perm(mp, j)) for j in range(1, mp)]
    b1_size = hidden // dp
    ins = [mine, proj_own] + got + [mlp_mine] + got_z
    outs = [
        sds((q_block, feats), F32), sds((1, q_block), F32), sds((heads, heads), F32),
        sds((heads, heads), F32), sds((1, heads), F32), sds((1, b1_size), F32),
    ] + [sds((1, block), F32)] * 8 + [sds((block, feats), F32)] * 3
    qkvw, qkvb, pre, post, postb, b1g, *vecs, fc1g, fc2g, projg = call(
        functools.partial(final_kernel, heads, q_block, mp - 1),
        (),
        ins,
        [IN_VMEM] * len(ins),
        outs,
        [IN_VMEM] * len(outs),
        [pltpu.VMEM((mp, share_rows, feats), F32)],
        name="final",
    )
    vecs = [a.reshape(-1) for a in vecs]
    return (
        layer_out,
        in_grad,
        vecs[0],
        vecs[1],
        qkvw.T,
        qkvb.reshape(-1),
        pre,
        post,
        postb.reshape(-1),
        projg.T,
        vecs[2],
        vecs[3],
        vecs[4],
        vecs[5],
        fc1g.T,
        b1g.reshape(-1),
        fc2g.T,
        vecs[6],
        vecs[7],
    )


def solution(mesh):
    tokens = P(("dp", "mp"), None, None)
    placed = (
        (tokens, P("dp")) + (P(),) * 12 + (P(None, "mp"), P("mp"), P("mp", None), P(), P(), tokens)
    )
    return jax.shard_map(
        functools.partial(per_device, mesh.shape["dp"], mesh.shape["mp"]),
        mesh=mesh,
        in_specs=placed,
        out_specs=(
            tokens, tokens, P("dp"), P("dp"), P(None, "dp"), P("dp"), P(), P(), P(),
            P(None, "dp"), P("dp"), P("dp"), P("dp"), P("dp"), P(None, ("mp", "dp")),
            P(("mp", "dp")), P("mp", "dp"), P("dp"), P("dp"),
        ),
        check_vma=False,
    )
```

```python
import functools

import jax
import jax.numpy as jnp
from jax import lax
from jax.experimental import pallas as pl
from jax.experimental.pallas import tpu as pltpu
from jax.sharding import PartitionSpec as P

BF = jnp.bfloat16
F32 = jnp.float32
EPS = 1e-06
VMEM_LIMIT = 20 * 1024 * 1024


def nn(a, b):
    return lax.dot_general(a, b, (((1,), (0,)), ((), ())), preferred_element_type=F32)


def nt(a, b):
    return lax.dot_general(a, b, (((1,), (1,)), ((), ())), preferred_element_type=F32)


def tn(a, b):
    return lax.dot_general(a, b, (((0,), (0,)), ((), ())), preferred_element_type=F32)


def exact(a, b, dims):
    return lax.dot_general(
        a, b, (dims, ((), ())), precision=lax.Precision.HIGHEST, preferred_element_type=F32
    )


def normalized(x):
    mean = jnp.mean(x, axis=-1, keepdims=True)
    c = x - mean
    r = lax.rsqrt(jnp.mean(c * c, axis=-1, keepdims=True) + EPS)
    return c * r, r


def norm_back(cot, n, r, gain):
    cg = cot * gain
    return r * (
        cg
        - jnp.mean(cg, axis=-1, keepdims=True)
        - n * jnp.mean(cg * n, axis=-1, keepdims=True)
    )


def colsum(x):
    return jnp.sum(x, axis=0, keepdims=True)


def split(x):
    hi = x.astype(BF)
    return jnp.concatenate([hi, (x - hi.astype(F32)).astype(BF)], axis=1)


def row(ref):
    return ref[...].reshape(1, ref.shape[0])


def gelu_parts(z):
    e = jnp.exp(z * z * -0.5)
    t = pl.reciprocal(1.0 + jnp.abs(z) * (0.3275911 * 0.7071067811865476), approx=True)
    poly = t * (
        0.5 * 0.254829592
        + t
        * (
            0.5 * -0.284496736
            + t * (0.5 * 1.421413741 + t * (0.5 * -1.453152027 + t * (0.5 * 1.061405429)))
        )
    )
    tail = poly * e
    phi = jnp.where(z >= 0, 1.0 - tail, tail)
    return phi, phi + z * e * 0.3989422804014327


def head_of_lane(shape, axis, head_dim):
    return lax.broadcasted_iota(jnp.int32, shape, axis) // head_dim


def chunks(count, size=16):
    return [slice(at, at + size) for at in range(0, count, size)]


def fold(x):
    return sum(x[at : at + 8] for at in range(8, x.shape[0], 8)) + x[0:8]


def pack_kernel(w1, w2, b1, *refs):
    many = (len(refs) - 3) // 2
    sources, other, held, b1_v, sems = refs[:many], refs[many], refs[many + 1 : -2], refs[-2], refs[-1]
    feats = w1.shape[0]
    core = jnp.bitwise_and(lax.axis_index("dp"), 1)
    bias_copy = pltpu.make_async_copy(b1, b1_v, sems.at[0])
    own = [pltpu.make_async_copy(w, other.at[0:feats], sems.at[1]) for w in (w1, w2)]
    copies = [
        pltpu.make_async_copy(sources[j], held[j], sems.at[2 + j]) for j in range(many)
    ]
    bias_copy.start()
    for j in range(2):
        pl.when(core == j)(own[j].start)
    for copy in copies:
        copy.start()
    bias_copy.wait()
    rest = row(b1_v)
    place = lax.broadcasted_iota(jnp.int32, (16, feats), 0)
    bias = jnp.zeros((16, feats), F32)
    for j in range(3):
        term = rest.astype(BF).astype(F32)
        bias = jnp.where(place == j, term, bias)
        rest = rest - term
    other[feats:, :] = bias.astype(BF)
    for j in range(2):
        pl.when(core == j)(own[j].wait)
    for copy in copies:
        copy.wait()


def attn_fwd_kernel(first, share, *refs):
    counts, post_s, postb_s, tok, og, n1g, n1b, qkvb, pre, post, postb, projb = refs[:12]
    gamma1, n2g, n2b, wqkv, wproj = refs[12:17]
    a1_o, q_o, k_o, v_o, p_o, o_o, x1_o, u_o, a2_o, dy_o, mpre, mpost, mixb = refs[-19:-6]
    pad, kk, attended_t, wide, logits, mixed = refs[-6:]
    images, patches, feats = tok.shape
    rows = pad.shape[0]
    heads = mpre.shape[0]
    head_dim = feats // heads
    slots = q_o.shape[1]

    spread = (
        head_of_lane((heads, feats), 1, head_dim)
        == lax.broadcasted_iota(jnp.int32, (heads, feats), 0)
    ).astype(F32)
    mpre[...] = exact(pre[...], spread, ((1,), (0,))) * head_dim**-0.5
    mpost[...] = exact(post[...], spread, ((0,), (0,)))
    mixb[...] = exact(row(postb), spread, ((1,), (0,)))

    @pl.loop(first, first + share)
    def _(i):
        pad[patches:, :] = jnp.zeros((rows - patches, feats), F32)
        live = (lax.axis_index("mp") * images + i < counts[0]).astype(F32)
        pad[0:patches, :] = og[i].astype(F32) * live
        dy_o[i] = pad[...].astype(BF)
        pad[0:patches, :] = tok[i].astype(F32)
        gain, shift = row(n1g), row(n1b)
        for c in chunks(rows):
            n, _ = normalized(pad[c, :])
            a1_o[i, c, :] = (n * gain + shift).astype(BF)
        wide[...] = nn(a1_o[i], wqkv[...])
        bias = row(qkvb)
        q_o[i, rows:] = jnp.zeros((slots - rows, feats), BF)
        for c in chunks(rows):
            q, k, v = (
                wide[c, j * feats : (j + 1) * feats] + bias[:, j * feats : (j + 1) * feats]
                for j in range(3)
            )
            q_o[i, c, :] = q.astype(BF)
            v_o[i, c, :] = v.astype(BF)
            k = k.astype(BF)
            k_o[i, c, :] = k
            kf = k.astype(F32)
            for g in range(heads):
                at = slice(g * rows + c.start, g * rows + c.stop)
                scaled = kf * mpre[g : g + 1, :]
                hi = scaled.astype(BF)
                kk[at, 0:feats] = hi
                kk[at, feats:] = (scaled - hi.astype(F32)).astype(BF)
        q2 = jnp.concatenate([q_o[i], q_o[i]], axis=1)
        vt = v_o[i].T
        many = heads // 2
        half = many * rows
        tail = patches // 8 * 8
        inside = lax.broadcasted_iota(jnp.int32, (rows - tail, 128), 0) < patches - tail
        real = (lax.broadcasted_iota(jnp.int32, (rows, 128), 0) < patches).astype(BF)
        start = nn(vt, real)
        for s in range(2):
            part = slice(s * half, (s + 1) * half)
            logits[part, :] = nt(kk[part, :], q2)
        for g in range(heads):
            for lane in range(0, slots, 128):
                x = logits[g * rows : (g + 1) * rows, lane : lane + 128]
                x = jnp.concatenate([x[0:tail], jnp.where(inside, x[tail:], -1e30)], axis=0)
                e = jnp.exp(x - jnp.max(x, axis=0, keepdims=True))
                inv = 1.0 / jnp.sum(e, axis=0, keepdims=True)
                p_o[i, g, :, lane : lane + 128] = (e * inv).astype(BF)
            mixed[g] = nn(vt, p_o[i, g])
        for c in chunks(feats):
            g = c.start // head_dim
            first = start[c] * postb_s[g]
            for lane in range(0, slots, 128):
                total = first
                for h in range(heads):
                    total = total + mixed[h, c, lane : lane + 128] * post_s[g, h]
                attended_t[c, lane : lane + 128] = total.astype(BF)
        o_o[i] = attended_t[...].T[0:rows]
        wide[:, 0:feats] = nn(o_o[i], wproj[...])
        bias, scale, gain, shift = row(projb), row(gamma1), row(n2g), row(n2b)
        for c in chunks(rows):
            u = wide[c, 0:feats] + bias
            x1 = pad[c, :] + scale * u
            u_o[i, c, :] = u
            x1_o[i, c, :] = x1
            n, _ = normalized(x1)
            a2_o[i, c, :] = (n * gain + shift).astype(BF)


def store_blocks(count, put):
    mine = lax.axis_index("dp")
    for core in range(2):

        @pl.when(jnp.bitwise_and(mine, 1) == core)
        def _(core=core):
            for b in range(count):
                place = jnp.bitwise_xor(jnp.int32(b >> 1), jnp.right_shift(mine, 1))
                put((b ^ core) & 1, place, b)


def mlp_units(a2, dfs, w1, b1, w2, hids, dzs, zs, ghs, units, store, use):
    size = a2.shape[0] // units
    width = w2.shape[0]
    lanes = zs.shape[2]
    places = [slice(u * size, (u + 1) * size) for u in range(units)]
    blocks = [(u, at) for u in range(units) for at in range(0, width, lanes)]

    def products(j):
        u, at = blocks[j]
        part = slice(at, at + lanes)
        zs[j % 2] = nn(a2[places[u], :], w1[:, part])
        ghs[j % 2] = nt(dfs[places[u], :], w2[part, :])

    def activation(j):
        u, at = blocks[j]
        part = slice(at, at + lanes)
        bias = b1[:, part]
        for c in chunks(size):
            zc = zs[j % 2, c, :] + bias
            phi, slope = gelu_parts(zc)
            rows = slice(places[u].start + c.start, places[u].start + c.stop)
            hids[rows, part] = (zc * phi).astype(BF)
            dzs[rows, part] = (ghs[j % 2, c, :] * slope).astype(BF)

    def finish(u):
        store(places[u], nn(hids[places[u], :], w2[...]), nt(dzs[places[u], :], w1[...]))

    products(0)
    for j, (u, at) in enumerate(blocks):
        if j + 1 < len(blocks):
            products(j + 1)
        if at == lanes and u > 0:
            finish(u - 1)
        activation(j)
        if at == 2 * lanes and u > 0:
            use(places[u - 1])
    finish(units - 1)
    use(places[units - 1])


def mlp_first_kernel(
    a2, dy, gamma2, w1_own, b1_own, w2_own, near, far,
    f_o, da2_o, hids, dzs, dfs,
    w1, w2, b1, zs, ghs,
):
    total, feats = f_o.shape
    w1[:, 0:feats] = w1_own[...]
    w2[0:feats, :] = w2_own[...]
    for core in range(2):

        @pl.when(jnp.bitwise_and(lax.axis_index("dp"), 1) == core)
        def _(core=core):
            one, two = (near, far) if core == 0 else (far, near)
            w1[:, feats:] = one[0, 0:feats]
            w2[feats:, :] = two[0, 0:feats]

    b1[:, 0:feats] = row(b1_own)
    b1[:, feats:] = colsum(near[0, feats : feats + 16].astype(F32))
    gain = row(gamma2)
    for c in chunks(total):
        dfs[c, :] = (dy[c, :].astype(F32) * gain).astype(BF)

    def store(rows, f, da2):
        f_o[rows, :] = f
        da2_o[rows, :] = da2

    mlp_units(a2, dfs, w1, b1, w2, hids, dzs, zs, ghs, 3, store, lambda rows: None)


def mlp_grad_kernel(a2, hids, dzs, dfs, grads, b1_o, a2t, dft):
    feats = a2.shape[1]
    a2t[0:feats, :] = a2[...].T
    a2t[feats:, :] = jnp.ones((a2t.shape[0] - feats, a2t.shape[1]), BF)
    dft[...] = dfs[...].T
    up = nn(a2t[...], dzs[...])
    b1_o[...] = up[feats : feats + 1]
    grads[0] = up[0:feats].astype(BF).T
    down = nn(dft[...], hids[...]).astype(BF)
    for c in range(2):
        grads[1, c * feats : (c + 1) * feats, :] = down[:, c * feats : (c + 1) * feats]


def mlp_rest_kernel(
    counts, a2, dy, dfs, x1, u, o, f0, da20, near, far, last, far_last, grads, a2t, dft, wproj,
    gamma1, n2g, fc2b, gamma2,
    out_o, dx1_o, do_o, keep, send, b1_o, acc_o,
    w1, w2, b1, hids, dzs, zs, ghs, fs, da2s, dus, ups, downs, projs, out_v, sems,
):
    total, feats = f0.shape
    images, patches = out_o.shape[:2]
    image_rows = total // images
    m_idx = lax.axis_index("mp")
    acc_o[...] = jnp.zeros_like(acc_o)
    b1[:, 0:feats] = colsum(near[1, feats : feats + 16].astype(F32))
    b1[:, feats:] = colsum(last[feats : feats + 16].astype(F32))
    for core in range(2):

        @pl.when(jnp.bitwise_and(lax.axis_index("dp"), 1) == core)
        def _(core=core):
            one, two = (near, far) if core == 0 else (far, near)
            w1[:, 0:feats] = one[1, 0:feats]
            w2[0:feats, :] = two[1, 0:feats]
            one, two = (last, far_last) if core == 0 else (far_last, last)
            w1[:, feats:] = one[0:feats]
            w2[feats:, :] = two[0:feats]

    gain2 = row(gamma2)
    bias, gain, scale = row(fc2b), row(n2g), row(gamma1)

    def out_copy(image):
        return pltpu.make_async_copy(out_v.at[image], out_o.at[image], sems.at[image])

    def store(rows, f, da2):
        fs[rows, :] = f
        da2s[rows, :] = da2

    def use(rows):
        sums = [jnp.zeros((8, feats), F32) for _ in range(6)]
        for c in chunks(rows.stop - rows.start):
            at = slice(rows.start + c.start, rows.start + c.stop)
            fc = fs[at, :] + f0[at, :] + bias
            dac = da2s[at, :] + da20[at, :]
            x1c = x1[at, :]
            dyc = dy[at, :].astype(F32)
            n, r = normalized(x1c)
            dx1 = dyc + norm_back(dac, n, r, gain)
            dx1_o[at, :] = dx1
            du = (dx1 * scale).astype(BF)
            dus[at, :] = du
            image = at.start // image_rows
            first = at.start - image * image_rows
            live = (m_idx * images + image < counts[0]).astype(F32)
            out = ((x1c + gain2 * fc) * live).astype(BF)
            if first + 16 <= patches:
                out_v[image, first : first + 16, :] = out
            else:
                out_v[image, first:patches, :] = out[0 : patches - first]
            terms = (
                du.astype(F32), u[at, :] * dx1, dac * n, dac, dfs[at, :].astype(F32), fc * dyc,
            )
            sums = [s + fold(t) for s, t in zip(sums, terms)]
        for j in range(6):
            acc_o[j : j + 1, :] += colsum(sums[j])
        do = nt(dus[rows, :], wproj[...]).astype(BF)
        for at in range(0, rows.stop - rows.start, image_rows):
            image = (rows.start + at) // image_rows
            out_copy(image).start()
            do_o[image, 0:image_rows] = do[at : at + image_rows]
            do_o[image, image_rows:] = jnp.zeros((do_o.shape[1] - image_rows, feats), BF)

    mlp_units(a2, dfs, w1, b1, w2, hids, dzs, zs, ghs, 3, store, use)
    up = nn(a2t[...], dzs[...])
    b1_o[...] = up[feats : feats + 1]
    ups[...] = up[0:feats].astype(BF).T
    downs[...] = nn(dft[...], hids[...]).astype(BF)
    projs[...] = tn(dus[...], o[...]).astype(BF)
    count = 2 * keep.shape[0]
    size = feats // count
    outs = (keep, send)

    def put(which, place, b):
        out = outs[which]
        for c in range(2):
            part = slice(c * feats, (c + 1) * feats)
            up = slice(c * feats + b * size, c * feats + (b + 1) * size)
            down = slice(b * size, (b + 1) * size)
            pieces = (grads[0, up, :], grads[1, up, :])
            for j, piece in enumerate(pieces):
                out[place, (2 * c + j) * size : (2 * c + j + 1) * size, :] = piece
            pieces = (ups[up, :], downs[down, part])
            for j, piece in enumerate(pieces):
                out[place, (4 + 2 * c + j) * size : (5 + 2 * c + j) * size, :] = piece
        out[place, 8 * size : 9 * size, :] = projs[b * size : (b + 1) * size, :]

    store_blocks(count, put)
    for image in range(images):
        out_copy(image).wait()


def attn_bwd_kernel(first, share, *refs):
    pre_s, do_r, q_r, k_r, v_r, p_r, dx1, tok, mpre, mpost, mixb, wqkv, n1g = refs[:13]
    if first:
        before, in_o = refs[14], refs[-13]
        dqkv_o, acc_o = refs[-14], refs[-12]
        vgs, dls, dq_t, dps, dvs, dks, dqs, da1, pad, in_v, sems = refs[-11:]
    else:
        dqkv_o, in_v, acc_o, vgs, dls, dq_t, dps, dvs, dks, dqs, da1, pad = refs[-12:]
    slots, feats = do_r.shape[1:]
    patches = tok.shape[1]
    rows = k_r.shape[1]
    heads = mpre.shape[0]
    head_dim = feats // heads
    acc_o[...] = jnp.zeros_like(acc_o)

    def in_copy(i):
        return pltpu.make_async_copy(in_v.at[i - first], in_o.at[i], sems.at[i])

    def early_copy(i):
        return pltpu.make_async_copy(before.at[i], in_o.at[i], sems.at[i])

    for i in range(first):
        early_copy(i).start()

    @pl.loop(first, first + share)
    def _(i):
        do_sum = jnp.zeros((8, feats), F32)
        for c in chunks(rows):
            do_sum = do_sum + fold(do_r[i, c, :].astype(F32))
        do_sum = colsum(do_sum)
        q = q_r[i]
        do = do_r[i]
        kt = k_r[i].T

        def products(pair):
            for c in chunks(rows):
                vf = v_r[i, c, :].astype(F32)
                for h in pair:
                    at = slice(h * rows + c.start, h * rows + c.stop)
                    vgs[at, :] = (vf * mpost[h : h + 1, :]).astype(BF)
            part = slice(pair[0] * rows, (pair[1] + 1) * rows)
            dps[part, :] = nt(vgs[part, :], do)
            dvs[part, :] = nn(p_r[i, pair[0] : pair[1] + 1].reshape(2 * rows, slots), do)

        products((0, 1))
        for h in range(heads):
            if h % 2 == 0 and h + 2 < heads:
                products((h + 2, h + 3))
            at = slice(h * rows, (h + 1) * rows)
            for lane in range(0, slots, 128):
                dp = dps[at, lane : lane + 128]
                pf = p_r[i, h, :, lane : lane + 128].astype(F32)
                mean = jnp.sum(dp * pf, axis=0, keepdims=True) / jnp.sum(
                    pf, axis=0, keepdims=True
                )
                dls[at, lane : lane + 128] = (pf * (dp - mean)).astype(BF)
            dqs[h] = nn(kt, dls[at, :])
            if h % 2 == 1:
                part = slice((h - 1) * rows, (h + 1) * rows)
                dks[part, :] = nn(dls[part, :], q)

        bias_row = mixb[...] * do_sum
        v_sum = jnp.zeros((8, feats), F32)
        dv_sum = jnp.zeros((8, feats), F32)
        sums = [jnp.zeros((8, feats), F32) for _ in range(heads)]
        for c in chunks(rows):
            vf = v_r[i, c, :].astype(F32)
            dv = bias_row
            for h in range(heads):
                this = dvs[h * rows + c.start : h * rows + c.stop, :]
                dv = dv + this * mpost[h : h + 1, :]
                sums[h] = sums[h] + fold(vf * this)
            if c.stop > patches:
                inside = lax.broadcasted_iota(jnp.int32, dv.shape, 0) < patches - c.start
                dv = jnp.where(inside, dv, 0.0)
                vf = jnp.where(inside, vf, 0.0)
            low = dv.astype(BF)
            dqkv_o[i, c, 2 * feats :] = low
            dv_sum = dv_sum + fold(low.astype(F32))
            v_sum = v_sum + fold(vf)
        for h in range(heads):
            acc_o[h : h + 1, :] += colsum(sums[h])
        acc_o[2 * heads : 2 * heads + 1, :] += do_sum * colsum(v_sum)
        acc_o[2 * heads + 10 : 2 * heads + 11, :] += colsum(dv_sum)

        for c in chunks(feats):
            g = c.start // head_dim
            for lane in range(0, slots, 128):
                total = 0.0
                for h in range(heads):
                    total = total + dqs[h, c, lane : lane + 128] * pre_s[h, g]
                dq_t[c, lane : lane + 128] = (total * head_dim**-0.5).astype(BF)
        dq = dq_t[...].T[0:rows]
        dqkv_o[i, :, 0:feats] = dq
        dk_sum = jnp.zeros((8, feats), F32)
        sums = [jnp.zeros((8, feats), F32) for _ in range(heads)]
        for c in chunks(rows):
            kf = k_r[i, c, :].astype(F32)
            dk = 0.0
            for h in range(heads):
                this = dks[h * rows + c.start : h * rows + c.stop, :]
                dk = dk + this * mpre[h : h + 1, :]
                sums[h] = sums[h] + fold(kf * this)
            low = dk.astype(BF)
            dqkv_o[i, c, feats : 2 * feats] = low
            dk_sum = dk_sum + fold(low.astype(F32))
        for h in range(heads):
            acc_o[heads + h : heads + h + 1, :] += colsum(sums[h])
        acc_o[2 * heads + 8 : 2 * heads + 9, :] += colsum(dq.astype(F32))
        acc_o[2 * heads + 9 : 2 * heads + 10, :] += colsum(dk_sum)

        pad[patches:, :] = jnp.zeros((rows - patches, feats), F32)
        pad[0:patches, :] = tok[i].astype(F32)
        da1[...] = nt(dqkv_o[i], wqkv[...])
        gain = row(n1g)
        sums = [jnp.zeros((8, feats), F32) for _ in range(2)]
        for c in chunks(rows):
            n, r = normalized(pad[c, :])
            cot = da1[c, :]
            grad = dx1[i, c, :] + norm_back(cot, n, r, gain)
            sums = [sums[0] + fold(cot * n), sums[1] + fold(cot)]
            if c.stop <= patches:
                in_v[i - first, c, :] = grad
            else:
                in_v[i - first, c.start : patches, :] = grad[0 : patches - c.start]
        for j in range(2):
            acc_o[2 * heads + 11 + j : 2 * heads + 12 + j, :] += colsum(sums[j])
        if first:
            in_copy(i).start()

    if first:
        for i in range(first):
            early_copy(i).wait()

        @pl.loop(first, first + share)
        def _(i):
            in_copy(i).wait()


def qkv_grad_kernel(heads, dqkv, *refs):
    accs = refs[:-8]
    a1, acc_mlp, b1_first, b1_rest, keep, send, small, grads = refs[-8:]
    feats = a1.shape[1]
    count = 2 * keep.shape[0]
    size = 3 * feats // count
    acc = accs[0][...]
    for other in accs[1:]:
        acc = acc + other[...]
    small[...] = jnp.zeros_like(small)
    small[0:2, :] = acc[2 * heads + 11 : 2 * heads + 13]
    small[2:8, :] = acc_mlp[0:6, :]
    small[8:11, :] = acc[2 * heads + 8 : 2 * heads + 11]
    head_dim = feats // heads
    lanes = 2 * heads * heads
    gather = (
        head_of_lane((feats, lanes), 0, head_dim)
        == lax.broadcasted_iota(jnp.int32, (feats, lanes), 1) % heads
    ).astype(F32)
    sums = exact(acc[0 : 2 * heads + 8], gather, ((1,), (0,)))
    place = head_of_lane((2 * heads, lanes), 1, heads) == lax.broadcasted_iota(
        jnp.int32, (2 * heads, lanes), 0
    )
    small[11:12, 0:lanes] = colsum(jnp.where(place, sums[0 : 2 * heads], 0.0))
    small[11:12, lanes : 2 * lanes] = sums[2 * heads : 2 * heads + 1]
    m_idx = lax.axis_index("mp")
    for c, ref in enumerate((b1_first, b1_first, b1_rest, b1_rest)):
        place = 12 + jnp.bitwise_xor(m_idx, c)
        small[pl.ds(place, 1), :] = ref[:, (c % 2) * feats : (c % 2 + 1) * feats]
    low = small[...].astype(BF)
    outs = (keep, send)

    grads[...] = tn(a1[...], dqkv[...]).astype(BF).T

    def put(which, place, b):
        outs[which][place, 0:size, :] = grads[b * size : (b + 1) * size, :]
        outs[which][place, size : size + 16, :] = low
        if outs[which].shape[1] > size + 16:
            outs[which][place, size + 16 :, :] = jnp.zeros_like(outs[which][place, size + 16 :, :])

    store_blocks(count, put)


def final_kernel(heads, size, many, mine, proj_own, *refs):
    got = refs[:many]
    mlp_mine, got_z = refs[many], refs[1 + many : 1 + 2 * many]
    qkv_o, qkvb_o, pre_o, post_o, postb_o, b1_o, *vecs_o, fc1_o, fc2_o, proj_o, held = refs[-18:]
    block, feats = fc1_o.shape
    for place, out in enumerate((fc1_o, fc2_o)):
        rows = slice(place * block, (place + 1) * block)
        out[...] = mlp_mine[rows, :] + sum(g[rows, :].astype(F32) for g in got_z)
    d_idx = lax.axis_index("dp")
    m_idx = lax.axis_index("mp")
    total = mine[...]
    held[m_idx] = proj_own[...].astype(F32)
    for j, part in enumerate(got):
        value = part[...].astype(F32)
        total = total + value[0 : size + 16]
        held[jnp.bitwise_xor(m_idx, j + 1)] = value[size + 16 :]
    proj_o[...] = held[...].reshape(-1, feats)[0:block]
    qkv_o[...] = total[0:size]
    small = total[size : size + 16]

    def own(value, width, index):
        lanes = value.shape[1]
        return pltpu.roll(value, lax.rem(lanes - index * width, lanes), axis=1)[:, 0:width]

    width = vecs_o[0].shape[1]
    vecs = own(small[0:8], width, d_idx)
    for j, ref in enumerate(vecs_o):
        ref[...] = vecs[j : j + 1]
    flat = jnp.concatenate([small[8 + j : 9 + j] for j in range(3)], axis=1)
    qkvb_o[...] = own(jnp.broadcast_to(flat, (8, 3 * feats)), qkvb_o.shape[1], d_idx)[0:1]
    b1 = own(small[8:16], b1_o.shape[1], d_idx)[4:8]
    pick = lax.broadcasted_iota(jnp.int32, b1.shape, 0) == m_idx
    b1_o[...] = colsum(jnp.where(pick, b1, 0.0))
    mix = small[11:12]
    hh = heads * heads
    line = lax.broadcasted_iota(jnp.int32, (heads, hh), 0)
    lane = lax.broadcasted_iota(jnp.int32, (heads, hh), 1)
    fold = (
        lax.broadcasted_iota(jnp.int32, (hh, heads), 0) % heads
        == lax.broadcasted_iota(jnp.int32, (hh, heads), 1)
    ).astype(F32)
    head_dim = feats // heads

    def square(values):
        return exact(jnp.where(lane // heads == line, values, 0.0), fold, ((1,), (0,)))

    post_o[...] = square(mix[:, 0:hh]).T
    pre_o[...] = square(mix[:, hh : 2 * hh]) * (head_dim**-0.5)
    postb_o[...] = mix[:, 2 * hh : 2 * hh + heads]


def whole(shape):
    return pl.BlockSpec(shape, lambda i: (0,) * len(shape))


def each(shape, first=0, many=1):
    return pl.BlockSpec((many,) + shape[1:], lambda i: (i + first,) + (0,) * (len(shape) - 1))


SCALARS = pl.BlockSpec(memory_space=pltpu.SMEM)
IN_VMEM = pl.BlockSpec(memory_space=pltpu.VMEM)
IN_HBM = pl.BlockSpec(memory_space=pltpu.HBM)


def kept(a):
    return pltpu.with_memory_space_constraint(a, pltpu.HBM)


def sds(shape, dtype):
    return jax.ShapeDtypeStruct(shape, dtype)


def call(
    kernel, grid, ins, in_specs, outs, out_specs, scratch=(), flops=0, name=None, aliases=None,
    limit=VMEM_LIMIT,
):
    size = lambda a: a.size * a.dtype.itemsize
    return pl.pallas_call(
        kernel,
        grid=grid,
        in_specs=in_specs,
        out_specs=out_specs,
        out_shape=outs,
        scratch_shapes=scratch,
        input_output_aliases=aliases or {},
        compiler_params=pltpu.CompilerParams(vmem_limit_bytes=limit),
        cost_estimate=pl.CostEstimate(
            flops=flops,
            bytes_accessed=sum(size(a) for a in ins) + sum(size(a) for a in outs),
            transcendentals=0,
        ),
        name=name,
    )(*ins)


def xor_perm(count, mask):
    return [(j, j ^ mask) for j in range(count)]


def dp_hops(dp):
    bits = dp.bit_length() - 1
    groups = []
    at = 1
    while at < bits:
        groups.append((at, min(2, bits - at)))
        at += groups[-1][1]
    return groups


def dp_scatter(value, dp):
    for at, many in dp_hops(dp):
        value = value.reshape((-1, 1 << many) + value.shape[1:])
        got = [
            lax.ppermute(value[:, j].astype(BF), "dp", xor_perm(dp, j << at))
            for j in range(1, 1 << many)
        ]
        value = value[:, 0] + sum(g.astype(F32) for g in got)
    return value.reshape(value.shape[-2:])


def per_device(
    dp, mp,
    tokens_in, image_counts, norm1_gain, norm1_bias, qkv_weight, qkv_bias,
    mix_pre, mix_post, mix_post_bias, proj_weight, proj_bias, gamma1,
    norm2_gain, norm2_bias, fc1_weight, fc1_bias, fc2_weight, fc2_bias, gamma2, out_grad,
):
    images, patches, feats = tokens_in.shape
    heads = mix_pre.shape[0]
    rows = -(-patches // 16) * 16
    slots = -(-patches // 128) * 128
    hidden = fc1_weight.shape[1]
    tok_rows = (images, rows, feats)
    slot_rows = (images, slots, feats)
    prob_shape = (images, heads, rows, slots)
    mix_shape = (heads, feats)
    operands = [
        tokens_in, out_grad, norm1_gain, norm1_bias, qkv_bias, mix_pre, mix_post,
        mix_post_bias, proj_bias, gamma1, norm2_gain, norm2_bias, qkv_weight, proj_weight,
    ]

    ins = [kept(a) for a in [fc1_weight, fc2_weight, fc1_bias] + operands]
    outs = [sds((feats + 16, hidden), BF)] + [sds(a.shape, a.dtype) for a in operands]
    other, *held = call(
        pack_kernel,
        (),
        ins,
        [IN_HBM] * len(ins),
        outs,
        [IN_VMEM] * len(outs),
        [pltpu.VMEM(fc1_bias.shape, F32), pltpu.SemaphoreType.DMA((2 + len(operands),))],
        name="pack",
    )
    near = [lax.ppermute(other, "mp", xor_perm(mp, j)) for j in (1, 2)]

    shares = [images - 1, 1] if images > 1 else [images]
    carried = []
    for s, share in enumerate(shares):
        first = sum(shares[:s])
        ins = [image_counts, mix_post, mix_post_bias] + held
        outs = call(
            functools.partial(attn_fwd_kernel, first, share),
            (),
            ins + carried,
            [SCALARS] * 3
            + [IN_VMEM] * 14
            + [pl.BlockSpec(memory_space=pl.ANY)] * len(carried),
            [
                sds(tok_rows, BF), sds(slot_rows, BF), sds(tok_rows, BF), sds(tok_rows, BF),
                sds(prob_shape, BF), sds(tok_rows, BF), sds(tok_rows, F32), sds(tok_rows, F32),
                sds(tok_rows, BF), sds(tok_rows, BF), sds(mix_shape, F32), sds(mix_shape, F32),
                sds((1, feats), F32),
            ],
            [IN_VMEM] * 13,
            [
                pltpu.VMEM((rows, feats), F32), pltpu.VMEM((heads * rows, 2 * feats), BF),
                pltpu.VMEM((feats, slots), BF), pltpu.VMEM((rows, 3 * feats), F32), pltpu.VMEM((heads * rows, slots), F32),
                pltpu.VMEM((heads, feats, slots), F32),
            ],
            flops=share * 15 * 10**8,
            name="attn_fwd",
            aliases={len(ins) + j: j for j in range(10)} if carried else None,
        )
        carried, (mpre, mpost, mixb) = list(outs[:10]), outs[10:]
        if s == 0:
            near, carried[0] = lax.optimization_barrier((near, carried[0]))
            last = lax.ppermute(near[1], "mp", xor_perm(mp, 1))
            near = jnp.stack(near)
            far = lax.ppermute(near, "dp", xor_perm(dp, 1))
    a1, q, k, v, prob, o, x1, u, a2, dy = carried
    far, a2 = lax.optimization_barrier((far, a2))

    block = feats // dp
    total = images * rows
    flat = (total, feats)
    a2, dy, x1, u, o = (a.reshape(flat) for a in (a2, dy, x1, u, o))
    ins = [a2, dy, gamma2, fc1_weight, fc1_bias, fc2_weight, near, far]
    wide = 2 * hidden
    grad_shape = (2, wide, feats)
    f0, da20, hids, dzs, dfs = call(
        mlp_first_kernel,
        (),
        ins,
        [IN_VMEM] * len(ins),
        [
            sds(flat, F32), sds(flat, F32), sds((total, wide), BF), sds((total, wide), BF),
            sds(flat, BF),
        ],
        [IN_VMEM] * 5,
        [
            pltpu.VMEM((feats, wide), BF), pltpu.VMEM((wide, feats), BF),
            pltpu.VMEM((1, wide), F32),
            pltpu.VMEM((2, total // 3, 256), F32), pltpu.VMEM((2, total // 3, 256), F32),
        ],
        flops=images * 5 * 10**8,
        name="mlp_first",
    )

    last, f0 = lax.optimization_barrier((last, f0))
    far_last = lax.ppermute(last, "dp", xor_perm(dp, 1))
    ins = [a2, hids, dzs, dfs]
    grads0, b1_0, a2t, dft = call(
        mlp_grad_kernel,
        (),
        ins,
        [IN_VMEM] * 4,
        [
            sds(grad_shape, BF), sds((1, wide), F32), sds((feats + 16, total), BF),
            sds((feats, total), BF),
        ],
        [IN_VMEM] * 4,
        flops=images * 3 * 10**8,
        name="mlp_grad",
    )

    grad_rows = 9 * block
    half_shape = (dp // 2, grad_rows, feats)
    ins = [
        image_counts, a2, dy, dfs, x1, u, o, f0, da20, near, far, last, far_last, grads0, a2t, dft,
        proj_weight, gamma1,
        norm2_gain, fc2_bias, gamma2,
    ]
    layer_out, dx1, do, keep, send, b1_1, acc_mlp = call(
        mlp_rest_kernel,
        (),
        ins,
        [SCALARS] + [IN_VMEM] * (len(ins) - 1),
        [
            sds(tokens_in.shape, BF), sds(flat, F32), sds(slot_rows, BF), sds(half_shape, BF),
            sds(half_shape, BF), sds((1, wide), F32), sds((8, feats), F32),
        ],
        [IN_HBM] + [IN_VMEM] * 6,
        [
            pltpu.VMEM((feats, wide), BF), pltpu.VMEM((wide, feats), BF),
            pltpu.VMEM((1, wide), F32), pltpu.VMEM((total, wide), BF),
            pltpu.VMEM((total, wide), BF),
            pltpu.VMEM((2, total // 3, 256), F32), pltpu.VMEM((2, total // 3, 256), F32),
            pltpu.VMEM(flat, F32), pltpu.VMEM(flat, F32), pltpu.VMEM(flat, BF),
            pltpu.VMEM((wide, feats), BF), pltpu.VMEM((feats, wide), BF),
            pltpu.VMEM((feats, feats), BF), pltpu.VMEM(tokens_in.shape, BF),
            pltpu.SemaphoreType.DMA((images,)),
        ],
        flops=images * 9 * 10**8,
        name="mlp_rest",
    )
    got = lax.ppermute(send, "dp", xor_perm(dp, 1))
    dx1 = dx1.reshape(tok_rows)

    shares = [1, images - 1] if images > 1 else [1]
    dqkv_shape = (images, rows, 3 * feats)
    carried, accs = [], []
    for s, share in enumerate(shares):
        first = sum(shares[:s])
        ins = [mix_pre, do, q, k, v, prob, dx1, tokens_in, mpre, mpost, mixb, qkv_weight, norm1_gain]
        in_shape = tokens_in.shape if first or share == images else (share,) + tokens_in.shape[1:]
        *carried, acc = call(
            functools.partial(attn_bwd_kernel, first, share),
            (),
            ins + carried,
            [SCALARS]
            + [IN_VMEM] * (len(ins) - 1)
            + [pl.BlockSpec(memory_space=pl.ANY), IN_VMEM][: len(carried)],
            [sds(dqkv_shape, BF), sds(in_shape, F32), sds((2 * heads + 16, feats), F32)],
            [IN_VMEM, IN_HBM if first else IN_VMEM, IN_VMEM],
            [
                pltpu.VMEM((heads * rows, feats), BF), pltpu.VMEM((heads * rows, slots), BF),
                pltpu.VMEM((feats, slots), BF), pltpu.VMEM((heads * rows, slots), F32),
                pltpu.VMEM((heads * rows, feats), F32), pltpu.VMEM((heads * rows, feats), F32),
                pltpu.VMEM((heads, feats, slots), F32), pltpu.VMEM((rows, feats), F32),
                pltpu.VMEM((rows, feats), F32),
            ]
            + [pltpu.VMEM((share, patches, feats), F32), pltpu.SemaphoreType.DMA((images,))]
            * bool(first),
            flops=share * 20 * 10**8,
            name="attn_bwd",
            aliases={len(ins): 0} if carried else None,
        )
        accs.append(acc)
        if s == 0:
            (keep, got), acc = lax.optimization_barrier(((keep, got), acc))
            mine = dp_scatter(keep.astype(F32) + got.astype(F32), dp)
            accs[0], do = lax.optimization_barrier((acc, do))
    dqkv, in_grad = carried
    mine, dqkv = lax.optimization_barrier((mine, dqkv))
    mlp_mine = mine
    low = mine.astype(BF)
    m_idx = lax.axis_index("mp")
    share_rows = -(-block // (16 * mp)) * 16
    proj = jnp.pad(mine[8 * block :], ((0, mp * share_rows - block), (0, 0)))

    def proj_share(j):
        return lax.dynamic_slice_in_dim(proj, jnp.bitwise_xor(m_idx, j) * share_rows, share_rows)

    got_z = [
        lax.ppermute(
            jnp.concatenate([low[2 * j * block : 2 * (j + 1) * block], proj_share(j).astype(BF)]),
            "mp",
            xor_perm(mp, j),
        )
        for j in range(1, mp)
    ]

    q_block = 3 * feats // dp
    half_shape = (dp // 2, q_block + 16, feats)
    ins = [dqkv.reshape(total, 3 * feats)] + accs + [a1.reshape(flat), acc_mlp, b1_0, b1_1]
    keep, send = call(
        functools.partial(qkv_grad_kernel, heads),
        (),
        ins,
        [IN_VMEM] * len(ins),
        [sds(half_shape, BF), sds(half_shape, BF)],
        [IN_VMEM] * 2,
        [pltpu.VMEM((16, feats), F32), pltpu.VMEM((3 * feats, feats), BF)],
        flops=11 * 10**8,
        name="qkv_grad",
    )
    got = lax.ppermute(send, "dp", xor_perm(dp, 1))
    mine = dp_scatter(keep.astype(F32) + got.astype(F32), dp)
    mine, got_z = lax.optimization_barrier((mine, got_z))

    proj_own = (proj_share(0) + sum(g[2 * block :].astype(F32) for g in got_z)).astype(BF)
    payload = jnp.concatenate([mine.astype(BF), proj_own])
    got = [lax.ppermute(payload, "mp", xor_perm(mp, j)) for j in range(1, mp)]
    b1_size = hidden // dp
    ins = [mine, proj_own] + got + [mlp_mine] + got_z
    outs = [
        sds((q_block, feats), F32), sds((1, q_block), F32), sds((heads, heads), F32),
        sds((heads, heads), F32), sds((1, heads), F32), sds((1, b1_size), F32),
    ] + [sds((1, block), F32)] * 8 + [sds((block, feats), F32)] * 3
    qkvw, qkvb, pre, post, postb, b1g, *vecs, fc1g, fc2g, projg = call(
        functools.partial(final_kernel, heads, q_block, mp - 1),
        (),
        ins,
        [IN_VMEM] * len(ins),
        outs,
        [IN_VMEM] * len(outs),
        [pltpu.VMEM((mp, share_rows, feats), F32)],
        name="final",
    )
    vecs = [a.reshape(-1) for a in vecs]
    return (
        layer_out,
        in_grad,
        vecs[0],
        vecs[1],
        qkvw.T,
        qkvb.reshape(-1),
        pre,
        post,
        postb.reshape(-1),
        projg.T,
        vecs[2],
        vecs[3],
        vecs[4],
        vecs[5],
        fc1g.T,
        b1g.reshape(-1),
        fc2g.T,
        vecs[6],
        vecs[7],
    )


def solution(mesh):
    tokens = P(("dp", "mp"), None, None)
    placed = (
        (tokens, P("dp")) + (P(),) * 12 + (P(None, "mp"), P("mp"), P("mp", None), P(), P(), tokens)
    )
    return jax.shard_map(
        functools.partial(per_device, mesh.shape["dp"], mesh.shape["mp"]),
        mesh=mesh,
        in_specs=placed,
        out_specs=(
            tokens, tokens, P("dp"), P("dp"), P(None, "dp"), P("dp"), P(), P(), P(),
            P(None, "dp"), P("dp"), P("dp"), P("dp"), P("dp"), P(None, ("mp", "dp")),
            P(("mp", "dp")), P("mp", "dp"), P("dp"), P("dp"),
        ),
        check_vma=False,
    )
```

```python
import functools

import jax
import jax.numpy as jnp
from jax import lax
from jax.experimental import pallas as pl
from jax.experimental.pallas import tpu as pltpu
from jax.sharding import PartitionSpec as P

BF = jnp.bfloat16
F32 = jnp.float32
LOG2E = 1.4426950408889634
EPS = 1e-06
VMEM_LIMIT = 20 * 1024 * 1024


def nn(a, b):
    return lax.dot_general(a, b, (((1,), (0,)), ((), ())), preferred_element_type=F32)


def nt(a, b):
    return lax.dot_general(a, b, (((1,), (1,)), ((), ())), preferred_element_type=F32)


def tn(a, b):
    return lax.dot_general(a, b, (((0,), (0,)), ((), ())), preferred_element_type=F32)


def exact(a, b, dims):
    return lax.dot_general(
        a, b, (dims, ((), ())), precision=lax.Precision.HIGHEST, preferred_element_type=F32
    )


def normalized(x):
    mean = jnp.mean(x, axis=-1, keepdims=True)
    c = x - mean
    r = lax.rsqrt(jnp.mean(c * c, axis=-1, keepdims=True) + EPS)
    return c * r, r


def norm_back(cot, n, r, gain):
    cg = cot * gain
    return r * (
        cg
        - jnp.mean(cg, axis=-1, keepdims=True)
        - n * jnp.mean(cg * n, axis=-1, keepdims=True)
    )


def colsum(x):
    return jnp.sum(x, axis=0, keepdims=True)


def split(x):
    hi = x.astype(BF)
    return jnp.concatenate([hi, (x - hi.astype(F32)).astype(BF)], axis=1)


def row(ref):
    return ref[...].reshape(1, ref.shape[0])


def gelu_parts(z):
    e = jnp.exp2(z * z * (-0.5 * LOG2E))
    t = pl.reciprocal(1.0 + jnp.abs(z) * (0.3275911 * 0.7071067811865476), approx=True)
    poly = t * (
        0.5 * 0.254829592
        + t
        * (
            0.5 * -0.284496736
            + t * (0.5 * 1.421413741 + t * (0.5 * -1.453152027 + t * (0.5 * 1.061405429)))
        )
    )
    tail = poly * e
    phi = jnp.where(z >= 0, 1.0 - tail, tail)
    return phi, phi + z * e * 0.3989422804014327


def head_of_lane(shape, axis, head_dim):
    return lax.broadcasted_iota(jnp.int32, shape, axis) // head_dim


def chunks(count, size=16):
    return [slice(at, at + size) for at in range(0, count, size)]


def fold(x):
    return sum(x[at : at + 8] for at in range(8, x.shape[0], 8)) + x[0:8]


def pack_kernel(w1, w2, b1, *refs):
    many = (len(refs) - 3) // 2
    sources, other, held, b1_v, sems = refs[:many], refs[many], refs[many + 1 : -2], refs[-2], refs[-1]
    feats = w1.shape[0]
    core = jnp.bitwise_and(lax.axis_index("dp"), 1)
    bias_copy = pltpu.make_async_copy(b1, b1_v, sems.at[0])
    own = [pltpu.make_async_copy(w, other.at[0:feats], sems.at[1]) for w in (w1, w2)]
    copies = [
        pltpu.make_async_copy(sources[j], held[j], sems.at[2 + j]) for j in range(many)
    ]
    bias_copy.start()
    for j in range(2):
        pl.when(core == j)(own[j].start)
    for copy in copies:
        copy.start()
    bias_copy.wait()
    rest = row(b1_v)
    place = lax.broadcasted_iota(jnp.int32, (16, feats), 0)
    bias = jnp.zeros((16, feats), F32)
    for j in range(3):
        term = rest.astype(BF).astype(F32)
        bias = jnp.where(place == j, term, bias)
        rest = rest - term
    other[feats:, :] = bias.astype(BF)
    for j in range(2):
        pl.when(core == j)(own[j].wait)
    for copy in copies:
        copy.wait()


def attn_fwd_kernel(first, share, *refs):
    counts, post_s, postb_s, tok, og, n1g, n1b, qkvb, pre, post, postb, projb = refs[:12]
    gamma1, n2g, n2b, wqkv, wproj = refs[12:17]
    if first:
        mpre = refs[17]
        a1_o, q_o, k_o, v_o, p_o, o_o, x1_o, u_o, a2_o, dy_o = refs[-16:-6]
    else:
        a1_o, q_o, k_o, v_o, p_o, o_o, x1_o, u_o, a2_o, dy_o, mpre, mpost, mixb = refs[-19:-6]
    pad, kk, attended_t, wide, logits, mixed = refs[-6:]
    images, patches, feats = tok.shape
    rows = pad.shape[0]
    heads = mpre.shape[0]
    head_dim = feats // heads
    slots = q_o.shape[1]

    if not first:
        spread = (
            head_of_lane((heads, feats), 1, head_dim)
            == lax.broadcasted_iota(jnp.int32, (heads, feats), 0)
        ).astype(F32)
        mpre[...] = exact(pre[...], spread, ((1,), (0,))) * (head_dim**-0.5 * LOG2E)
        mpost[...] = exact(post[...], spread, ((0,), (0,)))
        mixb[...] = exact(row(postb), spread, ((1,), (0,)))

    @pl.loop(first, first + share)
    def _(i):
        pad[patches:, :] = jnp.zeros((rows - patches, feats), F32)
        live = (lax.axis_index("mp") * images + i < counts[0]).astype(F32)
        pad[0:patches, :] = og[i].astype(F32) * live
        dy_o[i] = pad[...].astype(BF)
        pad[0:patches, :] = tok[i].astype(F32)
        gain, shift = row(n1g), row(n1b)
        for c in chunks(rows):
            n, _ = normalized(pad[c, :])
            a1_o[i, c, :] = (n * gain + shift).astype(BF)
        wide[...] = nn(a1_o[i], wqkv[...])
        bias = row(qkvb)
        q_o[i, rows:] = jnp.zeros((slots - rows, feats), BF)
        for c in chunks(rows):
            q, k, v = (
                wide[c, j * feats : (j + 1) * feats] + bias[:, j * feats : (j + 1) * feats]
                for j in range(3)
            )
            q_o[i, c, :] = q.astype(BF)
            v_o[i, c, :] = v.astype(BF)
            k = k.astype(BF)
            k_o[i, c, :] = k
            kf = k.astype(F32)
            for g in range(heads):
                at = slice(g * rows + c.start, g * rows + c.stop)
                scaled = kf * mpre[g : g + 1, :]
                hi = scaled.astype(BF)
                kk[at, 0:feats] = hi
                kk[at, feats:] = (scaled - hi.astype(F32)).astype(BF)
        q2 = jnp.concatenate([q_o[i], q_o[i]], axis=1)
        vt = v_o[i].T
        many = heads // 2
        half = many * rows
        tail = patches // 8 * 8
        inside = lax.broadcasted_iota(jnp.int32, (rows - tail, 128), 0) < patches - tail
        real = (lax.broadcasted_iota(jnp.int32, (rows, 128), 0) < patches).astype(BF)
        start = nn(vt, real)
        for s in range(2):
            part = slice(s * half, (s + 1) * half)
            logits[part, :] = nt(kk[part, :], q2)
        for g in range(heads):
            for lane in range(0, slots, 128):
                x = logits[g * rows : (g + 1) * rows, lane : lane + 128]
                x = jnp.concatenate([x[0:tail], jnp.where(inside, x[tail:], -1e30)], axis=0)
                e = jnp.exp2(x - jnp.max(x, axis=0, keepdims=True))
                inv = 1.0 / jnp.sum(e, axis=0, keepdims=True)
                p_o[i, g, :, lane : lane + 128] = (e * inv).astype(BF)
            mixed[g] = nn(vt, p_o[i, g])
        for c in chunks(feats):
            g = c.start // head_dim
            first = start[c] * postb_s[g]
            for lane in range(0, slots, 128):
                total = first
                for h in range(heads):
                    total = total + mixed[h, c, lane : lane + 128] * post_s[g, h]
                attended_t[c, lane : lane + 128] = total.astype(BF)
        o_o[i] = attended_t[...].T[0:rows]
        wide[:, 0:feats] = nn(o_o[i], wproj[...])
        bias, scale, gain, shift = row(projb), row(gamma1), row(n2g), row(n2b)
        for c in chunks(rows):
            u = wide[c, 0:feats] + bias
            x1 = pad[c, :] + scale * u
            u_o[i, c, :] = u
            x1_o[i, c, :] = x1
            n, _ = normalized(x1)
            a2_o[i, c, :] = (n * gain + shift).astype(BF)


def store_blocks(count, put):
    mine = lax.axis_index("dp")
    for core in range(2):

        @pl.when(jnp.bitwise_and(mine, 1) == core)
        def _(core=core):
            for b in range(count):
                place = jnp.bitwise_xor(jnp.int32(b >> 1), jnp.right_shift(mine, 1))
                put((b ^ core) & 1, place, b)


def mlp_units(a2, dfs, w1, b1, w2, hids, dzs, zs, ghs, units, store, use):
    size = a2.shape[0] // units
    width = w2.shape[0]
    lanes = zs.shape[2]
    places = [slice(u * size, (u + 1) * size) for u in range(units)]
    blocks = [(u, at) for u in range(units) for at in range(0, width, lanes)]

    def products(j):
        u, at = blocks[j]
        part = slice(at, at + lanes)
        zs[j % 2] = nn(a2[places[u], :], w1[:, part])
        ghs[j % 2] = nt(dfs[places[u], :], w2[part, :])

    def activation(j):
        u, at = blocks[j]
        part = slice(at, at + lanes)
        bias = b1[:, part]
        for c in chunks(size):
            zc = zs[j % 2, c, :] + bias
            phi, slope = gelu_parts(zc)
            rows = slice(places[u].start + c.start, places[u].start + c.stop)
            hids[rows, part] = (zc * phi).astype(BF)
            dzs[rows, part] = (ghs[j % 2, c, :] * slope).astype(BF)

    def finish(u):
        store(places[u], nn(hids[places[u], :], w2[...]), nt(dzs[places[u], :], w1[...]))

    products(0)
    for j, (u, at) in enumerate(blocks):
        if j + 1 < len(blocks):
            products(j + 1)
        if at == lanes and u > 0:
            finish(u - 1)
        activation(j)
        if at == 2 * lanes and u > 0:
            use(places[u - 1])
    finish(units - 1)
    use(places[units - 1])


def mlp_first_kernel(
    a2, dy, gamma2, w1_own, b1_own, w2_own, near, far,
    f_o, da2_o, hids, dzs, dfs,
    w1, w2, b1, zs, ghs,
):
    total, feats = f_o.shape
    w1[:, 0:feats] = w1_own[...]
    w2[0:feats, :] = w2_own[...]
    for core in range(2):

        @pl.when(jnp.bitwise_and(lax.axis_index("dp"), 1) == core)
        def _(core=core):
            one, two = (near, far) if core == 0 else (far, near)
            w1[:, feats:] = one[0, 0:feats]
            w2[feats:, :] = two[0, 0:feats]

    b1[:, 0:feats] = row(b1_own)
    b1[:, feats:] = colsum(near[0, feats : feats + 16].astype(F32))
    gain = row(gamma2)
    for c in chunks(total):
        dfs[c, :] = (dy[c, :].astype(F32) * gain).astype(BF)

    def store(rows, f, da2):
        f_o[rows, :] = f
        da2_o[rows, :] = da2

    mlp_units(a2, dfs, w1, b1, w2, hids, dzs, zs, ghs, 3, store, lambda rows: None)


def mlp_grad_kernel(a2, hids, dzs, dfs, grads, b1_o, a2t, dft):
    feats = a2.shape[1]
    a2t[0:feats, :] = a2[...].T
    a2t[feats:, :] = jnp.ones((a2t.shape[0] - feats, a2t.shape[1]), BF)
    dft[...] = dfs[...].T
    up = nn(a2t[...], dzs[...])
    b1_o[...] = up[feats : feats + 1]
    grads[0] = up[0:feats].astype(BF).T
    down = nn(dft[...], hids[...]).astype(BF)
    for c in range(2):
        grads[1, c * feats : (c + 1) * feats, :] = down[:, c * feats : (c + 1) * feats]


def mlp_rest_kernel(
    counts, a2, dy, dfs, x1, u, o, f0, da20, near, far, last, far_last, grads, a2t, dft, wproj,
    gamma1, n2g, fc2b, gamma2,
    out_o, dx1_o, do_o, keep, send, b1_o, acc_o,
    w1, w2, b1, hids, dzs, zs, ghs, fs, da2s, dus, ups, downs, projs, out_v, sems,
):
    total, feats = f0.shape
    images, patches = out_o.shape[:2]
    image_rows = total // images
    m_idx = lax.axis_index("mp")
    acc_o[...] = jnp.zeros_like(acc_o)
    b1[:, 0:feats] = colsum(near[1, feats : feats + 16].astype(F32))
    b1[:, feats:] = colsum(last[feats : feats + 16].astype(F32))
    for core in range(2):

        @pl.when(jnp.bitwise_and(lax.axis_index("dp"), 1) == core)
        def _(core=core):
            one, two = (near, far) if core == 0 else (far, near)
            w1[:, 0:feats] = one[1, 0:feats]
            w2[0:feats, :] = two[1, 0:feats]
            one, two = (last, far_last) if core == 0 else (far_last, last)
            w1[:, feats:] = one[0:feats]
            w2[feats:, :] = two[0:feats]

    gain2 = row(gamma2)
    bias, gain, scale = row(fc2b), row(n2g), row(gamma1)

    def out_copy(image):
        return pltpu.make_async_copy(out_v.at[image], out_o.at[image], sems.at[image])

    def store(rows, f, da2):
        fs[rows, :] = f
        da2s[rows, :] = da2

    def use(rows):
        sums = [jnp.zeros((8, feats), F32) for _ in range(6)]
        for c in chunks(rows.stop - rows.start):
            at = slice(rows.start + c.start, rows.start + c.stop)
            fc = fs[at, :] + f0[at, :] + bias
            dac = da2s[at, :] + da20[at, :]
            x1c = x1[at, :]
            dyc = dy[at, :].astype(F32)
            n, r = normalized(x1c)
            dx1 = dyc + norm_back(dac, n, r, gain)
            dx1_o[at, :] = dx1
            du = (dx1 * scale).astype(BF)
            dus[at, :] = du
            image = at.start // image_rows
            first = at.start - image * image_rows
            live = (m_idx * images + image < counts[0]).astype(F32)
            out = ((x1c + gain2 * fc) * live).astype(BF)
            if first + 16 <= patches:
                out_v[image, first : first + 16, :] = out
            else:
                out_v[image, first:patches, :] = out[0 : patches - first]
            terms = (
                du.astype(F32), u[at, :] * dx1, dac * n, dac, dfs[at, :].astype(F32), fc * dyc,
            )
            sums = [s + fold(t) for s, t in zip(sums, terms)]
        for j in range(6):
            acc_o[j : j + 1, :] += colsum(sums[j])
        do = nt(dus[rows, :], wproj[...]).astype(BF)
        for at in range(0, rows.stop - rows.start, image_rows):
            image = (rows.start + at) // image_rows
            out_copy(image).start()
            do_o[image, 0:image_rows] = do[at : at + image_rows]
            do_o[image, image_rows:] = jnp.zeros((do_o.shape[1] - image_rows, feats), BF)

    mlp_units(a2, dfs, w1, b1, w2, hids, dzs, zs, ghs, 3, store, use)
    up = nn(a2t[...], dzs[...])
    b1_o[...] = up[feats : feats + 1]
    ups[...] = up[0:feats].astype(BF).T
    downs[...] = nn(dft[...], hids[...]).astype(BF)
    projs[...] = tn(dus[...], o[...]).astype(BF)
    count = 2 * keep.shape[0]
    size = feats // count
    outs = (keep, send)

    def put(which, place, b):
        out = outs[which]
        for c in range(2):
            part = slice(c * feats, (c + 1) * feats)
            up = slice(c * feats + b * size, c * feats + (b + 1) * size)
            down = slice(b * size, (b + 1) * size)
            pieces = (grads[0, up, :], grads[1, up, :])
            for j, piece in enumerate(pieces):
                out[place, (2 * c + j) * size : (2 * c + j + 1) * size, :] = piece
            pieces = (ups[up, :], downs[down, part])
            for j, piece in enumerate(pieces):
                out[place, (4 + 2 * c + j) * size : (5 + 2 * c + j) * size, :] = piece
        out[place, 8 * size : 9 * size, :] = projs[b * size : (b + 1) * size, :]

    store_blocks(count, put)
    for image in range(images):
        out_copy(image).wait()


def attn_bwd_kernel(first, share, *refs):
    pre_s, do_r, q_r, k_r, v_r, p_r, dx1, tok, mpre, mpost, mixb, wqkv, n1g = refs[:13]
    if first:
        before, in_o = refs[14], refs[-13]
        dqkv_o, acc_o = refs[-14], refs[-12]
        vgs, dls, dq_t, dps, dvs, dks, dqs, da1, pad, in_v, sems = refs[-11:]
    else:
        dqkv_o, in_v, acc_o, vgs, dls, dq_t, dps, dvs, dks, dqs, da1, pad = refs[-12:]
    slots, feats = do_r.shape[1:]
    patches = tok.shape[1]
    rows = k_r.shape[1]
    heads = mpre.shape[0]
    head_dim = feats // heads
    acc_o[...] = jnp.zeros_like(acc_o)

    def in_copy(i):
        return pltpu.make_async_copy(in_v.at[i - first], in_o.at[i], sems.at[i])

    def early_copy(i):
        return pltpu.make_async_copy(before.at[i], in_o.at[i], sems.at[i])

    for i in range(first):
        early_copy(i).start()

    @pl.loop(first, first + share)
    def _(i):
        do_sum = jnp.zeros((8, feats), F32)
        for c in chunks(rows):
            do_sum = do_sum + fold(do_r[i, c, :].astype(F32))
        do_sum = colsum(do_sum)
        q = q_r[i]
        do = do_r[i]
        kt = k_r[i].T

        def products(pair):
            for c in chunks(rows):
                vf = v_r[i, c, :].astype(F32)
                for h in pair:
                    at = slice(h * rows + c.start, h * rows + c.stop)
                    vgs[at, :] = (vf * mpost[h : h + 1, :]).astype(BF)
            part = slice(pair[0] * rows, (pair[1] + 1) * rows)
            dps[part, :] = nt(vgs[part, :], do)
            dvs[part, :] = nn(p_r[i, pair[0] : pair[1] + 1].reshape(2 * rows, slots), do)

        products((0, 1))
        for h in range(heads):
            if h % 2 == 0 and h + 2 < heads:
                products((h + 2, h + 3))
            at = slice(h * rows, (h + 1) * rows)
            for lane in range(0, slots, 128):
                dp = dps[at, lane : lane + 128]
                pf = p_r[i, h, :, lane : lane + 128].astype(F32)
                mean = jnp.sum(dp * pf, axis=0, keepdims=True) / jnp.sum(
                    pf, axis=0, keepdims=True
                )
                dls[at, lane : lane + 128] = (pf * (dp - mean)).astype(BF)
            dqs[h] = nn(kt, dls[at, :])
            if h % 2 == 1:
                part = slice((h - 1) * rows, (h + 1) * rows)
                dks[part, :] = nn(dls[part, :], q)

        bias_row = mixb[...] * do_sum
        v_sum = jnp.zeros((8, feats), F32)
        dv_sum = jnp.zeros((8, feats), F32)
        sums = [jnp.zeros((8, feats), F32) for _ in range(heads)]
        for c in chunks(rows):
            vf = v_r[i, c, :].astype(F32)
            dv = bias_row
            for h in range(heads):
                this = dvs[h * rows + c.start : h * rows + c.stop, :]
                dv = dv + this * mpost[h : h + 1, :]
                sums[h] = sums[h] + fold(vf * this)
            if c.stop > patches:
                inside = lax.broadcasted_iota(jnp.int32, dv.shape, 0) < patches - c.start
                dv = jnp.where(inside, dv, 0.0)
                vf = jnp.where(inside, vf, 0.0)
            low = dv.astype(BF)
            dqkv_o[i, c, 2 * feats :] = low
            dv_sum = dv_sum + fold(low.astype(F32))
            v_sum = v_sum + fold(vf)
        for h in range(heads):
            acc_o[h : h + 1, :] += colsum(sums[h])
        acc_o[2 * heads : 2 * heads + 1, :] += do_sum * colsum(v_sum)
        acc_o[2 * heads + 10 : 2 * heads + 11, :] += colsum(dv_sum)

        for c in chunks(feats):
            g = c.start // head_dim
            for lane in range(0, slots, 128):
                total = 0.0
                for h in range(heads):
                    total = total + dqs[h, c, lane : lane + 128] * pre_s[h, g]
                dq_t[c, lane : lane + 128] = (total * head_dim**-0.5).astype(BF)
        dq = dq_t[...].T[0:rows]
        dqkv_o[i, :, 0:feats] = dq
        dk_sum = jnp.zeros((8, feats), F32)
        sums = [jnp.zeros((8, feats), F32) for _ in range(heads)]
        for c in chunks(rows):
            kf = k_r[i, c, :].astype(F32)
            dk = 0.0
            for h in range(heads):
                this = dks[h * rows + c.start : h * rows + c.stop, :]
                dk = dk + this * mpre[h : h + 1, :]
                sums[h] = sums[h] + fold(kf * this)
            low = (dk * (1.0 / LOG2E)).astype(BF)
            dqkv_o[i, c, feats : 2 * feats] = low
            dk_sum = dk_sum + fold(low.astype(F32))
        for h in range(heads):
            acc_o[heads + h : heads + h + 1, :] += colsum(sums[h])
        acc_o[2 * heads + 8 : 2 * heads + 9, :] += colsum(dq.astype(F32))
        acc_o[2 * heads + 9 : 2 * heads + 10, :] += colsum(dk_sum)

        pad[patches:, :] = jnp.zeros((rows - patches, feats), F32)
        pad[0:patches, :] = tok[i].astype(F32)
        da1[...] = nt(dqkv_o[i], wqkv[...])
        gain = row(n1g)
        sums = [jnp.zeros((8, feats), F32) for _ in range(2)]
        for c in chunks(rows):
            n, r = normalized(pad[c, :])
            cot = da1[c, :]
            grad = dx1[i, c, :] + norm_back(cot, n, r, gain)
            sums = [sums[0] + fold(cot * n), sums[1] + fold(cot)]
            if c.stop <= patches:
                in_v[i - first, c, :] = grad
            else:
                in_v[i - first, c.start : patches, :] = grad[0 : patches - c.start]
        for j in range(2):
            acc_o[2 * heads + 11 + j : 2 * heads + 12 + j, :] += colsum(sums[j])
        if first:
            in_copy(i).start()

    if first:
        for i in range(first):
            early_copy(i).wait()

        @pl.loop(first, first + share)
        def _(i):
            in_copy(i).wait()


def qkv_grad_kernel(heads, dqkv, *refs):
    accs = refs[:-8]
    a1, acc_mlp, b1_first, b1_rest, keep, send, small, grads = refs[-8:]
    feats = a1.shape[1]
    count = 2 * keep.shape[0]
    size = 3 * feats // count
    acc = accs[0][...]
    for other in accs[1:]:
        acc = acc + other[...]
    small[...] = jnp.zeros_like(small)
    small[0:2, :] = acc[2 * heads + 11 : 2 * heads + 13]
    small[2:8, :] = acc_mlp[0:6, :]
    small[8:11, :] = acc[2 * heads + 8 : 2 * heads + 11]
    head_dim = feats // heads
    lanes = 2 * heads * heads
    gather = (
        head_of_lane((feats, lanes), 0, head_dim)
        == lax.broadcasted_iota(jnp.int32, (feats, lanes), 1) % heads
    ).astype(F32)
    sums = exact(acc[0 : 2 * heads + 8], gather, ((1,), (0,)))
    place = head_of_lane((2 * heads, lanes), 1, heads) == lax.broadcasted_iota(
        jnp.int32, (2 * heads, lanes), 0
    )
    small[11:12, 0:lanes] = colsum(jnp.where(place, sums[0 : 2 * heads], 0.0))
    small[11:12, lanes : 2 * lanes] = sums[2 * heads : 2 * heads + 1]
    m_idx = lax.axis_index("mp")
    for c, ref in enumerate((b1_first, b1_first, b1_rest, b1_rest)):
        place = 12 + jnp.bitwise_xor(m_idx, c)
        small[pl.ds(place, 1), :] = ref[:, (c % 2) * feats : (c % 2 + 1) * feats]
    low = small[...].astype(BF)
    outs = (keep, send)

    grads[...] = tn(a1[...], dqkv[...]).astype(BF).T

    def put(which, place, b):
        outs[which][place, 0:size, :] = grads[b * size : (b + 1) * size, :]
        outs[which][place, size : size + 16, :] = low
        if outs[which].shape[1] > size + 16:
            outs[which][place, size + 16 :, :] = jnp.zeros_like(outs[which][place, size + 16 :, :])

    store_blocks(count, put)


def final_kernel(heads, size, many, mine, proj_own, *refs):
    got = refs[:many]
    mlp_mine, got_z = refs[many], refs[1 + many : 1 + 2 * many]
    qkv_o, qkvb_o, pre_o, post_o, postb_o, b1_o, *vecs_o, fc1_o, fc2_o, proj_o, held = refs[-18:]
    block, feats = fc1_o.shape
    for place, out in enumerate((fc1_o, fc2_o)):
        rows = slice(place * block, (place + 1) * block)
        out[...] = mlp_mine[rows, :] + sum(g[rows, :].astype(F32) for g in got_z)
    d_idx = lax.axis_index("dp")
    m_idx = lax.axis_index("mp")
    total = mine[...]
    held[m_idx] = proj_own[...].astype(F32)
    for j, part in enumerate(got):
        value = part[...].astype(F32)
        total = total + value[0 : size + 16]
        held[jnp.bitwise_xor(m_idx, j + 1)] = value[size + 16 :]
    proj_o[...] = held[...].reshape(-1, feats)[0:block]
    qkv_o[...] = total[0:size]
    small = total[size : size + 16]

    def own(value, width, index):
        lanes = value.shape[1]
        return pltpu.roll(value, lax.rem(lanes - index * width, lanes), axis=1)[:, 0:width]

    width = vecs_o[0].shape[1]
    vecs = own(small[0:8], width, d_idx)
    for j, ref in enumerate(vecs_o):
        ref[...] = vecs[j : j + 1]
    flat = jnp.concatenate([small[8 + j : 9 + j] for j in range(3)], axis=1)
    qkvb_o[...] = own(jnp.broadcast_to(flat, (8, 3 * feats)), qkvb_o.shape[1], d_idx)[0:1]
    b1 = own(small[8:16], b1_o.shape[1], d_idx)[4:8]
    pick = lax.broadcasted_iota(jnp.int32, b1.shape, 0) == m_idx
    b1_o[...] = colsum(jnp.where(pick, b1, 0.0))
    mix = small[11:12]
    hh = heads * heads
    line = lax.broadcasted_iota(jnp.int32, (heads, hh), 0)
    lane = lax.broadcasted_iota(jnp.int32, (heads, hh), 1)
    fold = (
        lax.broadcasted_iota(jnp.int32, (hh, heads), 0) % heads
        == lax.broadcasted_iota(jnp.int32, (hh, heads), 1)
    ).astype(F32)
    head_dim = feats // heads

    def square(values):
        return exact(jnp.where(lane // heads == line, values, 0.0), fold, ((1,), (0,)))

    post_o[...] = square(mix[:, 0:hh]).T
    pre_o[...] = square(mix[:, hh : 2 * hh]) * (head_dim**-0.5)
    postb_o[...] = mix[:, 2 * hh : 2 * hh + heads]


def whole(shape):
    return pl.BlockSpec(shape, lambda i: (0,) * len(shape))


def each(shape, first=0, many=1):
    return pl.BlockSpec((many,) + shape[1:], lambda i: (i + first,) + (0,) * (len(shape) - 1))


SCALARS = pl.BlockSpec(memory_space=pltpu.SMEM)
IN_VMEM = pl.BlockSpec(memory_space=pltpu.VMEM)
IN_HBM = pl.BlockSpec(memory_space=pltpu.HBM)


def kept(a):
    return pltpu.with_memory_space_constraint(a, pltpu.HBM)


def sds(shape, dtype):
    return jax.ShapeDtypeStruct(shape, dtype)


def call(
    kernel, grid, ins, in_specs, outs, out_specs, scratch=(), flops=0, name=None, aliases=None,
    limit=VMEM_LIMIT,
):
    size = lambda a: a.size * a.dtype.itemsize
    return pl.pallas_call(
        kernel,
        grid=grid,
        in_specs=in_specs,
        out_specs=out_specs,
        out_shape=outs,
        scratch_shapes=scratch,
        input_output_aliases=aliases or {},
        compiler_params=pltpu.CompilerParams(vmem_limit_bytes=limit),
        cost_estimate=pl.CostEstimate(
            flops=flops,
            bytes_accessed=sum(size(a) for a in ins) + sum(size(a) for a in outs),
            transcendentals=0,
        ),
        name=name,
    )(*ins)


def xor_perm(count, mask):
    return [(j, j ^ mask) for j in range(count)]


def dp_hops(dp):
    bits = dp.bit_length() - 1
    groups = []
    at = 1
    while at < bits:
        groups.append((at, min(2, bits - at)))
        at += groups[-1][1]
    return groups


def dp_scatter(value, dp):
    for at, many in dp_hops(dp):
        value = value.reshape((-1, 1 << many) + value.shape[1:])
        got = [
            lax.ppermute(value[:, j].astype(BF), "dp", xor_perm(dp, j << at))
            for j in range(1, 1 << many)
        ]
        value = value[:, 0] + sum(g.astype(F32) for g in got)
    return value.reshape(value.shape[-2:])


def per_device(
    dp, mp,
    tokens_in, image_counts, norm1_gain, norm1_bias, qkv_weight, qkv_bias,
    mix_pre, mix_post, mix_post_bias, proj_weight, proj_bias, gamma1,
    norm2_gain, norm2_bias, fc1_weight, fc1_bias, fc2_weight, fc2_bias, gamma2, out_grad,
):
    images, patches, feats = tokens_in.shape
    heads = mix_pre.shape[0]
    rows = -(-patches // 16) * 16
    slots = -(-patches // 128) * 128
    hidden = fc1_weight.shape[1]
    tok_rows = (images, rows, feats)
    slot_rows = (images, slots, feats)
    prob_shape = (images, heads, rows, slots)
    mix_shape = (heads, feats)
    operands = [
        tokens_in, out_grad, norm1_gain, norm1_bias, qkv_bias, mix_pre, mix_post,
        mix_post_bias, proj_bias, gamma1, norm2_gain, norm2_bias, qkv_weight, proj_weight,
    ]

    ins = [kept(a) for a in [fc1_weight, fc2_weight, fc1_bias] + operands]
    outs = [sds((feats + 16, hidden), BF)] + [sds(a.shape, a.dtype) for a in operands]
    other, *held = call(
        pack_kernel,
        (),
        ins,
        [IN_HBM] * len(ins),
        outs,
        [IN_VMEM] * len(outs),
        [pltpu.VMEM(fc1_bias.shape, F32), pltpu.SemaphoreType.DMA((2 + len(operands),))],
        name="pack",
    )
    near = [lax.ppermute(other, "mp", xor_perm(mp, j)) for j in (1, 2)]

    shares = [images - 1, 1] if images > 1 else [images]
    tables = [sds(mix_shape, F32), sds(mix_shape, F32), sds((1, feats), F32)]
    carried = []
    for s, share in enumerate(shares):
        first = sum(shares[:s])
        ins = [image_counts, mix_post, mix_post_bias] + held + ([mpre] if first else [])
        outs = call(
            functools.partial(attn_fwd_kernel, first, share),
            (),
            ins + carried,
            [SCALARS] * 3
            + [IN_VMEM] * (len(ins) - 3)
            + [pl.BlockSpec(memory_space=pl.ANY)] * len(carried),
            [
                sds(tok_rows, BF), sds(slot_rows, BF), sds(tok_rows, BF), sds(tok_rows, BF),
                sds(prob_shape, BF), sds(tok_rows, BF), sds(tok_rows, F32), sds(tok_rows, F32),
                sds(tok_rows, BF), sds(tok_rows, BF),
            ]
            + ([] if first else tables),
            [IN_VMEM] * (10 if first else 13),
            [
                pltpu.VMEM((rows, feats), F32), pltpu.VMEM((heads * rows, 2 * feats), BF),
                pltpu.VMEM((feats, slots), BF), pltpu.VMEM((rows, 3 * feats), F32), pltpu.VMEM((heads * rows, slots), F32),
                pltpu.VMEM((heads, feats, slots), F32),
            ],
            flops=share * 15 * 10**8,
            name="attn_fwd",
            aliases={len(ins) + j: j for j in range(10)} if carried else None,
        )
        carried = list(outs[:10])
        if not first:
            mpre, mpost, mixb = outs[10:]
        if s == 0:
            near, carried[0] = lax.optimization_barrier((near, carried[0]))
            last = lax.ppermute(near[1], "mp", xor_perm(mp, 1))
            near = jnp.stack(near)
            far = lax.ppermute(near, "dp", xor_perm(dp, 1))
    a1, q, k, v, prob, o, x1, u, a2, dy = carried
    far, a2 = lax.optimization_barrier((far, a2))

    block = feats // dp
    total = images * rows
    flat = (total, feats)
    a2, dy, x1, u, o = (a.reshape(flat) for a in (a2, dy, x1, u, o))
    ins = [a2, dy, gamma2, fc1_weight, fc1_bias, fc2_weight, near, far]
    wide = 2 * hidden
    grad_shape = (2, wide, feats)
    f0, da20, hids, dzs, dfs = call(
        mlp_first_kernel,
        (),
        ins,
        [IN_VMEM] * len(ins),
        [
            sds(flat, F32), sds(flat, F32), sds((total, wide), BF), sds((total, wide), BF),
            sds(flat, BF),
        ],
        [IN_VMEM] * 5,
        [
            pltpu.VMEM((feats, wide), BF), pltpu.VMEM((wide, feats), BF),
            pltpu.VMEM((1, wide), F32),
            pltpu.VMEM((2, total // 3, 256), F32), pltpu.VMEM((2, total // 3, 256), F32),
        ],
        flops=images * 5 * 10**8,
        name="mlp_first",
    )

    last, f0 = lax.optimization_barrier((last, f0))
    far_last = lax.ppermute(last, "dp", xor_perm(dp, 1))
    ins = [a2, hids, dzs, dfs]
    grads0, b1_0, a2t, dft = call(
        mlp_grad_kernel,
        (),
        ins,
        [IN_VMEM] * 4,
        [
            sds(grad_shape, BF), sds((1, wide), F32), sds((feats + 16, total), BF),
            sds((feats, total), BF),
        ],
        [IN_VMEM] * 4,
        flops=images * 3 * 10**8,
        name="mlp_grad",
    )

    grad_rows = 9 * block
    half_shape = (dp // 2, grad_rows, feats)
    ins = [
        image_counts, a2, dy, dfs, x1, u, o, f0, da20, near, far, last, far_last, grads0, a2t, dft,
        proj_weight, gamma1,
        norm2_gain, fc2_bias, gamma2,
    ]
    layer_out, dx1, do, keep, send, b1_1, acc_mlp = call(
        mlp_rest_kernel,
        (),
        ins,
        [SCALARS] + [IN_VMEM] * (len(ins) - 1),
        [
            sds(tokens_in.shape, BF), sds(flat, F32), sds(slot_rows, BF), sds(half_shape, BF),
            sds(half_shape, BF), sds((1, wide), F32), sds((8, feats), F32),
        ],
        [IN_HBM] + [IN_VMEM] * 6,
        [
            pltpu.VMEM((feats, wide), BF), pltpu.VMEM((wide, feats), BF),
            pltpu.VMEM((1, wide), F32), pltpu.VMEM((total, wide), BF),
            pltpu.VMEM((total, wide), BF),
            pltpu.VMEM((2, total // 3, 256), F32), pltpu.VMEM((2, total // 3, 256), F32),
            pltpu.VMEM(flat, F32), pltpu.VMEM(flat, F32), pltpu.VMEM(flat, BF),
            pltpu.VMEM((wide, feats), BF), pltpu.VMEM((feats, wide), BF),
            pltpu.VMEM((feats, feats), BF), pltpu.VMEM(tokens_in.shape, BF),
            pltpu.SemaphoreType.DMA((images,)),
        ],
        flops=images * 9 * 10**8,
        name="mlp_rest",
    )
    got = lax.ppermute(send, "dp", xor_perm(dp, 1))
    dx1 = dx1.reshape(tok_rows)

    shares = [1, images - 1] if images > 1 else [1]
    dqkv_shape = (images, rows, 3 * feats)
    carried, accs = [], []
    for s, share in enumerate(shares):
        first = sum(shares[:s])
        ins = [mix_pre, do, q, k, v, prob, dx1, tokens_in, mpre, mpost, mixb, qkv_weight, norm1_gain]
        in_shape = tokens_in.shape if first or share == images else (share,) + tokens_in.shape[1:]
        *carried, acc = call(
            functools.partial(attn_bwd_kernel, first, share),
            (),
            ins + carried,
            [SCALARS]
            + [IN_VMEM] * (len(ins) - 1)
            + [pl.BlockSpec(memory_space=pl.ANY), IN_VMEM][: len(carried)],
            [sds(dqkv_shape, BF), sds(in_shape, F32), sds((2 * heads + 16, feats), F32)],
            [IN_VMEM, IN_HBM if first else IN_VMEM, IN_VMEM],
            [
                pltpu.VMEM((heads * rows, feats), BF), pltpu.VMEM((heads * rows, slots), BF),
                pltpu.VMEM((feats, slots), BF), pltpu.VMEM((heads * rows, slots), F32),
                pltpu.VMEM((heads * rows, feats), F32), pltpu.VMEM((heads * rows, feats), F32),
                pltpu.VMEM((heads, feats, slots), F32), pltpu.VMEM((rows, feats), F32),
                pltpu.VMEM((rows, feats), F32),
            ]
            + [pltpu.VMEM((share, patches, feats), F32), pltpu.SemaphoreType.DMA((images,))]
            * bool(first),
            flops=share * 20 * 10**8,
            name="attn_bwd",
            aliases={len(ins): 0} if carried else None,
        )
        accs.append(acc)
        if s == 0:
            (keep, got), acc = lax.optimization_barrier(((keep, got), acc))
            mine = dp_scatter(keep.astype(F32) + got.astype(F32), dp)
            accs[0], do = lax.optimization_barrier((acc, do))
    dqkv, in_grad = carried
    mine, dqkv = lax.optimization_barrier((mine, dqkv))
    mlp_mine = mine
    low = mine.astype(BF)
    m_idx = lax.axis_index("mp")
    share_rows = -(-block // (16 * mp)) * 16
    proj = jnp.pad(mine[8 * block :], ((0, mp * share_rows - block), (0, 0)))

    def proj_share(j):
        return lax.dynamic_slice_in_dim(proj, jnp.bitwise_xor(m_idx, j) * share_rows, share_rows)

    got_z = [
        lax.ppermute(
            jnp.concatenate([low[2 * j * block : 2 * (j + 1) * block], proj_share(j).astype(BF)]),
            "mp",
            xor_perm(mp, j),
        )
        for j in range(1, mp)
    ]

    q_block = 3 * feats // dp
    half_shape = (dp // 2, q_block + 16, feats)
    ins = [dqkv.reshape(total, 3 * feats)] + accs + [a1.reshape(flat), acc_mlp, b1_0, b1_1]
    keep, send = call(
        functools.partial(qkv_grad_kernel, heads),
        (),
        ins,
        [IN_VMEM] * len(ins),
        [sds(half_shape, BF), sds(half_shape, BF)],
        [IN_VMEM] * 2,
        [pltpu.VMEM((16, feats), F32), pltpu.VMEM((3 * feats, feats), BF)],
        flops=11 * 10**8,
        name="qkv_grad",
    )
    got = lax.ppermute(send, "dp", xor_perm(dp, 1))
    mine = dp_scatter(keep.astype(F32) + got.astype(F32), dp)
    mine, got_z = lax.optimization_barrier((mine, got_z))

    proj_own = (proj_share(0) + sum(g[2 * block :].astype(F32) for g in got_z)).astype(BF)
    payload = jnp.concatenate([mine.astype(BF), proj_own])
    got = [lax.ppermute(payload, "mp", xor_perm(mp, j)) for j in range(1, mp)]
    b1_size = hidden // dp
    ins = [mine, proj_own] + got + [mlp_mine] + got_z
    outs = [
        sds((q_block, feats), F32), sds((1, q_block), F32), sds((heads, heads), F32),
        sds((heads, heads), F32), sds((1, heads), F32), sds((1, b1_size), F32),
    ] + [sds((1, block), F32)] * 8 + [sds((block, feats), F32)] * 3
    qkvw, qkvb, pre, post, postb, b1g, *vecs, fc1g, fc2g, projg = call(
        functools.partial(final_kernel, heads, q_block, mp - 1),
        (),
        ins,
        [IN_VMEM] * len(ins),
        outs,
        [IN_VMEM] * len(outs),
        [pltpu.VMEM((mp, share_rows, feats), F32)],
        name="final",
    )
    vecs = [a.reshape(-1) for a in vecs]
    return (
        layer_out,
        in_grad,
        vecs[0],
        vecs[1],
        qkvw.T,
        qkvb.reshape(-1),
        pre,
        post,
        postb.reshape(-1),
        projg.T,
        vecs[2],
        vecs[3],
        vecs[4],
        vecs[5],
        fc1g.T,
        b1g.reshape(-1),
        fc2g.T,
        vecs[6],
        vecs[7],
    )


def solution(mesh):
    tokens = P(("dp", "mp"), None, None)
    placed = (
        (tokens, P("dp")) + (P(),) * 12 + (P(None, "mp"), P("mp"), P("mp", None), P(), P(), tokens)
    )
    return jax.shard_map(
        functools.partial(per_device, mesh.shape["dp"], mesh.shape["mp"]),
        mesh=mesh,
        in_specs=placed,
        out_specs=(
            tokens, tokens, P("dp"), P("dp"), P(None, "dp"), P("dp"), P(), P(), P(),
            P(None, "dp"), P("dp"), P("dp"), P("dp"), P("dp"), P(None, ("mp", "dp")),
            P(("mp", "dp")), P("mp", "dp"), P("dp"), P("dp"),
        ),
        check_vma=False,
    )
```

```python
import functools

import jax
import jax.numpy as jnp
from jax import lax
from jax.experimental import pallas as pl
from jax.experimental.pallas import tpu as pltpu
from jax.sharding import PartitionSpec as P

BF = jnp.bfloat16
F32 = jnp.float32
LOG2E = 1.4426950408889634
EPS = 1e-06
VMEM_LIMIT = 20 * 1024 * 1024


def nn(a, b):
    return lax.dot_general(a, b, (((1,), (0,)), ((), ())), preferred_element_type=F32)


def nt(a, b):
    return lax.dot_general(a, b, (((1,), (1,)), ((), ())), preferred_element_type=F32)


def tn(a, b):
    return lax.dot_general(a, b, (((0,), (0,)), ((), ())), preferred_element_type=F32)


def exact(a, b, dims):
    return lax.dot_general(
        a, b, (dims, ((), ())), precision=lax.Precision.HIGHEST, preferred_element_type=F32
    )


def normalized(x):
    mean = jnp.mean(x, axis=-1, keepdims=True)
    c = x - mean
    r = lax.rsqrt(jnp.mean(c * c, axis=-1, keepdims=True) + EPS)
    return c * r, r


def norm_back(cot, n, r, gain):
    cg = cot * gain
    return r * (
        cg
        - jnp.mean(cg, axis=-1, keepdims=True)
        - n * jnp.mean(cg * n, axis=-1, keepdims=True)
    )


def colsum(x):
    return jnp.sum(x, axis=0, keepdims=True)


def split(x):
    hi = x.astype(BF)
    return jnp.concatenate([hi, (x - hi.astype(F32)).astype(BF)], axis=1)


def row(ref):
    return ref[...].reshape(1, ref.shape[0])


def gelu_parts(z):
    e = jnp.exp2(z * z * (-0.5 * LOG2E))
    t = pl.reciprocal(1.0 + jnp.abs(z) * (0.3275911 * 0.7071067811865476), approx=True)
    poly = t * (
        0.5 * 0.254829592
        + t
        * (
            0.5 * -0.284496736
            + t * (0.5 * 1.421413741 + t * (0.5 * -1.453152027 + t * (0.5 * 1.061405429)))
        )
    )
    tail = poly * e
    phi = jnp.where(z >= 0, 1.0 - tail, tail)
    return phi, phi + z * e * 0.3989422804014327


def head_of_lane(shape, axis, head_dim):
    return lax.broadcasted_iota(jnp.int32, shape, axis) // head_dim


def chunks(count, size=16):
    return [slice(at, at + size) for at in range(0, count, size)]


def fold(x):
    return sum(x[at : at + 8] for at in range(8, x.shape[0], 8)) + x[0:8]


def pack_kernel(w1, w2, b1, *refs):
    many = (len(refs) - 3) // 2
    sources, other, held, b1_v, sems = refs[:many], refs[many], refs[many + 1 : -2], refs[-2], refs[-1]
    feats = w1.shape[0]
    core = jnp.bitwise_and(lax.axis_index("dp"), 1)
    bias_copy = pltpu.make_async_copy(b1, b1_v, sems.at[0])
    own = [pltpu.make_async_copy(w, other.at[0:feats], sems.at[1]) for w in (w1, w2)]
    copies = [
        pltpu.make_async_copy(sources[j], held[j], sems.at[2 + j]) for j in range(many)
    ]
    bias_copy.start()
    for j in range(2):
        pl.when(core == j)(own[j].start)
    for copy in copies:
        copy.start()
    bias_copy.wait()
    rest = row(b1_v)
    place = lax.broadcasted_iota(jnp.int32, (16, feats), 0)
    bias = jnp.zeros((16, feats), F32)
    for j in range(3):
        term = rest.astype(BF).astype(F32)
        bias = jnp.where(place == j, term, bias)
        rest = rest - term
    other[feats:, :] = bias.astype(BF)
    for j in range(2):
        pl.when(core == j)(own[j].wait)
    for copy in copies:
        copy.wait()


def attn_fwd_kernel(first, share, *refs):
    counts, post_s, postb_s, tok, og, n1g, n1b, qkvb, pre, post, postb, projb = refs[:12]
    gamma1, n2g, n2b, wqkv, wproj = refs[12:17]
    if first:
        mpre = refs[17]
        a1_o, q_o, k_o, v_o, p_o, o_o, x1_o, u_o, a2_o, dy_o = refs[-16:-6]
    else:
        a1_o, q_o, k_o, v_o, p_o, o_o, x1_o, u_o, a2_o, dy_o, mpre, mpost, mixb = refs[-19:-6]
    pad, kk, attended_t, wide, logits, mixed = refs[-6:]
    images, patches, feats = tok.shape
    rows = pad.shape[0]
    heads = mpre.shape[0]
    head_dim = feats // heads
    slots = q_o.shape[1]

    if not first:
        spread = (
            head_of_lane((heads, feats), 1, head_dim)
            == lax.broadcasted_iota(jnp.int32, (heads, feats), 0)
        ).astype(F32)
        mpre[...] = exact(pre[...], spread, ((1,), (0,))) * (head_dim**-0.5 * LOG2E)
        mpost[...] = exact(post[...], spread, ((0,), (0,)))
        mixb[...] = exact(row(postb), spread, ((1,), (0,)))

    @pl.loop(first, first + share)
    def _(i):
        pad[patches:, :] = jnp.zeros((rows - patches, feats), F32)
        live = (lax.axis_index("mp") * images + i < counts[0]).astype(F32)
        pad[0:patches, :] = og[i].astype(F32) * live
        dy_o[i] = pad[...].astype(BF)
        pad[0:patches, :] = tok[i].astype(F32)
        gain, shift = row(n1g), row(n1b)
        for c in chunks(rows):
            n, _ = normalized(pad[c, :])
            a1_o[i, c, :] = (n * gain + shift).astype(BF)
        wide[...] = nn(a1_o[i], wqkv[...])
        bias = row(qkvb)
        q_o[i, rows:] = jnp.zeros((slots - rows, feats), BF)
        for c in chunks(rows):
            q, k, v = (
                wide[c, j * feats : (j + 1) * feats] + bias[:, j * feats : (j + 1) * feats]
                for j in range(3)
            )
            q_o[i, c, :] = q.astype(BF)
            v_o[i, c, :] = v.astype(BF)
            k = k.astype(BF)
            k_o[i, c, :] = k
            kf = k.astype(F32)
            for g in range(heads):
                at = slice(g * rows + c.start, g * rows + c.stop)
                scaled = kf * mpre[g : g + 1, :]
                hi = scaled.astype(BF)
                kk[at, 0:feats] = hi
                kk[at, feats:] = (scaled - hi.astype(F32)).astype(BF)
        q2 = jnp.concatenate([q_o[i], q_o[i]], axis=1)
        vt = v_o[i].T
        tail = patches // 8 * 8
        inside = lax.broadcasted_iota(jnp.int32, (rows - tail, 128), 0) < patches - tail
        real = (lax.broadcasted_iota(jnp.int32, (rows, 128), 0) < patches).astype(BF)
        start = nn(vt, real)

        def products(pair):
            part = slice(pair[0] * rows, (pair[1] + 1) * rows)
            logits[part, :] = nt(kk[part, :], q2)

        products((0, 1))
        for g in range(heads):
            if g % 2 == 0 and g + 2 < heads:
                products((g + 2, g + 3))
            for lane in range(0, slots, 128):
                x = logits[g * rows : (g + 1) * rows, lane : lane + 128]
                x = jnp.concatenate([x[0:tail], jnp.where(inside, x[tail:], -1e30)], axis=0)
                e = jnp.exp2(x - jnp.max(x, axis=0, keepdims=True))
                inv = 1.0 / jnp.sum(e, axis=0, keepdims=True)
                p_o[i, g, :, lane : lane + 128] = (e * inv).astype(BF)
            mixed[g] = nn(vt, p_o[i, g])
        for c in chunks(feats):
            g = c.start // head_dim
            first = start[c] * postb_s[g]
            for lane in range(0, slots, 128):
                total = first
                for h in range(heads):
                    total = total + mixed[h, c, lane : lane + 128] * post_s[g, h]
                attended_t[c, lane : lane + 128] = total.astype(BF)
        o_o[i] = attended_t[...].T[0:rows]
        wide[:, 0:feats] = nn(o_o[i], wproj[...])
        bias, scale, gain, shift = row(projb), row(gamma1), row(n2g), row(n2b)
        for c in chunks(rows):
            u = wide[c, 0:feats] + bias
            x1 = pad[c, :] + scale * u
            u_o[i, c, :] = u
            x1_o[i, c, :] = x1
            n, _ = normalized(x1)
            a2_o[i, c, :] = (n * gain + shift).astype(BF)


def store_blocks(count, put):
    mine = lax.axis_index("dp")
    for core in range(2):

        @pl.when(jnp.bitwise_and(mine, 1) == core)
        def _(core=core):
            for b in range(count):
                place = jnp.bitwise_xor(jnp.int32(b >> 1), jnp.right_shift(mine, 1))
                put((b ^ core) & 1, place, b)


def mlp_units(a2, dfs, w1, b1, w2, hids, dzs, zs, ghs, units, store, use):
    size = a2.shape[0] // units
    width = w2.shape[0]
    lanes = zs.shape[2]
    places = [slice(u * size, (u + 1) * size) for u in range(units)]
    blocks = [(u, at) for u in range(units) for at in range(0, width, lanes)]

    def products(j):
        u, at = blocks[j]
        part = slice(at, at + lanes)
        zs[j % 2] = nn(a2[places[u], :], w1[:, part])
        ghs[j % 2] = nt(dfs[places[u], :], w2[part, :])

    def activation(j):
        u, at = blocks[j]
        part = slice(at, at + lanes)
        bias = b1[:, part]
        for c in chunks(size):
            zc = zs[j % 2, c, :] + bias
            phi, slope = gelu_parts(zc)
            rows = slice(places[u].start + c.start, places[u].start + c.stop)
            hids[rows, part] = (zc * phi).astype(BF)
            dzs[rows, part] = (ghs[j % 2, c, :] * slope).astype(BF)

    def finish(u):
        store(places[u], nn(hids[places[u], :], w2[...]), nt(dzs[places[u], :], w1[...]))

    products(0)
    for j, (u, at) in enumerate(blocks):
        if j + 1 < len(blocks):
            products(j + 1)
        if at == lanes and u > 0:
            finish(u - 1)
        activation(j)
        if at == 2 * lanes and u > 0:
            use(places[u - 1])
    finish(units - 1)
    use(places[units - 1])


def mlp_first_kernel(
    a2, dy, gamma2, w1_own, b1_own, w2_own, near, far,
    f_o, da2_o, hids, dzs, dfs,
    w1, w2, b1, zs, ghs,
):
    total, feats = f_o.shape
    w1[:, 0:feats] = w1_own[...]
    w2[0:feats, :] = w2_own[...]
    for core in range(2):

        @pl.when(jnp.bitwise_and(lax.axis_index("dp"), 1) == core)
        def _(core=core):
            one, two = (near, far) if core == 0 else (far, near)
            w1[:, feats:] = one[0, 0:feats]
            w2[feats:, :] = two[0, 0:feats]

    b1[:, 0:feats] = row(b1_own)
    b1[:, feats:] = colsum(near[0, feats : feats + 16].astype(F32))
    gain = row(gamma2)
    for c in chunks(total):
        dfs[c, :] = (dy[c, :].astype(F32) * gain).astype(BF)

    def store(rows, f, da2):
        f_o[rows, :] = f
        da2_o[rows, :] = da2

    mlp_units(a2, dfs, w1, b1, w2, hids, dzs, zs, ghs, 3, store, lambda rows: None)


def mlp_grad_kernel(a2, hids, dzs, dfs, grads, b1_o, a2t, dft):
    feats = a2.shape[1]
    a2t[0:feats, :] = a2[...].T
    a2t[feats:, :] = jnp.ones((a2t.shape[0] - feats, a2t.shape[1]), BF)
    dft[...] = dfs[...].T
    up = nn(a2t[...], dzs[...])
    b1_o[...] = up[feats : feats + 1]
    grads[0] = up[0:feats].astype(BF).T
    down = nn(dft[...], hids[...]).astype(BF)
    for c in range(2):
        grads[1, c * feats : (c + 1) * feats, :] = down[:, c * feats : (c + 1) * feats]


def mlp_rest_kernel(
    counts, a2, dy, dfs, x1, u, o, f0, da20, near, far, last, far_last, grads, a2t, dft, wproj,
    gamma1, n2g, fc2b, gamma2,
    out_o, dx1_o, do_o, keep, send, b1_o, acc_o,
    w1, w2, b1, hids, dzs, zs, ghs, fs, da2s, dus, ups, downs, projs, out_v, sems,
):
    total, feats = f0.shape
    images, patches = out_o.shape[:2]
    image_rows = total // images
    m_idx = lax.axis_index("mp")
    acc_o[...] = jnp.zeros_like(acc_o)
    b1[:, 0:feats] = colsum(near[1, feats : feats + 16].astype(F32))
    b1[:, feats:] = colsum(last[feats : feats + 16].astype(F32))
    for core in range(2):

        @pl.when(jnp.bitwise_and(lax.axis_index("dp"), 1) == core)
        def _(core=core):
            one, two = (near, far) if core == 0 else (far, near)
            w1[:, 0:feats] = one[1, 0:feats]
            w2[0:feats, :] = two[1, 0:feats]
            one, two = (last, far_last) if core == 0 else (far_last, last)
            w1[:, feats:] = one[0:feats]
            w2[feats:, :] = two[0:feats]

    gain2 = row(gamma2)
    bias, gain, scale = row(fc2b), row(n2g), row(gamma1)

    def out_copy(image):
        return pltpu.make_async_copy(out_v.at[image], out_o.at[image], sems.at[image])

    def store(rows, f, da2):
        fs[rows, :] = f
        da2s[rows, :] = da2

    def use(rows):
        sums = [jnp.zeros((8, feats), F32) for _ in range(6)]
        for c in chunks(rows.stop - rows.start):
            at = slice(rows.start + c.start, rows.start + c.stop)
            fc = fs[at, :] + f0[at, :] + bias
            dac = da2s[at, :] + da20[at, :]
            x1c = x1[at, :]
            dyc = dy[at, :].astype(F32)
            n, r = normalized(x1c)
            dx1 = dyc + norm_back(dac, n, r, gain)
            dx1_o[at, :] = dx1
            du = (dx1 * scale).astype(BF)
            dus[at, :] = du
            image = at.start // image_rows
            first = at.start - image * image_rows
            live = (m_idx * images + image < counts[0]).astype(F32)
            out = ((x1c + gain2 * fc) * live).astype(BF)
            if first + 16 <= patches:
                out_v[image, first : first + 16, :] = out
            else:
                out_v[image, first:patches, :] = out[0 : patches - first]
            terms = (
                du.astype(F32), u[at, :] * dx1, dac * n, dac, dfs[at, :].astype(F32), fc * dyc,
            )
            sums = [s + fold(t) for s, t in zip(sums, terms)]
        for j in range(6):
            acc_o[j : j + 1, :] += colsum(sums[j])
        do = nt(dus[rows, :], wproj[...]).astype(BF)
        for at in range(0, rows.stop - rows.start, image_rows):
            image = (rows.start + at) // image_rows
            out_copy(image).start()
            do_o[image, 0:image_rows] = do[at : at + image_rows]
            do_o[image, image_rows:] = jnp.zeros((do_o.shape[1] - image_rows, feats), BF)

    mlp_units(a2, dfs, w1, b1, w2, hids, dzs, zs, ghs, 3, store, use)
    up = nn(a2t[...], dzs[...])
    b1_o[...] = up[feats : feats + 1]
    ups[...] = up[0:feats].astype(BF).T
    downs[...] = nn(dft[...], hids[...]).astype(BF)
    projs[...] = tn(dus[...], o[...]).astype(BF)
    count = 2 * keep.shape[0]
    size = feats // count
    outs = (keep, send)

    def put(which, place, b):
        out = outs[which]
        for c in range(2):
            part = slice(c * feats, (c + 1) * feats)
            up = slice(c * feats + b * size, c * feats + (b + 1) * size)
            down = slice(b * size, (b + 1) * size)
            pieces = (grads[0, up, :], grads[1, up, :])
            for j, piece in enumerate(pieces):
                out[place, (2 * c + j) * size : (2 * c + j + 1) * size, :] = piece
            pieces = (ups[up, :], downs[down, part])
            for j, piece in enumerate(pieces):
                out[place, (4 + 2 * c + j) * size : (5 + 2 * c + j) * size, :] = piece
        out[place, 8 * size : 9 * size, :] = projs[b * size : (b + 1) * size, :]

    store_blocks(count, put)
    for image in range(images):
        out_copy(image).wait()


def attn_bwd_kernel(first, share, *refs):
    pre_s, do_r, q_r, k_r, v_r, p_r, dx1, tok, mpre, mpost, mixb, wqkv, n1g = refs[:13]
    if first:
        before, in_o = refs[14], refs[-13]
        dqkv_o, acc_o = refs[-14], refs[-12]
        vgs, dls, dq_t, dps, dvs, dks, dqs, da1, pad, in_v, sems = refs[-11:]
    else:
        dqkv_o, in_v, acc_o, vgs, dls, dq_t, dps, dvs, dks, dqs, da1, pad = refs[-12:]
    slots, feats = do_r.shape[1:]
    patches = tok.shape[1]
    rows = k_r.shape[1]
    heads = mpre.shape[0]
    head_dim = feats // heads
    acc_o[...] = jnp.zeros_like(acc_o)

    def in_copy(i):
        return pltpu.make_async_copy(in_v.at[i - first], in_o.at[i], sems.at[i])

    def early_copy(i):
        return pltpu.make_async_copy(before.at[i], in_o.at[i], sems.at[i])

    for i in range(first):
        early_copy(i).start()

    @pl.loop(first, first + share)
    def _(i):
        do_sum = jnp.zeros((8, feats), F32)
        for c in chunks(rows):
            do_sum = do_sum + fold(do_r[i, c, :].astype(F32))
            vf = v_r[i, c, :].astype(F32)
            for h in range(heads):
                at = slice(h * rows + c.start, h * rows + c.stop)
                vgs[at, :] = (vf * mpost[h : h + 1, :]).astype(BF)
        do_sum = colsum(do_sum)
        q = q_r[i]
        do = do_r[i]
        kt = k_r[i].T

        def products(pair):
            part = slice(pair[0] * rows, (pair[1] + 1) * rows)
            dps[part, :] = nt(vgs[part, :], do)
            dvs[part, :] = nn(p_r[i, pair[0] : pair[1] + 1].reshape(2 * rows, slots), do)

        products((0, 1))
        for h in range(heads):
            if h % 2 == 0 and h + 2 < heads:
                products((h + 2, h + 3))
            at = slice(h * rows, (h + 1) * rows)
            for lane in range(0, slots, 128):
                dp = dps[at, lane : lane + 128]
                pf = p_r[i, h, :, lane : lane + 128].astype(F32)
                mean = jnp.sum(dp * pf, axis=0, keepdims=True) / jnp.sum(
                    pf, axis=0, keepdims=True
                )
                dls[at, lane : lane + 128] = (pf * (dp - mean)).astype(BF)
            dqs[h] = nn(kt, dls[at, :])
            if h % 2 == 1:
                part = slice((h - 1) * rows, (h + 1) * rows)
                dks[part, :] = nn(dls[part, :], q)

        bias_row = mixb[...] * do_sum
        v_sum = jnp.zeros((8, feats), F32)
        dv_sum = jnp.zeros((8, feats), F32)
        sums = [jnp.zeros((8, feats), F32) for _ in range(heads)]
        for c in chunks(rows):
            vf = v_r[i, c, :].astype(F32)
            dv = bias_row
            for h in range(heads):
                this = dvs[h * rows + c.start : h * rows + c.stop, :]
                dv = dv + this * mpost[h : h + 1, :]
                sums[h] = sums[h] + fold(vf * this)
            if c.stop > patches:
                inside = lax.broadcasted_iota(jnp.int32, dv.shape, 0) < patches - c.start
                dv = jnp.where(inside, dv, 0.0)
                vf = jnp.where(inside, vf, 0.0)
            low = dv.astype(BF)
            dqkv_o[i, c, 2 * feats :] = low
            dv_sum = dv_sum + fold(low.astype(F32))
            v_sum = v_sum + fold(vf)
        for h in range(heads):
            acc_o[h : h + 1, :] += colsum(sums[h])
        acc_o[2 * heads : 2 * heads + 1, :] += do_sum * colsum(v_sum)
        acc_o[2 * heads + 10 : 2 * heads + 11, :] += colsum(dv_sum)

        for c in chunks(feats):
            g = c.start // head_dim
            for lane in range(0, slots, 128):
                total = 0.0
                for h in range(heads):
                    total = total + dqs[h, c, lane : lane + 128] * pre_s[h, g]
                dq_t[c, lane : lane + 128] = (total * head_dim**-0.5).astype(BF)
        dq = dq_t[...].T[0:rows]
        dqkv_o[i, :, 0:feats] = dq
        dk_sum = jnp.zeros((8, feats), F32)
        sums = [jnp.zeros((8, feats), F32) for _ in range(heads)]
        for c in chunks(rows):
            kf = k_r[i, c, :].astype(F32)
            dk = 0.0
            for h in range(heads):
                this = dks[h * rows + c.start : h * rows + c.stop, :]
                dk = dk + this * mpre[h : h + 1, :]
                sums[h] = sums[h] + fold(kf * this)
            low = (dk * (1.0 / LOG2E)).astype(BF)
            dqkv_o[i, c, feats : 2 * feats] = low
            dk_sum = dk_sum + fold(low.astype(F32))
        for h in range(heads):
            acc_o[heads + h : heads + h + 1, :] += colsum(sums[h])
        acc_o[2 * heads + 8 : 2 * heads + 9, :] += colsum(dq.astype(F32))
        acc_o[2 * heads + 9 : 2 * heads + 10, :] += colsum(dk_sum)

        pad[patches:, :] = jnp.zeros((rows - patches, feats), F32)
        pad[0:patches, :] = tok[i].astype(F32)
        da1[...] = nt(dqkv_o[i], wqkv[...])
        gain = row(n1g)
        sums = [jnp.zeros((8, feats), F32) for _ in range(2)]
        for c in chunks(rows):
            n, r = normalized(pad[c, :])
            cot = da1[c, :]
            grad = dx1[i, c, :] + norm_back(cot, n, r, gain)
            sums = [sums[0] + fold(cot * n), sums[1] + fold(cot)]
            if c.stop <= patches:
                in_v[i - first, c, :] = grad
            else:
                in_v[i - first, c.start : patches, :] = grad[0 : patches - c.start]
        for j in range(2):
            acc_o[2 * heads + 11 + j : 2 * heads + 12 + j, :] += colsum(sums[j])
        if first:
            in_copy(i).start()

    if first:
        for i in range(first):
            early_copy(i).wait()

        @pl.loop(first, first + share)
        def _(i):
            in_copy(i).wait()


def qkv_grad_kernel(heads, dqkv, *refs):
    accs = refs[:-8]
    a1, acc_mlp, b1_first, b1_rest, keep, send, small, grads = refs[-8:]
    feats = a1.shape[1]
    count = 2 * keep.shape[0]
    size = 3 * feats // count
    acc = accs[0][...]
    for other in accs[1:]:
        acc = acc + other[...]
    small[...] = jnp.zeros_like(small)
    small[0:2, :] = acc[2 * heads + 11 : 2 * heads + 13]
    small[2:8, :] = acc_mlp[0:6, :]
    small[8:11, :] = acc[2 * heads + 8 : 2 * heads + 11]
    head_dim = feats // heads
    lanes = 2 * heads * heads
    gather = (
        head_of_lane((feats, lanes), 0, head_dim)
        == lax.broadcasted_iota(jnp.int32, (feats, lanes), 1) % heads
    ).astype(F32)
    sums = exact(acc[0 : 2 * heads + 8], gather, ((1,), (0,)))
    place = head_of_lane((2 * heads, lanes), 1, heads) == lax.broadcasted_iota(
        jnp.int32, (2 * heads, lanes), 0
    )
    small[11:12, 0:lanes] = colsum(jnp.where(place, sums[0 : 2 * heads], 0.0))
    small[11:12, lanes : 2 * lanes] = sums[2 * heads : 2 * heads + 1]
    m_idx = lax.axis_index("mp")
    for c, ref in enumerate((b1_first, b1_first, b1_rest, b1_rest)):
        place = 12 + jnp.bitwise_xor(m_idx, c)
        small[pl.ds(place, 1), :] = ref[:, (c % 2) * feats : (c % 2 + 1) * feats]
    low = small[...].astype(BF)
    outs = (keep, send)

    grads[...] = tn(a1[...], dqkv[...]).astype(BF).T

    def put(which, place, b):
        outs[which][place, 0:size, :] = grads[b * size : (b + 1) * size, :]
        outs[which][place, size : size + 16, :] = low
        if outs[which].shape[1] > size + 16:
            outs[which][place, size + 16 :, :] = jnp.zeros_like(outs[which][place, size + 16 :, :])

    store_blocks(count, put)


def final_kernel(heads, size, many, mine, proj_own, *refs):
    got = refs[:many]
    mlp_mine, got_z = refs[many], refs[1 + many : 1 + 2 * many]
    qkv_o, qkvb_o, pre_o, post_o, postb_o, b1_o, *vecs_o, fc1_o, fc2_o, proj_o, held = refs[-18:]
    block, feats = fc1_o.shape
    for place, out in enumerate((fc1_o, fc2_o)):
        rows = slice(place * block, (place + 1) * block)
        out[...] = mlp_mine[rows, :] + sum(g[rows, :].astype(F32) for g in got_z)
    d_idx = lax.axis_index("dp")
    m_idx = lax.axis_index("mp")
    total = mine[...]
    held[m_idx] = proj_own[...].astype(F32)
    for j, part in enumerate(got):
        value = part[...].astype(F32)
        total = total + value[0 : size + 16]
        held[jnp.bitwise_xor(m_idx, j + 1)] = value[size + 16 :]
    proj_o[...] = held[...].reshape(-1, feats)[0:block]
    qkv_o[...] = total[0:size]
    small = total[size : size + 16]

    def own(value, width, index):
        lanes = value.shape[1]
        return pltpu.roll(value, lax.rem(lanes - index * width, lanes), axis=1)[:, 0:width]

    width = vecs_o[0].shape[1]
    vecs = own(small[0:8], width, d_idx)
    for j, ref in enumerate(vecs_o):
        ref[...] = vecs[j : j + 1]
    flat = jnp.concatenate([small[8 + j : 9 + j] for j in range(3)], axis=1)
    qkvb_o[...] = own(jnp.broadcast_to(flat, (8, 3 * feats)), qkvb_o.shape[1], d_idx)[0:1]
    b1 = own(small[8:16], b1_o.shape[1], d_idx)[4:8]
    pick = lax.broadcasted_iota(jnp.int32, b1.shape, 0) == m_idx
    b1_o[...] = colsum(jnp.where(pick, b1, 0.0))
    mix = small[11:12]
    hh = heads * heads
    line = lax.broadcasted_iota(jnp.int32, (heads, hh), 0)
    lane = lax.broadcasted_iota(jnp.int32, (heads, hh), 1)
    fold = (
        lax.broadcasted_iota(jnp.int32, (hh, heads), 0) % heads
        == lax.broadcasted_iota(jnp.int32, (hh, heads), 1)
    ).astype(F32)
    head_dim = feats // heads

    def square(values):
        return exact(jnp.where(lane // heads == line, values, 0.0), fold, ((1,), (0,)))

    post_o[...] = square(mix[:, 0:hh]).T
    pre_o[...] = square(mix[:, hh : 2 * hh]) * (head_dim**-0.5)
    postb_o[...] = mix[:, 2 * hh : 2 * hh + heads]


def whole(shape):
    return pl.BlockSpec(shape, lambda i: (0,) * len(shape))


def each(shape, first=0, many=1):
    return pl.BlockSpec((many,) + shape[1:], lambda i: (i + first,) + (0,) * (len(shape) - 1))


SCALARS = pl.BlockSpec(memory_space=pltpu.SMEM)
IN_VMEM = pl.BlockSpec(memory_space=pltpu.VMEM)
IN_HBM = pl.BlockSpec(memory_space=pltpu.HBM)


def kept(a):
    return pltpu.with_memory_space_constraint(a, pltpu.HBM)


def sds(shape, dtype):
    return jax.ShapeDtypeStruct(shape, dtype)


def call(
    kernel, grid, ins, in_specs, outs, out_specs, scratch=(), flops=0, name=None, aliases=None,
    limit=VMEM_LIMIT,
):
    size = lambda a: a.size * a.dtype.itemsize
    return pl.pallas_call(
        kernel,
        grid=grid,
        in_specs=in_specs,
        out_specs=out_specs,
        out_shape=outs,
        scratch_shapes=scratch,
        input_output_aliases=aliases or {},
        compiler_params=pltpu.CompilerParams(vmem_limit_bytes=limit),
        cost_estimate=pl.CostEstimate(
            flops=flops,
            bytes_accessed=sum(size(a) for a in ins) + sum(size(a) for a in outs),
            transcendentals=0,
        ),
        name=name,
    )(*ins)


def xor_perm(count, mask):
    return [(j, j ^ mask) for j in range(count)]


def dp_hops(dp):
    bits = dp.bit_length() - 1
    groups = []
    at = 1
    while at < bits:
        groups.append((at, min(2, bits - at)))
        at += groups[-1][1]
    return groups


def dp_scatter(value, dp):
    for at, many in dp_hops(dp):
        value = value.reshape((-1, 1 << many) + value.shape[1:])
        got = [
            lax.ppermute(value[:, j].astype(BF), "dp", xor_perm(dp, j << at))
            for j in range(1, 1 << many)
        ]
        value = value[:, 0] + sum(g.astype(F32) for g in got)
    return value.reshape(value.shape[-2:])


def per_device(
    dp, mp,
    tokens_in, image_counts, norm1_gain, norm1_bias, qkv_weight, qkv_bias,
    mix_pre, mix_post, mix_post_bias, proj_weight, proj_bias, gamma1,
    norm2_gain, norm2_bias, fc1_weight, fc1_bias, fc2_weight, fc2_bias, gamma2, out_grad,
):
    images, patches, feats = tokens_in.shape
    heads = mix_pre.shape[0]
    rows = -(-patches // 16) * 16
    slots = -(-patches // 128) * 128
    hidden = fc1_weight.shape[1]
    tok_rows = (images, rows, feats)
    slot_rows = (images, slots, feats)
    prob_shape = (images, heads, rows, slots)
    mix_shape = (heads, feats)
    operands = [
        tokens_in, out_grad, norm1_gain, norm1_bias, qkv_bias, mix_pre, mix_post,
        mix_post_bias, proj_bias, gamma1, norm2_gain, norm2_bias, qkv_weight, proj_weight,
    ]

    ins = [kept(a) for a in [fc1_weight, fc2_weight, fc1_bias] + operands]
    outs = [sds((feats + 16, hidden), BF)] + [sds(a.shape, a.dtype) for a in operands]
    other, *held = call(
        pack_kernel,
        (),
        ins,
        [IN_HBM] * len(ins),
        outs,
        [IN_VMEM] * len(outs),
        [pltpu.VMEM(fc1_bias.shape, F32), pltpu.SemaphoreType.DMA((2 + len(operands),))],
        name="pack",
    )
    near = [lax.ppermute(other, "mp", xor_perm(mp, j)) for j in (1, 2)]

    shares = [images - 1, 1] if images > 1 else [images]
    tables = [sds(mix_shape, F32), sds(mix_shape, F32), sds((1, feats), F32)]
    carried = []
    for s, share in enumerate(shares):
        first = sum(shares[:s])
        ins = [image_counts, mix_post, mix_post_bias] + held + ([mpre] if first else [])
        outs = call(
            functools.partial(attn_fwd_kernel, first, share),
            (),
            ins + carried,
            [SCALARS] * 3
            + [IN_VMEM] * (len(ins) - 3)
            + [pl.BlockSpec(memory_space=pl.ANY)] * len(carried),
            [
                sds(tok_rows, BF), sds(slot_rows, BF), sds(tok_rows, BF), sds(tok_rows, BF),
                sds(prob_shape, BF), sds(tok_rows, BF), sds(tok_rows, F32), sds(tok_rows, F32),
                sds(tok_rows, BF), sds(tok_rows, BF),
            ]
            + ([] if first else tables),
            [IN_VMEM] * (10 if first else 13),
            [
                pltpu.VMEM((rows, feats), F32), pltpu.VMEM((heads * rows, 2 * feats), BF),
                pltpu.VMEM((feats, slots), BF), pltpu.VMEM((rows, 3 * feats), F32), pltpu.VMEM((heads * rows, slots), F32),
                pltpu.VMEM((heads, feats, slots), F32),
            ],
            flops=share * 15 * 10**8,
            name="attn_fwd",
            aliases={len(ins) + j: j for j in range(10)} if carried else None,
        )
        carried = list(outs[:10])
        if not first:
            mpre, mpost, mixb = outs[10:]
        if s == 0:
            near, carried[0] = lax.optimization_barrier((near, carried[0]))
            last = lax.ppermute(near[1], "mp", xor_perm(mp, 1))
            near = jnp.stack(near)
            far = lax.ppermute(near, "dp", xor_perm(dp, 1))
    a1, q, k, v, prob, o, x1, u, a2, dy = carried
    far, a2 = lax.optimization_barrier((far, a2))

    block = feats // dp
    total = images * rows
    flat = (total, feats)
    a2, dy, x1, u, o = (a.reshape(flat) for a in (a2, dy, x1, u, o))
    ins = [a2, dy, gamma2, fc1_weight, fc1_bias, fc2_weight, near, far]
    wide = 2 * hidden
    grad_shape = (2, wide, feats)
    f0, da20, hids, dzs, dfs = call(
        mlp_first_kernel,
        (),
        ins,
        [IN_VMEM] * len(ins),
        [
            sds(flat, F32), sds(flat, F32), sds((total, wide), BF), sds((total, wide), BF),
            sds(flat, BF),
        ],
        [IN_VMEM] * 5,
        [
            pltpu.VMEM((feats, wide), BF), pltpu.VMEM((wide, feats), BF),
            pltpu.VMEM((1, wide), F32),
            pltpu.VMEM((2, total // 3, 256), F32), pltpu.VMEM((2, total // 3, 256), F32),
        ],
        flops=images * 5 * 10**8,
        name="mlp_first",
    )

    last, f0 = lax.optimization_barrier((last, f0))
    far_last = lax.ppermute(last, "dp", xor_perm(dp, 1))
    ins = [a2, hids, dzs, dfs]
    grads0, b1_0, a2t, dft = call(
        mlp_grad_kernel,
        (),
        ins,
        [IN_VMEM] * 4,
        [
            sds(grad_shape, BF), sds((1, wide), F32), sds((feats + 16, total), BF),
            sds((feats, total), BF),
        ],
        [IN_VMEM] * 4,
        flops=images * 3 * 10**8,
        name="mlp_grad",
    )

    grad_rows = 9 * block
    half_shape = (dp // 2, grad_rows, feats)
    ins = [
        image_counts, a2, dy, dfs, x1, u, o, f0, da20, near, far, last, far_last, grads0, a2t, dft,
        proj_weight, gamma1,
        norm2_gain, fc2_bias, gamma2,
    ]
    layer_out, dx1, do, keep, send, b1_1, acc_mlp = call(
        mlp_rest_kernel,
        (),
        ins,
        [SCALARS] + [IN_VMEM] * (len(ins) - 1),
        [
            sds(tokens_in.shape, BF), sds(flat, F32), sds(slot_rows, BF), sds(half_shape, BF),
            sds(half_shape, BF), sds((1, wide), F32), sds((8, feats), F32),
        ],
        [IN_HBM] + [IN_VMEM] * 6,
        [
            pltpu.VMEM((feats, wide), BF), pltpu.VMEM((wide, feats), BF),
            pltpu.VMEM((1, wide), F32), pltpu.VMEM((total, wide), BF),
            pltpu.VMEM((total, wide), BF),
            pltpu.VMEM((2, total // 3, 256), F32), pltpu.VMEM((2, total // 3, 256), F32),
            pltpu.VMEM(flat, F32), pltpu.VMEM(flat, F32), pltpu.VMEM(flat, BF),
            pltpu.VMEM((wide, feats), BF), pltpu.VMEM((feats, wide), BF),
            pltpu.VMEM((feats, feats), BF), pltpu.VMEM(tokens_in.shape, BF),
            pltpu.SemaphoreType.DMA((images,)),
        ],
        flops=images * 9 * 10**8,
        name="mlp_rest",
    )
    got = lax.ppermute(send, "dp", xor_perm(dp, 1))
    dx1 = dx1.reshape(tok_rows)

    shares = [1, images - 1] if images > 1 else [1]
    dqkv_shape = (images, rows, 3 * feats)
    carried, accs = [], []
    for s, share in enumerate(shares):
        first = sum(shares[:s])
        ins = [mix_pre, do, q, k, v, prob, dx1, tokens_in, mpre, mpost, mixb, qkv_weight, norm1_gain]
        in_shape = tokens_in.shape if first or share == images else (share,) + tokens_in.shape[1:]
        *carried, acc = call(
            functools.partial(attn_bwd_kernel, first, share),
            (),
            ins + carried,
            [SCALARS]
            + [IN_VMEM] * (len(ins) - 1)
            + [pl.BlockSpec(memory_space=pl.ANY), IN_VMEM][: len(carried)],
            [sds(dqkv_shape, BF), sds(in_shape, F32), sds((2 * heads + 16, feats), F32)],
            [IN_VMEM, IN_HBM if first else IN_VMEM, IN_VMEM],
            [
                pltpu.VMEM((heads * rows, feats), BF), pltpu.VMEM((heads * rows, slots), BF),
                pltpu.VMEM((feats, slots), BF), pltpu.VMEM((heads * rows, slots), F32),
                pltpu.VMEM((heads * rows, feats), F32), pltpu.VMEM((heads * rows, feats), F32),
                pltpu.VMEM((heads, feats, slots), F32), pltpu.VMEM((rows, feats), F32),
                pltpu.VMEM((rows, feats), F32),
            ]
            + [pltpu.VMEM((share, patches, feats), F32), pltpu.SemaphoreType.DMA((images,))]
            * bool(first),
            flops=share * 20 * 10**8,
            name="attn_bwd",
            aliases={len(ins): 0} if carried else None,
        )
        accs.append(acc)
        if s == 0:
            (keep, got), acc = lax.optimization_barrier(((keep, got), acc))
            mine = dp_scatter(keep.astype(F32) + got.astype(F32), dp)
            accs[0], do = lax.optimization_barrier((acc, do))
    dqkv, in_grad = carried
    mine, dqkv = lax.optimization_barrier((mine, dqkv))
    mlp_mine = mine
    low = mine.astype(BF)
    m_idx = lax.axis_index("mp")
    share_rows = -(-block // (16 * mp)) * 16
    proj = jnp.pad(mine[8 * block :], ((0, mp * share_rows - block), (0, 0)))

    def proj_share(j):
        return lax.dynamic_slice_in_dim(proj, jnp.bitwise_xor(m_idx, j) * share_rows, share_rows)

    got_z = [
        lax.ppermute(
            jnp.concatenate([low[2 * j * block : 2 * (j + 1) * block], proj_share(j).astype(BF)]),
            "mp",
            xor_perm(mp, j),
        )
        for j in range(1, mp)
    ]

    q_block = 3 * feats // dp
    half_shape = (dp // 2, q_block + 16, feats)
    ins = [dqkv.reshape(total, 3 * feats)] + accs + [a1.reshape(flat), acc_mlp, b1_0, b1_1]
    keep, send = call(
        functools.partial(qkv_grad_kernel, heads),
        (),
        ins,
        [IN_VMEM] * len(ins),
        [sds(half_shape, BF), sds(half_shape, BF)],
        [IN_VMEM] * 2,
        [pltpu.VMEM((16, feats), F32), pltpu.VMEM((3 * feats, feats), BF)],
        flops=11 * 10**8,
        name="qkv_grad",
    )
    got = lax.ppermute(send, "dp", xor_perm(dp, 1))
    mine = dp_scatter(keep.astype(F32) + got.astype(F32), dp)
    mine, got_z = lax.optimization_barrier((mine, got_z))

    proj_own = (proj_share(0) + sum(g[2 * block :].astype(F32) for g in got_z)).astype(BF)
    payload = jnp.concatenate([mine.astype(BF), proj_own])
    got = [lax.ppermute(payload, "mp", xor_perm(mp, j)) for j in range(1, mp)]
    b1_size = hidden // dp
    ins = [mine, proj_own] + got + [mlp_mine] + got_z
    outs = [
        sds((q_block, feats), F32), sds((1, q_block), F32), sds((heads, heads), F32),
        sds((heads, heads), F32), sds((1, heads), F32), sds((1, b1_size), F32),
    ] + [sds((1, block), F32)] * 8 + [sds((block, feats), F32)] * 3
    qkvw, qkvb, pre, post, postb, b1g, *vecs, fc1g, fc2g, projg = call(
        functools.partial(final_kernel, heads, q_block, mp - 1),
        (),
        ins,
        [IN_VMEM] * len(ins),
        outs,
        [IN_VMEM] * len(outs),
        [pltpu.VMEM((mp, share_rows, feats), F32)],
        name="final",
    )
    vecs = [a.reshape(-1) for a in vecs]
    return (
        layer_out,
        in_grad,
        vecs[0],
        vecs[1],
        qkvw.T,
        qkvb.reshape(-1),
        pre,
        post,
        postb.reshape(-1),
        projg.T,
        vecs[2],
        vecs[3],
        vecs[4],
        vecs[5],
        fc1g.T,
        b1g.reshape(-1),
        fc2g.T,
        vecs[6],
        vecs[7],
    )


def solution(mesh):
    tokens = P(("dp", "mp"), None, None)
    placed = (
        (tokens, P("dp")) + (P(),) * 12 + (P(None, "mp"), P("mp"), P("mp", None), P(), P(), tokens)
    )
    return jax.shard_map(
        functools.partial(per_device, mesh.shape["dp"], mesh.shape["mp"]),
        mesh=mesh,
        in_specs=placed,
        out_specs=(
            tokens, tokens, P("dp"), P("dp"), P(None, "dp"), P("dp"), P(), P(), P(),
            P(None, "dp"), P("dp"), P("dp"), P("dp"), P("dp"), P(None, ("mp", "dp")),
            P(("mp", "dp")), P("mp", "dp"), P("dp"), P("dp"),
        ),
        check_vma=False,
    )
```
